32 devices in a mesh: seq: 8 (over y, x, core), wshard: 4 (over z).
Axes of the slice: x: 2, y: 2, z: 4, core: 2. Of those that a mesh axis runs over, the one named last changes fastest.
Arguments:
- tokens: bfloat16 [4, 4096, 1024], P('wshard', 'seq'), may hold values from -6 to 6
- slot_lengths: int32 [4, 3], P('wshard'), may hold values from 1 to 3584, as said below
- live_lengths: int32 [4, 3], P('wshard'), may hold values from 1 to 3584, as said below
- norm_gain: bfloat16 [1024], P('wshard'), may hold values from 0.099609375 to 1.8984375
- w_qkv: bfloat16 [1024, 3072], P('wshard'), may hold values from -0.1875 to 0.1875
- w_beta: bfloat16 [1024, 8], P('wshard'), may hold values from -0.1875 to 0.1875
- w_outgate: bfloat16 [1024, 1024], P('wshard'), may hold values from -0.1875 to 0.1875
- conv_weight: bfloat16 [4, 3072], P(None, 'wshard'), may hold values from -3 to 3
- ridge: bfloat16 [1024], P('wshard'), may hold values from 0.5 to 4
- head_gain: bfloat16 [1024], P('wshard'), may hold values from 0.099609375 to 1.8984375
- w_out: bfloat16 [1024, 1024], P('wshard'), may hold values from -0.1875 to 0.1875
- ffn_gain: bfloat16 [1024], P('wshard'), may hold values from 0.099609375 to 1.8984375
- w_gate: bfloat16 [1024, 2816], P('wshard'), may hold values from -0.1875 to 0.1875
- w_up: bfloat16 [1024, 2816], P('wshard'), may hold values from -0.1875 to 0.1875
- w_down: bfloat16 [2816, 1024], P('wshard'), may hold values from -0.109375 to 0.109375
- cotangent: bfloat16 [4, 4096, 1024], P('wshard', 'seq'), may hold values from -6 to 6
Outputs:
- output: bfloat16 [4, 4096, 1024], P('wshard', 'seq')
- grad_tokens: bfloat16 [4, 4096, 1024], P('wshard', 'seq')
- grad_norm_gain: float32 [1024], P('wshard')
- grad_w_qkv: float32 [1024, 3072], P('wshard')
- grad_w_beta: float32 [1024, 8], P('wshard')
- grad_w_outgate: float32 [1024, 1024], P('wshard')
- grad_conv_weight: float32 [4, 3072], P(None, 'wshard')
- grad_ridge: float32 [1024], P('wshard')
- grad_head_gain: float32 [1024], P('wshard')
- grad_w_out: float32 [1024, 1024], P('wshard')
- grad_ffn_gain: float32 [1024], P('wshard')
- grad_w_gate: float32 [1024, 2816], P('wshard')
- grad_w_up: float32 [1024, 2816], P('wshard')
- grad_w_down: float32 [2816, 1024], P('wshard')
The draws below stay inside these ranges and needn't reach their ends.
Inputs may be any that keep to these rules, and one draw needn't show every extreme that they name: `slot_lengths`: each batch row has three slots that cover its 4096 positions in order: a head slot shorter than 512, a middle slot of exactly 3584 positions, and a tail slot; head and tail together hold 512 positions. `live_lengths`: A live length is at least 1 and at most its slot's length; the middle slot is live in full.
All inputs are finite; a program needn't handle non-finite values.
Results may differ from the reference program's by a relative error of at most 0.018.
The reference program's roundings to bfloat16 on the way count: a program that leaves them out, or rounds other values in their place, can miss the bound.
Values may be sent and summed in bfloat16 or wider, within the bound.
A program may use at most 256 MiB of HBM per device.

```python
import math
import jax
import jax.numpy as jnp
from jax import lax

D = 1024
HEADS = 8
HEAD_DIM = 128
FF = 2816
TAPS = 4
WINDOW = 1024
ITERS = 2
TOK_DEV = 512
SEQ_TOK = 4096
BATCH = 4


def slot_plan(key):
    heads_len = jax.random.randint(key, (BATCH, 1), 1, TOK_DEV, dtype=jnp.int32)
    middle = jnp.full((BATCH, 1), SEQ_TOK - TOK_DEV, jnp.int32)
    tails_len = (TOK_DEV - heads_len).astype(jnp.int32)
    return jnp.concatenate([heads_len, middle, tails_len], axis=1).astype(jnp.int32)


def draw_slot_lengths(key, part):
    slots = slot_plan(key)
    return slots


def draw_live_lengths(key, part):
    slots = slot_plan(key)
    key = jax.random.fold_in(key, 5)
    drawn = jax.random.randint(key, slots.shape, 0, 1 << 20, dtype=jnp.int32)
    trimmed = (1 + drawn % slots).astype(jnp.int32)
    column = jnp.arange(3, dtype=jnp.int32)[None, :]
    return jnp.where(column == 1, slots, trimmed).astype(jnp.int32)


def shard_levels(key, extent, cuts, low, largest):
    level, own = 1.0, jax.random.fold_in(key, 6)
    for dim, blocks in cuts:
        draws = jnp.exp(jax.random.uniform(jax.random.fold_in(own, dim), (blocks,), jnp.float32, low / len(cuts), largest / len(cuts)))
        level = level * jnp.repeat(draws, extent[dim] // blocks).reshape([-1 if axis == dim else 1 for axis in range(len(extent))])
    return level


def scatter_about(key, dims, spread, most, split=(), held_as=jnp.bfloat16):
    values = spread * jax.random.normal(key, dims, jnp.float32)
    if split:
        values = values * shard_levels(key, dims, split, -0.22, 0.18)
    return jnp.clip(values, -most, most).astype(held_as)


def setup_inputs(seed: int = 0) -> dict:
    seeds = jax.random.split(jax.random.key(seed), 17)
    return {
        "tokens": scatter_about(seeds[0], (BATCH, SEQ_TOK, D), 1.0, 6.0, ((0, 4), (1, 8))),
        "slot_lengths": draw_slot_lengths(jax.random.fold_in(seeds[16], 71), 0),
        "live_lengths": draw_live_lengths(jax.random.fold_in(seeds[16], 71), 0),
        "norm_gain": jnp.clip(1.0 + 0.18 * jax.random.normal(seeds[3], (D,), jnp.float32), 0.099609375, 1.8984375).astype(jnp.bfloat16),
        "w_qkv": scatter_about(seeds[4], (D, 3 * D), D ** -0.5, 0.1875, ((0, 4),)),
        "w_beta": scatter_about(seeds[5], (D, HEADS), D ** -0.5, 0.1875, ((0, 4),)),
        "w_outgate": scatter_about(seeds[6], (D, D), D ** -0.5, 0.1875, ((0, 4),)),
        "conv_weight": scatter_about(seeds[7], (TAPS, 3 * D), 0.5, 3.0, ((1, 4),)),
        "ridge": jnp.clip(jnp.exp(math.log(4.0) - 2.0794415 * jax.random.uniform(seeds[8], (D,), jnp.float32) ** shard_levels(seeds[8], (D,), ((0, 4),), -0.2, 0.2)), 0.5, 4.0).astype(jnp.bfloat16),
        "head_gain": jnp.clip(1.0 + 0.18 * jax.random.normal(seeds[9], (D,), jnp.float32), 0.099609375, 1.8984375).astype(jnp.bfloat16),
        "w_out": scatter_about(seeds[10], (D, D), D ** -0.5, 0.1875, ((0, 4),)),
        "ffn_gain": jnp.clip(1.0 + 0.18 * jax.random.normal(seeds[11], (D,), jnp.float32), 0.099609375, 1.8984375).astype(jnp.bfloat16),
        "w_gate": scatter_about(seeds[12], (D, FF), D ** -0.5, 0.1875, ((0, 4),)),
        "w_up": scatter_about(seeds[13], (D, FF), D ** -0.5, 0.1875, ((0, 4),)),
        "w_down": scatter_about(seeds[14], (FF, D), FF ** -0.5, 0.109375, ((0, 4),)),
        "cotangent": scatter_about(seeds[15], (BATCH, SEQ_TOK, D), 1.0, 6.0, ((0, 4), (1, 8))),
    }


@jax.custom_vjp
def low(v):
    return lax.optimization_barrier(v.astype(jnp.bfloat16)).astype(jnp.float32)

@jax.custom_vjp
def low_back(v):
    return v

def low_keep(v):
    return (low(v), None)

def low_pass(kept, grad):
    return (grad,)

def back_keep(v):
    return (v, None)

def back_low(kept, grad):
    return (low(grad),)
low.defvjp(low_keep, low_pass)
low_back.defvjp(back_keep, back_low)

def matmul(left, right):
    return jnp.dot(left, right, precision=lax.Precision.HIGHEST, preferred_element_type=jnp.float32)

def matmul_t(left, right):
    return lax.dot_general(left, right, (((1,), (1,)), ((), ())), precision=lax.Precision.HIGHEST, preferred_element_type=jnp.float32)

def token_layout(slot_row, live_row, positions):
    starts = (jnp.cumsum(slot_row) - slot_row).astype(jnp.int32)
    after = positions[:, None] >= starts[None, :]
    segment = (lax.optimization_barrier(jnp.sum(after.astype(jnp.int32), axis=1)) - 1).astype(jnp.int32)
    chosen = segment[:, None] == jnp.arange(slot_row.shape[0], dtype=jnp.int32)[None, :]
    begin = lax.optimization_barrier(jnp.sum(jnp.where(chosen, starts[None, :], 0), axis=1)).astype(jnp.int32)
    limit = lax.optimization_barrier(jnp.sum(jnp.where(chosen, live_row[None, :], 0), axis=1)).astype(jnp.int32)
    valid = (segment >= 0) & (positions - begin < limit)
    return (segment, valid)

def conv_same(seg_conv, seg_own):
    row_count = seg_own.shape[0]
    stacked = jnp.stack([seg_conv[TAPS - 1 - tap_index:TAPS - 1 - tap_index + row_count] == seg_own for tap_index in range(TAPS)])
    return stacked.astype(jnp.float32)[:, :, None]

def build_mask(query_pos, key_pos, seg_queries, seg_keys, valid_keys):
    spacing = query_pos[:, None] - key_pos[None, :]
    inside = (spacing >= 0) & (spacing < WINDOW) & (seg_keys[None, :] == seg_queries[:, None]) & valid_keys[None, :]
    return inside.astype(jnp.float32)

def by_heads(array):
    return array.reshape(array.shape[0], HEADS, HEAD_DIM).transpose(1, 0, 2)

def from_heads(array):
    return array.transpose(1, 0, 2).reshape(array.shape[1], D)

def section_in(xrow, gain_in, mat_qkv, mat_beta, mat_og):
    hidden = low(xrow * lax.rsqrt(lax.optimization_barrier(jnp.mean(xrow * xrow, axis=-1, keepdims=True)) + 1e-06) * gain_in)
    qkv = low_back(low(matmul(hidden, mat_qkv)))
    beta = low(jax.nn.sigmoid(low_back(matmul(hidden, mat_beta))))
    gate_pre = low_back(matmul(hidden, mat_og))
    return (qkv, beta, gate_pre)

def section_conv(qkv_ext, conv_taps, same):
    row_count = qkv_ext.shape[0] - (TAPS - 1)
    total = jnp.zeros((row_count, qkv_ext.shape[1]), jnp.float32)
    for tap_index in range(TAPS):
        source = qkv_ext[TAPS - 1 - tap_index:TAPS - 1 - tap_index + row_count]
        total = total + conv_taps[tap_index] * source * same[tap_index]
    active = jax.nn.silu(total)

    def unit_rows(block):
        shaped = block.reshape(row_count, HEADS, HEAD_DIM)
        shaped = shaped * lax.rsqrt(lax.optimization_barrier(jnp.sum(shaped * shaped, axis=-1, keepdims=True)) + 1e-06)
        return shaped.reshape(row_count, D)
    return (low(unit_rows(active[:, :D])), low(unit_rows(active[:, D:2 * D])), low(active[:, 2 * D:]))

def head_mix(queries, key_rows, value_rows, weight, ridge_head, window_mask):
    scaling = window_mask * weight[None, :]

    def apply_stats(vector):
        scores = low_back(matmul_t(low(vector), key_rows))
        return low_back(matmul(low(scaling * scores), key_rows)) + ridge_head[None, :] * vector
    solution = jnp.zeros_like(queries)
    residue = queries
    direction = queries
    energy = lax.optimization_barrier(jnp.sum(residue * residue, axis=-1, keepdims=True))
    for sweep in range(ITERS):
        image_vec = apply_stats(direction)
        step_size = energy / lax.optimization_barrier(jnp.sum(direction * image_vec, axis=-1, keepdims=True))
        solution = solution + step_size * direction
        residue = residue - step_size * image_vec
        energy_next = lax.optimization_barrier(jnp.sum(residue * residue, axis=-1, keepdims=True))
        direction = residue + energy_next / energy * direction
        energy = energy_next
    scores = low_back(matmul_t(low(solution), key_rows))
    return low_back(matmul(low(scaling * scores), value_rows))

def section_out(xrow, mixed, gate_pre, gain_head, mat_out, gain_ffn, mat_gate, mat_up, mat_down, valid):
    row_count = xrow.shape[0]
    shaped = mixed.reshape(row_count, HEADS, HEAD_DIM)
    shaped = shaped * lax.rsqrt(lax.optimization_barrier(jnp.mean(shaped * shaped, axis=-1, keepdims=True)) + 1e-05)
    normed = shaped.reshape(row_count, D) * gain_head
    gated = low(normed * jax.nn.silu(gate_pre))
    middle = xrow + low_back(matmul(gated, mat_out))
    hidden = low(middle * lax.rsqrt(lax.optimization_barrier(jnp.mean(middle * middle, axis=-1, keepdims=True)) + 1e-06) * gain_ffn)
    inner = low(jax.nn.silu(low_back(matmul(hidden, mat_gate))) * low_back(matmul(hidden, mat_up)))
    return valid[:, None] * (middle + low_back(matmul(inner, mat_down)))

def row_forward(xrow, slot_row, live_row, gain_in, mat_qkv, mat_beta, mat_og, conv_taps, ridge_all, gain_head, mat_out, gain_ffn, mat_gate, mat_up, mat_down):
    positions = jnp.arange(SEQ_TOK, dtype=jnp.int32)
    segment, valid = token_layout(slot_row, live_row, positions)
    qkv, beta, gate_pre = section_in(xrow, gain_in, mat_qkv, mat_beta, mat_og)
    seg_conv = jnp.concatenate([jnp.full((TAPS - 1,), -1, jnp.int32), segment])
    same = conv_same(seg_conv, segment)
    qkv_ext = jnp.concatenate([jnp.zeros((TAPS - 1, 3 * D), jnp.float32), qkv])
    queries, key_rows, value_rows = section_conv(qkv_ext, conv_taps, same)
    depth = (WINDOW + TOK_DEV - 1) // TOK_DEV
    halo_rows = depth * TOK_DEV
    span = halo_rows + TOK_DEV
    key_pad = jnp.concatenate([jnp.zeros((halo_rows, D), jnp.float32), key_rows])
    value_pad = jnp.concatenate([jnp.zeros((halo_rows, D), jnp.float32), value_rows])
    beta_pad = jnp.concatenate([jnp.zeros((halo_rows, HEADS), jnp.float32), beta])
    seg_pad = jnp.concatenate([jnp.full((halo_rows,), -1, jnp.int32), segment])
    valid_pad = jnp.concatenate([jnp.zeros((halo_rows,), bool), valid])
    ridge_heads = ridge_all.reshape(HEADS, HEAD_DIM)

    def one_block(block_index):
        offset = (block_index * TOK_DEV).astype(jnp.int32)
        query_block = lax.dynamic_slice_in_dim(queries, offset, TOK_DEV, 0)
        key_block = lax.dynamic_slice_in_dim(key_pad, offset, span, 0)
        value_block = lax.dynamic_slice_in_dim(value_pad, offset, span, 0)
        beta_block = lax.dynamic_slice_in_dim(beta_pad, offset, span, 0)
        seg_keys = lax.dynamic_slice_in_dim(seg_pad, offset, span, 0)
        valid_keys = lax.dynamic_slice_in_dim(valid_pad, offset, span, 0)
        seg_queries = lax.dynamic_slice_in_dim(segment, offset, TOK_DEV, 0)
        query_pos = offset + jnp.arange(TOK_DEV, dtype=jnp.int32)
        key_pos = offset - halo_rows + jnp.arange(span, dtype=jnp.int32)
        window_mask = build_mask(query_pos, key_pos, seg_queries, seg_keys, valid_keys)
        heads_out = jax.vmap(head_mix, in_axes=(0, 0, 0, 0, 0, None))(by_heads(query_block), by_heads(key_block), by_heads(value_block), beta_block.T, ridge_heads, window_mask)
        return from_heads(heads_out)
    mixed = lax.map(jax.checkpoint(one_block), jnp.arange(SEQ_TOK // TOK_DEV, dtype=jnp.int32))
    mixed = mixed.reshape(SEQ_TOK, D)
    return section_out(xrow, mixed, gate_pre, gain_head, mat_out, gain_ffn, mat_gate, mat_up, mat_down, valid.astype(jnp.float32))

def reference(tokens, slot_lengths, live_lengths, norm_gain, w_qkv, w_beta, w_outgate, conv_weight, ridge, head_gain, w_out, ffn_gain, w_gate, w_up, w_down, cotangent):
    params = tuple((member.astype(jnp.float32) for member in (norm_gain, w_qkv, w_beta, w_outgate, conv_weight, ridge, head_gain, w_out, ffn_gain, w_gate, w_up, w_down)))

    def one_row(row_index):
        xrow = tokens[row_index].astype(jnp.float32)
        slot_row = slot_lengths[row_index]
        live_row = live_lengths[row_index]

        def forward(xrow, *weights):
            return row_forward(xrow, slot_row, live_row, *weights)
        result, pullback = jax.vjp(forward, xrow, *params)
        grads = pullback(cotangent[row_index].astype(jnp.float32))
        return (result, grads)
    results, grads = lax.map(one_row, jnp.arange(BATCH, dtype=jnp.int32))
    sums = [lax.optimization_barrier(jnp.sum(member, axis=0)) for member in grads[1:]]
    return (results.astype(jnp.bfloat16), grads[0].astype(jnp.bfloat16), sums[0], sums[1], sums[2], sums[3], sums[4], sums[5], sums[6], sums[7], sums[8], sums[9], sums[10], sums[11])
```

```python
import jax
import jax.numpy as jnp
from jax import lax
from jax.sharding import PartitionSpec as P

D = 1024
HEADS = 8
HEAD_DIM = 128
TAPS = 4
WINDOW = 1024
ITERS = 2


def passed_along(value, axis, steps):
    count = lax.axis_size(axis)
    initial, last = (max(0, -steps), min(count, count - steps))
    return lax.ppermute(value, axis, [(source, source + steps) for source in range(initial, last)])


def token_layout(slot_row, live_row, positions):
    starts = (jnp.cumsum(slot_row) - slot_row).astype(jnp.int32)
    after = positions[:, None] >= starts[None, :]
    segment = (jnp.sum(after.astype(jnp.int32), axis=1) - 1).astype(jnp.int32)
    chosen = segment[:, None] == jnp.arange(slot_row.shape[0], dtype=jnp.int32)[None, :]
    begin = jnp.sum(jnp.where(chosen, starts[None, :], 0), axis=1).astype(jnp.int32)
    limit = jnp.sum(jnp.where(chosen, live_row[None, :], 0), axis=1).astype(jnp.int32)
    valid = (segment >= 0) & (positions - begin < limit)
    return (segment, valid)


def conv_same(seg_conv, seg_own):
    row_count = seg_own.shape[0]
    stacked = jnp.stack(
        [
            seg_conv[TAPS - 1 - tap_index : TAPS - 1 - tap_index + row_count] == seg_own
            for tap_index in range(TAPS)
        ]
    )
    return stacked.astype(jnp.float32)[:, :, None]


def build_mask(query_pos, key_pos, seg_queries, seg_keys, valid_keys):
    spacing = query_pos[:, None] - key_pos[None, :]
    inside = (
        (spacing >= 0)
        & (spacing < WINDOW)
        & (seg_keys[None, :] == seg_queries[:, None])
        & valid_keys[None, :]
    )
    return inside.astype(jnp.float32)


def by_heads(array):
    return array.reshape(array.shape[0], HEADS, HEAD_DIM).transpose(1, 0, 2)


def from_heads(array):
    return array.transpose(1, 0, 2).reshape(array.shape[1], D)


def make_kit():

    @jax.custom_vjp
    def low(v):
        return lax.optimization_barrier(v.astype(jnp.bfloat16)).astype(jnp.float32)

    @jax.custom_vjp
    def low_back(v):
        return v

    def low_keep(v):
        return (low(v), None)

    def low_pass(kept, grad):
        return (grad,)

    def back_keep(v):
        return (v, None)

    def back_low(kept, grad):
        return (low(grad),)

    low.defvjp(low_keep, low_pass)
    low_back.defvjp(back_keep, back_low)

    @jax.custom_vjp
    def matmul(left, right):
        return jnp.dot(
            left.astype(jnp.bfloat16),
            right.astype(jnp.bfloat16),
            preferred_element_type=jnp.float32,
        )

    def matmul_keep(left, right):
        left_low = left.astype(jnp.bfloat16)
        right_low = right.astype(jnp.bfloat16)
        return (
            jnp.dot(left_low, right_low, preferred_element_type=jnp.float32),
            (left_low, right_low),
        )

    def matmul_grads(kept, grad):
        left_low, right_low = kept
        grad_low = grad.astype(jnp.bfloat16)
        grad_left = lax.dot_general(
            grad_low, right_low, (((1,), (1,)), ((), ())), preferred_element_type=jnp.float32
        )
        grad_right = lax.dot_general(
            left_low, grad_low, (((0,), (0,)), ((), ())), preferred_element_type=jnp.float32
        )
        return (grad_left, grad_right)

    matmul.defvjp(matmul_keep, matmul_grads)

    @jax.custom_vjp
    def matmul_t(left, right):
        return lax.dot_general(
            left.astype(jnp.bfloat16),
            right.astype(jnp.bfloat16),
            (((1,), (1,)), ((), ())),
            preferred_element_type=jnp.float32,
        )

    def matmul_t_keep(left, right):
        left_low = left.astype(jnp.bfloat16)
        right_low = right.astype(jnp.bfloat16)
        value = lax.dot_general(
            left_low, right_low, (((1,), (1,)), ((), ())), preferred_element_type=jnp.float32
        )
        return (value, (left_low, right_low))

    def matmul_t_grads(kept, grad):
        left_low, right_low = kept
        grad_low = grad.astype(jnp.bfloat16)
        grad_left = jnp.dot(grad_low, right_low, preferred_element_type=jnp.float32)
        grad_right = lax.dot_general(
            grad_low, left_low, (((0,), (0,)), ((), ())), preferred_element_type=jnp.float32
        )
        return (grad_left, grad_right)

    matmul_t.defvjp(matmul_t_keep, matmul_t_grads)

    def section_in(x_ext, gain_in, mat_qkv, mat_beta, mat_og, conv_taps, same, halo_rows):
        hidden = low(
            x_ext * lax.rsqrt(jnp.mean(x_ext * x_ext, axis=-1, keepdims=True) + 1e-06) * gain_in
        )
        skip = PRE - (TAPS - 1)
        q_in = low_back(low(matmul(hidden[halo_rows:], mat_qkv[:, :D])))
        kv_in = low_back(low(matmul(hidden, mat_qkv[:, D:])))
        beta = low(jax.nn.sigmoid(low_back(matmul(hidden[PRE:], mat_beta))))
        gate_pre = low_back(matmul(hidden[PRE + halo_rows :], mat_og))
        queries = section_conv(q_in[skip:], conv_taps[:, :D], same[:, halo_rows:], True)
        keys = section_conv(kv_in[skip:, :D], conv_taps[:, D : 2 * D], same, True)
        values = section_conv(kv_in[skip:, D:], conv_taps[:, 2 * D :], same, False)
        return (queries, keys, values, beta, gate_pre)

    def section_conv(rows_in, conv_taps, same, unit):
        row_count = rows_in.shape[0] - (TAPS - 1)
        total = jnp.zeros((row_count, rows_in.shape[1]), jnp.float32)
        for tap_index in range(TAPS):
            source = rows_in[TAPS - 1 - tap_index : TAPS - 1 - tap_index + row_count]
            total = total + conv_taps[tap_index] * source * same[tap_index]
        active = jax.nn.silu(total)
        if unit:
            shaped = active.reshape(row_count, HEADS, HEAD_DIM)
            shaped = shaped * lax.rsqrt(jnp.sum(shaped * shaped, axis=-1, keepdims=True) + 1e-06)
            active = shaped.reshape(row_count, D)
        return low(active)

    def head_mix(queries, key_rows, value_rows, weight, ridge_head, window_mask):
        scaling = window_mask * weight[None, :]
        solution = jnp.zeros_like(queries)
        residue = queries
        direction = queries
        energy = jnp.sum(residue * residue, axis=-1, keepdims=True)
        for sweep in range(ITERS):
            apply_scores = low_back(matmul_t(low(direction), key_rows))
            image_vec = (
                low_back(matmul(low(scaling * apply_scores), key_rows))
                + ridge_head[None, :] * direction
            )
            step_size = energy / jnp.sum(direction * image_vec, axis=-1, keepdims=True)
            solution = solution + step_size * direction
            residue = residue - step_size * image_vec
            energy_next = jnp.sum(residue * residue, axis=-1, keepdims=True)
            direction = residue + energy_next / energy * direction
            energy = energy_next
        scores = low_back(matmul_t(low(solution), key_rows))
        return low_back(matmul(low(scaling * scores), value_rows))

    def section_out(
        xrow, mixed, gate_pre, gain_head, mat_out, gain_ffn, mat_gate, mat_up, mat_down, valid
    ):
        row_count = xrow.shape[0]
        shaped = mixed.reshape(row_count, HEADS, HEAD_DIM)
        shaped = shaped * lax.rsqrt(jnp.mean(shaped * shaped, axis=-1, keepdims=True) + 1e-05)
        normed = shaped.reshape(row_count, D) * gain_head
        gated = low(normed * jax.nn.silu(gate_pre))
        middle = xrow + low_back(matmul(gated, mat_out))
        hidden = low(
            middle * lax.rsqrt(jnp.mean(middle * middle, axis=-1, keepdims=True) + 1e-06) * gain_ffn
        )
        inner = low(
            jax.nn.silu(low_back(matmul(hidden, mat_gate))) * low_back(matmul(hidden, mat_up))
        )
        return valid[:, None] * (middle + low_back(matmul(inner, mat_down)))

    return (section_in, section_conv, head_mix, section_out)


def bit_of(rank, bit):
    return lax.rem(lax.div(rank, 1 << bit), 2)


def swap_bit(value, bit):
    count = lax.axis_size("seq")
    return lax.ppermute(value, "seq", [(source, source ^ (1 << bit)) for source in range(count)])


def rotate(value, steps):
    count = lax.axis_size("wshard")
    return lax.ppermute(
        value, "wshard", [(source, (source + steps) % count) for source in range(count)]
    )


def seq_orders():
    bits = lax.axis_size("seq").bit_length() - 1
    far = list(range(1, bits))
    return far, far[::-1]


def gather_seq(value, order, lead):
    rank = lax.axis_index("seq")
    done = []
    for bit in order:
        other = swap_bit(value, bit)
        place = lead + sum(1 for earlier in done if earlier > bit)
        upper = bit_of(rank, bit) == 1
        low_half = jnp.where(upper, other, value)
        high_half = jnp.where(upper, value, other)
        value = jnp.stack([low_half, high_half], axis=place)
        done.append(bit)
    shape = value.shape
    return value.reshape(shape[:lead] + (1 << len(order),) + shape[lead + len(order) :])


def gather_seq_both(value, lead):
    half = value.shape[-1] // 2
    one, two = seq_orders()
    return jnp.concatenate(
        [
            gather_seq(value[..., :half], one + [0], lead),
            gather_seq(value[..., half:], two + [0], lead),
        ],
        axis=-1,
    )


def gather_weight(shard):
    rank = lax.axis_index("seq")
    place = lax.axis_index("wshard")
    parts = lax.axis_size("seq")
    shards = lax.axis_size("wshard")
    rows, columns = shard.shape
    piece = lax.dynamic_slice_in_dim(shard, rank * (rows // parts), rows // parts, 0)
    foreign = jnp.stack([rotate(piece, step) for step in range(1, shards)])
    foreign = gather_seq_both(foreign, 1).reshape(shards - 1, rows, columns)
    pieces = jnp.concatenate([shard[None], foreign])
    return jnp.concatenate(
        [
            lax.dynamic_index_in_dim(pieces, lax.rem(place - index + shards, shards), 0, False)
            for index in range(shards)
        ]
    )


def add_low(left, right):
    return (left.astype(jnp.float32) + right.astype(jnp.float32)).astype(jnp.bfloat16)


def halve_seq(value, order, remaining):
    rank = lax.axis_index("seq")
    remaining = list(remaining)
    for bit in order:
        axis = 1 + sum(1 for other in remaining if other > bit)
        mine = bit_of(rank, bit)
        keep = lax.dynamic_index_in_dim(value, mine, axis, False)
        send = lax.dynamic_index_in_dim(value, 1 - mine, axis, False)
        value = add_low(keep, swap_bit(send, bit))
        remaining.remove(bit)
    return value


def sum_weight(grad):
    place = lax.axis_index("wshard")
    parts = lax.axis_size("seq")
    shards = lax.axis_size("wshard")
    rows, columns = grad.shape
    bits = parts.bit_length() - 1
    everything = list(range(bits))
    piece_rows = rows // shards // parts
    value = grad.astype(jnp.bfloat16).reshape((shards,) + (2,) * bits + (piece_rows, columns))
    value = halve_seq(value, [0], everything)
    half = columns // 2
    one, two = seq_orders()
    value = jnp.concatenate(
        [
            halve_seq(value[..., :half], one, everything[1:]),
            halve_seq(value[..., half:], two, everything[1:]),
        ],
        axis=-1,
    )
    total = lax.dynamic_index_in_dim(value, place, 0, False).astype(jnp.float32)
    for step in range(1, shards):
        target = lax.rem(place + step, shards)
        arrived = rotate(lax.dynamic_index_in_dim(value, target, 0, False), step)
        total = total + arrived.astype(jnp.float32)
    whole = gather_seq_both(total.astype(jnp.bfloat16), 0)
    return whole.reshape(rows // shards, columns).astype(jnp.float32)


PRE = 16
SMALL = 128


def on_device(
    tokens,
    slot_lengths,
    live_lengths,
    norm_gain,
    w_qkv,
    w_beta,
    w_outgate,
    conv_weight,
    ridge,
    head_gain,
    w_out,
    ffn_gain,
    w_gate,
    w_up,
    w_down,
    cotangent,
):
    section_in, section_conv, head_mix, section_out = make_kit()
    row_count = tokens.shape[1]
    depth = (WINDOW + row_count - 1) // row_count
    halo_rows = depth * row_count
    shards = lax.axis_size("wshard")
    shard_rows = norm_gain.shape[0]
    tap_columns = TAPS * conv_weight.shape[1] // shard_rows

    own_tokens = tokens[0]
    pieces = [passed_along(own_tokens[row_count - PRE :], "seq", depth + 1)]
    for hop_count in range(depth, 0, -1):
        pieces.append(passed_along(own_tokens, "seq", hop_count))
    ext_tokens = jnp.concatenate(pieces + [own_tokens])

    small = jnp.concatenate(
        [
            w_beta,
            norm_gain[:, None],
            ridge[:, None],
            head_gain[:, None],
            ffn_gain[:, None],
            conv_weight.reshape(shard_rows, tap_columns),
        ],
        axis=1,
    )
    small = jnp.pad(small, ((0, 0), (0, SMALL - small.shape[1])))
    front = gather_weight(jnp.concatenate([w_qkv, small], axis=1))
    middle = gather_weight(jnp.concatenate([w_outgate, w_out, w_gate, w_up], axis=1))
    all_down = gather_weight(w_down)
    all_qkv = front[:, : 3 * D]
    small = front[:, 3 * D :].astype(jnp.float32)
    all_beta = small[:, :HEADS]
    gain_in, all_ridge, gain_head, gain_ffn = (small[:, HEADS + index] for index in range(4))
    taps = small[:, HEADS + 4 : HEADS + 4 + tap_columns]
    taps = taps.reshape(shards, TAPS, -1).transpose(1, 0, 2).reshape(TAPS, 3 * D)
    ffn = w_gate.shape[1]
    all_og = middle[:, :D].astype(jnp.float32)
    all_out = middle[:, D : 2 * D].astype(jnp.float32)
    all_gate = middle[:, 2 * D : 2 * D + ffn].astype(jnp.float32)
    all_up = middle[:, 2 * D + ffn :].astype(jnp.float32)
    all_down = all_down.astype(jnp.float32)
    all_qkv = all_qkv.astype(jnp.float32)

    rank = lax.axis_index("seq")
    first = rank * row_count - halo_rows - PRE
    positions = first + jnp.arange(PRE + halo_rows + row_count, dtype=jnp.int32)
    segment, valid = token_layout(slot_lengths[0], live_lengths[0], positions)
    seg_own = segment[PRE + halo_rows :]
    valid_own = valid[PRE + halo_rows :].astype(jnp.float32)
    same = conv_same(segment[PRE - (TAPS - 1) :], segment[PRE:])
    window_mask = build_mask(
        positions[PRE + halo_rows :], positions[PRE:], seg_own, segment[PRE:], valid[PRE:]
    )

    def back_half(xrow, mixed, gate_pre, gain_head, mat_out, gain_ffn, mat_gate, mat_up, mat_down):
        return section_out(
            xrow, mixed, gate_pre, gain_head, mat_out, gain_ffn, mat_gate, mat_up, mat_down, valid_own
        )

    def head_local(queries, key_rows, value_rows, weight, ridge_head):
        return head_mix(queries, key_rows, value_rows, weight, ridge_head, window_mask)

    def front_half(x_ext, gain_in, mat_qkv, mat_beta, mat_og, conv_taps):
        return section_in(
            x_ext, gain_in, mat_qkv, mat_beta, mat_og, conv_taps, same, halo_rows
        )

    x_ext = ext_tokens.astype(jnp.float32)
    xrow = x_ext[PRE + halo_rows :]
    (queries, key_ext, value_ext, beta_ext, gate_pre), pull_front = jax.vjp(
        front_half, x_ext, gain_in, all_qkv, all_beta, all_og, taps
    )
    head_inputs = (
        by_heads(queries),
        by_heads(key_ext),
        by_heads(value_ext),
        beta_ext.T,
        all_ridge.reshape(HEADS, HEAD_DIM),
    )
    mixed = from_heads(lax.map(lambda packed: head_local(*packed), head_inputs))
    output, pull_back = jax.vjp(
        back_half, xrow, mixed, gate_pre, gain_head, all_out, gain_ffn, all_gate, all_up, all_down
    )
    grad_out = cotangent[0].astype(jnp.float32)
    d_xout, d_mixed, d_gate, d_ghead, d_wout, d_gffn, d_wgate, d_wup, d_wdown = pull_back(grad_out)

    total_down = sum_weight(d_wdown)
    total_ffn = sum_weight(jnp.concatenate([d_wgate, d_wup], axis=1).astype(jnp.bfloat16))

    def head_grads(packed):
        head_values, pullback = jax.vjp(
            head_local, packed[0], packed[1], packed[2], packed[3], packed[4]
        )
        return pullback(packed[5])

    d_heads = lax.map(head_grads, head_inputs + (by_heads(d_mixed),))
    d_query = from_heads(d_heads[0])
    d_key_ext = from_heads(d_heads[1])
    d_value_ext = from_heads(d_heads[2])
    d_beta_ext = d_heads[3].T
    d_ridge = d_heads[4].reshape(D)
    d_xext, d_gin, d_wqkv, d_wbeta, d_wog, d_taps = pull_front(
        (d_query, d_key_ext, d_value_ext, d_beta_ext, d_gate)
    )
    d_tokens = d_xout + d_xext[PRE + halo_rows :]
    for hop_count in range(1, depth + 1):
        start = PRE + halo_rows - hop_count * row_count
        part = d_xext[start : start + row_count].astype(jnp.bfloat16)
        d_tokens = d_tokens + passed_along(part, "seq", -hop_count).astype(jnp.float32)
    part = passed_along(d_xext[:PRE].astype(jnp.bfloat16), "seq", -(depth + 1))
    part = jnp.pad(part.astype(jnp.float32), ((row_count - PRE, 0), (0, 0)))
    d_tokens = d_tokens + part

    d_small = jnp.concatenate(
        [
            d_wbeta,
            d_gin[:, None],
            d_ridge[:, None],
            d_ghead[:, None],
            d_gffn[:, None],
            d_taps.reshape(TAPS, shards, -1).transpose(1, 0, 2).reshape(D, tap_columns),
        ],
        axis=1,
    )
    d_small = jnp.pad(d_small, ((0, 0), (0, SMALL - d_small.shape[1])))
    total_middle = sum_weight(jnp.concatenate([d_wog, d_wout], axis=1).astype(jnp.bfloat16))
    total_front = sum_weight(jnp.concatenate([d_wqkv, d_small], axis=1).astype(jnp.bfloat16))
    t_small = total_front[:, 3 * D :]
    return (
        output.astype(jnp.bfloat16)[None],
        d_tokens.astype(jnp.bfloat16)[None],
        t_small[:, HEADS],
        total_front[:, : 3 * D],
        t_small[:, :HEADS],
        total_middle[:, :D],
        t_small[:, HEADS + 4 : HEADS + 4 + tap_columns].reshape(TAPS, -1),
        t_small[:, HEADS + 1],
        t_small[:, HEADS + 2],
        total_middle[:, D:],
        t_small[:, HEADS + 3],
        total_ffn[:, :ffn],
        total_ffn[:, ffn:],
        total_down,
    )


def solution(mesh):
    return jax.shard_map(
        on_device,
        mesh=mesh,
        in_specs=(
            P("wshard", "seq", None),
            P("wshard", None),
            P("wshard", None),
            P("wshard"),
            P("wshard", None),
            P("wshard", None),
            P("wshard", None),
            P(None, "wshard"),
            P("wshard"),
            P("wshard"),
            P("wshard", None),
            P("wshard"),
            P("wshard", None),
            P("wshard", None),
            P("wshard", None),
            P("wshard", "seq", None),
        ),
        out_specs=(
            P("wshard", "seq", None),
            P("wshard", "seq", None),
            P("wshard"),
            P("wshard", None),
            P("wshard", None),
            P("wshard", None),
            P(None, "wshard"),
            P("wshard"),
            P("wshard"),
            P("wshard", None),
            P("wshard"),
            P("wshard", None),
            P("wshard", None),
            P("wshard", None),
        ),
        check_vma=False,
    )
```

```python
import functools
import jax
import jax.numpy as jnp
from jax import lax
from jax.experimental import pallas as pl
from jax.experimental.pallas import tpu as pltpu
from jax.sharding import PartitionSpec as P

D = 1024
HEADS = 8
HEAD_DIM = 128
TAPS = 4
WINDOW = 1024
PRE = 16
SMALL = 128
f32 = jnp.float32
bf16 = jnp.bfloat16
QB = 256
CH = 256
ROWS = 256


def mm(left, right):
    return jnp.dot(left, right, preferred_element_type=f32)


def mm_t(left, right):
    return lax.dot_general(left, right, (((1,), (1,)), ((), ())), preferred_element_type=f32)


def conv_total(ext_ref, slot, same, taps):
    total = taps[0:1] * ext_ref[slot, 8 : 8 + ROWS, :]
    for tap in range(1, TAPS):
        total = total + taps[tap : tap + 1] * ext_ref[slot, 8 - tap : 8 - tap + ROWS, :] * same[tap]
    return total


def unit_scale(active):
    return lax.rsqrt(jnp.sum(active * active, axis=-1, keepdims=True) + 1e-06)


def in_heads(work, *arrays):
    width = arrays[0].shape[1]
    return jnp.concatenate(
        [
            work(*(array[:, at : at + HEAD_DIM] for array in arrays))
            for at in range(0, width, HEAD_DIM)
        ],
        axis=1,
    )


def row_norm(x, gain):
    return (x * lax.rsqrt(jnp.mean(x * x, axis=-1, keepdims=True) + 1e-06) * gain).astype(bf16)


def front_kernel(
    first_own,
    x_ref,
    same_ref,
    gain_ref,
    w_ref,
    taps_ref,
    hid_ref,
    kvin_ref,
    qin_ref,
    qpre_ref,
    q_ref,
    k_ref,
    v_ref,
    beta_ref,
    ext_ref,
    tail_ref,
):
    step = pl.program_id(0)
    gain = gain_ref[...]
    kv_slots = 2 * D // CH

    @pl.when(step == 0)
    def before():
        hidden = row_norm(x_ref[0:PRE].astype(f32), gain)
        hid_ref[0:PRE] = hidden
        for slot in range(kv_slots):
            rows = mm(hidden, w_ref[:, D + CH * slot : D + CH * (slot + 1)]).astype(bf16)
            kvin_ref[0:PRE, CH * slot : CH * (slot + 1)] = rows
            ext_ref[slot, ROWS : ROWS + 8, :] = rows.astype(f32)[PRE - 8 :]

    def through(slot, hidden, same, column, in_ref, at):
        ext_ref[slot, 0:8, :] = ext_ref[slot, ROWS : ROWS + 8, :]
        rows = mm(hidden, w_ref[:, column : column + CH]).astype(bf16)
        in_ref[:, at : at + CH] = rows
        ext_ref[slot, 8 : 8 + ROWS, :] = rows.astype(f32)
        total = conv_total(ext_ref, slot, same, taps_ref[:, column : column + CH])
        return total * jax.nn.sigmoid(total)

    def unit(active):
        return in_heads(lambda part: part * unit_scale(part), active).astype(bf16)

    @pl.when(step > 0)
    def main():
        same = [same_ref[:, tap : tap + 1] for tap in range(TAPS)]
        hidden = row_norm(x_ref[...].astype(f32), gain)
        hid_ref[...] = hidden
        for slot in range(kv_slots):
            at = CH * slot
            active = through(slot, hidden, same, D + at, kvin_ref, at)
            if at < D:
                k_ref[:, at : at + CH] = unit(active)
            else:
                v_ref[:, at - D : at - D + CH] = active.astype(bf16)
        gates = jax.nn.sigmoid(mm(hidden, w_ref[:, 3 * D : 3 * D + SMALL])).astype(bf16)
        lane = lax.broadcasted_iota(jnp.int32, (ROWS, SMALL), 1)
        beta_ref[...] = jnp.where(lane < HEADS, gates.astype(f32), 0.0)

        @pl.when(step == first_own + 1)
        def own_history():
            rows = mm(tail_ref[...], w_ref[:, :D]).astype(bf16)
            qpre_ref[...] = rows
            for slot in range(D // CH):
                ext_ref[kv_slots + slot, ROWS : ROWS + 8, :] = rows.astype(f32)[
                    PRE - 8 :, CH * slot : CH * (slot + 1)
                ]

        @pl.when(step > first_own)
        def own():
            for slot in range(D // CH):
                at = CH * slot
                active = through(kv_slots + slot, hidden, same, at, qin_ref, at)
                q_ref[:, at : at + CH] = unit(active)

        tail_ref[...] = hidden[ROWS - PRE :]


def front(ext_tokens, same, gain, w_front, taps, own_rows):
    ext_rows = ext_tokens.shape[0]
    main_rows = ext_rows - PRE
    blocks = main_rows // ROWS
    first_own = (main_rows - own_rows) // ROWS

    def ext_block(step):
        return (jnp.where(step == 0, blocks, step - 1), 0)

    def main_block(step):
        return (jnp.maximum(step - 1, 0), 0)

    def own_block(step):
        return (jnp.maximum(step - 1 - first_own, 0), 0)

    def fixed(array):
        return pl.BlockSpec(array.shape, lambda step: (0, 0))

    shape = jax.ShapeDtypeStruct
    return pl.pallas_call(
        functools.partial(front_kernel, first_own),
        grid=(blocks + 1,),
        in_specs=[
            pl.BlockSpec((ROWS, D), ext_block),
            pl.BlockSpec((ROWS, TAPS), main_block),
            fixed(gain),
            fixed(w_front),
            fixed(taps),
        ],
        out_specs=[
            pl.BlockSpec((ROWS, D), ext_block),
            pl.BlockSpec((ROWS, 2 * D), ext_block),
            pl.BlockSpec((ROWS, D), own_block),
            pl.BlockSpec((PRE, D), lambda step: (0, 0)),
            pl.BlockSpec((ROWS, D), own_block),
            pl.BlockSpec((ROWS, D), main_block),
            pl.BlockSpec((ROWS, D), main_block),
            pl.BlockSpec((ROWS, SMALL), main_block),
        ],
        out_shape=[
            shape((ext_rows, D), bf16),
            shape((ext_rows, 2 * D), bf16),
            shape((own_rows, D), bf16),
            shape((PRE, D), bf16),
            shape((own_rows, D), bf16),
            shape((main_rows, D), bf16),
            shape((main_rows, D), bf16),
            shape((main_rows, SMALL), f32),
        ],
        scratch_shapes=[
            pltpu.VMEM((3 * D // CH, 8 + ROWS, CH), f32),
            pltpu.VMEM((PRE, D), bf16),
        ],
        compiler_params=pltpu.CompilerParams(
            dimension_semantics=("arbitrary",), vmem_limit_bytes=50 << 20
        ),
        cost_estimate=pl.CostEstimate(
            flops=4 * (main_rows * 2 + own_rows) * D * D, bytes_accessed=30 << 20, transcendentals=0
        ),
        name="front",
    )(ext_tokens, same, gain, w_front, taps)


def back_kernel(
    blocks,
    first_own,
    x_ref,
    kvin_ref,
    kvprev_ref,
    same_ref,
    qin_ref,
    qprev_ref,
    qpre_ref,
    dk_ref,
    dv_ref,
    dq_ref,
    beta_ref,
    dbeta_ref,
    dgate_ref,
    dres_ref,
    gain_ref,
    w_ref,
    wog_ref,
    taps_ref,
    dkvin_ref,
    dqin_ref,
    dqpre_ref,
    dbp_ref,
    dxhalo_ref,
    dxown_ref,
    dgain_ref,
    dtaps_ref,
    ext_ref,
    buf_ref,
    dh_ref,
):
    step = pl.program_id(0)
    block = blocks - 1 - step
    kv_slots = 2 * D // CH
    gain = gain_ref[...]

    @pl.when(step == 0)
    def clear():
        dgain_ref[...] = jnp.zeros_like(dgain_ref)
        dtaps_ref[...] = jnp.zeros_like(dtaps_ref)
        buf_ref[:, :, ROWS : ROWS + 8, :] = jnp.zeros_like(buf_ref[:, :, ROWS : ROWS + 8, :])

    def norm_back(x, dh):
        scale = lax.rsqrt(jnp.mean(x * x, axis=-1, keepdims=True) + 1e-06)
        normal = x * scale
        dgain_ref[...] += jnp.sum(dh * normal, axis=0, keepdims=True)
        scaled = dh * gain
        return scale * (scaled - normal * jnp.mean(scaled * normal, axis=-1, keepdims=True))

    def shifted(slot, start, count):
        total = buf_ref[slot, 1, start + 1 : start + 1 + count, :]
        for tap in range(2, TAPS):
            total = total + buf_ref[slot, tap, start + tap : start + tap + count, :]
        return total

    def through(slot, column, history, rows, grad, unit, same):
        ext_ref[slot, 0:8, :] = history
        ext_ref[slot, 8 : 8 + ROWS, :] = rows.astype(f32)
        taps = taps_ref[:, column : column + CH]
        total = conv_total(ext_ref, slot, same, taps)
        gate = jax.nn.sigmoid(total)
        active = total * gate
        if unit:

            def unit_back(part, part_grad):
                scale = unit_scale(part)
                normal = part * scale
                return scale * (
                    part_grad - normal * jnp.sum(part_grad * normal, axis=-1, keepdims=True)
                )

            grad = in_heads(unit_back, active, grad)
        grad = grad * (gate + active * (1.0 - gate))
        result = grad * taps[0:1]
        dtaps_ref[0:1, column : column + CH] += jnp.sum(
            grad * ext_ref[slot, 8 : 8 + ROWS, :], axis=0, keepdims=True
        )
        for tap in range(1, TAPS):
            held = grad * same[tap]
            dtaps_ref[tap : tap + 1, column : column + CH] += jnp.sum(
                held * ext_ref[slot, 8 - tap : 8 - tap + ROWS, :], axis=0, keepdims=True
            )
            buf_ref[slot, tap, 0:ROWS, :] = held * taps[tap : tap + 1]
        result = (result + shifted(slot, 0, ROWS)).astype(bf16)
        for tap in range(1, TAPS):
            buf_ref[slot, tap, ROWS : ROWS + 8, :] = buf_ref[slot, tap, 0:8, :]
        return result

    def before_rows(slot):
        for tap in range(1, TAPS):
            buf_ref[slot, tap, ROWS - PRE : ROWS, :] = jnp.zeros((PRE, CH), f32)
        return shifted(slot, ROWS - PRE, PRE).astype(bf16)

    @pl.when(step < blocks)
    def main():
        same = [same_ref[:, tap : tap + 1] for tap in range(TAPS)]
        beta = beta_ref[...]
        gates = (dbeta_ref[...] * beta * (1.0 - beta)).astype(bf16)
        dbp_ref[...] = gates
        dh = mm_t(gates, w_ref[:, 3 * D : 3 * D + SMALL])
        for slot in range(kv_slots):
            at = CH * slot
            grad = dk_ref[:, at : at + CH] if at < D else dv_ref[:, at - D : at - D + CH]
            history = kvprev_ref[PRE - 8 : PRE, at : at + CH].astype(f32)
            rows = kvin_ref[:, at : at + CH]
            rows = through(slot, D + at, history, rows, grad, at < D, same)
            dkvin_ref[:, at : at + CH] = rows
            dh = dh + mm_t(rows, w_ref[:, D + at : D + at + CH])
        dh_ref[...] = dh

        @pl.when(block >= first_own)
        def own():
            dh = mm_t(dgate_ref[...], wog_ref[...])
            for slot in range(D // CH):
                at = CH * slot
                history = jnp.where(
                    block == first_own,
                    qpre_ref[PRE - 8 :, at : at + CH].astype(f32),
                    qprev_ref[PRE - 8 :, at : at + CH].astype(f32),
                )
                rows = qin_ref[:, at : at + CH]
                rows = through(
                    kv_slots + slot, at, history, rows, dq_ref[:, at : at + CH], True, same
                )
                dqin_ref[:, at : at + CH] = rows
                dh = dh + mm_t(rows, w_ref[:, at : at + CH])
            dxown_ref[...] = dres_ref[...] + norm_back(x_ref[...].astype(f32), dh_ref[...] + dh)

        @pl.when(block == first_own - 1)
        def own_history():
            dh = jnp.zeros((PRE, D), f32)
            for slot in range(D // CH):
                at = CH * slot
                rows = before_rows(kv_slots + slot)
                dqpre_ref[:, at : at + CH] = rows
                dh = dh + mm_t(rows, w_ref[:, at : at + CH])
            dh_ref[ROWS - PRE : ROWS, :] += dh

        @pl.when(block < first_own)
        def halo():
            dxhalo_ref[...] = norm_back(x_ref[...].astype(f32), dh_ref[...]).astype(bf16)

    @pl.when(step == blocks)
    def before():
        dh = jnp.zeros((PRE, D), f32)
        for slot in range(kv_slots):
            at = CH * slot
            rows = before_rows(slot)
            dkvin_ref[0:PRE, at : at + CH] = rows
            dh = dh + mm_t(rows, w_ref[:, D + at : D + at + CH])
        dxhalo_ref[0:PRE, :] = norm_back(x_ref[0:PRE].astype(f32), dh).astype(bf16)


def back(
    ext_tokens, kvin, same, qin, qpre, dk, dv, dq, beta, dbeta, dgate, dres, gain, w_front, w_og, taps
):
    ext_rows = ext_tokens.shape[0]
    main_rows = ext_rows - PRE
    own_rows = dq.shape[0]
    blocks = main_rows // ROWS
    first_own = (main_rows - own_rows) // ROWS
    small_blocks = ROWS // PRE

    def ext_block(step):
        return (jnp.where(step == blocks, blocks, blocks - 1 - step), 0)

    def main_block(step):
        return (jnp.maximum(blocks - 1 - step, 0), 0)

    def prev_block(step):
        block = blocks - 1 - step
        return (jnp.where(block <= 0, blocks * small_blocks, small_blocks * block - 1), 0)

    def own_block(step):
        return (jnp.maximum(blocks - 1 - step - first_own, 0), 0)

    def own_prev_block(step):
        return (jnp.maximum(small_blocks * (blocks - 1 - step - first_own) - 1, 0), 0)

    def halo_block(step):
        block = jnp.minimum(blocks - 1 - step, first_own - 1)
        return (jnp.where(step == blocks, first_own, block), 0)

    def fixed(array):
        return pl.BlockSpec(array.shape, lambda step: (0, 0))

    shape = jax.ShapeDtypeStruct
    return pl.pallas_call(
        functools.partial(back_kernel, blocks, first_own),
        grid=(blocks + 1,),
        in_specs=[
            pl.BlockSpec((ROWS, D), ext_block),
            pl.BlockSpec((ROWS, 2 * D), ext_block),
            pl.BlockSpec((PRE, 2 * D), prev_block),
            pl.BlockSpec((ROWS, TAPS), main_block),
            pl.BlockSpec((ROWS, D), own_block),
            pl.BlockSpec((PRE, D), own_prev_block),
            fixed(qpre),
            pl.BlockSpec((ROWS, D), main_block),
            pl.BlockSpec((ROWS, D), main_block),
            pl.BlockSpec((ROWS, D), own_block),
            pl.BlockSpec((ROWS, SMALL), main_block),
            pl.BlockSpec((ROWS, SMALL), main_block),
            pl.BlockSpec((ROWS, D), own_block),
            pl.BlockSpec((ROWS, D), own_block),
            fixed(gain),
            fixed(w_front),
            fixed(w_og),
            fixed(taps),
        ],
        out_specs=[
            pl.BlockSpec((ROWS, 2 * D), ext_block),
            pl.BlockSpec((ROWS, D), own_block),
            pl.BlockSpec((PRE, D), lambda step: (0, 0)),
            pl.BlockSpec((ROWS, SMALL), main_block),
            pl.BlockSpec((ROWS, D), halo_block),
            pl.BlockSpec((ROWS, D), own_block),
            pl.BlockSpec((1, D), lambda step: (0, 0)),
            pl.BlockSpec((TAPS, 3 * D), lambda step: (0, 0)),
        ],
        out_shape=[
            shape((ext_rows, 2 * D), bf16),
            shape((own_rows, D), bf16),
            shape((PRE, D), bf16),
            shape((main_rows, SMALL), bf16),
            shape((main_rows - own_rows + PRE, D), bf16),
            shape((own_rows, D), f32),
            shape((1, D), f32),
            shape((TAPS, 3 * D), f32),
        ],
        scratch_shapes=[
            pltpu.VMEM((3 * D // CH, 8 + ROWS, CH), f32),
            pltpu.VMEM((3 * D // CH, TAPS, ROWS + 8, CH), f32),
            pltpu.VMEM((ROWS, D), f32),
        ],
        compiler_params=pltpu.CompilerParams(
            dimension_semantics=("arbitrary",), vmem_limit_bytes=56 << 20
        ),
        cost_estimate=pl.CostEstimate(
            flops=6 * (main_rows * 2 + own_rows) * D * D, bytes_accessed=40 << 20, transcendentals=0
        ),
        name="back",
    )(
        ext_tokens,
        kvin,
        kvin,
        same,
        qin,
        qin,
        qpre,
        dk,
        dv,
        dq,
        beta,
        dbeta,
        dgate,
        dres,
        gain,
        w_front,
        w_og,
        taps,
    )


def total(v):
    return jnp.sum(v,axis=0,keepdims=True)

def head_column(beta_ref, h):
    beta=beta_ref[...]
    lane=lax.broadcasted_iota(jnp.int32,beta.shape,1)
    return jnp.sum(jnp.where(lane==h,beta,0.0),axis=1,keepdims=True)

def attn_fwd_kernel(q_ref,k_ref,v_ref,beta_ref,mask_ref,ridge_ref,o_ref,a0_ref,a1_ref,kt_ref,vt_ref,w_ref):
    h=pl.program_id(0)
    rows=q_ref.shape[0]
    span=WINDOW+QB
    kt_ref[...]=k_ref[...].T
    vt_ref[...]=v_ref[...].T
    column=head_column(beta_ref,h)
    ridge=ridge_ref[...]
    blocks=range(rows//QB)
    chunks=range(span//CH)
    for b in blocks:
        for c in chunks:
            at=slice(QB*b+CH*c,QB*b+CH*(c+1))
            w_ref[b,CH*c:CH*(c+1),:]=mask_ref[at,QB*b:QB*(b+1)].astype(f32)*column[at]
    def apply(b,vector,right):
        low=vector.astype(bf16)
        out=jnp.zeros((HEAD_DIM,QB),f32)
        for c in chunks:
            at=slice(QB*b+CH*c,QB*b+CH*(c+1))
            s=mm(k_ref[at,:],low)
            s=(w_ref[b,CH*c:CH*(c+1),:]*s).astype(bf16)
            out=out+mm(right[:,at],s)
        return out
    q=[q_ref[QB*b:QB*(b+1),:].astype(f32).T for b in blocks]
    a0=[apply(b,q[b],kt_ref)+ridge*q[b] for b in blocks]
    for b in blocks: a0_ref[:,QB*b:QB*(b+1)]=a0[b]
    x1=[];p1=[];r1=[];e1=[]
    for b in blocks:
        e0=total(q[b]*q[b])
        s0=e0/total(q[b]*a0[b])
        x1.append(s0*q[b])
        r=q[b]-s0*a0[b]
        e=total(r*r)
        r1.append(r);e1.append(e)
        p1.append(r+e/e0*q[b])
    a1=[apply(b,p1[b],kt_ref)+ridge*p1[b] for b in blocks]
    for b in blocks: a1_ref[:,QB*b:QB*(b+1)]=a1[b]
    x2=[x1[b]+e1[b]/total(p1[b]*a1[b])*p1[b] for b in blocks]
    for b in blocks:
        o_ref[QB*b:QB*(b+1),:]=apply(b,x2[b],vt_ref).T

def attn_fwd(q,k,v,beta,mask_t,ridge):
    rows=q.shape[0]; keys=k.shape[0]
    head=lambda n: pl.BlockSpec((n,HEAD_DIM),lambda h:(0,h))
    heads_t=pl.BlockSpec((HEAD_DIM,rows),lambda h:(h,0))
    fixed=lambda a: pl.BlockSpec(a.shape,lambda h:(0,0))
    flops=6*2*rows*(WINDOW+QB)*D
    return pl.pallas_call(
        attn_fwd_kernel, grid=(HEADS,),
        in_specs=[head(rows),head(keys),head(keys),fixed(beta),fixed(mask_t),pl.BlockSpec((HEAD_DIM,1),lambda h:(h,0))],
        out_specs=[head(rows),heads_t,heads_t],
        out_shape=[jax.ShapeDtypeStruct((rows,D),f32)]+[jax.ShapeDtypeStruct((D,rows),f32)]*2,
        scratch_shapes=[pltpu.VMEM((HEAD_DIM,keys),bf16)]*2+[pltpu.VMEM((rows//QB,WINDOW+QB,QB),f32)],
        compiler_params=pltpu.CompilerParams(dimension_semantics=("arbitrary",),vmem_limit_bytes=48<<20),
        cost_estimate=pl.CostEstimate(flops=2*flops,bytes_accessed=20<<20,transcendentals=0),
        name="attn_fwd",
    )(q,k,v,beta,mask_t,ridge)

def attn_bwd_kernel(q_ref,k_ref,v_ref,beta_ref,mask_ref,ridge_ref,a0_ref,a1_ref,do_ref,dq_ref,dk_ref,dv_ref,dbeta_ref,dridge_ref,kt_ref,w_ref,acc_ref):
    h=pl.program_id(0)
    rows=q_ref.shape[0]
    span=WINDOW+QB
    kt_ref[...]=k_ref[...].T
    column=head_column(beta_ref,h)
    ridge=ridge_ref[...]
    blocks=range(rows//QB)
    chunks=range(span//CH)
    dk_ref[...]=jnp.zeros_like(dk_ref)
    dv_ref[...]=jnp.zeros_like(dv_ref)
    acc_ref[...]=jnp.zeros_like(acc_ref)
    for b in blocks:
        for c in chunks:
            at=slice(QB*b+CH*c,QB*b+CH*(c+1))
            w_ref[b,CH*c:CH*(c+1),:]=mask_ref[at,QB*b:QB*(b+1)].astype(f32)*column[at]
    def apply_back(b,vector,grad,grad_rows,right_ref,dright_ref):
        low=vector.astype(bf16)
        low_rows=vector.T.astype(bf16)
        out=jnp.zeros((HEAD_DIM,QB),f32)
        for c in chunks:
            at=slice(QB*b+CH*c,QB*b+CH*(c+1))
            w=w_ref[b,CH*c:CH*(c+1),:]
            s=mm(k_ref[at,:],low)
            dw=mm(right_ref[at,:],grad)
            masked=dw*mask_ref[at,QB*b:QB*(b+1)].astype(f32)
            for_beta=masked*s
            part=for_beta[:,:128]
            for lane in range(128,QB,128):
                part=part+for_beta[:,lane:lane+128]
            acc_ref[at,:]+=part
            ws=(w*s).astype(bf16)
            ds=(w*dw).astype(bf16)
            out=out+mm(kt_ref[:,at],ds)
            dright_ref[at,:]+=mm(ws,grad_rows)
            dk_ref[at,:]+=mm(ds,low_rows)
        return out
    st=[]
    for b in blocks:
        cols=slice(QB*b,QB*(b+1))
        q=q_ref[cols,:].astype(f32).T
        a0=a0_ref[:,cols]; a1=a1_ref[:,cols]
        e0=total(q*q); d0=total(q*a0); s0=e0/d0
        x1=s0*q; r1=q-s0*a0; e1=total(r1*r1); b0=e1/e0
        p1=r1+b0*q; d1=total(p1*a1); s1=e1/d1
        x2=x1+s1*p1
        st.append((q,a0,a1,e0,d0,s0,r1,e1,b0,p1,d1,s1,x2))
    dx2=[]
    for b in blocks:
        do=do_ref[QB*b:QB*(b+1),:]
        dx2.append(apply_back(b,st[b][12],do.astype(f32).T.astype(bf16),do,v_ref,dv_ref))
    da1=[];dp1=[];de1=[];dr=0
    for b in blocks:
        q,a0,a1,e0,d0,s0,r1,e1,b0,p1,d1,s1,x2=st[b]
        ds1=total(dx2[b]*p1)
        de1.append(ds1/d1)
        dd1=-ds1*s1/d1
        g=dd1*p1
        da1.append(g)
        dp1.append(s1*dx2[b]+dd1*a1+ridge*g)
        dr=dr+jnp.sum(g*p1,axis=1,keepdims=True)
    for b in blocks:
        g=da1[b]
        dp1[b]=dp1[b]+apply_back(b,st[b][9],g.astype(bf16),g.T.astype(bf16),k_ref,dk_ref)
    da0=[];dq=[]
    for b in blocks:
        q,a0,a1,e0,d0,s0,r1,e1,b0,p1,d1,s1,x2=st[b]
        db0=total(dp1[b]*q)
        dpq=b0*dp1[b]
        de=de1[b]+db0/e0
        de0=-db0*b0/e0
        dr1=dp1[b]+2.0*de*r1
        ds0=total(dx2[b]*q)-total(dr1*a0)
        dpq=dpq+s0*dx2[b]
        g=-s0*dr1
        de0=de0+ds0/d0
        dd0=-ds0*s0/d0
        dpq=dpq+dd0*a0
        g=g+dd0*q
        dpq=dpq+dr1+2.0*de0*q+ridge*g
        da0.append(g);dq.append(dpq)
        dr=dr+jnp.sum(g*q,axis=1,keepdims=True)
    for b in blocks:
        g=da0[b]
        t=dq[b]+apply_back(b,st[b][0],g.astype(bf16),g.T.astype(bf16),k_ref,dk_ref)
        dq_ref[QB*b:QB*(b+1),:]=t.T
    dridge_ref[...]=dr
    found=jnp.sum(acc_ref[...],axis=1,keepdims=True)
    lane=lax.broadcasted_iota(jnp.int32,dbeta_ref.shape,1)
    @pl.when(h==0)
    def _():
        dbeta_ref[...]=jnp.zeros_like(dbeta_ref)
    dbeta_ref[...]=jnp.where(lane==h,found,dbeta_ref[...])

def attn_bwd(q,k,v,beta,mask_t,ridge,a0,a1,do):
    rows=q.shape[0]; keys=k.shape[0]
    head=lambda n: pl.BlockSpec((n,HEAD_DIM),lambda h:(0,h))
    heads_t=pl.BlockSpec((HEAD_DIM,rows),lambda h:(h,0))
    fixed=lambda a: pl.BlockSpec(a.shape,lambda h:(0,0))
    rd=pl.BlockSpec((HEAD_DIM,1),lambda h:(h,0))
    flops=15*2*rows*(WINDOW+QB)*D
    return pl.pallas_call(
        attn_bwd_kernel, grid=(HEADS,),
        in_specs=[head(rows),head(keys),head(keys),fixed(beta),fixed(mask_t),rd,heads_t,heads_t,head(rows)],
        out_specs=[head(rows),head(keys),head(keys),fixed(beta),rd],
        out_shape=[jax.ShapeDtypeStruct((rows,D),f32),jax.ShapeDtypeStruct((keys,D),f32),jax.ShapeDtypeStruct((keys,D),f32),jax.ShapeDtypeStruct(beta.shape,f32),jax.ShapeDtypeStruct((D,1),f32)],
        scratch_shapes=[pltpu.VMEM((HEAD_DIM,keys),bf16),pltpu.VMEM((rows//QB,WINDOW+QB,QB),f32),pltpu.VMEM((keys,128),f32)],
        compiler_params=pltpu.CompilerParams(dimension_semantics=("arbitrary",),vmem_limit_bytes=48<<20),
        cost_estimate=pl.CostEstimate(flops=2*flops,bytes_accessed=30<<20,transcendentals=0),
        name="attn_bwd",
    )(q,k,v,beta,mask_t,ridge,a0,a1,do)


def passed_along(value, axis, steps):
    count = lax.axis_size(axis)
    initial, last = (max(0, -steps), min(count, count - steps))
    return lax.ppermute(value, axis, [(source, source + steps) for source in range(initial, last)])


def token_layout(slot_row, live_row, positions):
    starts = (jnp.cumsum(slot_row) - slot_row).astype(jnp.int32)
    after = positions[:, None] >= starts[None, :]
    segment = (jnp.sum(after.astype(jnp.int32), axis=1) - 1).astype(jnp.int32)
    chosen = segment[:, None] == jnp.arange(slot_row.shape[0], dtype=jnp.int32)[None, :]
    begin = jnp.sum(jnp.where(chosen, starts[None, :], 0), axis=1).astype(jnp.int32)
    limit = jnp.sum(jnp.where(chosen, live_row[None, :], 0), axis=1).astype(jnp.int32)
    valid = (segment >= 0) & (positions - begin < limit)
    return (segment, valid)


def make_kit():

    @jax.custom_vjp
    def low(v):
        return lax.optimization_barrier(v.astype(jnp.bfloat16)).astype(jnp.float32)

    @jax.custom_vjp
    def low_back(v):
        return v

    def low_keep(v):
        return (low(v), None)

    def low_pass(kept, grad):
        return (grad,)

    def back_keep(v):
        return (v, None)

    def back_low(kept, grad):
        return (low(grad),)

    low.defvjp(low_keep, low_pass)
    low_back.defvjp(back_keep, back_low)

    @jax.custom_vjp
    def matmul(left, right):
        return jnp.dot(
            left.astype(jnp.bfloat16),
            right.astype(jnp.bfloat16),
            preferred_element_type=jnp.float32,
        )

    def matmul_keep(left, right):
        left_low = left.astype(jnp.bfloat16)
        right_low = right.astype(jnp.bfloat16)
        return (
            jnp.dot(left_low, right_low, preferred_element_type=jnp.float32),
            (left_low, right_low),
        )

    def matmul_grads(kept, grad):
        left_low, right_low = kept
        grad_low = grad.astype(jnp.bfloat16)
        grad_left = lax.dot_general(
            grad_low, right_low, (((1,), (1,)), ((), ())), preferred_element_type=jnp.float32
        )
        grad_right = lax.dot_general(
            left_low, grad_low, (((0,), (0,)), ((), ())), preferred_element_type=jnp.float32
        )
        return (grad_left, grad_right)

    matmul.defvjp(matmul_keep, matmul_grads)

    def section_out(
        xrow, mixed, gate_pre, gain_head, mat_out, gain_ffn, mat_gate, mat_up, mat_down, valid
    ):
        row_count = xrow.shape[0]
        shaped = mixed.reshape(row_count, HEADS, HEAD_DIM)
        shaped = shaped * lax.rsqrt(jnp.mean(shaped * shaped, axis=-1, keepdims=True) + 1e-05)
        normed = shaped.reshape(row_count, D) * gain_head
        gated = low(normed * jax.nn.silu(gate_pre))
        middle = xrow + low_back(matmul(gated, mat_out))
        hidden = low(
            middle * lax.rsqrt(jnp.mean(middle * middle, axis=-1, keepdims=True) + 1e-06) * gain_ffn
        )
        inner = low(
            jax.nn.silu(low_back(matmul(hidden, mat_gate))) * low_back(matmul(hidden, mat_up))
        )
        return valid[:, None] * (middle + low_back(matmul(inner, mat_down)))

    return section_out


def bit_of(rank, bit):
    return lax.rem(lax.div(rank, 1 << bit), 2)


def swap_bit(value, bit):
    count = lax.axis_size("seq")
    return lax.ppermute(value, "seq", [(source, source ^ (1 << bit)) for source in range(count)])


def rotate(value, steps):
    count = lax.axis_size("wshard")
    return lax.ppermute(
        value, "wshard", [(source, (source + steps) % count) for source in range(count)]
    )


def seq_orders():
    bits = lax.axis_size("seq").bit_length() - 1
    far = list(range(1, bits))
    return far, far[::-1]


def gather_seq(value, order, lead):
    rank = lax.axis_index("seq")
    done = []
    for bit in order:
        other = swap_bit(value, bit)
        place = lead + sum(1 for earlier in done if earlier > bit)
        upper = bit_of(rank, bit) == 1
        low_half = jnp.where(upper, other, value)
        high_half = jnp.where(upper, value, other)
        value = jnp.stack([low_half, high_half], axis=place)
        done.append(bit)
    shape = value.shape
    return value.reshape(shape[:lead] + (1 << len(order),) + shape[lead + len(order) :])


def gather_seq_both(value, lead):
    half = value.shape[-1] // 2
    one, two = seq_orders()
    return jnp.concatenate(
        [
            gather_seq(value[..., :half], one + [0], lead),
            gather_seq(value[..., half:], two + [0], lead),
        ],
        axis=-1,
    )


def gather_weight(shard):
    rank = lax.axis_index("seq")
    place = lax.axis_index("wshard")
    parts = lax.axis_size("seq")
    shards = lax.axis_size("wshard")
    rows, columns = shard.shape
    piece = lax.dynamic_slice_in_dim(shard, rank * (rows // parts), rows // parts, 0)
    foreign = jnp.stack([rotate(piece, step) for step in range(1, shards)])
    foreign = gather_seq_both(foreign, 1).reshape(shards - 1, rows, columns)
    pieces = jnp.concatenate([shard[None], foreign])
    return jnp.concatenate(
        [
            lax.dynamic_index_in_dim(pieces, lax.rem(place - index + shards, shards), 0, False)
            for index in range(shards)
        ]
    )


def add_low(left, right):
    return (left.astype(jnp.float32) + right.astype(jnp.float32)).astype(jnp.bfloat16)


def halve_seq(value, order, remaining):
    rank = lax.axis_index("seq")
    remaining = list(remaining)
    for bit in order:
        axis = 1 + sum(1 for other in remaining if other > bit)
        mine = bit_of(rank, bit)
        keep = lax.dynamic_index_in_dim(value, mine, axis, False)
        send = lax.dynamic_index_in_dim(value, 1 - mine, axis, False)
        value = add_low(keep, swap_bit(send, bit))
        remaining.remove(bit)
    return value


def sum_weight(grad):
    place = lax.axis_index("wshard")
    parts = lax.axis_size("seq")
    shards = lax.axis_size("wshard")
    rows, columns = grad.shape
    bits = parts.bit_length() - 1
    everything = list(range(bits))
    piece_rows = rows // shards // parts
    value = grad.astype(jnp.bfloat16).reshape((shards,) + (2,) * bits + (piece_rows, columns))
    value = halve_seq(value, [0], everything)
    half = columns // 2
    one, two = seq_orders()
    value = jnp.concatenate(
        [
            halve_seq(value[..., :half], one, everything[1:]),
            halve_seq(value[..., half:], two, everything[1:]),
        ],
        axis=-1,
    )
    total = lax.dynamic_index_in_dim(value, place, 0, False).astype(jnp.float32)
    for step in range(1, shards):
        target = lax.rem(place + step, shards)
        arrived = rotate(lax.dynamic_index_in_dim(value, target, 0, False), step)
        total = total + arrived.astype(jnp.float32)
    whole = gather_seq_both(total.astype(jnp.bfloat16), 0)
    return whole.reshape(rows // shards, columns).astype(jnp.float32)


def on_device(
    tokens,
    slot_lengths,
    live_lengths,
    norm_gain,
    w_qkv,
    w_beta,
    w_outgate,
    conv_weight,
    ridge,
    head_gain,
    w_out,
    ffn_gain,
    w_gate,
    w_up,
    w_down,
    cotangent,
):
    section_out = make_kit()
    row_count = tokens.shape[1]
    depth = (WINDOW + row_count - 1) // row_count
    halo_rows = depth * row_count
    main_rows = halo_rows + row_count
    shards = lax.axis_size("wshard")
    shard_rows = norm_gain.shape[0]
    tap_columns = TAPS * conv_weight.shape[1] // shard_rows
    ffn = w_gate.shape[1]

    own_tokens = tokens[0]
    pieces = [passed_along(own_tokens, "seq", hop) for hop in range(depth, 0, -1)]
    pieces.append(own_tokens)
    pieces.append(passed_along(own_tokens[row_count - PRE :], "seq", depth + 1))
    ext_tokens = jnp.concatenate(pieces)

    small = jnp.concatenate(
        [
            w_beta,
            norm_gain[:, None],
            ridge[:, None],
            head_gain[:, None],
            ffn_gain[:, None],
            conv_weight.reshape(shard_rows, tap_columns),
        ],
        axis=1,
    )
    small = jnp.pad(small, ((0, 0), (0, SMALL - small.shape[1])))
    w_front = gather_weight(jnp.concatenate([w_qkv, small], axis=1))
    middle = gather_weight(jnp.concatenate([w_outgate, w_out, w_gate, w_up], axis=1))
    all_down = gather_weight(w_down)
    small = w_front[:, 3 * D :].astype(f32)
    gain_in, all_ridge, gain_head, gain_ffn = (small[:, HEADS + index] for index in range(4))
    taps = small[:, HEADS + 4 : HEADS + 4 + tap_columns]
    taps = taps.reshape(shards, TAPS, -1).transpose(1, 0, 2).reshape(TAPS, 3 * D)
    all_og = middle[:, :D]
    all_out = middle[:, D : 2 * D].astype(f32)
    all_gate = middle[:, 2 * D : 2 * D + ffn].astype(f32)
    all_up = middle[:, 2 * D + ffn :].astype(f32)
    all_down = all_down.astype(f32)

    rank = lax.axis_index("seq")
    first = rank * row_count - halo_rows - PRE
    positions = first + jnp.arange(PRE + main_rows, dtype=jnp.int32)
    segment, valid = token_layout(slot_lengths[0], live_lengths[0], positions)
    main_seg = segment[PRE:]
    own_seg = main_seg[halo_rows:]
    valid_own = valid[PRE + halo_rows :].astype(f32)
    same = jnp.stack(
        [segment[PRE - tap : PRE - tap + main_rows] == main_seg for tap in range(TAPS)], axis=1
    ).astype(f32)
    spacing = positions[None, PRE + halo_rows :] - positions[PRE:, None]
    mask = (
        (spacing >= 0)
        & (spacing < WINDOW)
        & (main_seg[:, None] == own_seg[None, :])
        & valid[PRE:, None]
    ).astype(bf16)
    gain_row = gain_in[None, :]
    ridge_column = all_ridge[:, None]
    x_own = own_tokens.astype(f32)

    hidden, kv_in, q_in, q_pre, queries, keys, values, beta = front(
        ext_tokens, same, gain_row, w_front, taps, row_count
    )
    hidden_own = hidden[halo_rows:main_rows]
    gate_pre = jnp.dot(hidden_own, all_og, preferred_element_type=f32)
    mixed, image0, image1 = attn_fwd(queries, keys, values, beta, mask, ridge_column)

    def back_half(xrow, mixed, gate_pre, gain_head, mat_out, gain_ffn, mat_gate, mat_up, mat_down):
        return section_out(
            xrow, mixed, gate_pre, gain_head, mat_out, gain_ffn, mat_gate, mat_up, mat_down, valid_own
        )

    output, pull_back = jax.vjp(
        back_half, x_own, mixed, gate_pre, gain_head, all_out, gain_ffn, all_gate, all_up, all_down
    )
    grad_out = cotangent[0].astype(f32)
    d_xout, d_mixed, d_gate, d_ghead, d_wout, d_gffn, d_wgate, d_wup, d_wdown = pull_back(grad_out)
    d_gate = d_gate.astype(bf16)

    total_down = sum_weight(d_wdown)
    total_ffn = sum_weight(jnp.concatenate([d_wgate, d_wup], axis=1).astype(bf16))

    d_query, d_key, d_value, d_beta, d_ridge = attn_bwd(
        queries, keys, values, beta, mask, ridge_column, image0, image1, d_mixed.astype(bf16)
    )
    d_kv_in, d_q_in, d_q_pre, d_beta_pre, d_halo, d_own, d_gain, d_taps = back(
        ext_tokens,
        kv_in,
        same,
        q_in,
        q_pre,
        d_key,
        d_value,
        d_query,
        beta,
        d_beta,
        d_gate,
        d_xout,
        gain_row,
        w_front,
        all_og,
        taps,
    )

    def weight_grad(left, right):
        return lax.dot_general(
            left, right, (((0,), (0,)), ((), ())), preferred_element_type=f32
        ).astype(bf16)

    d_wog = weight_grad(hidden_own, d_gate)
    d_wq = weight_grad(
        hidden[halo_rows - PRE : main_rows], jnp.concatenate([d_q_pre, d_q_in])
    )
    d_wkv = weight_grad(hidden, d_kv_in)
    d_wbeta = weight_grad(hidden[:main_rows], d_beta_pre)[:, :HEADS]

    d_tokens = d_own
    for hop in range(1, depth + 1):
        start = halo_rows - hop * row_count
        part = passed_along(d_halo[start : start + row_count], "seq", -hop)
        d_tokens = d_tokens + part.astype(f32)
    part = passed_along(d_halo[halo_rows:], "seq", -(depth + 1)).astype(f32)
    d_tokens = d_tokens + jnp.pad(part, ((row_count - PRE, 0), (0, 0)))

    d_small = jnp.concatenate(
        [
            d_wbeta.astype(f32),
            d_gain.reshape(D, 1),
            d_ridge,
            d_ghead[:, None],
            d_gffn[:, None],
            d_taps.reshape(TAPS, shards, -1).transpose(1, 0, 2).reshape(D, tap_columns),
        ],
        axis=1,
    ).astype(bf16)
    d_small = jnp.pad(d_small, ((0, 0), (0, SMALL - d_small.shape[1])))
    total_middle = sum_weight(jnp.concatenate([d_wog, d_wout.astype(bf16)], axis=1))
    total_front = sum_weight(jnp.concatenate([d_wq, d_wkv, d_small], axis=1))
    t_small = total_front[:, 3 * D :]
    return (
        output.astype(bf16)[None],
        d_tokens.astype(bf16)[None],
        t_small[:, HEADS],
        total_front[:, : 3 * D],
        t_small[:, :HEADS],
        total_middle[:, :D],
        t_small[:, HEADS + 4 : HEADS + 4 + tap_columns].reshape(TAPS, -1),
        t_small[:, HEADS + 1],
        t_small[:, HEADS + 2],
        total_middle[:, D:],
        t_small[:, HEADS + 3],
        total_ffn[:, :ffn],
        total_ffn[:, ffn:],
        total_down,
    )


def solution(mesh):
    return jax.shard_map(
        on_device,
        mesh=mesh,
        in_specs=(
            P("wshard", "seq", None),
            P("wshard", None),
            P("wshard", None),
            P("wshard"),
            P("wshard", None),
            P("wshard", None),
            P("wshard", None),
            P(None, "wshard"),
            P("wshard"),
            P("wshard"),
            P("wshard", None),
            P("wshard"),
            P("wshard", None),
            P("wshard", None),
            P("wshard", None),
            P("wshard", "seq", None),
        ),
        out_specs=(
            P("wshard", "seq", None),
            P("wshard", "seq", None),
            P("wshard"),
            P("wshard", None),
            P("wshard", None),
            P("wshard", None),
            P(None, "wshard"),
            P("wshard"),
            P("wshard"),
            P("wshard", None),
            P("wshard"),
            P("wshard", None),
            P("wshard", None),
            P("wshard", None),
        ),
        check_vma=False,
    )
```

```python
import functools
import jax
import jax.numpy as jnp
from jax import lax
from jax.experimental import pallas as pl
from jax.experimental.pallas import tpu as pltpu
from jax.sharding import PartitionSpec as P

D = 1024
HEADS = 8
HEAD_DIM = 128
TAPS = 4
WINDOW = 1024
PRE = 16
SMALL = 128
EXTRA = 512
MESH = pl.DeviceIdType.MESH
f32 = jnp.float32
bf16 = jnp.bfloat16
QB = 256
CH = 256
ROWS = 256


def mm(left, right):
    return jnp.dot(left, right, preferred_element_type=f32)


def mm_t(left, right):
    return lax.dot_general(left, right, (((1,), (1,)), ((), ())), preferred_element_type=f32)


def conv_total(ext_ref, slot, same, taps):
    total = taps[0:1] * ext_ref[slot, 8 : 8 + ROWS, :]
    for tap in range(1, TAPS):
        total = total + taps[tap : tap + 1] * ext_ref[slot, 8 - tap : 8 - tap + ROWS, :] * same[tap]
    return total


def unit_scale(active):
    return lax.rsqrt(jnp.sum(active * active, axis=-1, keepdims=True) + 1e-06)


def in_heads(work, *arrays):
    width = arrays[0].shape[1]
    return jnp.concatenate(
        [
            work(*(array[:, at : at + HEAD_DIM] for array in arrays))
            for at in range(0, width, HEAD_DIM)
        ],
        axis=1,
    )


def row_norm(x, gain):
    return (x * lax.rsqrt(jnp.mean(x * x, axis=-1, keepdims=True) + 1e-06) * gain).astype(bf16)


def front_kernel(
    first_own,
    x_ref,
    same_ref,
    gain_ref,
    w_ref,
    taps_ref,
    hid_ref,
    kvin_ref,
    qin_ref,
    qpre_ref,
    q_ref,
    k_ref,
    v_ref,
    beta_ref,
    ext_ref,
    tail_ref,
):
    step = pl.program_id(0)
    gain = gain_ref[...]
    kv_slots = 2 * D // CH

    @pl.when(step == 0)
    def before():
        hidden = row_norm(x_ref[0:PRE].astype(f32), gain)
        hid_ref[0:PRE] = hidden
        for slot in range(kv_slots):
            rows = mm(hidden, w_ref[:, D + CH * slot : D + CH * (slot + 1)]).astype(bf16)
            kvin_ref[0:PRE, CH * slot : CH * (slot + 1)] = rows
            ext_ref[slot, ROWS : ROWS + 8, :] = rows.astype(f32)[PRE - 8 :]

    def through(slot, hidden, same, column, in_ref, at):
        ext_ref[slot, 0:8, :] = ext_ref[slot, ROWS : ROWS + 8, :]
        rows = mm(hidden, w_ref[:, column : column + CH]).astype(bf16)
        in_ref[:, at : at + CH] = rows
        ext_ref[slot, 8 : 8 + ROWS, :] = rows.astype(f32)
        total = conv_total(ext_ref, slot, same, taps_ref[:, column : column + CH])
        return total * jax.nn.sigmoid(total)

    def unit(active):
        return in_heads(lambda part: part * unit_scale(part), active).astype(bf16)

    @pl.when(step > 0)
    def main():
        same = [same_ref[:, tap : tap + 1] for tap in range(TAPS)]
        hidden = row_norm(x_ref[...].astype(f32), gain)
        hid_ref[...] = hidden
        for slot in range(kv_slots):
            at = CH * slot
            active = through(slot, hidden, same, D + at, kvin_ref, at)
            if at < D:
                k_ref[:, at : at + CH] = unit(active)
            else:
                v_ref[:, at - D : at - D + CH] = active.astype(bf16)
        gates = jax.nn.sigmoid(mm(hidden, w_ref[:, 3 * D : 3 * D + SMALL])).astype(bf16)
        lane = lax.broadcasted_iota(jnp.int32, (ROWS, SMALL), 1)
        beta_ref[...] = jnp.where(lane < HEADS, gates.astype(f32), 0.0)

        @pl.when(step == first_own + 1)
        def own_history():
            rows = mm(tail_ref[...], w_ref[:, :D]).astype(bf16)
            qpre_ref[...] = rows
            for slot in range(D // CH):
                ext_ref[kv_slots + slot, ROWS : ROWS + 8, :] = rows.astype(f32)[
                    PRE - 8 :, CH * slot : CH * (slot + 1)
                ]

        @pl.when(step > first_own)
        def own():
            for slot in range(D // CH):
                at = CH * slot
                active = through(kv_slots + slot, hidden, same, at, qin_ref, at)
                q_ref[:, at : at + CH] = unit(active)

        tail_ref[...] = hidden[ROWS - PRE :]


def front(ext_tokens, same, gain, w_front, taps, own_rows):
    ext_rows = ext_tokens.shape[0]
    main_rows = ext_rows - PRE
    blocks = main_rows // ROWS
    first_own = (main_rows - own_rows) // ROWS

    def ext_block(step):
        return (jnp.where(step == 0, blocks, step - 1), 0)

    def main_block(step):
        return (jnp.maximum(step - 1, 0), 0)

    def own_block(step):
        return (jnp.maximum(step - 1 - first_own, 0), 0)

    def fixed(array):
        return pl.BlockSpec(array.shape, lambda step: (0, 0))

    shape = jax.ShapeDtypeStruct
    return pl.pallas_call(
        functools.partial(front_kernel, first_own),
        grid=(blocks + 1,),
        in_specs=[
            pl.BlockSpec((ROWS, D), ext_block),
            pl.BlockSpec((ROWS, TAPS), main_block),
            fixed(gain),
            fixed(w_front),
            fixed(taps),
        ],
        out_specs=[
            pl.BlockSpec((ROWS, D), ext_block),
            pl.BlockSpec((ROWS, 2 * D), ext_block),
            pl.BlockSpec((ROWS, D), own_block),
            pl.BlockSpec((PRE, D), lambda step: (0, 0)),
            pl.BlockSpec((ROWS, D), own_block),
            pl.BlockSpec((ROWS, D), main_block),
            pl.BlockSpec((ROWS, D), main_block),
            pl.BlockSpec((ROWS, SMALL), main_block),
        ],
        out_shape=[
            shape((ext_rows, D), bf16),
            shape((ext_rows, 2 * D), bf16),
            shape((own_rows, D), bf16),
            shape((PRE, D), bf16),
            shape((own_rows, D), bf16),
            shape((main_rows, D), bf16),
            shape((main_rows, D), bf16),
            shape((main_rows, SMALL), f32),
        ],
        scratch_shapes=[
            pltpu.VMEM((3 * D // CH, 8 + ROWS, CH), f32),
            pltpu.VMEM((PRE, D), bf16),
        ],
        compiler_params=pltpu.CompilerParams(
            dimension_semantics=("arbitrary",), vmem_limit_bytes=50 << 20
        ),
        cost_estimate=pl.CostEstimate(
            flops=4 * (main_rows * 2 + own_rows) * D * D, bytes_accessed=30 << 20, transcendentals=0
        ),
        name="front",
    )(ext_tokens, same, gain, w_front, taps)


def back_kernel(
    blocks,
    first_own,
    x_ref,
    kvin_ref,
    kvprev_ref,
    same_ref,
    qin_ref,
    qprev_ref,
    qpre_ref,
    dk_ref,
    dv_ref,
    dq_ref,
    beta_ref,
    dbeta_ref,
    dgate_ref,
    dres_ref,
    gain_ref,
    w_ref,
    wog_ref,
    taps_ref,
    dkvin_ref,
    dqin_ref,
    dqpre_ref,
    dbp_ref,
    dxhalo_ref,
    dxown_ref,
    dgain_ref,
    dtaps_ref,
    ext_ref,
    buf_ref,
    dh_ref,
):
    step = pl.program_id(0)
    block = blocks - 1 - step
    kv_slots = 2 * D // CH
    gain = gain_ref[...]

    @pl.when(step == 0)
    def clear():
        dgain_ref[...] = jnp.zeros_like(dgain_ref)
        dtaps_ref[...] = jnp.zeros_like(dtaps_ref)
        buf_ref[:, :, ROWS : ROWS + 8, :] = jnp.zeros_like(buf_ref[:, :, ROWS : ROWS + 8, :])

    def norm_back(x, dh):
        scale = lax.rsqrt(jnp.mean(x * x, axis=-1, keepdims=True) + 1e-06)
        normal = x * scale
        dgain_ref[...] += jnp.sum(dh * normal, axis=0, keepdims=True)
        scaled = dh * gain
        return scale * (scaled - normal * jnp.mean(scaled * normal, axis=-1, keepdims=True))

    def shifted(slot, start, count):
        total = buf_ref[slot, 1, start + 1 : start + 1 + count, :]
        for tap in range(2, TAPS):
            total = total + buf_ref[slot, tap, start + tap : start + tap + count, :]
        return total

    def through(slot, column, history, rows, grad, unit, same):
        ext_ref[slot, 0:8, :] = history
        ext_ref[slot, 8 : 8 + ROWS, :] = rows.astype(f32)
        taps = taps_ref[:, column : column + CH]
        total = conv_total(ext_ref, slot, same, taps)
        gate = jax.nn.sigmoid(total)
        active = total * gate
        if unit:

            def unit_back(part, part_grad):
                scale = unit_scale(part)
                normal = part * scale
                return scale * (
                    part_grad - normal * jnp.sum(part_grad * normal, axis=-1, keepdims=True)
                )

            grad = in_heads(unit_back, active, grad)
        grad = grad * (gate + active * (1.0 - gate))
        result = grad * taps[0:1]
        dtaps_ref[0:1, column : column + CH] += jnp.sum(
            grad * ext_ref[slot, 8 : 8 + ROWS, :], axis=0, keepdims=True
        )
        for tap in range(1, TAPS):
            held = grad * same[tap]
            dtaps_ref[tap : tap + 1, column : column + CH] += jnp.sum(
                held * ext_ref[slot, 8 - tap : 8 - tap + ROWS, :], axis=0, keepdims=True
            )
            buf_ref[slot, tap, 0:ROWS, :] = held * taps[tap : tap + 1]
        result = (result + shifted(slot, 0, ROWS)).astype(bf16)
        for tap in range(1, TAPS):
            buf_ref[slot, tap, ROWS : ROWS + 8, :] = buf_ref[slot, tap, 0:8, :]
        return result

    def before_rows(slot):
        for tap in range(1, TAPS):
            buf_ref[slot, tap, ROWS - PRE : ROWS, :] = jnp.zeros((PRE, CH), f32)
        return shifted(slot, ROWS - PRE, PRE).astype(bf16)

    @pl.when(step < blocks)
    def main():
        same = [same_ref[:, tap : tap + 1] for tap in range(TAPS)]
        beta = beta_ref[...]
        gates = (dbeta_ref[...] * beta * (1.0 - beta)).astype(bf16)
        dbp_ref[...] = gates
        dh = mm_t(gates, w_ref[:, 3 * D : 3 * D + SMALL])
        for slot in range(kv_slots):
            at = CH * slot
            grad = dk_ref[:, at : at + CH] if at < D else dv_ref[:, at - D : at - D + CH]
            history = kvprev_ref[PRE - 8 : PRE, at : at + CH].astype(f32)
            rows = kvin_ref[:, at : at + CH]
            rows = through(slot, D + at, history, rows, grad, at < D, same)
            dkvin_ref[:, at : at + CH] = rows
            dh = dh + mm_t(rows, w_ref[:, D + at : D + at + CH])
        dh_ref[...] = dh

        @pl.when(block >= first_own)
        def own():
            dh = mm_t(dgate_ref[...], wog_ref[...])
            for slot in range(D // CH):
                at = CH * slot
                history = jnp.where(
                    block == first_own,
                    qpre_ref[PRE - 8 :, at : at + CH].astype(f32),
                    qprev_ref[PRE - 8 :, at : at + CH].astype(f32),
                )
                rows = qin_ref[:, at : at + CH]
                rows = through(
                    kv_slots + slot, at, history, rows, dq_ref[:, at : at + CH], True, same
                )
                dqin_ref[:, at : at + CH] = rows
                dh = dh + mm_t(rows, w_ref[:, at : at + CH])
            dxown_ref[...] = dres_ref[...] + norm_back(x_ref[...].astype(f32), dh_ref[...] + dh)

        @pl.when(block == first_own - 1)
        def own_history():
            dh = jnp.zeros((PRE, D), f32)
            for slot in range(D // CH):
                at = CH * slot
                rows = before_rows(kv_slots + slot)
                dqpre_ref[:, at : at + CH] = rows
                dh = dh + mm_t(rows, w_ref[:, at : at + CH])
            dh_ref[ROWS - PRE : ROWS, :] += dh

        @pl.when(block < first_own)
        def halo():
            dxhalo_ref[...] = norm_back(x_ref[...].astype(f32), dh_ref[...]).astype(bf16)

    @pl.when(step == blocks)
    def before():
        dh = jnp.zeros((PRE, D), f32)
        for slot in range(kv_slots):
            at = CH * slot
            rows = before_rows(slot)
            dkvin_ref[0:PRE, at : at + CH] = rows
            dh = dh + mm_t(rows, w_ref[:, D + at : D + at + CH])
        dxhalo_ref[0:PRE, :] = norm_back(x_ref[0:PRE].astype(f32), dh).astype(bf16)


def back(
    ext_tokens, kvin, same, qin, qpre, dk, dv, dq, beta, dbeta, dgate, dres, gain, w_front, w_og, taps
):
    ext_rows = ext_tokens.shape[0]
    main_rows = ext_rows - PRE
    own_rows = dq.shape[0]
    blocks = main_rows // ROWS
    first_own = (main_rows - own_rows) // ROWS
    small_blocks = ROWS // PRE

    def ext_block(step):
        return (jnp.where(step == blocks, blocks, blocks - 1 - step), 0)

    def main_block(step):
        return (jnp.maximum(blocks - 1 - step, 0), 0)

    def prev_block(step):
        block = blocks - 1 - step
        return (jnp.where(block <= 0, blocks * small_blocks, small_blocks * block - 1), 0)

    def own_block(step):
        return (jnp.maximum(blocks - 1 - step - first_own, 0), 0)

    def own_prev_block(step):
        return (jnp.maximum(small_blocks * (blocks - 1 - step - first_own) - 1, 0), 0)

    def halo_block(step):
        block = jnp.minimum(blocks - 1 - step, first_own - 1)
        return (jnp.where(step == blocks, first_own, block), 0)

    def fixed(array):
        return pl.BlockSpec(array.shape, lambda step: (0, 0))

    shape = jax.ShapeDtypeStruct
    return pl.pallas_call(
        functools.partial(back_kernel, blocks, first_own),
        grid=(blocks + 1,),
        in_specs=[
            pl.BlockSpec((ROWS, D), ext_block),
            pl.BlockSpec((ROWS, 2 * D), ext_block),
            pl.BlockSpec((PRE, 2 * D), prev_block),
            pl.BlockSpec((ROWS, TAPS), main_block),
            pl.BlockSpec((ROWS, D), own_block),
            pl.BlockSpec((PRE, D), own_prev_block),
            fixed(qpre),
            pl.BlockSpec((ROWS, D), main_block),
            pl.BlockSpec((ROWS, D), main_block),
            pl.BlockSpec((ROWS, D), own_block),
            pl.BlockSpec((ROWS, SMALL), main_block),
            pl.BlockSpec((ROWS, SMALL), main_block),
            pl.BlockSpec((ROWS, D), own_block),
            pl.BlockSpec((ROWS, D), own_block),
            fixed(gain),
            fixed(w_front),
            fixed(w_og),
            fixed(taps),
        ],
        out_specs=[
            pl.BlockSpec((ROWS, 2 * D), ext_block),
            pl.BlockSpec((ROWS, D), own_block),
            pl.BlockSpec((PRE, D), lambda step: (0, 0)),
            pl.BlockSpec((ROWS, SMALL), main_block),
            pl.BlockSpec((ROWS, D), halo_block),
            pl.BlockSpec((ROWS, D), own_block),
            pl.BlockSpec((1, D), lambda step: (0, 0)),
            pl.BlockSpec((TAPS, 3 * D), lambda step: (0, 0)),
        ],
        out_shape=[
            shape((ext_rows, 2 * D), bf16),
            shape((own_rows, D), bf16),
            shape((PRE, D), bf16),
            shape((main_rows, SMALL), bf16),
            shape((main_rows - own_rows + PRE, D), bf16),
            shape((own_rows, D), f32),
            shape((1, D), f32),
            shape((TAPS, 3 * D), f32),
        ],
        scratch_shapes=[
            pltpu.VMEM((3 * D // CH, 8 + ROWS, CH), f32),
            pltpu.VMEM((3 * D // CH, TAPS, ROWS + 8, CH), f32),
            pltpu.VMEM((ROWS, D), f32),
        ],
        compiler_params=pltpu.CompilerParams(
            dimension_semantics=("arbitrary",), vmem_limit_bytes=56 << 20
        ),
        cost_estimate=pl.CostEstimate(
            flops=6 * (main_rows * 2 + own_rows) * D * D, bytes_accessed=40 << 20, transcendentals=0
        ),
        name="back",
    )(
        ext_tokens,
        kvin,
        kvin,
        same,
        qin,
        qin,
        qpre,
        dk,
        dv,
        dq,
        beta,
        dbeta,
        dgate,
        dres,
        gain,
        w_front,
        w_og,
        taps,
    )


def total(v):
    return jnp.sum(v,axis=0,keepdims=True)

def head_column(beta_ref, h):
    beta=beta_ref[...]
    lane=lax.broadcasted_iota(jnp.int32,beta.shape,1)
    return jnp.sum(jnp.where(lane==h,beta,0.0),axis=1,keepdims=True)

def attn_fwd_kernel(q_ref,k_ref,v_ref,beta_ref,mask_ref,ridge_ref,o_ref,a0_ref,a1_ref,kt_ref,vt_ref,w_ref):
    h=pl.program_id(0)
    rows=q_ref.shape[0]
    span=WINDOW+QB
    kt_ref[...]=k_ref[...].T
    vt_ref[...]=v_ref[...].T
    column=head_column(beta_ref,h)
    ridge=ridge_ref[...]
    blocks=range(rows//QB)
    chunks=range(span//CH)
    for b in blocks:
        for c in chunks:
            at=slice(QB*b+CH*c,QB*b+CH*(c+1))
            w_ref[b,CH*c:CH*(c+1),:]=mask_ref[at,QB*b:QB*(b+1)].astype(f32)*column[at]
    def apply(b,vector,right):
        low=vector.astype(bf16)
        out=jnp.zeros((HEAD_DIM,QB),f32)
        for c in chunks:
            at=slice(QB*b+CH*c,QB*b+CH*(c+1))
            s=mm(k_ref[at,:],low)
            s=(w_ref[b,CH*c:CH*(c+1),:]*s).astype(bf16)
            out=out+mm(right[:,at],s)
        return out
    q=[q_ref[QB*b:QB*(b+1),:].astype(f32).T for b in blocks]
    a0=[apply(b,q[b],kt_ref)+ridge*q[b] for b in blocks]
    for b in blocks: a0_ref[:,QB*b:QB*(b+1)]=a0[b]
    x1=[];p1=[];r1=[];e1=[]
    for b in blocks:
        e0=total(q[b]*q[b])
        s0=e0/total(q[b]*a0[b])
        x1.append(s0*q[b])
        r=q[b]-s0*a0[b]
        e=total(r*r)
        r1.append(r);e1.append(e)
        p1.append(r+e/e0*q[b])
    a1=[apply(b,p1[b],kt_ref)+ridge*p1[b] for b in blocks]
    for b in blocks: a1_ref[:,QB*b:QB*(b+1)]=a1[b]
    x2=[x1[b]+e1[b]/total(p1[b]*a1[b])*p1[b] for b in blocks]
    for b in blocks:
        o_ref[QB*b:QB*(b+1),:]=apply(b,x2[b],vt_ref).T

def attn_fwd(q,k,v,beta,mask_t,ridge):
    rows=q.shape[0]; keys=k.shape[0]
    head=lambda n: pl.BlockSpec((n,HEAD_DIM),lambda h:(0,h))
    heads_t=pl.BlockSpec((HEAD_DIM,rows),lambda h:(h,0))
    fixed=lambda a: pl.BlockSpec(a.shape,lambda h:(0,0))
    flops=6*2*rows*(WINDOW+QB)*D
    return pl.pallas_call(
        attn_fwd_kernel, grid=(HEADS,),
        in_specs=[head(rows),head(keys),head(keys),fixed(beta),fixed(mask_t),pl.BlockSpec((HEAD_DIM,1),lambda h:(h,0))],
        out_specs=[head(rows),heads_t,heads_t],
        out_shape=[jax.ShapeDtypeStruct((rows,D),f32)]+[jax.ShapeDtypeStruct((D,rows),f32)]*2,
        scratch_shapes=[pltpu.VMEM((HEAD_DIM,keys),bf16)]*2+[pltpu.VMEM((rows//QB,WINDOW+QB,QB),f32)],
        compiler_params=pltpu.CompilerParams(dimension_semantics=("arbitrary",),vmem_limit_bytes=48<<20),
        cost_estimate=pl.CostEstimate(flops=2*flops,bytes_accessed=20<<20,transcendentals=0),
        name="attn_fwd",
    )(q,k,v,beta,mask_t,ridge)

def attn_bwd_kernel(q_ref,k_ref,v_ref,beta_ref,mask_ref,ridge_ref,a0_ref,a1_ref,do_ref,dq_ref,dk_ref,dv_ref,dbeta_ref,dridge_ref,kt_ref,w_ref,acc_ref):
    h=pl.program_id(0)
    rows=q_ref.shape[0]
    span=WINDOW+QB
    kt_ref[...]=k_ref[...].T
    column=head_column(beta_ref,h)
    ridge=ridge_ref[...]
    blocks=range(rows//QB)
    chunks=range(span//CH)
    dk_ref[...]=jnp.zeros_like(dk_ref)
    dv_ref[...]=jnp.zeros_like(dv_ref)
    acc_ref[...]=jnp.zeros_like(acc_ref)
    for b in blocks:
        for c in chunks:
            at=slice(QB*b+CH*c,QB*b+CH*(c+1))
            w_ref[b,CH*c:CH*(c+1),:]=mask_ref[at,QB*b:QB*(b+1)].astype(f32)*column[at]
    def apply_back(b,vector,grad,grad_rows,right_ref,dright_ref):
        low=vector.astype(bf16)
        low_rows=vector.T.astype(bf16)
        out=jnp.zeros((HEAD_DIM,QB),f32)
        for c in chunks:
            at=slice(QB*b+CH*c,QB*b+CH*(c+1))
            w=w_ref[b,CH*c:CH*(c+1),:]
            s=mm(k_ref[at,:],low)
            dw=mm(right_ref[at,:],grad)
            masked=dw*mask_ref[at,QB*b:QB*(b+1)].astype(f32)
            for_beta=masked*s
            part=for_beta[:,:128]
            for lane in range(128,QB,128):
                part=part+for_beta[:,lane:lane+128]
            acc_ref[at,:]+=part
            ws=(w*s).astype(bf16)
            ds=(w*dw).astype(bf16)
            out=out+mm(kt_ref[:,at],ds)
            dright_ref[at,:]+=mm(ws,grad_rows)
            dk_ref[at,:]+=mm(ds,low_rows)
        return out
    st=[]
    for b in blocks:
        cols=slice(QB*b,QB*(b+1))
        q=q_ref[cols,:].astype(f32).T
        a0=a0_ref[:,cols]; a1=a1_ref[:,cols]
        e0=total(q*q); d0=total(q*a0); s0=e0/d0
        x1=s0*q; r1=q-s0*a0; e1=total(r1*r1); b0=e1/e0
        p1=r1+b0*q; d1=total(p1*a1); s1=e1/d1
        x2=x1+s1*p1
        st.append((q,a0,a1,e0,d0,s0,r1,e1,b0,p1,d1,s1,x2))
    dx2=[]
    for b in blocks:
        do=do_ref[QB*b:QB*(b+1),:]
        dx2.append(apply_back(b,st[b][12],do.astype(f32).T.astype(bf16),do,v_ref,dv_ref))
    da1=[];dp1=[];de1=[];dr=0
    for b in blocks:
        q,a0,a1,e0,d0,s0,r1,e1,b0,p1,d1,s1,x2=st[b]
        ds1=total(dx2[b]*p1)
        de1.append(ds1/d1)
        dd1=-ds1*s1/d1
        g=dd1*p1
        da1.append(g)
        dp1.append(s1*dx2[b]+dd1*a1+ridge*g)
        dr=dr+jnp.sum(g*p1,axis=1,keepdims=True)
    for b in blocks:
        g=da1[b]
        dp1[b]=dp1[b]+apply_back(b,st[b][9],g.astype(bf16),g.T.astype(bf16),k_ref,dk_ref)
    da0=[];dq=[]
    for b in blocks:
        q,a0,a1,e0,d0,s0,r1,e1,b0,p1,d1,s1,x2=st[b]
        db0=total(dp1[b]*q)
        dpq=b0*dp1[b]
        de=de1[b]+db0/e0
        de0=-db0*b0/e0
        dr1=dp1[b]+2.0*de*r1
        ds0=total(dx2[b]*q)-total(dr1*a0)
        dpq=dpq+s0*dx2[b]
        g=-s0*dr1
        de0=de0+ds0/d0
        dd0=-ds0*s0/d0
        dpq=dpq+dd0*a0
        g=g+dd0*q
        dpq=dpq+dr1+2.0*de0*q+ridge*g
        da0.append(g);dq.append(dpq)
        dr=dr+jnp.sum(g*q,axis=1,keepdims=True)
    for b in blocks:
        g=da0[b]
        t=dq[b]+apply_back(b,st[b][0],g.astype(bf16),g.T.astype(bf16),k_ref,dk_ref)
        dq_ref[QB*b:QB*(b+1),:]=t.T
    dridge_ref[...]=dr
    found=jnp.sum(acc_ref[...],axis=1,keepdims=True)
    lane=lax.broadcasted_iota(jnp.int32,dbeta_ref.shape,1)
    @pl.when(h==0)
    def _():
        dbeta_ref[...]=jnp.zeros_like(dbeta_ref)
    dbeta_ref[...]=jnp.where(lane==h,found,dbeta_ref[...])

def attn_bwd(q,k,v,beta,mask_t,ridge,a0,a1,do):
    rows=q.shape[0]; keys=k.shape[0]
    head=lambda n: pl.BlockSpec((n,HEAD_DIM),lambda h:(0,h))
    heads_t=pl.BlockSpec((HEAD_DIM,rows),lambda h:(h,0))
    fixed=lambda a: pl.BlockSpec(a.shape,lambda h:(0,0))
    rd=pl.BlockSpec((HEAD_DIM,1),lambda h:(h,0))
    flops=15*2*rows*(WINDOW+QB)*D
    return pl.pallas_call(
        attn_bwd_kernel, grid=(HEADS,),
        in_specs=[head(rows),head(keys),head(keys),fixed(beta),fixed(mask_t),rd,heads_t,heads_t,head(rows)],
        out_specs=[head(rows),head(keys),head(keys),fixed(beta),rd],
        out_shape=[jax.ShapeDtypeStruct((rows,D),f32),jax.ShapeDtypeStruct((keys,D),f32),jax.ShapeDtypeStruct((keys,D),f32),jax.ShapeDtypeStruct(beta.shape,f32),jax.ShapeDtypeStruct((D,1),f32)],
        scratch_shapes=[pltpu.VMEM((HEAD_DIM,keys),bf16),pltpu.VMEM((rows//QB,WINDOW+QB,QB),f32),pltpu.VMEM((keys,128),f32)],
        compiler_params=pltpu.CompilerParams(dimension_semantics=("arbitrary",),vmem_limit_bytes=48<<20),
        cost_estimate=pl.CostEstimate(flops=2*flops,bytes_accessed=30<<20,transcendentals=0),
        name="attn_bwd",
    )(q,k,v,beta,mask_t,ridge,a0,a1,do)


def passed_along(value, axis, steps):
    count = lax.axis_size(axis)
    initial, last = (max(0, -steps), min(count, count - steps))
    return lax.ppermute(value, axis, [(source, source + steps) for source in range(initial, last)])


def token_layout(slot_row, live_row, positions):
    starts = (jnp.cumsum(slot_row) - slot_row).astype(jnp.int32)
    after = positions[:, None] >= starts[None, :]
    segment = (jnp.sum(after.astype(jnp.int32), axis=1) - 1).astype(jnp.int32)
    chosen = segment[:, None] == jnp.arange(slot_row.shape[0], dtype=jnp.int32)[None, :]
    begin = jnp.sum(jnp.where(chosen, starts[None, :], 0), axis=1).astype(jnp.int32)
    limit = jnp.sum(jnp.where(chosen, live_row[None, :], 0), axis=1).astype(jnp.int32)
    valid = (segment >= 0) & (positions - begin < limit)
    return (segment, valid)


def make_kit():

    @jax.custom_vjp
    def low(v):
        return lax.optimization_barrier(v.astype(jnp.bfloat16)).astype(jnp.float32)

    @jax.custom_vjp
    def low_back(v):
        return v

    def low_keep(v):
        return (low(v), None)

    def low_pass(kept, grad):
        return (grad,)

    def back_keep(v):
        return (v, None)

    def back_low(kept, grad):
        return (low(grad),)

    low.defvjp(low_keep, low_pass)
    low_back.defvjp(back_keep, back_low)

    @jax.custom_vjp
    def matmul(left, right):
        return jnp.dot(
            left.astype(jnp.bfloat16),
            right.astype(jnp.bfloat16),
            preferred_element_type=jnp.float32,
        )

    def matmul_keep(left, right):
        left_low = left.astype(jnp.bfloat16)
        right_low = right.astype(jnp.bfloat16)
        return (
            jnp.dot(left_low, right_low, preferred_element_type=jnp.float32),
            (left_low, right_low),
        )

    def matmul_grads(kept, grad):
        left_low, right_low = kept
        grad_low = grad.astype(jnp.bfloat16)
        grad_left = lax.dot_general(
            grad_low, right_low, (((1,), (1,)), ((), ())), preferred_element_type=jnp.float32
        )
        grad_right = lax.dot_general(
            left_low, grad_low, (((0,), (0,)), ((), ())), preferred_element_type=jnp.float32
        )
        return (grad_left, grad_right)

    matmul.defvjp(matmul_keep, matmul_grads)

    def section_out(
        xrow, mixed, gate_pre, gain_head, mat_out, gain_ffn, mat_gate, mat_up, mat_down, valid
    ):
        row_count = xrow.shape[0]
        shaped = mixed.reshape(row_count, HEADS, HEAD_DIM)
        shaped = shaped * lax.rsqrt(jnp.mean(shaped * shaped, axis=-1, keepdims=True) + 1e-05)
        normed = shaped.reshape(row_count, D) * gain_head
        gated = low(normed * jax.nn.silu(gate_pre))
        middle = xrow + low_back(matmul(gated, mat_out))
        hidden = low(
            middle * lax.rsqrt(jnp.mean(middle * middle, axis=-1, keepdims=True) + 1e-06) * gain_ffn
        )
        inner = low(
            jax.nn.silu(low_back(matmul(hidden, mat_gate))) * low_back(matmul(hidden, mat_up))
        )
        return valid[:, None] * (middle + low_back(matmul(inner, mat_down)))

    return section_out


class Here:
    def __init__(self):
        rank = lax.axis_index("seq")
        self.place = lax.axis_index("wshard")
        self.shards = lax.axis_size("wshard")
        self.core = rank % 2
        self.x = (rank // 2) % 2
        self.y = (rank // 4) % 2
        self.core_next = rank + 1 - 2 * self.core
        self.x_next = rank + 2 - 4 * self.x
        self.y_next = rank + 4 - 8 * self.y

    def other(self, step):
        return (self.place + step) % self.shards

    def meet(self):
        barrier = pltpu.get_barrier_semaphore()
        for near in (self.core_next, self.x_next, self.y_next):
            pl.semaphore_signal(barrier, inc=1, device_id={"seq": near}, device_id_type=MESH)
        for step in range(1, self.shards):
            pl.semaphore_signal(
                barrier, inc=1, device_id={"wshard": self.other(step)}, device_id_type=MESH
            )
        pl.semaphore_wait(barrier, 3 + self.shards - 1)


class Sends:
    def __init__(self, send_sems, recv_sems):
        self.send_sems = send_sems
        self.recv_sems = recv_sems

    def make(self, index, source, target, **device):
        return pltpu.make_async_remote_copy(
            src_ref=source,
            dst_ref=target,
            send_sem=self.send_sems.at[index],
            recv_sem=self.recv_sems.at[index],
            device_id=device,
            device_id_type=MESH,
        )


def span(start, size):
    return pl.ds(pl.multiple_of(start, 128), size)


GATHER_COPIES = 18


def gather_copies(here, sends, source, target, phase):
    half = source.shape[-1] // 2
    quarter = half // 2
    mine = span(here.core * half, half)
    one = span(here.core * half, quarter)
    two = span(here.core * half + quarter, quarter)
    y, x = here.y, here.x
    others = range(1, here.shards)
    if phase == 0:
        return [
            sends.make(
                step - 1,
                source.at[y, x, :, mine],
                target.at[here.place, y, x, :, mine],
                wshard=here.other(step),
            )
            for step in others
        ]
    found = []
    for step in others:
        at = target.at[here.other(step)]
        if phase == 1:
            found.append((at.at[y, x, :, one], here.x_next))
            found.append((at.at[y, x, :, two], here.y_next))
        elif phase == 2:
            found.append((at.at[y, :, :, one], here.y_next))
            found.append((at.at[:, x, :, two], here.x_next))
        else:
            found.append((at.at[:, :, :, mine], here.core_next))
    first = {1: 3, 2: 9, 3: 15}[phase]
    return [
        sends.make(first + index, ref, ref, seq=near) for index, (ref, near) in enumerate(found)
    ]


def gather_kernel(count, *refs):
    sources = refs[:count]
    targets = refs[count : 2 * count]
    send_sems, recv_sems, own_sems = refs[2 * count :]
    here = Here()
    here.meet()
    every = []
    local = []
    for index in range(count):
        sends = Sends(send_sems.at[index], recv_sems.at[index])
        every.append(
            [
                gather_copies(here, sends, sources[index], targets[index], phase)
                for phase in range(4)
            ]
        )
        local.append(
            pltpu.make_async_copy(
                sources[index], targets[index].at[here.place], own_sems.at[index]
            )
        )
    for slot in range(count + 4):
        for index in range(count):
            phase = slot - index
            if 1 <= phase <= 4:
                for copy in every[index][phase - 1]:
                    copy.wait_recv()
            if 0 <= phase <= 3:
                for copy in every[index][phase]:
                    copy.start()
                if phase == 0:
                    local[index].start()
    for index in range(count):
        for phase in range(4):
            for copy in every[index][phase]:
                copy.wait_send()
        local[index].wait()


def gather(shards, collective_id):
    places = lax.axis_size("wshard")
    split = [shard.reshape(2, 2, shard.shape[0] // 4, shard.shape[1]) for shard in shards]
    count = len(shards)
    anywhere = pl.BlockSpec(memory_space=pl.ANY)
    whole = pl.pallas_call(
        functools.partial(gather_kernel, count),
        in_specs=[anywhere] * count,
        out_specs=[anywhere] * count,
        out_shape=[jax.ShapeDtypeStruct((places,) + part.shape, part.dtype) for part in split],
        scratch_shapes=[
            pltpu.SemaphoreType.DMA((count, GATHER_COPIES)),
            pltpu.SemaphoreType.DMA((count, GATHER_COPIES)),
            pltpu.SemaphoreType.DMA((count,)),
        ],
        compiler_params=pltpu.CompilerParams(
            collective_id=collective_id, has_side_effects=True, vmem_limit_bytes=50 << 20
        ),
        name="gather",
    )(*split)
    return [
        part.reshape(places * shard.shape[0], shard.shape[1]) for part, shard in zip(whole, shards)
    ]


SUM_COPIES = 13


class SumPart:
    def __init__(self, here, sends, local, grad, out, held, core_in, far_a, far_b, next_a, next_b, last, total):
        self.here, self.sends, self.local = here, sends, local
        self.grad, self.out, self.held = grad, out, held
        self.core_in, self.far_a, self.far_b = core_in, far_a, far_b
        self.next_a, self.next_b, self.last, self.total = next_a, next_b, last, total
        self.half = held.shape[-1]
        self.quarter = self.half // 2
        self.waiting = []
        self.sent = []

    def launch(self, copies):
        for copy in copies:
            copy.start()
        self.waiting = copies
        self.sent += copies

    def arrive(self):
        for copy in self.waiting:
            copy.wait_recv()

    def local_copy(self, index, source, target):
        return pltpu.make_async_copy(source, target, self.local.at[index])

    def step(self, phase):
        here, make, half, quarter = self.here, self.sends.make, self.half, self.quarter
        y, x, held, out = here.y, here.x, self.held, self.out
        places = here.shards
        one, two = pl.ds(0, quarter), pl.ds(quarter, quarter)
        mine = span(here.core * half, half)
        yours = span((1 - here.core) * half, half)
        out_one = span(here.core * half, quarter)
        out_two = span(here.core * half + quarter, quarter)
        self.arrive()
        if phase == 0:
            self.own = self.local_copy(0, self.grad.at[:, :, :, :, mine], held)
            self.own.start()
            self.launch(
                [make(0, self.grad.at[:, :, :, :, yours], self.core_in, seq=here.core_next)]
            )
        elif phase == 1:
            self.own.wait()

            def add(index, carry):
                at = (index // 4, (index // 2) % 2, index % 2)
                held[at] = (held[at].astype(f32) + self.core_in[at].astype(f32)).astype(bf16)
                return carry

            lax.fori_loop(0, 4 * places, add, 0)
            self.launch(
                [
                    make(1, held.at[:, :, 1 - x, :, one], self.far_a, seq=here.x_next),
                    make(2, held.at[:, 1 - y, :, :, two], self.far_b, seq=here.y_next),
                ]
            )
        elif phase == 2:

            def add(index, carry):
                place, side = index // 2, index % 2
                at = (place, side, x, slice(None), slice(0, quarter))
                held[at] = (
                    held[at].astype(f32) + self.far_a[place, side].astype(f32)
                ).astype(bf16)
                at = (place, y, side, slice(None), slice(quarter, half))
                held[at] = (
                    held[at].astype(f32) + self.far_b[place, side].astype(f32)
                ).astype(bf16)
                return carry

            lax.fori_loop(0, 2 * places, add, 0)
            self.launch(
                [
                    make(3, held.at[:, 1 - y, x, :, one], self.next_a, seq=here.y_next),
                    make(4, held.at[:, y, 1 - x, :, two], self.next_b, seq=here.x_next),
                ]
            )
        elif phase == 3:

            def add(place, carry):
                at = (place, y, x, slice(None), slice(0, quarter))
                held[at] = (held[at].astype(f32) + self.next_a[place].astype(f32)).astype(bf16)
                at = (place, y, x, slice(None), slice(quarter, half))
                held[at] = (held[at].astype(f32) + self.next_b[place].astype(f32)).astype(bf16)
                return carry

            lax.fori_loop(0, places, add, 0)
            self.launch(
                [
                    make(
                        4 + step,
                        held.at[here.other(step), y, x],
                        self.last.at[step - 1],
                        wshard=here.other(step),
                    )
                    for step in range(1, places)
                ]
            )
        elif phase == 4:
            total = held[here.place, y, x].astype(f32)
            for step in range(places - 1):
                total = total + self.last[step].astype(f32)
            self.total[...] = total.astype(bf16)
            self.own = self.local_copy(1, self.total, out.at[y, x, :, mine])
            self.own.start()
            self.launch(
                [
                    make(8, self.total.at[:, one], out.at[y, x, :, out_one], seq=here.y_next),
                    make(9, self.total.at[:, two], out.at[y, x, :, out_two], seq=here.x_next),
                ]
            )
        elif phase == 5:
            self.own.wait()
            both_one, both_two = out.at[:, x, :, out_one], out.at[y, :, :, out_two]
            self.launch(
                [
                    make(10, both_one, both_one, seq=here.x_next),
                    make(11, both_two, both_two, seq=here.y_next),
                ]
            )
        elif phase == 6:
            ref = out.at[:, :, :, mine]
            self.launch([make(12, ref, ref, seq=here.core_next)])

    def finish(self):
        for copy in self.sent:
            copy.wait_send()


def sum_kernel(parts, *refs):
    count = max(part[0] for part in parts) + 1
    grads = refs[:count]
    outs = refs[count : 2 * count]
    send_sems, recv_sems, local_sems = refs[2 * count : 2 * count + 3]
    scratch = refs[2 * count + 3 :]
    here = Here()
    here.meet()
    moving = []
    for index, (which, start, size) in enumerate(parts):
        rows = pl.ds(start, size)
        moving.append(
            SumPart(
                here,
                Sends(send_sems.at[index], recv_sems.at[index]),
                local_sems.at[index],
                grads[which].at[:, :, :, rows],
                outs[which].at[:, :, rows],
                *scratch[8 * index : 8 * index + 8],
            )
        )
    phases = 7
    for slot in range(len(parts) + phases):
        for index, part in enumerate(moving):
            phase = slot - index
            if 0 <= phase < phases:
                part.step(phase)
            elif phase == phases:
                part.arrive()
    for part in moving:
        part.finish()


def sum_over_devices(grads, parts, collective_id):
    places = lax.axis_size("wshard")
    split = [grad.reshape(places, 2, 2, grad.shape[0] // places // 4, grad.shape[1]) for grad in grads]
    anywhere = pl.BlockSpec(memory_space=pl.ANY)
    scratch = []
    for which, start, size in parts:
        half = grads[which].shape[1] // 2
        quarter = half // 2
        scratch += [
            pltpu.VMEM((places, 2, 2, size, half), bf16),
            pltpu.VMEM((places, 2, 2, size, half), bf16),
            pltpu.VMEM((places, 2, size, quarter), bf16),
            pltpu.VMEM((places, 2, size, quarter), bf16),
            pltpu.VMEM((places, size, quarter), bf16),
            pltpu.VMEM((places, size, quarter), bf16),
            pltpu.VMEM((places - 1, size, half), bf16),
            pltpu.VMEM((size, half), bf16),
        ]
    outs = pl.pallas_call(
        functools.partial(sum_kernel, parts),
        in_specs=[anywhere] * len(grads),
        out_specs=[anywhere] * len(grads),
        out_shape=[jax.ShapeDtypeStruct(part.shape[1:], bf16) for part in split],
        scratch_shapes=[
            pltpu.SemaphoreType.DMA((len(parts), SUM_COPIES)),
            pltpu.SemaphoreType.DMA((len(parts), SUM_COPIES)),
            pltpu.SemaphoreType.DMA((len(parts), 2)),
        ]
        + scratch,
        compiler_params=pltpu.CompilerParams(
            collective_id=collective_id, has_side_effects=True, vmem_limit_bytes=60 << 20
        ),
        name="sum_over_devices",
    )(*split)
    count = lax.axis_size("seq")
    bit = 8
    while bit < count:
        pairs = [(source, source ^ bit) for source in range(count)]
        outs = [
            (part.astype(f32) + lax.ppermute(part, "seq", pairs).astype(f32)).astype(bf16)
            for part in outs
        ]
        bit *= 2
    return [
        part.reshape(grad.shape[0] // places, grad.shape[1]).astype(f32)
        for part, grad in zip(outs, grads)
    ]


def on_device(
    tokens,
    slot_lengths,
    live_lengths,
    norm_gain,
    w_qkv,
    w_beta,
    w_outgate,
    conv_weight,
    ridge,
    head_gain,
    w_out,
    ffn_gain,
    w_gate,
    w_up,
    w_down,
    cotangent,
):
    section_out = make_kit()
    row_count = tokens.shape[1]
    depth = (WINDOW + row_count - 1) // row_count
    halo_rows = depth * row_count
    main_rows = halo_rows + row_count
    shards = lax.axis_size("wshard")
    shard_rows = norm_gain.shape[0]
    tap_columns = TAPS * conv_weight.shape[1] // shard_rows
    ffn = w_gate.shape[1]

    own_tokens = tokens[0]
    pieces = [passed_along(own_tokens, "seq", hop) for hop in range(depth, 0, -1)]
    pieces.append(own_tokens)
    pieces.append(passed_along(own_tokens[row_count - PRE :], "seq", depth + 1))
    ext_tokens = jnp.concatenate(pieces)

    small = jnp.concatenate(
        [
            w_beta,
            norm_gain[:, None],
            ridge[:, None],
            head_gain[:, None],
            ffn_gain[:, None],
            conv_weight.reshape(shard_rows, tap_columns),
        ],
        axis=1,
    )
    small = jnp.pad(small, ((0, 0), (0, EXTRA - small.shape[1])))
    (w_front,) = gather([jnp.concatenate([w_qkv, small], axis=1)], 0)
    mats, ffn_in, all_down = gather(
        [
            jnp.concatenate([w_outgate, w_out], axis=1),
            jnp.concatenate([w_gate, w_up], axis=1),
            w_down,
        ],
        1,
    )
    small = w_front[:, 3 * D :].astype(f32)
    gain_in, all_ridge, gain_head, gain_ffn = (small[:, HEADS + index] for index in range(4))
    taps = small[:, HEADS + 4 : HEADS + 4 + tap_columns]
    taps = taps.reshape(shards, TAPS, -1).transpose(1, 0, 2).reshape(TAPS, 3 * D)
    all_og = mats[:, :D]
    all_out = mats[:, D:].astype(f32)
    all_gate = ffn_in[:, :ffn].astype(f32)
    all_up = ffn_in[:, ffn:].astype(f32)
    all_down = all_down.astype(f32)

    rank = lax.axis_index("seq")
    first = rank * row_count - halo_rows - PRE
    positions = first + jnp.arange(PRE + main_rows, dtype=jnp.int32)
    segment, valid = token_layout(slot_lengths[0], live_lengths[0], positions)
    main_seg = segment[PRE:]
    own_seg = main_seg[halo_rows:]
    valid_own = valid[PRE + halo_rows :].astype(f32)
    same = jnp.stack(
        [segment[PRE - tap : PRE - tap + main_rows] == main_seg for tap in range(TAPS)], axis=1
    ).astype(f32)
    spacing = positions[None, PRE + halo_rows :] - positions[PRE:, None]
    mask = (
        (spacing >= 0)
        & (spacing < WINDOW)
        & (main_seg[:, None] == own_seg[None, :])
        & valid[PRE:, None]
    ).astype(bf16)
    gain_row = gain_in[None, :]
    ridge_column = all_ridge[:, None]
    x_own = own_tokens.astype(f32)

    hidden, kv_in, q_in, q_pre, queries, keys, values, beta = front(
        ext_tokens, same, gain_row, w_front, taps, row_count
    )
    hidden_own = hidden[halo_rows:main_rows]
    gate_pre = jnp.dot(hidden_own, all_og, preferred_element_type=f32)
    mixed, image0, image1 = attn_fwd(queries, keys, values, beta, mask, ridge_column)

    def back_half(xrow, mixed, gate_pre, gain_head, mat_out, gain_ffn, mat_gate, mat_up, mat_down):
        return section_out(
            xrow, mixed, gate_pre, gain_head, mat_out, gain_ffn, mat_gate, mat_up, mat_down, valid_own
        )

    output, pull_back = jax.vjp(
        back_half, x_own, mixed, gate_pre, gain_head, all_out, gain_ffn, all_gate, all_up, all_down
    )
    grad_out = cotangent[0].astype(f32)
    d_xout, d_mixed, d_gate, d_ghead, d_wout, d_gffn, d_wgate, d_wup, d_wdown = pull_back(grad_out)
    d_gate = d_gate.astype(bf16)

    d_query, d_key, d_value, d_beta, d_ridge = attn_bwd(
        queries, keys, values, beta, mask, ridge_column, image0, image1, d_mixed.astype(bf16)
    )
    d_kv_in, d_q_in, d_q_pre, d_beta_pre, d_halo, d_own, d_gain, d_taps = back(
        ext_tokens,
        kv_in,
        same,
        q_in,
        q_pre,
        d_key,
        d_value,
        d_query,
        beta,
        d_beta,
        d_gate,
        d_xout,
        gain_row,
        w_front,
        all_og,
        taps,
    )

    def weight_grad(left, right):
        return lax.dot_general(
            left, right, (((0,), (0,)), ((), ())), preferred_element_type=f32
        ).astype(bf16)

    d_wog = weight_grad(hidden_own, d_gate)
    d_wq = weight_grad(
        hidden[halo_rows - PRE : main_rows], jnp.concatenate([d_q_pre, d_q_in])
    )
    d_wkv = weight_grad(hidden, d_kv_in)
    d_wbeta = weight_grad(hidden[:main_rows], d_beta_pre)[:, :HEADS]

    d_tokens = d_own
    for hop in range(1, depth + 1):
        start = halo_rows - hop * row_count
        part = passed_along(d_halo[start : start + row_count], "seq", -hop)
        d_tokens = d_tokens + part.astype(f32)
    part = passed_along(d_halo[halo_rows:], "seq", -(depth + 1)).astype(f32)
    d_tokens = d_tokens + jnp.pad(part, ((row_count - PRE, 0), (0, 0)))

    d_small = jnp.concatenate(
        [
            d_wbeta.astype(f32),
            d_gain.reshape(D, 1),
            d_ridge,
            d_ghead[:, None],
            d_gffn[:, None],
            d_taps.reshape(TAPS, shards, -1).transpose(1, 0, 2).reshape(D, tap_columns),
        ],
        axis=1,
    ).astype(bf16)
    d_small = jnp.pad(d_small, ((0, 0), (0, EXTRA - d_small.shape[1])))
    all_grads = [
        d_wdown.astype(bf16),
        jnp.concatenate([d_wgate, d_wup], axis=1).astype(bf16),
        jnp.concatenate([d_wog, d_wout.astype(bf16)], axis=1),
        jnp.concatenate([d_wq, d_wkv, d_small], axis=1),
    ]
    parts = [
        (0, 0, w_down.shape[0] // 4),
        (1, 0, shard_rows // 8),
        (1, shard_rows // 8, shard_rows // 8),
        (2, 0, shard_rows // 4),
        (3, 0, shard_rows // 4),
    ]
    total_down, total_ffn, total_middle, total_front = sum_over_devices(all_grads, parts, 2)
    t_small = total_front[:, 3 * D :]
    return (
        output.astype(bf16)[None],
        d_tokens.astype(bf16)[None],
        t_small[:, HEADS],
        total_front[:, : 3 * D],
        t_small[:, :HEADS],
        total_middle[:, :D],
        t_small[:, HEADS + 4 : HEADS + 4 + tap_columns].reshape(TAPS, -1),
        t_small[:, HEADS + 1],
        t_small[:, HEADS + 2],
        total_middle[:, D:],
        t_small[:, HEADS + 3],
        total_ffn[:, :ffn],
        total_ffn[:, ffn:],
        total_down,
    )


def solution(mesh):
    return jax.shard_map(
        on_device,
        mesh=mesh,
        in_specs=(
            P("wshard", "seq", None),
            P("wshard", None),
            P("wshard", None),
            P("wshard"),
            P("wshard", None),
            P("wshard", None),
            P("wshard", None),
            P(None, "wshard"),
            P("wshard"),
            P("wshard"),
            P("wshard", None),
            P("wshard"),
            P("wshard", None),
            P("wshard", None),
            P("wshard", None),
            P("wshard", "seq", None),
        ),
        out_specs=(
            P("wshard", "seq", None),
            P("wshard", "seq", None),
            P("wshard"),
            P("wshard", None),
            P("wshard", None),
            P("wshard", None),
            P(None, "wshard"),
            P("wshard"),
            P("wshard"),
            P("wshard", None),
            P("wshard"),
            P("wshard", None),
            P("wshard", None),
            P("wshard", None),
        ),
        check_vma=False,
    )
```

```python
import functools
import jax
import jax.numpy as jnp
from jax import lax
from jax.experimental import pallas as pl
from jax.experimental.pallas import tpu as pltpu
from jax.sharding import PartitionSpec as P

D = 1024
HEADS = 8
HEAD_DIM = 128
TAPS = 4
WINDOW = 1024
PRE = 16
SMALL = 128
EXTRA = 512
MESH = pl.DeviceIdType.MESH
f32 = jnp.float32
bf16 = jnp.bfloat16
QB = 256
CH = 256
ROWS = 256


def mm(left, right):
    return jnp.dot(left, right, preferred_element_type=f32)


def mm_t(left, right):
    return lax.dot_general(left, right, (((1,), (1,)), ((), ())), preferred_element_type=f32)


def conv_total(ext_ref, slot, same, taps):
    total = taps[0:1] * ext_ref[slot, 8 : 8 + ROWS, :]
    for tap in range(1, TAPS):
        total = total + taps[tap : tap + 1] * ext_ref[slot, 8 - tap : 8 - tap + ROWS, :] * same[tap]
    return total


def unit_scale(active):
    return lax.rsqrt(jnp.sum(active * active, axis=-1, keepdims=True) + 1e-06)


def in_heads(work, *arrays):
    width = arrays[0].shape[1]
    return jnp.concatenate(
        [
            work(*(array[:, at : at + HEAD_DIM] for array in arrays))
            for at in range(0, width, HEAD_DIM)
        ],
        axis=1,
    )


def row_norm(x, gain):
    return (x * lax.rsqrt(jnp.mean(x * x, axis=-1, keepdims=True) + 1e-06) * gain).astype(bf16)


def front_kernel(
    first_own,
    x_ref,
    same_ref,
    gain_ref,
    w_ref,
    taps_ref,
    hid_ref,
    kvin_ref,
    qin_ref,
    qpre_ref,
    q_ref,
    k_ref,
    v_ref,
    beta_ref,
    ext_ref,
    tail_ref,
):
    step = pl.program_id(0)
    gain = gain_ref[...]
    main_rows = k_ref.shape[0]
    before_at = pl.ds(main_rows, PRE)
    rows_at = pl.ds(pl.multiple_of(jnp.maximum(step - 1, 0) * ROWS, ROWS), ROWS)
    own_at = pl.ds(pl.multiple_of(jnp.maximum(step - 1 - first_own, 0) * ROWS, ROWS), ROWS)
    kv_slots = 2 * D // CH

    @pl.when(step == 0)
    def before():
        hidden = row_norm(x_ref[before_at].astype(f32), gain)
        hid_ref[before_at] = hidden
        for slot in range(kv_slots):
            rows = mm(hidden, w_ref[:, D + CH * slot : D + CH * (slot + 1)]).astype(bf16)
            kvin_ref[before_at, CH * slot : CH * (slot + 1)] = rows
            ext_ref[slot, ROWS : ROWS + 8, :] = rows.astype(f32)[PRE - 8 :]

    def through(slot, hidden, same, column, in_ref, in_rows, at):
        ext_ref[slot, 0:8, :] = ext_ref[slot, ROWS : ROWS + 8, :]
        rows = mm(hidden, w_ref[:, column : column + CH]).astype(bf16)
        in_ref[in_rows, at : at + CH] = rows
        ext_ref[slot, 8 : 8 + ROWS, :] = rows.astype(f32)
        total = conv_total(ext_ref, slot, same, taps_ref[:, column : column + CH])
        return total * jax.nn.sigmoid(total)

    def unit(active):
        return in_heads(lambda part: part * unit_scale(part), active).astype(bf16)

    @pl.when(step > 0)
    def main():
        same = [same_ref[rows_at, tap : tap + 1] for tap in range(TAPS)]
        hidden = row_norm(x_ref[rows_at].astype(f32), gain)
        hid_ref[rows_at] = hidden
        for slot in range(kv_slots):
            at = CH * slot
            active = through(slot, hidden, same, D + at, kvin_ref, rows_at, at)
            if at < D:
                k_ref[rows_at, at : at + CH] = unit(active)
            else:
                v_ref[rows_at, at - D : at - D + CH] = active.astype(bf16)
        gates = jax.nn.sigmoid(mm(hidden, w_ref[:, 3 * D : 3 * D + SMALL])).astype(bf16)
        lane = lax.broadcasted_iota(jnp.int32, (ROWS, SMALL), 1)
        beta_ref[rows_at] = jnp.where(lane < HEADS, gates.astype(f32), 0.0)

        @pl.when(step == first_own + 1)
        def own_history():
            rows = mm(tail_ref[...], w_ref[:, :D]).astype(bf16)
            qpre_ref[...] = rows
            for slot in range(D // CH):
                ext_ref[kv_slots + slot, ROWS : ROWS + 8, :] = rows.astype(f32)[
                    PRE - 8 :, CH * slot : CH * (slot + 1)
                ]

        @pl.when(step > first_own)
        def own():
            for slot in range(D // CH):
                at = CH * slot
                active = through(kv_slots + slot, hidden, same, at, qin_ref, own_at, at)
                q_ref[own_at, at : at + CH] = unit(active)

        tail_ref[...] = hidden[ROWS - PRE :]


def front(ext_tokens, same, gain, w_front, taps, own_rows, **riding):
    ext_rows = ext_tokens.shape[0]
    main_rows = ext_rows - PRE
    blocks = main_rows // ROWS
    first_own = (main_rows - own_rows) // ROWS

    def fixed(array):
        return pl.BlockSpec(array.shape, lambda step: (0, 0), pipeline_mode=pl.Buffered(1))

    shape = jax.ShapeDtypeStruct
    outs = [
        shape((ext_rows, D), bf16),
        shape((ext_rows, 2 * D), bf16),
        shape((own_rows, D), bf16),
        shape((PRE, D), bf16),
        shape((own_rows, D), bf16),
        shape((main_rows, D), bf16),
        shape((main_rows, D), bf16),
        shape((main_rows, SMALL), f32),
    ]
    return call(
        functools.partial(front_kernel, first_own),
        blocks + 1,
        (ext_tokens, same, gain, w_front, taps),
        [fixed(array) for array in (ext_tokens, same, gain, w_front, taps)],
        [fixed(array) for array in outs],
        outs,
        [
            pltpu.VMEM((3 * D // CH, 8 + ROWS, CH), f32),
            pltpu.VMEM((PRE, D), bf16),
        ],
        vmem=50,
        flops=4 * (main_rows * 2 + own_rows) * D * D,
        traffic=30 << 20,
        name="front",
        **riding,
    )


def back_kernel(
    blocks,
    first_own,
    x_ref,
    kvin_ref,
    kvprev_ref,
    same_ref,
    qin_ref,
    qprev_ref,
    qpre_ref,
    dk_ref,
    dv_ref,
    dq_ref,
    beta_ref,
    dbeta_ref,
    dgate_ref,
    dres_ref,
    gain_ref,
    w_ref,
    wog_ref,
    taps_ref,
    dkvin_ref,
    dqin_ref,
    dqpre_ref,
    dbp_ref,
    dxhalo_ref,
    dxown_ref,
    dgain_ref,
    dtaps_ref,
    ext_ref,
    buf_ref,
    dh_ref,
):
    step = pl.program_id(0)
    block = blocks - 1 - step
    kv_slots = 2 * D // CH
    gain = gain_ref[...]

    @pl.when(step == 0)
    def clear():
        dgain_ref[...] = jnp.zeros_like(dgain_ref)
        dtaps_ref[...] = jnp.zeros_like(dtaps_ref)
        buf_ref[:, :, ROWS : ROWS + 8, :] = jnp.zeros_like(buf_ref[:, :, ROWS : ROWS + 8, :])

    def norm_back(x, dh):
        scale = lax.rsqrt(jnp.mean(x * x, axis=-1, keepdims=True) + 1e-06)
        normal = x * scale
        dgain_ref[...] += jnp.sum(dh * normal, axis=0, keepdims=True)
        scaled = dh * gain
        return scale * (scaled - normal * jnp.mean(scaled * normal, axis=-1, keepdims=True))

    def shifted(slot, start, count):
        total = buf_ref[slot, 0, start + 1 : start + 1 + count, :]
        for tap in range(2, TAPS):
            total = total + buf_ref[slot, tap - 1, start + tap : start + tap + count, :]
        return total

    def through(slot, column, history, rows, grad, unit, same):
        ext_ref[slot, 0:8, :] = history
        ext_ref[slot, 8 : 8 + ROWS, :] = rows.astype(f32)
        taps = taps_ref[:, column : column + CH]
        total = conv_total(ext_ref, slot, same, taps)
        gate = jax.nn.sigmoid(total)
        active = total * gate
        if unit:

            def unit_back(part, part_grad):
                scale = unit_scale(part)
                normal = part * scale
                return scale * (
                    part_grad - normal * jnp.sum(part_grad * normal, axis=-1, keepdims=True)
                )

            grad = in_heads(unit_back, active, grad)
        grad = grad * (gate + active * (1.0 - gate))
        result = grad * taps[0:1]
        dtaps_ref[0:1, column : column + CH] += jnp.sum(
            grad * ext_ref[slot, 8 : 8 + ROWS, :], axis=0, keepdims=True
        )
        for tap in range(1, TAPS):
            held = grad * same[tap]
            dtaps_ref[tap : tap + 1, column : column + CH] += jnp.sum(
                held * ext_ref[slot, 8 - tap : 8 - tap + ROWS, :], axis=0, keepdims=True
            )
            buf_ref[slot, tap - 1, 0:ROWS, :] = held * taps[tap : tap + 1]
        result = (result + shifted(slot, 0, ROWS)).astype(bf16)
        for tap in range(1, TAPS):
            buf_ref[slot, tap - 1, ROWS : ROWS + 8, :] = buf_ref[slot, tap - 1, 0:8, :]
        return result

    def before_rows(slot):
        for tap in range(1, TAPS):
            buf_ref[slot, tap - 1, ROWS - PRE : ROWS, :] = jnp.zeros((PRE, CH), f32)
        return shifted(slot, ROWS - PRE, PRE).astype(bf16)

    @pl.when(step < blocks)
    def main():
        same = [same_ref[:, tap : tap + 1] for tap in range(TAPS)]
        beta = beta_ref[...]
        gates = (dbeta_ref[...] * beta * (1.0 - beta)).astype(bf16)
        dbp_ref[...] = gates
        dh = mm_t(gates, w_ref[:, 3 * D : 3 * D + SMALL])
        for slot in range(kv_slots):
            at = CH * slot
            grad = dk_ref[:, at : at + CH] if at < D else dv_ref[:, at - D : at - D + CH]
            history = kvprev_ref[PRE - 8 : PRE, at : at + CH].astype(f32)
            rows = kvin_ref[:, at : at + CH]
            rows = through(slot, D + at, history, rows, grad, at < D, same)
            dkvin_ref[:, at : at + CH] = rows
            dh = dh + mm_t(rows, w_ref[:, D + at : D + at + CH])
        dh_ref[...] = dh

        @pl.when(block >= first_own)
        def own():
            dh = mm_t(dgate_ref[...], wog_ref[...])
            for slot in range(D // CH):
                at = CH * slot
                history = jnp.where(
                    block == first_own,
                    qpre_ref[PRE - 8 :, at : at + CH].astype(f32),
                    qprev_ref[PRE - 8 :, at : at + CH].astype(f32),
                )
                rows = qin_ref[:, at : at + CH]
                rows = through(
                    kv_slots + slot, at, history, rows, dq_ref[:, at : at + CH], True, same
                )
                dqin_ref[:, at : at + CH] = rows
                dh = dh + mm_t(rows, w_ref[:, at : at + CH])
            dxown_ref[...] = dres_ref[...] + norm_back(x_ref[...].astype(f32), dh_ref[...] + dh)

        @pl.when(block == first_own - 1)
        def own_history():
            dh = jnp.zeros((PRE, D), f32)
            for slot in range(D // CH):
                at = CH * slot
                rows = before_rows(kv_slots + slot)
                dqpre_ref[:, at : at + CH] = rows
                dh = dh + mm_t(rows, w_ref[:, at : at + CH])
            dh_ref[ROWS - PRE : ROWS, :] += dh

        @pl.when(block < first_own)
        def halo():
            dxhalo_ref[...] = norm_back(x_ref[...].astype(f32), dh_ref[...]).astype(bf16)

    @pl.when(step == blocks)
    def before():
        dh = jnp.zeros((PRE, D), f32)
        for slot in range(kv_slots):
            at = CH * slot
            rows = before_rows(slot)
            dkvin_ref[0:PRE, at : at + CH] = rows
            dh = dh + mm_t(rows, w_ref[:, D + at : D + at + CH])
        dxhalo_ref[0:PRE, :] = norm_back(x_ref[0:PRE].astype(f32), dh).astype(bf16)


def back(
    ext_tokens, kvin, same, qin, qpre, dk, dv, dq, beta, dbeta, dgate, dres, gain, w_front, w_og, taps, **riding
):
    ext_rows = ext_tokens.shape[0]
    main_rows = ext_rows - PRE
    own_rows = dq.shape[0]
    blocks = main_rows // ROWS
    first_own = (main_rows - own_rows) // ROWS
    small_blocks = ROWS // PRE

    def ext_block(step):
        return (jnp.where(step == blocks, blocks, blocks - 1 - step), 0)

    def main_block(step):
        return (jnp.maximum(blocks - 1 - step, 0), 0)

    def prev_block(step):
        block = blocks - 1 - step
        return (jnp.where(block <= 0, blocks * small_blocks, small_blocks * block - 1), 0)

    def own_block(step):
        return (jnp.maximum(blocks - 1 - step - first_own, 0), 0)

    def own_prev_block(step):
        return (jnp.maximum(small_blocks * (blocks - 1 - step - first_own) - 1, 0), 0)

    def halo_block(step):
        block = jnp.minimum(blocks - 1 - step, first_own - 1)
        return (jnp.where(step == blocks, first_own, block), 0)

    def fixed(array):
        return pl.BlockSpec(array.shape, lambda step: (0, 0), pipeline_mode=pl.Buffered(1))

    shape = jax.ShapeDtypeStruct
    return call(
        functools.partial(back_kernel, blocks, first_own),
        blocks + 1,
        (
            ext_tokens,
            kvin,
            kvin,
            same,
            qin,
            qin,
            qpre,
            dk,
            dv,
            dq,
            beta,
            dbeta,
            dgate,
            dres,
            gain,
            w_front,
            w_og,
            taps,
        ),
        [
            pl.BlockSpec((ROWS, D), ext_block),
            pl.BlockSpec((ROWS, 2 * D), ext_block),
            pl.BlockSpec((PRE, 2 * D), prev_block),
            pl.BlockSpec((ROWS, TAPS), main_block),
            pl.BlockSpec((ROWS, D), own_block),
            pl.BlockSpec((PRE, D), own_prev_block),
            fixed(qpre),
            pl.BlockSpec((ROWS, D), main_block),
            pl.BlockSpec((ROWS, D), main_block),
            pl.BlockSpec((ROWS, D), own_block),
            pl.BlockSpec((ROWS, SMALL), main_block),
            pl.BlockSpec((ROWS, SMALL), main_block),
            pl.BlockSpec((ROWS, D), own_block),
            pl.BlockSpec((ROWS, D), own_block),
            fixed(gain),
            fixed(w_front),
            fixed(w_og),
            fixed(taps),
        ],
        [
            pl.BlockSpec((ROWS, 2 * D), ext_block),
            pl.BlockSpec((ROWS, D), own_block),
            pl.BlockSpec((PRE, D), lambda step: (0, 0)),
            pl.BlockSpec((ROWS, SMALL), main_block),
            pl.BlockSpec((ROWS, D), halo_block),
            pl.BlockSpec((ROWS, D), own_block),
            pl.BlockSpec((1, D), lambda step: (0, 0)),
            pl.BlockSpec((TAPS, 3 * D), lambda step: (0, 0)),
        ],
        [
            shape((ext_rows, 2 * D), bf16),
            shape((own_rows, D), bf16),
            shape((PRE, D), bf16),
            shape((main_rows, SMALL), bf16),
            shape((main_rows - own_rows + PRE, D), bf16),
            shape((own_rows, D), f32),
            shape((1, D), f32),
            shape((TAPS, 3 * D), f32),
        ],
        [
            pltpu.VMEM((3 * D // CH, 8 + ROWS, CH), f32),
            pltpu.VMEM((3 * D // CH, TAPS - 1, ROWS + 8, CH), f32),
            pltpu.VMEM((ROWS, D), f32),
        ],
        vmem=62,
        flops=6 * (main_rows * 2 + own_rows) * D * D,
        traffic=40 << 20,
        name="back",
        **riding,
    )


def total(v):
    return jnp.sum(v,axis=0,keepdims=True)

def head_column(beta_ref, h):
    beta=beta_ref[...]
    lane=lax.broadcasted_iota(jnp.int32,beta.shape,1)
    return jnp.sum(jnp.where(lane==h,beta,0.0),axis=1,keepdims=True)

def attn_fwd_kernel(q_ref,k_ref,v_ref,beta_ref,mask_ref,ridge_ref,o_ref,a0_ref,a1_ref,kt_ref,vt_ref,w_ref):
    h=pl.program_id(0)
    rows=q_ref.shape[0]
    span=WINDOW+QB
    kt_ref[...]=k_ref[...].T
    vt_ref[...]=v_ref[...].T
    column=head_column(beta_ref,h)
    ridge=ridge_ref[...]
    blocks=range(rows//QB)
    chunks=range(span//CH)
    for b in blocks:
        for c in chunks:
            at=slice(QB*b+CH*c,QB*b+CH*(c+1))
            w_ref[b,CH*c:CH*(c+1),:]=mask_ref[at,QB*b:QB*(b+1)].astype(f32)*column[at]
    def apply(b,vector,right):
        low=vector.astype(bf16)
        out=jnp.zeros((HEAD_DIM,QB),f32)
        for c in chunks:
            at=slice(QB*b+CH*c,QB*b+CH*(c+1))
            s=mm(k_ref[at,:],low)
            s=(w_ref[b,CH*c:CH*(c+1),:]*s).astype(bf16)
            out=out+mm(right[:,at],s)
        return out
    q=[q_ref[QB*b:QB*(b+1),:].astype(f32).T for b in blocks]
    a0=[apply(b,q[b],kt_ref)+ridge*q[b] for b in blocks]
    for b in blocks: a0_ref[:,QB*b:QB*(b+1)]=a0[b]
    x1=[];p1=[];r1=[];e1=[]
    for b in blocks:
        e0=total(q[b]*q[b])
        s0=e0/total(q[b]*a0[b])
        x1.append(s0*q[b])
        r=q[b]-s0*a0[b]
        e=total(r*r)
        r1.append(r);e1.append(e)
        p1.append(r+e/e0*q[b])
    a1=[apply(b,p1[b],kt_ref)+ridge*p1[b] for b in blocks]
    for b in blocks: a1_ref[:,QB*b:QB*(b+1)]=a1[b]
    x2=[x1[b]+e1[b]/total(p1[b]*a1[b])*p1[b] for b in blocks]
    for b in blocks:
        o_ref[QB*b:QB*(b+1),:]=apply(b,x2[b],vt_ref).T

def attn_fwd(q,k,v,beta,mask_t,ridge,**riding):
    rows=q.shape[0]; keys=k.shape[0]
    head=lambda n: pl.BlockSpec((n,HEAD_DIM),lambda h:(0,h))
    heads_t=pl.BlockSpec((HEAD_DIM,rows),lambda h:(h,0))
    fixed=lambda a: pl.BlockSpec(a.shape,lambda h:(0,0))
    flops=6*2*rows*(WINDOW+QB)*D
    return call(
        attn_fwd_kernel,
        HEADS,
        (q, k, v, beta, mask_t, ridge),
        [head(rows), head(keys), head(keys), fixed(beta), fixed(mask_t), pl.BlockSpec((HEAD_DIM, 1), lambda h: (h, 0))],
        [head(rows), heads_t, heads_t],
        [jax.ShapeDtypeStruct((rows, D), f32)] + [jax.ShapeDtypeStruct((D, rows), f32)] * 2,
        [pltpu.VMEM((HEAD_DIM, keys), bf16)] * 2 + [pltpu.VMEM((rows // QB, WINDOW + QB, QB), f32)],
        flops=2 * flops,
        traffic=20 << 20,
        name="attn_fwd",
        **riding,
    )


def attn_bwd_kernel(q_ref,k_ref,v_ref,beta_ref,mask_ref,ridge_ref,a0_ref,a1_ref,do_ref,dq_ref,dk_ref,dv_ref,dbeta_ref,dridge_ref,kt_ref,w_ref,acc_ref):
    h=pl.program_id(0)
    rows=q_ref.shape[0]
    span=WINDOW+QB
    kt_ref[...]=k_ref[...].T
    column=head_column(beta_ref,h)
    ridge=ridge_ref[...]
    blocks=range(rows//QB)
    chunks=range(span//CH)
    dk_ref[...]=jnp.zeros_like(dk_ref)
    dv_ref[...]=jnp.zeros_like(dv_ref)
    acc_ref[...]=jnp.zeros_like(acc_ref)
    for b in blocks:
        for c in chunks:
            at=slice(QB*b+CH*c,QB*b+CH*(c+1))
            w_ref[b,CH*c:CH*(c+1),:]=mask_ref[at,QB*b:QB*(b+1)].astype(f32)*column[at]
    def apply_back(b,vector,grad,grad_rows,right_ref,dright_ref):
        low=vector.astype(bf16)
        low_rows=vector.T.astype(bf16)
        out=jnp.zeros((HEAD_DIM,QB),f32)
        for c in chunks:
            at=slice(QB*b+CH*c,QB*b+CH*(c+1))
            w=w_ref[b,CH*c:CH*(c+1),:]
            s=mm(k_ref[at,:],low)
            dw=mm(right_ref[at,:],grad)
            masked=dw*mask_ref[at,QB*b:QB*(b+1)].astype(f32)
            for_beta=masked*s
            part=for_beta[:,:128]
            for lane in range(128,QB,128):
                part=part+for_beta[:,lane:lane+128]
            acc_ref[at,:]+=part
            ws=(w*s).astype(bf16)
            ds=(w*dw).astype(bf16)
            out=out+mm(kt_ref[:,at],ds)
            dright_ref[at,:]+=mm(ws,grad_rows)
            dk_ref[at,:]+=mm(ds,low_rows)
        return out
    st=[]
    for b in blocks:
        cols=slice(QB*b,QB*(b+1))
        q=q_ref[cols,:].astype(f32).T
        a0=a0_ref[:,cols]; a1=a1_ref[:,cols]
        e0=total(q*q); d0=total(q*a0); s0=e0/d0
        x1=s0*q; r1=q-s0*a0; e1=total(r1*r1); b0=e1/e0
        p1=r1+b0*q; d1=total(p1*a1); s1=e1/d1
        x2=x1+s1*p1
        st.append((q,a0,a1,e0,d0,s0,r1,e1,b0,p1,d1,s1,x2))
    dx2=[]
    for b in blocks:
        do=do_ref[QB*b:QB*(b+1),:]
        dx2.append(apply_back(b,st[b][12],do.astype(f32).T.astype(bf16),do,v_ref,dv_ref))
    da1=[];dp1=[];de1=[];dr=0
    for b in blocks:
        q,a0,a1,e0,d0,s0,r1,e1,b0,p1,d1,s1,x2=st[b]
        ds1=total(dx2[b]*p1)
        de1.append(ds1/d1)
        dd1=-ds1*s1/d1
        g=dd1*p1
        da1.append(g)
        dp1.append(s1*dx2[b]+dd1*a1+ridge*g)
        dr=dr+jnp.sum(g*p1,axis=1,keepdims=True)
    for b in blocks:
        g=da1[b]
        dp1[b]=dp1[b]+apply_back(b,st[b][9],g.astype(bf16),g.T.astype(bf16),k_ref,dk_ref)
    da0=[];dq=[]
    for b in blocks:
        q,a0,a1,e0,d0,s0,r1,e1,b0,p1,d1,s1,x2=st[b]
        db0=total(dp1[b]*q)
        dpq=b0*dp1[b]
        de=de1[b]+db0/e0
        de0=-db0*b0/e0
        dr1=dp1[b]+2.0*de*r1
        ds0=total(dx2[b]*q)-total(dr1*a0)
        dpq=dpq+s0*dx2[b]
        g=-s0*dr1
        de0=de0+ds0/d0
        dd0=-ds0*s0/d0
        dpq=dpq+dd0*a0
        g=g+dd0*q
        dpq=dpq+dr1+2.0*de0*q+ridge*g
        da0.append(g);dq.append(dpq)
        dr=dr+jnp.sum(g*q,axis=1,keepdims=True)
    for b in blocks:
        g=da0[b]
        t=dq[b]+apply_back(b,st[b][0],g.astype(bf16),g.T.astype(bf16),k_ref,dk_ref)
        dq_ref[QB*b:QB*(b+1),:]=t.T
    dridge_ref[...]=dr
    found=jnp.sum(acc_ref[...],axis=1,keepdims=True)
    lane=lax.broadcasted_iota(jnp.int32,dbeta_ref.shape,1)
    @pl.when(h==0)
    def _():
        dbeta_ref[...]=jnp.zeros_like(dbeta_ref)
    dbeta_ref[...]=jnp.where(lane==h,found,dbeta_ref[...])

def attn_bwd(q,k,v,beta,mask_t,ridge,a0,a1,do,**riding):
    rows=q.shape[0]; keys=k.shape[0]
    head=lambda n: pl.BlockSpec((n,HEAD_DIM),lambda h:(0,h))
    heads_t=pl.BlockSpec((HEAD_DIM,rows),lambda h:(h,0))
    fixed=lambda a: pl.BlockSpec(a.shape,lambda h:(0,0))
    rd=pl.BlockSpec((HEAD_DIM,1),lambda h:(h,0))
    flops=15*2*rows*(WINDOW+QB)*D
    return call(
        attn_bwd_kernel,
        HEADS,
        (q, k, v, beta, mask_t, ridge, a0, a1, do),
        [head(rows), head(keys), head(keys), fixed(beta), fixed(mask_t), rd, heads_t, heads_t, head(rows)],
        [head(rows), head(keys), head(keys), fixed(beta), rd],
        [
            jax.ShapeDtypeStruct((rows, D), f32),
            jax.ShapeDtypeStruct((keys, D), f32),
            jax.ShapeDtypeStruct((keys, D), f32),
            jax.ShapeDtypeStruct(beta.shape, f32),
            jax.ShapeDtypeStruct((D, 1), f32),
        ],
        [
            pltpu.VMEM((HEAD_DIM, keys), bf16),
            pltpu.VMEM((rows // QB, WINDOW + QB, QB), f32),
            pltpu.VMEM((keys, 128), f32),
        ],
        flops=2 * flops,
        traffic=30 << 20,
        name="attn_bwd",
        **riding,
    )


def token_layout(slot_row, live_row, positions):
    starts = (jnp.cumsum(slot_row) - slot_row).astype(jnp.int32)
    after = positions[:, None] >= starts[None, :]
    segment = (jnp.sum(after.astype(jnp.int32), axis=1) - 1).astype(jnp.int32)
    chosen = segment[:, None] == jnp.arange(slot_row.shape[0], dtype=jnp.int32)[None, :]
    begin = jnp.sum(jnp.where(chosen, starts[None, :], 0), axis=1).astype(jnp.int32)
    limit = jnp.sum(jnp.where(chosen, live_row[None, :], 0), axis=1).astype(jnp.int32)
    valid = (segment >= 0) & (positions - begin < limit)
    return (segment, valid)


def make_kit():

    @jax.custom_vjp
    def low(v):
        return lax.optimization_barrier(v.astype(jnp.bfloat16)).astype(jnp.float32)

    @jax.custom_vjp
    def low_back(v):
        return v

    def low_keep(v):
        return (low(v), None)

    def low_pass(kept, grad):
        return (grad,)

    def back_keep(v):
        return (v, None)

    def back_low(kept, grad):
        return (low(grad),)

    low.defvjp(low_keep, low_pass)
    low_back.defvjp(back_keep, back_low)

    @jax.custom_vjp
    def matmul(left, right):
        return jnp.dot(
            left.astype(jnp.bfloat16),
            right.astype(jnp.bfloat16),
            preferred_element_type=jnp.float32,
        )

    def matmul_keep(left, right):
        left_low = left.astype(jnp.bfloat16)
        right_low = right.astype(jnp.bfloat16)
        return (
            jnp.dot(left_low, right_low, preferred_element_type=jnp.float32),
            (left_low, right_low),
        )

    def matmul_grads(kept, grad):
        left_low, right_low = kept
        grad_low = grad.astype(jnp.bfloat16)
        grad_left = lax.dot_general(
            grad_low, right_low, (((1,), (1,)), ((), ())), preferred_element_type=jnp.float32
        )
        grad_right = lax.dot_general(
            left_low, grad_low, (((0,), (0,)), ((), ())), preferred_element_type=jnp.float32
        )
        return (grad_left, grad_right)

    matmul.defvjp(matmul_keep, matmul_grads)

    def section_out(
        xrow, mixed, gate_pre, gain_head, mat_out, gain_ffn, mat_gate, mat_up, mat_down, valid
    ):
        row_count = xrow.shape[0]
        shaped = mixed.reshape(row_count, HEADS, HEAD_DIM)
        shaped = shaped * lax.rsqrt(jnp.mean(shaped * shaped, axis=-1, keepdims=True) + 1e-05)
        normed = shaped.reshape(row_count, D) * gain_head
        gated = low(normed * jax.nn.silu(gate_pre))
        middle = xrow + low_back(matmul(gated, mat_out))
        hidden = low(
            middle * lax.rsqrt(jnp.mean(middle * middle, axis=-1, keepdims=True) + 1e-06) * gain_ffn
        )
        inner = low(
            jax.nn.silu(low_back(matmul(hidden, mat_gate))) * low_back(matmul(hidden, mat_up))
        )
        return valid[:, None] * (middle + low_back(matmul(inner, mat_down)))

    return section_out


class Here:
    def __init__(self):
        self.rank = lax.axis_index("seq")
        self.ranks = lax.axis_size("seq")
        self.place = lax.axis_index("wshard")
        self.shards = lax.axis_size("wshard")
        self.core = self.rank % 2
        self.x = (self.rank // 2) % 2
        self.y = (self.rank // 4) % 2
        self.core_next = self.rank + 1 - 2 * self.core
        self.x_next = self.rank + 2 - 4 * self.x
        self.y_next = self.rank + 4 - 8 * self.y

    def other(self, step):
        return (self.place + step) % self.shards

    def along(self, step):
        return (self.rank + step + self.ranks) % self.ranks

    def meet(self, reach):
        barrier = pltpu.get_barrier_semaphore()
        near = [self.core_next, self.x_next, self.y_next]
        for step in range(1, reach + 1):
            near += [self.along(step), self.along(-step)]
        for device in near:
            pl.semaphore_signal(barrier, inc=1, device_id={"seq": device}, device_id_type=MESH)
        for step in range(1, self.shards):
            pl.semaphore_signal(
                barrier, inc=1, device_id={"wshard": self.other(step)}, device_id_type=MESH
            )
        pl.semaphore_wait(barrier, len(near) + self.shards - 1)


def span(start, size):
    return pl.ds(pl.multiple_of(start, 128), size)


class Rider:
    reach = 0
    first, last = 0, 0
    inputs, outputs, scratch, aliases = (), (), (), ()

    def bind(self, here, inputs, outputs, scratch):
        self.here = here
        self.inputs_, self.outputs_ = inputs, outputs
        self.send_sems, self.recv_sems, self.local_sems = scratch[:3]
        self.held = scratch[3:]

    def semaphores(self):
        return [
            pltpu.SemaphoreType.DMA((self.remote_count,)),
            pltpu.SemaphoreType.DMA((self.remote_count,)),
            pltpu.SemaphoreType.DMA((self.local_count,)),
        ]

    def send(self, index, source, target, **device):
        return pltpu.make_async_remote_copy(
            src_ref=source,
            dst_ref=target,
            send_sem=self.send_sems.at[index],
            recv_sem=self.recv_sems.at[index],
            device_id=device,
            device_id_type=MESH,
        )

    def keep(self, index, source, target):
        return pltpu.make_async_copy(source, target, self.local_sems.at[index])

    def remote(self, phase):
        return []

    def local(self, phase):
        return []

    def work(self, phase):
        pass

    def run(self, phase):
        if phase > self.first:
            for copy in self.remote(phase - 1):
                copy.wait_recv()
            for copy in self.local(phase - 1):
                copy.wait()
        if phase <= self.last:
            self.work(phase)
            for copy in self.remote(phase) + self.local(phase):
                copy.start()

    def finish(self):
        for phase in range(self.first, self.last + 1):
            for copy in self.remote(phase):
                copy.wait_send()


class Gather(Rider):
    remote_count, local_count = 18, 2

    def __init__(self, shard, first=0, last=3, begun=None):
        self.first, self.last = first, last
        if begun is None:
            split = shard.reshape(2, 2, shard.shape[0] // 4, shard.shape[1])
            places = lax.axis_size("wshard")
            self.inputs = (split,)
            self.outputs = (jax.ShapeDtypeStruct((places,) + split.shape, shard.dtype),)
            self.scratch = (pltpu.VMEM(split.shape, shard.dtype),)
        else:
            self.inputs = (begun,)
            self.outputs = (jax.ShapeDtypeStruct(begun.shape, begun.dtype),)
            self.aliases = ((0, 0),)

    def work(self, phase):
        if phase == 0:
            copy = self.keep(1, self.inputs_[0], self.held[0])
            copy.start()
            copy.wait()

    def local(self, phase):
        if phase:
            return []
        return [self.keep(0, self.held[0], self.outputs_[0].at[self.here.place])]

    def remote(self, phase):
        here, (target,) = self.here, self.outputs_
        half = target.shape[-1] // 2
        quarter = half // 2
        mine = span(here.core * half, half)
        one = span(here.core * half, quarter)
        two = span(here.core * half + quarter, quarter)
        y, x = here.y, here.x
        if phase == 0:
            return [
                self.send(
                    step - 1,
                    self.inputs_[0].at[y, x, :, mine],
                    target.at[here.place, y, x, :, mine],
                    wshard=here.other(step),
                )
                for step in range(1, here.shards)
            ]
        found = []
        for step in range(1, here.shards):
            at = target.at[here.other(step)]
            if phase == 1:
                found.append((at.at[y, x, :, one], here.x_next))
                found.append((at.at[y, x, :, two], here.y_next))
            elif phase == 2:
                found.append((at.at[y, :, :, one], here.y_next))
                found.append((at.at[:, x, :, two], here.x_next))
            else:
                found.append((at.at[:, :, :, mine], here.core_next))
        start = {1: 3, 2: 9, 3: 15}[phase]
        return [
            self.send(start + index, ref, ref, seq=near) for index, (ref, near) in enumerate(found)
        ]


class WindowTokens(Rider):
    last = 1
    remote_count, local_count = 0, 2

    def __init__(self, tokens, depth):
        self.depth = depth
        self.reach = depth + 1
        self.remote_count = depth + 1
        self.rows = tokens.shape[0]
        self.inputs = (tokens,)
        rows = self.rows * (depth + 1) + PRE
        self.outputs = (jax.ShapeDtypeStruct((rows, tokens.shape[1]), tokens.dtype),)
        self.scratch = (pltpu.VMEM(tokens.shape, tokens.dtype),)

    def work(self, phase):
        if phase == 0:
            copy = self.keep(1, self.inputs_[0], self.held[0])
            copy.start()
            copy.wait()

    def local(self, phase):
        rows = pl.ds(self.depth * self.rows, self.rows)
        return [self.keep(0, self.held[0], self.outputs_[0].at[rows])] if phase == 0 else []

    def remote(self, phase):
        here, rows, depth = self.here, self.rows, self.depth
        (own,), (ext,) = self.inputs_, self.outputs_
        if phase == 1:
            start = pl.multiple_of((1 - here.core) * depth * rows + here.core * (depth - 2) * rows, 16)
            ref = ext.at[pl.ds((depth - 1) * rows, rows)]
            return [self.send(0, ext.at[pl.ds(start, rows)], ref, seq=here.core_next)]
        found = [
            self.send(
                hop - 1, own, ext.at[pl.ds((depth - hop) * rows, rows)], seq=here.along(hop)
            )
            for hop in range(2, depth + 1)
        ]
        found.append(
            self.send(
                depth,
                own.at[pl.ds(rows - PRE, PRE)],
                ext.at[pl.ds((depth + 1) * rows, PRE)],
                seq=here.along(depth + 1),
            )
        )
        return found


class WindowGrads(Rider):
    local_count = 1

    def __init__(self, grads, rows, depth):
        self.rows, self.depth = rows, depth
        self.reach = depth + 1
        self.remote_count = depth + 1
        self.inputs = (grads,)
        columns = grads.shape[1]
        self.outputs = (
            jax.ShapeDtypeStruct((depth, rows, columns), grads.dtype),
            jax.ShapeDtypeStruct((PRE, columns), grads.dtype),
        )

    def remote(self, phase):
        here, rows, depth = self.here, self.rows, self.depth
        (grads,), (near, far) = self.inputs_, self.outputs_
        found = [
            self.send(
                hop - 1,
                grads.at[pl.ds((depth - hop) * rows, rows)],
                near.at[hop - 1],
                seq=here.along(-hop),
            )
            for hop in range(1, depth + 1)
        ]
        found.append(
            self.send(
                depth, grads.at[pl.ds(depth * rows, PRE)], far, seq=here.along(-depth - 1)
            )
        )
        return found


def add_into(target, at, value):
    target[at] = (target[at].astype(f32) + value.astype(f32)).astype(bf16)


class SumFar(Rider):
    last = 3
    remote_count, local_count = 5, 2

    def __init__(self, grad, start=0, size=None):
        places = lax.axis_size("wshard")
        if grad.ndim == 2:
            grad = grad.reshape(places, 2, 2, grad.shape[0] // places // 4, grad.shape[1])
        size = grad.shape[3] if size is None else size
        self.rows = pl.ds(start, size)
        half = grad.shape[-1] // 2
        quarter = half // 2
        self.inputs = (grad,)
        self.outputs = (jax.ShapeDtypeStruct((places, size, half), bf16),)
        self.scratch = (
            pltpu.VMEM((places, 2, 2, size, half), bf16),
            pltpu.VMEM((places, 2, 2, size, half), bf16),
            pltpu.VMEM((places, 2, size, quarter), bf16),
            pltpu.VMEM((places, 2, size, quarter), bf16),
            pltpu.VMEM((places, size, quarter), bf16),
            pltpu.VMEM((places, size, quarter), bf16),
        )
        self.half = half

    def local(self, phase):
        here, held = self.here, self.held[0]
        if phase == 0:
            mine = span(here.core * self.half, self.half)
            return [self.keep(0, self.inputs_[0].at[:, :, :, self.rows, mine], held)]
        if phase == 3:
            return [self.keep(1, held.at[:, here.y, here.x], self.outputs_[0])]
        return []

    def remote(self, phase):
        here = self.here
        y, x = here.y, here.x
        held, core_in, far_a, far_b, next_a, next_b = self.held
        one, two = pl.ds(0, self.half // 2), pl.ds(self.half // 2, self.half // 2)
        if phase == 0:
            yours = span((1 - here.core) * self.half, self.half)
            ref = self.inputs_[0].at[:, :, :, self.rows, yours]
            return [self.send(0, ref, core_in, seq=here.core_next)]
        if phase == 1:
            return [
                self.send(1, held.at[:, :, 1 - x, :, one], far_a, seq=here.x_next),
                self.send(2, held.at[:, 1 - y, :, :, two], far_b, seq=here.y_next),
            ]
        if phase == 2:
            return [
                self.send(3, held.at[:, 1 - y, x, :, one], next_a, seq=here.y_next),
                self.send(4, held.at[:, y, 1 - x, :, two], next_b, seq=here.x_next),
            ]
        return []

    def work(self, phase):
        y, x = self.here.y, self.here.x
        held, core_in, far_a, far_b, next_a, next_b = self.held
        places = held.shape[0]
        one, two = slice(0, self.half // 2), slice(self.half // 2, self.half)
        every = slice(None)
        if phase == 1:

            def add(index, carry):
                at = (index // 4, (index // 2) % 2, index % 2)
                add_into(held, at, core_in[at])
                return carry

            lax.fori_loop(0, 4 * places, add, 0)
        elif phase == 2:

            def add(index, carry):
                place, side = index // 2, index % 2
                add_into(held, (place, side, x, every, one), far_a[place, side])
                add_into(held, (place, y, side, every, two), far_b[place, side])
                return carry

            lax.fori_loop(0, 2 * places, add, 0)
        elif phase == 3:

            def add(place, carry):
                add_into(held, (place, y, x, every, one), next_a[place])
                add_into(held, (place, y, x, every, two), next_b[place])
                return carry

            lax.fori_loop(0, places, add, 0)


class SumNear(Rider):
    last = 3
    local_count = 2

    def __init__(self, sums=None, after=None):
        self.after = after
        places, size, half = (sums if after is None else after.outputs[0]).shape
        self.remote_count = places - 1 + 5
        self.half = half
        self.inputs = (sums,) if after is None else ()
        self.outputs = (jax.ShapeDtypeStruct((2, 2, size, 2 * half), bf16),)
        self.scratch = (pltpu.VMEM((places, size, half), bf16), pltpu.VMEM((size, half), bf16))

    def bind(self, here, inputs, outputs, scratch):
        super().bind(here, inputs, outputs, scratch)
        if self.after is not None:
            self.inputs_ = self.after.outputs_

    def local(self, phase):
        here = self.here
        arrived, total = self.held
        if phase == 0:
            return [self.keep(0, self.inputs_[0].at[here.place], arrived.at[0])]
        if phase == 1:
            mine = span(here.core * self.half, self.half)
            return [self.keep(1, total, self.outputs_[0].at[here.y, here.x, :, mine])]
        return []

    def remote(self, phase):
        here = self.here
        y, x = here.y, here.x
        arrived, total = self.held
        (out,) = self.outputs_
        quarter = self.half // 2
        others = here.shards - 1
        if phase == 0:
            return [
                self.send(
                    step - 1,
                    self.inputs_[0].at[here.other(step)],
                    arrived.at[step],
                    wshard=here.other(step),
                )
                for step in range(1, here.shards)
            ]
        one = span(here.core * self.half, quarter)
        two = span(here.core * self.half + quarter, quarter)
        if phase == 1:
            held_one, held_two = total.at[:, pl.ds(0, quarter)], total.at[:, pl.ds(quarter, quarter)]
            return [
                self.send(others, held_one, out.at[y, x, :, one], seq=here.y_next),
                self.send(others + 1, held_two, out.at[y, x, :, two], seq=here.x_next),
            ]
        if phase == 2:
            both_one, both_two = out.at[:, x, :, one], out.at[y, :, :, two]
            return [
                self.send(others + 2, both_one, both_one, seq=here.x_next),
                self.send(others + 3, both_two, both_two, seq=here.y_next),
            ]
        ref = out.at[:, :, :, span(here.core * self.half, self.half)]
        return [self.send(others + 4, ref, ref, seq=here.core_next)]

    def work(self, phase):
        if phase == 1:
            arrived, total = self.held
            value = arrived[0].astype(f32)
            for step in range(1, arrived.shape[0]):
                value = value + arrived[step].astype(f32)
            total[...] = value.astype(bf16)


def call(
    kernel,
    grid,
    args,
    in_specs,
    out_specs,
    out_shape,
    scratch_shapes=(),
    riders=(),
    table=None,
    collective_id=None,
    vmem=48,
    flops=0,
    traffic=0,
    name=None,
):
    anywhere = pl.BlockSpec(memory_space=pl.ANY)
    sizes = [len(args), len(out_shape), len(scratch_shapes)]
    rider_in = [array for rider in riders for array in rider.inputs]
    rider_out = [shape for rider in riders for shape in rider.outputs]
    rider_scratch = [entry for rider in riders for entry in rider.semaphores() + list(rider.scratch)]
    aliases = {}
    at_in, at_out = sizes[0], sizes[1]
    for rider in riders:
        for source, target in rider.aliases:
            aliases[at_in + source] = at_out + target
        at_in += len(rider.inputs)
        at_out += len(rider.outputs)

    def body(*refs):
        refs = list(refs)

        def take(count):
            found = refs[:count]
            del refs[:count]
            return found

        own_in, their_in = take(sizes[0]), take(len(rider_in))
        own_out, their_out = take(sizes[1]), take(len(rider_out))
        own_scratch, their_scratch = take(sizes[2]), refs
        if not riders:
            return kernel(*own_in, *own_out, *own_scratch)
        here = Here()
        step = pl.program_id(0)
        reach = max(rider.reach for rider in riders)

        @pl.when(step == 0)
        def start():
            here.meet(reach)

        for rider in riders:
            counts = (len(rider.inputs), len(rider.outputs), 3 + len(rider.scratch))
            parts = []
            for pool, count in zip((their_in, their_out, their_scratch), counts):
                parts.append(pool[:count])
                del pool[:count]
            rider.bind(here, *parts)

        def run(events):
            for which, phase in events:
                riders[which].run(phase)

        for at in sorted(table):
            if at < grid:

                @pl.when(step == at)
                def early():
                    run(table[at])

        kernel(*own_in, *own_out, *own_scratch)

        @pl.when(step == grid - 1)
        def late():
            for at in sorted(table):
                if at >= grid:
                    run(table[at])
            for rider in riders:
                rider.finish()

    found = pl.pallas_call(
        body,
        grid=(grid,),
        in_specs=list(in_specs) + [anywhere] * len(rider_in),
        out_specs=list(out_specs) + [anywhere] * len(rider_out),
        out_shape=list(out_shape) + rider_out,
        scratch_shapes=list(scratch_shapes) + rider_scratch,
        input_output_aliases=aliases,
        compiler_params=pltpu.CompilerParams(
            dimension_semantics=("arbitrary",),
            vmem_limit_bytes=vmem << 20,
            **({"collective_id": collective_id, "has_side_effects": True} if riders else {}),
        ),
        cost_estimate=pl.CostEstimate(flops=flops, bytes_accessed=traffic, transcendentals=0),
        name=name,
    )(*args, *rider_in)
    own, found = found[: sizes[1]], found[sizes[1] :]
    carried = []
    for rider in riders:
        carried.append(found[: len(rider.outputs)])
        found = found[len(rider.outputs) :]
    return own, carried


def whole_rows(gathered):
    return gathered.reshape(-1, gathered.shape[-1])


def finish_sum(part):
    count = lax.axis_size("seq")
    bit = 8
    while bit < count:
        pairs = [(source, source ^ bit) for source in range(count)]
        part = (part.astype(f32) + lax.ppermute(part, "seq", pairs).astype(f32)).astype(bf16)
        bit *= 2
    return part


def on_device(
    tokens,
    slot_lengths,
    live_lengths,
    norm_gain,
    w_qkv,
    w_beta,
    w_outgate,
    conv_weight,
    ridge,
    head_gain,
    w_out,
    ffn_gain,
    w_gate,
    w_up,
    w_down,
    cotangent,
):
    section_out = make_kit()
    row_count = tokens.shape[1]
    depth = (WINDOW + row_count - 1) // row_count
    halo_rows = depth * row_count
    main_rows = halo_rows + row_count
    shards = lax.axis_size("wshard")
    shard_rows = norm_gain.shape[0]
    tap_columns = TAPS * conv_weight.shape[1] // shard_rows
    ffn = w_gate.shape[1]

    own_tokens = tokens[0]
    small = jnp.concatenate(
        [
            w_beta,
            norm_gain[:, None],
            ridge[:, None],
            head_gain[:, None],
            ffn_gain[:, None],
            conv_weight.reshape(shard_rows, tap_columns),
        ],
        axis=1,
    )
    small = jnp.pad(small, ((0, 0), (0, EXTRA - small.shape[1])))
    out_mats = jnp.concatenate([w_outgate, w_out], axis=1)
    ffn_mats = jnp.concatenate([w_gate, w_up], axis=1)

    riders = [
        Gather(jnp.concatenate([w_qkv, small], axis=1)),
        WindowTokens(own_tokens, depth),
        Gather(ffn_mats, 0, 0),
    ]
    events = [(1, 0), (0, 0), (0, 1), (2, 0), (1, 1), (0, 2), (0, 3), (0, 4), (1, 2), (2, 1)]
    _, ((w_front,), (ext_tokens,), (ffn_in,)) = call(
        lambda: None, 1, (), [], [], [], riders=riders, table={0: events}, collective_id=0, name="begin"
    )
    w_front = whole_rows(w_front)
    small = w_front[:, 3 * D :].astype(f32)
    gain_in, all_ridge, gain_head, gain_ffn = (small[:, HEADS + index] for index in range(4))
    taps = small[:, HEADS + 4 : HEADS + 4 + tap_columns]
    taps = taps.reshape(shards, TAPS, -1).transpose(1, 0, 2).reshape(TAPS, 3 * D)

    rank = lax.axis_index("seq")
    first = rank * row_count - halo_rows - PRE
    positions = first + jnp.arange(PRE + main_rows, dtype=jnp.int32)
    segment, valid = token_layout(slot_lengths[0], live_lengths[0], positions)
    main_seg = segment[PRE:]
    own_seg = main_seg[halo_rows:]
    valid_own = valid[PRE + halo_rows :].astype(f32)
    same = jnp.stack(
        [segment[PRE - tap : PRE - tap + main_rows] == main_seg for tap in range(TAPS)], axis=1
    ).astype(f32)
    spacing = positions[None, PRE + halo_rows :] - positions[PRE:, None]
    mask = (
        (spacing >= 0)
        & (spacing < WINDOW)
        & (main_seg[:, None] == own_seg[None, :])
        & valid[PRE:, None]
    ).astype(bf16)
    gain_row = gain_in[None, :]
    ridge_column = all_ridge[:, None]
    x_own = own_tokens.astype(f32)

    (hidden, kv_in, q_in, q_pre, queries, keys, values, beta), ((ffn_in,), (mats,), (all_down,)) = front(
        ext_tokens,
        same,
        gain_row,
        w_front,
        taps,
        row_count,
        riders=[Gather(None, 1, 2, ffn_in), Gather(out_mats, 0, 0), Gather(w_down, 0, 0)],
        table={0: [(0, 1), (1, 0), (2, 0)], 4: [(0, 2)], 99: [(1, 1), (2, 1), (0, 3)]},
        collective_id=1,
    )
    (mixed, image0, image1), ((ffn_in,), (mats,), (all_down,)) = attn_fwd(
        queries,
        keys,
        values,
        beta,
        mask,
        ridge_column,
        riders=[Gather(None, 3, 3, ffn_in), Gather(None, 1, 3, mats), Gather(None, 1, 3, all_down)],
        table={
            0: [(1, 1), (2, 1), (0, 3)],
            2: [(1, 2)],
            3: [(2, 2)],
            5: [(1, 3)],
            99: [(2, 3), (0, 4), (1, 4), (2, 4)],
        },
        collective_id=2,
    )
    mats, ffn_in, all_down = (whole_rows(part) for part in (mats, ffn_in, all_down))
    all_og = mats[:, :D]
    all_out = mats[:, D:].astype(f32)
    all_gate = ffn_in[:, :ffn].astype(f32)
    all_up = ffn_in[:, ffn:].astype(f32)
    all_down = all_down.astype(f32)
    hidden_own = hidden[halo_rows:main_rows]
    gate_pre = jnp.dot(hidden_own, all_og, preferred_element_type=f32)

    def back_half(xrow, mixed, gate_pre, gain_head, mat_out, gain_ffn, mat_gate, mat_up, mat_down):
        return section_out(
            xrow, mixed, gate_pre, gain_head, mat_out, gain_ffn, mat_gate, mat_up, mat_down, valid_own
        )

    output, pull_back = jax.vjp(
        back_half, x_own, mixed, gate_pre, gain_head, all_out, gain_ffn, all_gate, all_up, all_down
    )
    grad_out = cotangent[0].astype(f32)
    d_xout, d_mixed, d_gate, d_ghead, d_wout, d_gffn, d_wgate, d_wup, d_wdown = pull_back(grad_out)
    d_gate = d_gate.astype(bf16)

    def weight_grad(left, right):
        return lax.dot_general(
            left, right, (((0,), (0,)), ((), ())), preferred_element_type=f32
        ).astype(bf16)

    part_rows = shard_rows // 8
    grad_down = d_wdown.astype(bf16)
    grad_ffn = jnp.concatenate([d_wgate.astype(bf16), d_wup.astype(bf16)], axis=1)
    grad_mats = jnp.concatenate([weight_grad(hidden_own, d_gate), d_wout.astype(bf16)], axis=1)
    (d_query, d_key, d_value, d_beta, d_ridge), ((sum_down,), (sum_ffn0,)) = attn_bwd(
        queries,
        keys,
        values,
        beta,
        mask,
        ridge_column,
        image0,
        image1,
        d_mixed.astype(bf16),
        riders=[SumFar(grad_down), SumFar(grad_ffn, 0, part_rows)],
        table={
            0: [(0, 0), (1, 0)],
            1: [(0, 1), (1, 1)],
            4: [(0, 2)],
            5: [(1, 2), (0, 3)],
            7: [(1, 3)],
            99: [(0, 4), (1, 4)],
        },
        collective_id=3,
    )
    (
        (d_kv_in, d_q_in, d_q_pre, d_beta_pre, d_halo, d_own, d_gain, d_taps),
        ((total_down,), (total_ffn0,), (sum_ffn1,), (sum_mats,)),
    ) = back(
        ext_tokens,
        kv_in,
        same,
        q_in,
        q_pre,
        d_key,
        d_value,
        d_query,
        beta,
        d_beta,
        d_gate,
        d_xout,
        gain_row,
        w_front,
        all_og,
        taps,
        riders=[
            SumNear(sum_down),
            SumNear(sum_ffn0),
            SumFar(grad_ffn, part_rows, part_rows),
            SumFar(grad_mats),
        ],
        table={
            0: [(2, 0), (3, 0), (0, 0), (1, 0)],
            1: [(2, 1)],
            2: [(3, 1)],
            3: [(2, 2)],
            4: [(0, 1), (1, 1), (3, 2)],
            5: [(2, 3), (0, 2), (1, 2)],
            6: [(3, 3), (0, 3), (1, 3)],
            99: [(0, 4), (1, 4), (2, 4), (3, 4)],
        },
        collective_id=4,
    )
    d_wq = weight_grad(hidden[halo_rows - PRE : main_rows], jnp.concatenate([d_q_pre, d_q_in]))
    d_wkv = weight_grad(hidden, d_kv_in)
    d_wbeta = weight_grad(hidden[:main_rows], d_beta_pre)[:, :HEADS]

    d_small = jnp.concatenate(
        [
            d_wbeta.astype(f32),
            d_gain.reshape(D, 1),
            d_ridge,
            d_ghead[:, None],
            d_gffn[:, None],
            d_taps.reshape(TAPS, shards, -1).transpose(1, 0, 2).reshape(D, tap_columns),
        ],
        axis=1,
    ).astype(bf16)
    d_small = jnp.pad(d_small, ((0, 0), (0, EXTRA - d_small.shape[1])))
    grad_front = jnp.concatenate([d_wq, d_wkv, d_small], axis=1)
    far0, far1 = SumFar(grad_front, 0, part_rows), SumFar(grad_front, part_rows, part_rows)
    riders = [
        WindowGrads(d_halo, row_count, depth),
        SumNear(sum_ffn1),
        SumNear(sum_mats),
        far0,
        far1,
        SumNear(after=far0),
        SumNear(after=far1),
    ]
    events = [
        (3, 0), (4, 0), (0, 0), (1, 0), (2, 0),
        (3, 1), (4, 1), (3, 2), (4, 2), (1, 1), (2, 1),
        (3, 3), (3, 4), (5, 0), (4, 3), (4, 4), (6, 0),
        (1, 2), (2, 2), (1, 3), (2, 3), (0, 1),
        (5, 1), (6, 1), (5, 2), (6, 2), (5, 3), (6, 3),
        (1, 4), (2, 4), (5, 4), (6, 4),
    ]
    _, (back_grads, (total_ffn1,), (total_mats,), _, _, (total0,), (total1,)) = call(
        lambda: None, 1, (), [], [], [], riders=riders, table={0: events}, collective_id=5, vmem=60, name="end"
    )
    near, far = back_grads
    d_tokens = d_own
    for hop in range(depth):
        d_tokens = d_tokens + near[hop].astype(f32)
    d_tokens = d_tokens + jnp.pad(far.astype(f32), ((row_count - PRE, 0), (0, 0)))

    def final(*sums):
        whole = jnp.concatenate([finish_sum(part) for part in sums], axis=2)
        return whole.reshape(-1, whole.shape[-1]).astype(f32)

    total_down = final(total_down)
    total_ffn = final(total_ffn0, total_ffn1)
    total_middle = final(total_mats)
    total_front = final(total0, total1)
    t_small = total_front[:, 3 * D :]
    return (
        output.astype(bf16)[None],
        d_tokens.astype(bf16)[None],
        t_small[:, HEADS],
        total_front[:, : 3 * D],
        t_small[:, :HEADS],
        total_middle[:, :D],
        t_small[:, HEADS + 4 : HEADS + 4 + tap_columns].reshape(TAPS, -1),
        t_small[:, HEADS + 1],
        t_small[:, HEADS + 2],
        total_middle[:, D:],
        t_small[:, HEADS + 3],
        total_ffn[:, :ffn],
        total_ffn[:, ffn:],
        total_down,
    )


def solution(mesh):
    return jax.shard_map(
        on_device,
        mesh=mesh,
        in_specs=(
            P("wshard", "seq", None),
            P("wshard", None),
            P("wshard", None),
            P("wshard"),
            P("wshard", None),
            P("wshard", None),
            P("wshard", None),
            P(None, "wshard"),
            P("wshard"),
            P("wshard"),
            P("wshard", None),
            P("wshard"),
            P("wshard", None),
            P("wshard", None),
            P("wshard", None),
            P("wshard", "seq", None),
        ),
        out_specs=(
            P("wshard", "seq", None),
            P("wshard", "seq", None),
            P("wshard"),
            P("wshard", None),
            P("wshard", None),
            P("wshard", None),
            P(None, "wshard"),
            P("wshard"),
            P("wshard"),
            P("wshard", None),
            P("wshard"),
            P("wshard", None),
            P("wshard", None),
            P("wshard", None),
        ),
        check_vma=False,
    )
```

```python
import functools
import jax
import jax.numpy as jnp
from jax import lax
from jax.experimental import pallas as pl
from jax.experimental.pallas import tpu as pltpu
from jax.sharding import PartitionSpec as P

D = 1024
HEADS = 8
HEAD_DIM = 128
TAPS = 4
WINDOW = 1024
PRE = 16
SMALL = 128
EXTRA = 512
MESH = pl.DeviceIdType.MESH
f32 = jnp.float32
bf16 = jnp.bfloat16
QB = 256
CH = 256
KEYS = 640
ROWS = 256


def mm(left, right):
    return jnp.dot(left, right, preferred_element_type=f32)


def mm_t(left, right):
    return lax.dot_general(left, right, (((1,), (1,)), ((), ())), preferred_element_type=f32)


def conv_total(ext_ref, slot, same, taps):
    total = taps[0:1] * ext_ref[slot, 8 : 8 + ROWS, :]
    for tap in range(1, TAPS):
        total = total + taps[tap : tap + 1] * ext_ref[slot, 8 - tap : 8 - tap + ROWS, :] * same[tap]
    return total


def unit_scale(active):
    return lax.rsqrt(jnp.sum(active * active, axis=-1, keepdims=True) + 1e-06)


def in_heads(work, *arrays):
    width = arrays[0].shape[1]
    return jnp.concatenate(
        [
            work(*(array[:, at : at + HEAD_DIM] for array in arrays))
            for at in range(0, width, HEAD_DIM)
        ],
        axis=1,
    )


def row_norm(x, gain):
    return (x * lax.rsqrt(jnp.mean(x * x, axis=-1, keepdims=True) + 1e-06) * gain).astype(bf16)


def front_kernel(
    first_own,
    x_ref,
    same_ref,
    gain_ref,
    w_ref,
    taps_ref,
    hid_ref,
    kvin_ref,
    qin_ref,
    qpre_ref,
    q_ref,
    k_ref,
    v_ref,
    beta_ref,
    ext_ref,
    tail_ref,
):
    step = pl.program_id(0)
    gain = gain_ref[...]
    main_rows = k_ref.shape[0]
    before_at = pl.ds(main_rows, PRE)
    rows_at = pl.ds(pl.multiple_of(jnp.maximum(step - 1, 0) * ROWS, ROWS), ROWS)
    own_at = pl.ds(pl.multiple_of(jnp.maximum(step - 1 - first_own, 0) * ROWS, ROWS), ROWS)
    kv_slots = 2 * D // CH

    @pl.when(step == 0)
    def before():
        hidden = row_norm(x_ref[before_at].astype(f32), gain)
        hid_ref[before_at] = hidden
        for slot in range(kv_slots):
            rows = mm(hidden, w_ref[:, D + CH * slot : D + CH * (slot + 1)]).astype(bf16)
            kvin_ref[before_at, CH * slot : CH * (slot + 1)] = rows
            ext_ref[slot, ROWS : ROWS + 8, :] = rows.astype(f32)[PRE - 8 :]

    def through(slot, hidden, same, column, in_ref, in_rows, at):
        ext_ref[slot, 0:8, :] = ext_ref[slot, ROWS : ROWS + 8, :]
        rows = mm(hidden, w_ref[:, column : column + CH]).astype(bf16)
        in_ref[in_rows, at : at + CH] = rows
        ext_ref[slot, 8 : 8 + ROWS, :] = rows.astype(f32)
        total = conv_total(ext_ref, slot, same, taps_ref[:, column : column + CH])
        return total * jax.nn.sigmoid(total)

    def unit(active):
        return in_heads(lambda part: part * unit_scale(part), active).astype(bf16)

    @pl.when(step > 0)
    def main():
        same = [same_ref[rows_at, tap : tap + 1] for tap in range(TAPS)]
        hidden = row_norm(x_ref[rows_at].astype(f32), gain)
        hid_ref[rows_at] = hidden
        for slot in range(kv_slots):
            at = CH * slot
            active = through(slot, hidden, same, D + at, kvin_ref, rows_at, at)
            if at < D:
                k_ref[rows_at, at : at + CH] = unit(active)
            else:
                v_ref[rows_at, at - D : at - D + CH] = active.astype(bf16)
        gates = jax.nn.sigmoid(mm(hidden, w_ref[:, 3 * D : 3 * D + SMALL])).astype(bf16)
        lane = lax.broadcasted_iota(jnp.int32, (ROWS, SMALL), 1)
        beta_ref[rows_at] = jnp.where(lane < HEADS, gates.astype(f32), 0.0)

        @pl.when(step == first_own + 1)
        def own_history():
            rows = mm(tail_ref[...], w_ref[:, :D]).astype(bf16)
            qpre_ref[...] = rows
            for slot in range(D // CH):
                ext_ref[kv_slots + slot, ROWS : ROWS + 8, :] = rows.astype(f32)[
                    PRE - 8 :, CH * slot : CH * (slot + 1)
                ]

        @pl.when(step > first_own)
        def own():
            for slot in range(D // CH):
                at = CH * slot
                active = through(kv_slots + slot, hidden, same, at, qin_ref, own_at, at)
                q_ref[own_at, at : at + CH] = unit(active)

        tail_ref[...] = hidden[ROWS - PRE :]


def front(ext_tokens, same, gain, w_front, taps, own_rows, **riding):
    ext_rows = ext_tokens.shape[0]
    main_rows = ext_rows - PRE
    blocks = main_rows // ROWS
    first_own = (main_rows - own_rows) // ROWS

    def fixed(array):
        return pl.BlockSpec(array.shape, lambda step: (0, 0), pipeline_mode=pl.Buffered(1))

    shape = jax.ShapeDtypeStruct
    outs = [
        shape((ext_rows, D), bf16),
        shape((ext_rows, 2 * D), bf16),
        shape((own_rows, D), bf16),
        shape((PRE, D), bf16),
        shape((own_rows, D), bf16),
        shape((main_rows, D), bf16),
        shape((main_rows, D), bf16),
        shape((main_rows, SMALL), f32),
    ]
    return call(
        functools.partial(front_kernel, first_own),
        blocks + 1,
        (ext_tokens, same, gain, w_front, taps),
        [fixed(array) for array in (ext_tokens, same, gain, w_front, taps)],
        [fixed(array) for array in outs],
        outs,
        [
            pltpu.VMEM((3 * D // CH, 8 + ROWS, CH), f32),
            pltpu.VMEM((PRE, D), bf16),
        ],
        vmem=62,
        flops=4 * (main_rows * 2 + own_rows) * D * D,
        traffic=30 << 20,
        name="front",
        **riding,
    )


def back_kernel(
    blocks,
    first_own,
    x_ref,
    kvin_ref,
    kvprev_ref,
    same_ref,
    qin_ref,
    qprev_ref,
    qpre_ref,
    dk_ref,
    dv_ref,
    dq_ref,
    beta_ref,
    dbeta_ref,
    dgate_ref,
    dres_ref,
    gain_ref,
    w_ref,
    wog_ref,
    taps_ref,
    dkvin_ref,
    dqin_ref,
    dqpre_ref,
    dbp_ref,
    dgain_ref,
    dtaps_ref,
    ext_ref,
    buf_ref,
    dh_ref,
    dxhalo_ref,
    dxown_ref,
):
    step = pl.program_id(0)
    block = blocks - 1 - step
    kv_slots = 2 * D // CH
    gain = gain_ref[...]

    @pl.when(step == 0)
    def clear():
        dgain_ref[...] = jnp.zeros_like(dgain_ref)
        dtaps_ref[...] = jnp.zeros_like(dtaps_ref)
        buf_ref[:, :, ROWS : ROWS + 8, :] = jnp.zeros_like(buf_ref[:, :, ROWS : ROWS + 8, :])

    def norm_back(x, dh):
        scale = lax.rsqrt(jnp.mean(x * x, axis=-1, keepdims=True) + 1e-06)
        normal = x * scale
        dgain_ref[...] += jnp.sum(dh * normal, axis=0, keepdims=True)
        scaled = dh * gain
        return scale * (scaled - normal * jnp.mean(scaled * normal, axis=-1, keepdims=True))

    def shifted(slot, start, count):
        total = buf_ref[slot, 0, start + 1 : start + 1 + count, :]
        for tap in range(2, TAPS):
            total = total + buf_ref[slot, tap - 1, start + tap : start + tap + count, :]
        return total

    def through(slot, column, history, rows, grad, unit, same):
        ext_ref[slot, 0:8, :] = history
        ext_ref[slot, 8 : 8 + ROWS, :] = rows.astype(f32)
        taps = taps_ref[:, column : column + CH]
        total = conv_total(ext_ref, slot, same, taps)
        gate = jax.nn.sigmoid(total)
        active = total * gate
        if unit:

            def unit_back(part, part_grad):
                scale = unit_scale(part)
                normal = part * scale
                return scale * (
                    part_grad - normal * jnp.sum(part_grad * normal, axis=-1, keepdims=True)
                )

            grad = in_heads(unit_back, active, grad)
        grad = grad * (gate + active * (1.0 - gate))
        result = grad * taps[0:1]
        dtaps_ref[0:1, column : column + CH] += jnp.sum(
            grad * ext_ref[slot, 8 : 8 + ROWS, :], axis=0, keepdims=True
        )
        for tap in range(1, TAPS):
            held = grad * same[tap]
            dtaps_ref[tap : tap + 1, column : column + CH] += jnp.sum(
                held * ext_ref[slot, 8 - tap : 8 - tap + ROWS, :], axis=0, keepdims=True
            )
            buf_ref[slot, tap - 1, 0:ROWS, :] = held * taps[tap : tap + 1]
        result = (result + shifted(slot, 0, ROWS)).astype(bf16)
        for tap in range(1, TAPS):
            buf_ref[slot, tap - 1, ROWS : ROWS + 8, :] = buf_ref[slot, tap - 1, 0:8, :]
        return result

    def before_rows(slot):
        for tap in range(1, TAPS):
            buf_ref[slot, tap - 1, ROWS - PRE : ROWS, :] = jnp.zeros((PRE, CH), f32)
        return shifted(slot, ROWS - PRE, PRE).astype(bf16)

    @pl.when(step < blocks)
    def main():
        same = [same_ref[:, tap : tap + 1] for tap in range(TAPS)]
        beta = beta_ref[...]
        gates = (dbeta_ref[...] * beta * (1.0 - beta)).astype(bf16)
        dbp_ref[...] = gates
        dh = mm_t(gates, w_ref[:, 3 * D : 3 * D + SMALL])
        for slot in range(kv_slots):
            at = CH * slot
            grad = dk_ref[:, at : at + CH] if at < D else dv_ref[:, at - D : at - D + CH]
            history = kvprev_ref[PRE - 8 : PRE, at : at + CH].astype(f32)
            rows = kvin_ref[:, at : at + CH]
            rows = through(slot, D + at, history, rows, grad, at < D, same)
            dkvin_ref[:, at : at + CH] = rows
            dh = dh + mm_t(rows, w_ref[:, D + at : D + at + CH])
        dh_ref[...] = dh

        @pl.when(block >= first_own)
        def own():
            dh = mm_t(dgate_ref[...], wog_ref[...])
            for slot in range(D // CH):
                at = CH * slot
                history = jnp.where(
                    block == first_own,
                    qpre_ref[PRE - 8 :, at : at + CH].astype(f32),
                    qprev_ref[PRE - 8 :, at : at + CH].astype(f32),
                )
                rows = qin_ref[:, at : at + CH]
                rows = through(
                    kv_slots + slot, at, history, rows, dq_ref[:, at : at + CH], True, same
                )
                dqin_ref[:, at : at + CH] = rows
                dh = dh + mm_t(rows, w_ref[:, at : at + CH])
            at = pl.ds(pl.multiple_of((block - first_own) * ROWS, ROWS), ROWS)
            dxown_ref[at] = dres_ref[...] + norm_back(x_ref[...].astype(f32), dh_ref[...] + dh)

        @pl.when(block == first_own - 1)
        def own_history():
            dh = jnp.zeros((PRE, D), f32)
            for slot in range(D // CH):
                at = CH * slot
                rows = before_rows(kv_slots + slot)
                dqpre_ref[:, at : at + CH] = rows
                dh = dh + mm_t(rows, w_ref[:, at : at + CH])
            dh_ref[ROWS - PRE : ROWS, :] += dh

        @pl.when(block < first_own)
        def halo():
            at = pl.ds(pl.multiple_of(block * ROWS, ROWS), ROWS)
            dxhalo_ref[at] = norm_back(x_ref[...].astype(f32), dh_ref[...]).astype(bf16)

    @pl.when(step == blocks)
    def before():
        dh = jnp.zeros((PRE, D), f32)
        for slot in range(kv_slots):
            at = CH * slot
            rows = before_rows(slot)
            dkvin_ref[0:PRE, at : at + CH] = rows
            dh = dh + mm_t(rows, w_ref[:, D + at : D + at + CH])
        dxhalo_ref[first_own * ROWS : first_own * ROWS + PRE, :] = norm_back(x_ref[0:PRE].astype(f32), dh).astype(bf16)


def back(
    ext_tokens, kvin, same, qin, qpre, dk, dv, dq, beta, dbeta, dgate, dres, gain, w_front, mats, taps, **riding
):
    ext_rows = ext_tokens.shape[0]
    main_rows = ext_rows - PRE
    own_rows = dq.shape[0]
    blocks = main_rows // ROWS
    first_own = (main_rows - own_rows) // ROWS
    small_blocks = ROWS // PRE

    def ext_block(step):
        return (jnp.where(step == blocks, blocks, blocks - 1 - step), 0)

    def main_block(step):
        return (jnp.maximum(blocks - 1 - step, 0), 0)

    def prev_block(step):
        block = blocks - 1 - step
        return (jnp.where(block <= 0, blocks * small_blocks, small_blocks * block - 1), 0)

    def own_block(step):
        return (jnp.maximum(blocks - 1 - step - first_own, 0), 0)

    def own_prev_block(step):
        return (jnp.maximum(small_blocks * (blocks - 1 - step - first_own) - 1, 0), 0)

    def fixed(array):
        return pl.BlockSpec(array.shape, lambda step: (0, 0), pipeline_mode=pl.Buffered(1))

    shape = jax.ShapeDtypeStruct
    return call(
        functools.partial(back_kernel, blocks, first_own),
        blocks + 1,
        (
            ext_tokens,
            kvin,
            kvin,
            same,
            qin,
            qin,
            qpre,
            dk,
            dv,
            dq,
            beta,
            dbeta,
            dgate,
            dres,
            gain,
            w_front,
            mats,
            taps,
        ),
        [
            pl.BlockSpec((ROWS, D), ext_block),
            pl.BlockSpec((ROWS, 2 * D), ext_block),
            pl.BlockSpec((PRE, 2 * D), prev_block),
            pl.BlockSpec((ROWS, TAPS), main_block),
            pl.BlockSpec((ROWS, D), own_block),
            pl.BlockSpec((PRE, D), own_prev_block),
            fixed(qpre),
            pl.BlockSpec((ROWS, D), main_block),
            pl.BlockSpec((ROWS, D), main_block),
            pl.BlockSpec((ROWS, D), own_block),
            pl.BlockSpec((ROWS, SMALL), main_block),
            pl.BlockSpec((ROWS, SMALL), main_block),
            pl.BlockSpec((ROWS, D), own_block),
            pl.BlockSpec((ROWS, D), own_block),
            fixed(gain),
            fixed(w_front),
            pl.BlockSpec((D, D), lambda step: (0, 0), pipeline_mode=pl.Buffered(1)),
            fixed(taps),
        ],
        [
            pl.BlockSpec((ROWS, 2 * D), ext_block),
            pl.BlockSpec((ROWS, D), own_block),
            pl.BlockSpec((PRE, D), lambda step: (0, 0)),
            pl.BlockSpec((ROWS, SMALL), main_block),
            pl.BlockSpec((1, D), lambda step: (0, 0)),
            pl.BlockSpec((TAPS, 3 * D), lambda step: (0, 0)),
        ],
        [
            shape((ext_rows, 2 * D), bf16),
            shape((own_rows, D), bf16),
            shape((PRE, D), bf16),
            shape((main_rows, SMALL), bf16),
            shape((1, D), f32),
            shape((TAPS, 3 * D), f32),
        ],
        [
            pltpu.VMEM((3 * D // CH, 8 + ROWS, CH), f32),
            pltpu.VMEM((3 * D // CH, TAPS - 1, ROWS + 8, CH), f32),
            pltpu.VMEM((ROWS, D), f32),
            pltpu.VMEM((main_rows - own_rows + PRE, D), bf16),
            pltpu.VMEM((own_rows, D), f32),
        ],
        vmem=62,
        flops=6 * (main_rows * 2 + own_rows) * D * D,
        traffic=40 << 20,
        name="back",
        **riding,
    )


def total(v):
    return jnp.sum(v,axis=0,keepdims=True)

def head_column(beta_ref, h):
    beta=beta_ref[...]
    lane=lax.broadcasted_iota(jnp.int32,beta.shape,1)
    return jnp.sum(jnp.where(lane==h,beta,0.0),axis=1,keepdims=True)

def attn_fwd_kernel(q_ref,k_ref,v_ref,beta_ref,mask_ref,ridge_ref,o_ref,a0_ref,a1_ref,kt_ref,vt_ref,w_ref):
    h=pl.program_id(0)
    rows=q_ref.shape[0]
    span=WINDOW+QB
    kt_ref[...]=k_ref[...].T
    vt_ref[...]=v_ref[...].T
    column=head_column(beta_ref,h)
    ridge=ridge_ref[...]
    blocks=range(rows//QB)
    chunks=range(span//KEYS)
    for b in blocks:
        for c in chunks:
            at=slice(QB*b+KEYS*c,QB*b+KEYS*(c+1))
            w_ref[b,KEYS*c:KEYS*(c+1),:]=mask_ref[at,QB*b:QB*(b+1)].astype(f32)*column[at]
    def apply(b,vector,right):
        low=vector.astype(bf16)
        out=jnp.zeros((HEAD_DIM,QB),f32)
        for c in chunks:
            at=slice(QB*b+KEYS*c,QB*b+KEYS*(c+1))
            s=mm(k_ref[at,:],low)
            s=(w_ref[b,KEYS*c:KEYS*(c+1),:]*s).astype(bf16)
            out=out+mm(right[:,at],s)
        return out
    q=[q_ref[QB*b:QB*(b+1),:].astype(f32).T for b in blocks]
    a0=[apply(b,q[b],kt_ref)+ridge*q[b] for b in blocks]
    for b in blocks: a0_ref[:,QB*b:QB*(b+1)]=a0[b]
    x1=[];p1=[];r1=[];e1=[]
    for b in blocks:
        e0=total(q[b]*q[b])
        s0=e0/total(q[b]*a0[b])
        x1.append(s0*q[b])
        r=q[b]-s0*a0[b]
        e=total(r*r)
        r1.append(r);e1.append(e)
        p1.append(r+e/e0*q[b])
    a1=[apply(b,p1[b],kt_ref)+ridge*p1[b] for b in blocks]
    for b in blocks: a1_ref[:,QB*b:QB*(b+1)]=a1[b]
    x2=[x1[b]+e1[b]/total(p1[b]*a1[b])*p1[b] for b in blocks]
    for b in blocks:
        o_ref[QB*b:QB*(b+1),:]=apply(b,x2[b],vt_ref).T

def attn_fwd(q,k,v,beta,mask_t,ridge,**riding):
    rows=q.shape[0]; keys=k.shape[0]
    head=lambda n: pl.BlockSpec((n,HEAD_DIM),lambda h:(0,h))
    heads_t=pl.BlockSpec((HEAD_DIM,rows),lambda h:(h,0))
    fixed=lambda a: pl.BlockSpec(a.shape,lambda h:(0,0))
    flops=6*2*rows*(WINDOW+QB)*D
    return call(
        attn_fwd_kernel,
        HEADS,
        (q, k, v, beta, mask_t, ridge),
        [head(rows), head(keys), head(keys), fixed(beta), fixed(mask_t), pl.BlockSpec((HEAD_DIM, 1), lambda h: (h, 0))],
        [head(rows), heads_t, heads_t],
        [jax.ShapeDtypeStruct((rows, D), f32)] + [jax.ShapeDtypeStruct((D, rows), f32)] * 2,
        [pltpu.VMEM((HEAD_DIM, keys), bf16)] * 2 + [pltpu.VMEM((rows // QB, WINDOW + QB, QB), f32)],
        vmem=62,
        flops=2 * flops,
        traffic=20 << 20,
        name="attn_fwd",
        **riding,
    )


def attn_bwd_kernel(q_ref,k_ref,v_ref,beta_ref,mask_ref,ridge_ref,a0_ref,a1_ref,do_ref,dq_ref,dk_ref,dv_ref,dbeta_ref,dridge_ref,kt_ref,w_ref,acc_ref):
    h=pl.program_id(0)
    rows=q_ref.shape[0]
    span=WINDOW+QB
    kt_ref[...]=k_ref[...].T
    column=head_column(beta_ref,h)
    ridge=ridge_ref[...]
    blocks=range(rows//QB)
    chunks=range(span//KEYS)
    dk_ref[...]=jnp.zeros_like(dk_ref)
    dv_ref[...]=jnp.zeros_like(dv_ref)
    acc_ref[...]=jnp.zeros_like(acc_ref)
    for b in blocks:
        for c in chunks:
            at=slice(QB*b+KEYS*c,QB*b+KEYS*(c+1))
            w_ref[b,KEYS*c:KEYS*(c+1),:]=mask_ref[at,QB*b:QB*(b+1)].astype(f32)*column[at]
    def apply_back(b,vector,grad,grad_rows,right_ref,dright_ref):
        low=vector.astype(bf16)
        low_rows=vector.T.astype(bf16)
        out=jnp.zeros((HEAD_DIM,QB),f32)
        for c in chunks:
            at=slice(QB*b+KEYS*c,QB*b+KEYS*(c+1))
            w=w_ref[b,KEYS*c:KEYS*(c+1),:]
            s=mm(k_ref[at,:],low)
            dw=mm(right_ref[at,:],grad)
            masked=dw*mask_ref[at,QB*b:QB*(b+1)].astype(f32)
            for_beta=masked*s
            part=for_beta[:,:128]
            for lane in range(128,QB,128):
                part=part+for_beta[:,lane:lane+128]
            acc_ref[at,:]+=part
            ws=(w*s).astype(bf16)
            ds=(w*dw).astype(bf16)
            out=out+mm(kt_ref[:,at],ds)
            dright_ref[at,:]+=mm(ws,grad_rows)
            dk_ref[at,:]+=mm(ds,low_rows)
        return out
    st=[]
    for b in blocks:
        cols=slice(QB*b,QB*(b+1))
        q=q_ref[cols,:].astype(f32).T
        a0=a0_ref[:,cols]; a1=a1_ref[:,cols]
        e0=total(q*q); d0=total(q*a0); s0=e0/d0
        x1=s0*q; r1=q-s0*a0; e1=total(r1*r1); b0=e1/e0
        p1=r1+b0*q; d1=total(p1*a1); s1=e1/d1
        x2=x1+s1*p1
        st.append((q,a0,a1,e0,d0,s0,r1,e1,b0,p1,d1,s1,x2))
    dx2=[]
    for b in blocks:
        do=do_ref[QB*b:QB*(b+1),:]
        dx2.append(apply_back(b,st[b][12],do.astype(f32).T.astype(bf16),do,v_ref,dv_ref))
    da1=[];dp1=[];de1=[];dr=0
    for b in blocks:
        q,a0,a1,e0,d0,s0,r1,e1,b0,p1,d1,s1,x2=st[b]
        ds1=total(dx2[b]*p1)
        de1.append(ds1/d1)
        dd1=-ds1*s1/d1
        g=dd1*p1
        da1.append(g)
        dp1.append(s1*dx2[b]+dd1*a1+ridge*g)
        dr=dr+jnp.sum(g*p1,axis=1,keepdims=True)
    for b in blocks:
        g=da1[b]
        dp1[b]=dp1[b]+apply_back(b,st[b][9],g.astype(bf16),g.T.astype(bf16),k_ref,dk_ref)
    da0=[];dq=[]
    for b in blocks:
        q,a0,a1,e0,d0,s0,r1,e1,b0,p1,d1,s1,x2=st[b]
        db0=total(dp1[b]*q)
        dpq=b0*dp1[b]
        de=de1[b]+db0/e0
        de0=-db0*b0/e0
        dr1=dp1[b]+2.0*de*r1
        ds0=total(dx2[b]*q)-total(dr1*a0)
        dpq=dpq+s0*dx2[b]
        g=-s0*dr1
        de0=de0+ds0/d0
        dd0=-ds0*s0/d0
        dpq=dpq+dd0*a0
        g=g+dd0*q
        dpq=dpq+dr1+2.0*de0*q+ridge*g
        da0.append(g);dq.append(dpq)
        dr=dr+jnp.sum(g*q,axis=1,keepdims=True)
    for b in blocks:
        g=da0[b]
        t=dq[b]+apply_back(b,st[b][0],g.astype(bf16),g.T.astype(bf16),k_ref,dk_ref)
        dq_ref[QB*b:QB*(b+1),:]=t.T
    dridge_ref[...]=dr
    found=jnp.sum(acc_ref[...],axis=1,keepdims=True)
    lane=lax.broadcasted_iota(jnp.int32,dbeta_ref.shape,1)
    @pl.when(h==0)
    def _():
        dbeta_ref[...]=jnp.zeros_like(dbeta_ref)
    dbeta_ref[...]=jnp.where(lane==h,found,dbeta_ref[...])

def attn_bwd(q,k,v,beta,mask_t,ridge,a0,a1,do,**riding):
    rows=q.shape[0]; keys=k.shape[0]
    head=lambda n: pl.BlockSpec((n,HEAD_DIM),lambda h:(0,h))
    heads_t=pl.BlockSpec((HEAD_DIM,rows),lambda h:(h,0))
    fixed=lambda a: pl.BlockSpec(a.shape,lambda h:(0,0))
    rd=pl.BlockSpec((HEAD_DIM,1),lambda h:(h,0))
    flops=15*2*rows*(WINDOW+QB)*D
    return call(
        attn_bwd_kernel,
        HEADS,
        (q, k, v, beta, mask_t, ridge, a0, a1, do),
        [head(rows), head(keys), head(keys), fixed(beta), fixed(mask_t), rd, heads_t, heads_t, head(rows)],
        [head(rows), head(keys), head(keys), fixed(beta), rd],
        [
            jax.ShapeDtypeStruct((rows, D), f32),
            jax.ShapeDtypeStruct((keys, D), f32),
            jax.ShapeDtypeStruct((keys, D), f32),
            jax.ShapeDtypeStruct(beta.shape, f32),
            jax.ShapeDtypeStruct((D, 1), f32),
        ],
        [
            pltpu.VMEM((HEAD_DIM, keys), bf16),
            pltpu.VMEM((rows // QB, WINDOW + QB, QB), f32),
            pltpu.VMEM((keys, 128), f32),
        ],
        vmem=62,
        flops=2 * flops,
        traffic=30 << 20,
        name="attn_bwd",
        **riding,
    )


def slot_of(positions, lengths):
    slot = (positions >= 0).astype(jnp.int32) - 1
    start = 0
    for index in range(lengths.shape[0] - 1):
        start = start + lengths[index]
        slot = slot + (positions >= start).astype(jnp.int32)
    return slot


def is_live(positions, lengths, live):
    found = positions < 0
    start = 0
    for index in range(lengths.shape[0]):
        found = found | ((positions >= start) & (positions < start + live[index]))
        start = start + lengths[index]
    return found & (positions >= 0)


class Here:
    def __init__(self):
        self.rank = lax.axis_index("seq")
        self.ranks = lax.axis_size("seq")
        self.place = lax.axis_index("wshard")
        self.shards = lax.axis_size("wshard")
        self.core = self.rank % 2
        self.x = (self.rank // 2) % 2
        self.y = (self.rank // 4) % 2
        self.core_next = self.rank + 1 - 2 * self.core
        self.x_next = self.rank + 2 - 4 * self.x
        self.y_next = self.rank + 4 - 8 * self.y

    def other(self, step):
        return (self.place + step) % self.shards

    def along(self, step):
        return (self.rank + step + self.ranks) % self.ranks

    def meet(self, reach):
        barrier = pltpu.get_barrier_semaphore()
        near = [self.core_next, self.x_next, self.y_next]
        for step in range(1, reach + 1):
            near += [self.along(step), self.along(-step)]
        for device in near:
            pl.semaphore_signal(barrier, inc=1, device_id={"seq": device}, device_id_type=MESH)
        for step in range(1, self.shards):
            pl.semaphore_signal(
                barrier, inc=1, device_id={"wshard": self.other(step)}, device_id_type=MESH
            )
        pl.semaphore_wait(barrier, len(near) + self.shards - 1)


def span(start, size):
    return pl.ds(pl.multiple_of(start, 128), size)


class Rider:
    reach = 0
    first, last = 0, 0
    inside = 0
    inputs, outputs, scratch, aliases = (), (), (), ()

    def bind(self, here, inputs, outputs, scratch):
        self.here = here
        self.inputs_, self.outputs_ = inputs, outputs
        self.send_sems, self.recv_sems, self.local_sems = scratch[:3]
        self.held = scratch[3:]

    def semaphores(self):
        return [
            pltpu.SemaphoreType.DMA((self.remote_count,)),
            pltpu.SemaphoreType.DMA((self.remote_count,)),
            pltpu.SemaphoreType.DMA((self.local_count,)),
        ]

    def send(self, index, source, target, **device):
        return pltpu.make_async_remote_copy(
            src_ref=source,
            dst_ref=target,
            send_sem=self.send_sems.at[index],
            recv_sem=self.recv_sems.at[index],
            device_id=device,
            device_id_type=MESH,
        )

    def keep(self, index, source, target):
        return pltpu.make_async_copy(source, target, self.local_sems.at[index])

    def remote(self, phase):
        return []

    def local(self, phase):
        return []

    def work(self, phase):
        pass

    def run(self, phase):
        if phase > self.first:
            for copy in self.remote(phase - 1):
                copy.wait_recv()
            for copy in self.local(phase - 1):
                copy.wait()
        if phase <= self.last:
            self.work(phase)
            for copy in self.remote(phase) + self.local(phase):
                copy.start()

    def finish(self):
        for phase in range(self.first, self.last + 1):
            for copy in self.remote(phase):
                copy.wait_send()


class Gather(Rider):
    remote_count, local_count = 18, 2

    def __init__(self, shard, first=0, last=3, begun=None):
        self.first, self.last = first, last
        if begun is None:
            split = shard.reshape(2, 2, shard.shape[0] // 4, shard.shape[1])
            places = lax.axis_size("wshard")
            self.inputs = (split,)
            self.outputs = (jax.ShapeDtypeStruct((places,) + split.shape, shard.dtype),)
            self.scratch = (pltpu.VMEM(split.shape, shard.dtype),)
        else:
            self.inputs = (begun,)
            self.outputs = (jax.ShapeDtypeStruct(begun.shape, begun.dtype),)
            self.aliases = ((0, 0),)

    def work(self, phase):
        if phase == 0:
            copy = self.keep(1, self.inputs_[0], self.held[0])
            copy.start()
            copy.wait()

    def local(self, phase):
        if phase:
            return []
        return [self.keep(0, self.held[0], self.outputs_[0].at[self.here.place])]

    def remote(self, phase):
        here, (target,) = self.here, self.outputs_
        half = target.shape[-1] // 2
        quarter = half // 2
        mine = span(here.core * half, half)
        one = span(here.core * half, quarter)
        two = span(here.core * half + quarter, quarter)
        y, x = here.y, here.x
        if phase == 0:
            return [
                self.send(
                    step - 1,
                    self.inputs_[0].at[y, x, :, mine],
                    target.at[here.place, y, x, :, mine],
                    wshard=here.other(step),
                )
                for step in range(1, here.shards)
            ]
        found = []
        for step in range(1, here.shards):
            at = target.at[here.other(step)]
            if phase == 1:
                found.append((at.at[y, x, :, one], here.x_next))
                found.append((at.at[y, x, :, two], here.y_next))
            elif phase == 2:
                found.append((at.at[y, :, :, one], here.y_next))
                found.append((at.at[:, x, :, two], here.x_next))
            else:
                found.append((at.at[:, :, :, mine], here.core_next))
        start = {1: 3, 2: 9, 3: 15}[phase]
        return [
            self.send(start + index, ref, ref, seq=near) for index, (ref, near) in enumerate(found)
        ]


class WindowTokens(Rider):
    last = 1
    remote_count, local_count = 0, 2

    def __init__(self, tokens, depth):
        self.depth = depth
        self.reach = depth + 1
        self.remote_count = depth + 1
        self.rows = tokens.shape[0]
        self.inputs = (tokens,)
        rows = self.rows * (depth + 1) + PRE
        self.outputs = (jax.ShapeDtypeStruct((rows, tokens.shape[1]), tokens.dtype),)
        self.scratch = (pltpu.VMEM(tokens.shape, tokens.dtype),)

    def work(self, phase):
        if phase == 0:
            copy = self.keep(1, self.inputs_[0], self.held[0])
            copy.start()
            copy.wait()

    def local(self, phase):
        rows = pl.ds(self.depth * self.rows, self.rows)
        return [self.keep(0, self.held[0], self.outputs_[0].at[rows])] if phase == 0 else []

    def remote(self, phase):
        here, rows, depth = self.here, self.rows, self.depth
        (own,), (ext,) = self.inputs_, self.outputs_
        if phase == 1:
            start = pl.multiple_of((1 - here.core) * depth * rows + here.core * (depth - 2) * rows, 16)
            ref = ext.at[pl.ds((depth - 1) * rows, rows)]
            return [self.send(0, ext.at[pl.ds(start, rows)], ref, seq=here.core_next)]
        found = [
            self.send(
                hop - 1, own, ext.at[pl.ds((depth - hop) * rows, rows)], seq=here.along(hop)
            )
            for hop in range(2, depth + 1)
        ]
        found.append(
            self.send(
                depth,
                own.at[pl.ds(rows - PRE, PRE)],
                ext.at[pl.ds((depth + 1) * rows, PRE)],
                seq=here.along(depth + 1),
            )
        )
        return found


class WindowGrads(Rider):
    inside = 2
    last = 4
    remote_count, local_count = 4, 1

    def __init__(self, rows, columns, depth):
        assert depth == 2
        self.rows = rows
        self.reach = depth + 1
        self.outputs = (jax.ShapeDtypeStruct((rows, columns), bf16),)
        self.scratch = (
            pltpu.VMEM((rows, columns), bf16),
            pltpu.VMEM((rows, columns), bf16),
            pltpu.VMEM((PRE, columns), bf16),
        )

    def remote(self, phase):
        here, rows = self.here, self.rows
        grads, _ = self.inputs_
        given, near, far = self.held
        if phase == 0:
            return [self.send(0, grads.at[pl.ds(rows, rows)], given, seq=here.core_next)]
        if phase == 1 or phase == 2:
            half = pl.ds((2 - phase) * (rows // 2), rows // 2)
            return [self.send(phase, grads.at[half], near.at[half], seq=here.along(-2))]
        if phase == 3:
            return [self.send(3, grads.at[pl.ds(2 * rows, PRE)], far, seq=here.along(-3))]
        return []

    def run(self, phase):
        grads, own = self.inputs_
        given, near, far = self.held
        half = self.rows // 2
        chunk = 2 * PRE
        if phase == 1:
            self.remote(0)[0].wait_recv()
        if phase == 1 or phase == 2:

            @pl.when(self.here.core == 1)
            def join():
                def add(index, carry):
                    start = (2 - phase) * half + index * chunk
                    at = pl.ds(pl.multiple_of(start, chunk), chunk)
                    add_into(grads, at, given[at])
                    return carry

                lax.fori_loop(0, half // chunk, add, 0)

        if phase == 4:
            for earlier in (1, 2, 3):
                self.remote(earlier)[0].wait_recv()
            own[self.rows - PRE :, :] += far[...].astype(f32)
            first_core = (self.here.core == 0).astype(f32)

            def add_up(index, carry):
                at = pl.ds(pl.multiple_of(index * chunk, chunk), chunk)
                value = own[at] + near[at].astype(f32) + first_core * given[at].astype(f32)
                given[at] = value.astype(bf16)
                return carry

            lax.fori_loop(0, self.rows // chunk, add_up, 0)
            self.keep(0, given, self.outputs_[0]).start()
        elif phase == 5:
            self.keep(0, given, self.outputs_[0]).wait()
        else:
            self.remote(phase)[0].start()


def add_into(target, at, value):
    target[at] = (target[at].astype(f32) + value.astype(f32)).astype(bf16)


class SumFar(Rider):
    last = 3
    remote_count, local_count = 5, 2

    def __init__(self, grad=None, start=0, size=None, columns=None, offset=0):
        places = lax.axis_size("wshard")
        self.inside = int(grad is None)
        self.offset = offset
        if not self.inside:
            columns = grad.shape[-1]
            grad = grad.reshape(places, 2, 2, grad.shape[0] // places // 4, columns)
            size = grad.shape[3] if size is None else size
            self.inputs = (grad,)
        self.rows = pl.ds(start, size)
        half = columns // 2
        quarter = half // 2
        self.outputs = (jax.ShapeDtypeStruct((places, size, half), bf16),)
        self.scratch = (
            pltpu.VMEM((places, 2, 2, size, half), bf16),
            pltpu.VMEM((places, 2, 2, size, half), bf16),
            pltpu.VMEM((places, 2, size, quarter), bf16),
            pltpu.VMEM((places, 2, size, quarter), bf16),
            pltpu.VMEM((places, size, quarter), bf16),
            pltpu.VMEM((places, size, quarter), bf16),
        )
        self.half = half

    def local(self, phase):
        here, held = self.here, self.held[0]
        if phase == 0:
            mine = span(self.offset + here.core * self.half, self.half)
            return [self.keep(0, self.inputs_[0].at[:, :, :, self.rows, mine], held)]
        if phase == 3:
            return [self.keep(1, held.at[:, here.y, here.x], self.outputs_[0])]
        return []

    def remote(self, phase):
        here = self.here
        y, x = here.y, here.x
        held, core_in, far_a, far_b, next_a, next_b = self.held
        one, two = pl.ds(0, self.half // 2), pl.ds(self.half // 2, self.half // 2)
        if phase == 0:
            yours = span(self.offset + (1 - here.core) * self.half, self.half)
            ref = self.inputs_[0].at[:, :, :, self.rows, yours]
            return [self.send(0, ref, core_in, seq=here.core_next)]
        if phase == 1:
            return [
                self.send(1, held.at[:, :, 1 - x, :, one], far_a, seq=here.x_next),
                self.send(2, held.at[:, 1 - y, :, :, two], far_b, seq=here.y_next),
            ]
        if phase == 2:
            return [
                self.send(3, held.at[:, 1 - y, x, :, one], next_a, seq=here.y_next),
                self.send(4, held.at[:, y, 1 - x, :, two], next_b, seq=here.x_next),
            ]
        return []

    def work(self, phase):
        y, x = self.here.y, self.here.x
        held, core_in, far_a, far_b, next_a, next_b = self.held
        places = held.shape[0]
        one, two = slice(0, self.half // 2), slice(self.half // 2, self.half)
        every = slice(None)
        if phase == 1:

            def add(index, carry):
                at = (index // 4, (index // 2) % 2, index % 2)
                add_into(held, at, core_in[at])
                return carry

            lax.fori_loop(0, 4 * places, add, 0)
        elif phase == 2:

            def add(index, carry):
                place, side = index // 2, index % 2
                add_into(held, (place, side, x, every, one), far_a[place, side])
                add_into(held, (place, y, side, every, two), far_b[place, side])
                return carry

            lax.fori_loop(0, 2 * places, add, 0)
        elif phase == 3:

            def add(place, carry):
                add_into(held, (place, y, x, every, one), next_a[place])
                add_into(held, (place, y, x, every, two), next_b[place])
                return carry

            lax.fori_loop(0, places, add, 0)


class SumNear(Rider):
    last = 3
    local_count = 2

    def __init__(self, sums=None, after=None, stop=False, total=None):
        self.after, self.stop, self.resume = after, stop, total is not None
        if self.resume:
            (size, half), places = total.shape, lax.axis_size("wshard")
            self.inputs = (total,)
        else:
            places, size, half = (sums if after is None else after.outputs[0]).shape
            self.inputs = (sums,) if after is None else ()
        self.remote_count = places - 1 + 5
        self.half = half
        self.outputs = (jax.ShapeDtypeStruct((2, 2, size, 2 * half), bf16),)
        if stop:
            self.last = 1
            self.outputs = (jax.ShapeDtypeStruct((size, half), bf16),)
        arrived = (1, 16, 128) if self.resume else (places, size, half)
        self.scratch = (pltpu.VMEM(arrived, bf16), pltpu.VMEM((size, half), bf16))

    def bind(self, here, inputs, outputs, scratch):
        super().bind(here, inputs, outputs, scratch)
        if self.after is not None:
            self.inputs_ = self.after.outputs_

    def local(self, phase):
        here = self.here
        arrived, total = self.held
        if phase == 0 and self.resume:
            return [self.keep(0, self.inputs_[0], total)]
        if phase == 0:
            return [self.keep(0, self.inputs_[0].at[here.place], arrived.at[0])]
        if phase == 1 and self.stop:
            return [self.keep(1, total, self.outputs_[0])]
        if phase == 1:
            mine = span(here.core * self.half, self.half)
            return [self.keep(1, total, self.outputs_[0].at[here.y, here.x, :, mine])]
        return []

    def remote(self, phase):
        here = self.here
        y, x = here.y, here.x
        arrived, total = self.held
        (out,) = self.outputs_
        quarter = self.half // 2
        others = here.shards - 1
        if (phase == 0 and self.resume) or (phase == 1 and self.stop):
            return []
        if phase == 0:
            return [
                self.send(
                    step - 1,
                    self.inputs_[0].at[here.other(step)],
                    arrived.at[step],
                    wshard=here.other(step),
                )
                for step in range(1, here.shards)
            ]
        one = span(here.core * self.half, quarter)
        two = span(here.core * self.half + quarter, quarter)
        if phase == 1:
            held_one, held_two = total.at[:, pl.ds(0, quarter)], total.at[:, pl.ds(quarter, quarter)]
            return [
                self.send(others, held_one, out.at[y, x, :, one], seq=here.y_next),
                self.send(others + 1, held_two, out.at[y, x, :, two], seq=here.x_next),
            ]
        if phase == 2:
            both_one, both_two = out.at[:, x, :, one], out.at[y, :, :, two]
            return [
                self.send(others + 2, both_one, both_one, seq=here.x_next),
                self.send(others + 3, both_two, both_two, seq=here.y_next),
            ]
        ref = out.at[:, :, :, span(here.core * self.half, self.half)]
        return [self.send(others + 4, ref, ref, seq=here.core_next)]

    def work(self, phase):
        if phase == 1 and not self.resume:
            arrived, total = self.held
            value = arrived[0].astype(f32)
            for step in range(1, arrived.shape[0]):
                value = value + arrived[step].astype(f32)
            total[...] = value.astype(bf16)


class SumPlace(Rider):
    last = 2
    local_count = 2

    def __init__(self, grad):
        places = lax.axis_size("wshard")
        size, columns = grad.shape[0] // places // 4, grad.shape[1]
        self.half = columns // 2
        self.remote_count = places
        self.inputs = (grad.reshape(places, 2, 2, size, columns),)
        part = (2, 2, size, self.half)
        self.outputs = (jax.ShapeDtypeStruct(part, bf16),)
        self.scratch = (
            pltpu.VMEM((places,) + part, bf16),
            pltpu.VMEM((places,) + part, bf16),
            pltpu.VMEM((places - 1,) + part, bf16),
        )

    def local(self, phase):
        held, core_in, _ = self.held
        if phase == 0:
            mine = span(self.here.core * self.half, self.half)
            return [self.keep(0, self.inputs_[0].at[:, :, :, :, mine], held)]
        if phase == 2:
            return [self.keep(1, core_in.at[0], self.outputs_[0])]
        return []

    def remote(self, phase):
        here = self.here
        held, core_in, arrived = self.held
        if phase == 0:
            yours = span((1 - here.core) * self.half, self.half)
            return [self.send(0, self.inputs_[0].at[:, :, :, :, yours], core_in, seq=here.core_next)]
        if phase == 1:
            return [
                self.send(
                    step,
                    held.at[here.other(step)],
                    arrived.at[step - 1],
                    wshard=here.other(step),
                )
                for step in range(1, here.shards)
            ]
        return []

    def work(self, phase):
        held, core_in, arrived = self.held
        if phase == 1:

            def add(index, carry):
                at = (index // 4, (index // 2) % 2, index % 2)
                add_into(held, at, core_in[at])
                return carry

            lax.fori_loop(0, 4 * held.shape[0], add, 0)
        elif phase == 2:

            def gather_up(index, carry):
                at = (index // 2, index % 2)
                value = held[(self.here.place,) + at].astype(f32)
                for step in range(arrived.shape[0]):
                    value = value + arrived[(step,) + at].astype(f32)
                core_in[(0,) + at] = value.astype(bf16)
                return carry

            lax.fori_loop(0, 4, gather_up, 0)


class SumSpread(Rider):
    last = 5
    remote_count, local_count = 9, 2

    def __init__(self, sums):
        _, _, size, half = sums.shape
        self.half = half
        quarter = half // 2
        self.inputs = (sums,)
        self.outputs = (jax.ShapeDtypeStruct((2, 2, size, 2 * half), bf16),)
        self.scratch = (
            pltpu.VMEM((2, 2, size, half), bf16),
            pltpu.VMEM((2, size, quarter), bf16),
            pltpu.VMEM((2, size, quarter), bf16),
            pltpu.VMEM((size, quarter), bf16),
            pltpu.VMEM((size, quarter), bf16),
        )

    def local(self, phase):
        here, held = self.here, self.held[0]
        if phase == 0:
            return [self.keep(0, self.inputs_[0], held)]
        if phase == 3:
            mine = span(here.core * self.half, self.half)
            return [self.keep(1, held.at[here.y, here.x], self.outputs_[0].at[here.y, here.x, :, mine])]
        return []

    def remote(self, phase):
        here, (out,) = self.here, self.outputs_
        y, x, quarter = here.y, here.x, self.half // 2
        held, far_a, far_b, next_a, next_b = self.held
        one, two = pl.ds(0, quarter), pl.ds(quarter, quarter)
        out_one = span(here.core * self.half, quarter)
        out_two = span(here.core * self.half + quarter, quarter)
        if phase == 1:
            return [
                self.send(0, held.at[:, 1 - x, :, one], far_a, seq=here.x_next),
                self.send(1, held.at[1 - y, :, :, two], far_b, seq=here.y_next),
            ]
        if phase == 2:
            return [
                self.send(2, held.at[1 - y, x, :, one], next_a, seq=here.y_next),
                self.send(3, held.at[y, 1 - x, :, two], next_b, seq=here.x_next),
            ]
        if phase == 3:
            return [
                self.send(4, held.at[y, x, :, one], out.at[y, x, :, out_one], seq=here.y_next),
                self.send(5, held.at[y, x, :, two], out.at[y, x, :, out_two], seq=here.x_next),
            ]
        if phase == 4:
            both_one, both_two = out.at[:, x, :, out_one], out.at[y, :, :, out_two]
            return [
                self.send(6, both_one, both_one, seq=here.x_next),
                self.send(7, both_two, both_two, seq=here.y_next),
            ]
        if phase == 5:
            ref = out.at[:, :, :, span(here.core * self.half, self.half)]
            return [self.send(8, ref, ref, seq=here.core_next)]
        return []

    def work(self, phase):
        y, x = self.here.y, self.here.x
        held, far_a, far_b, next_a, next_b = self.held
        every = slice(None)
        one, two = slice(0, self.half // 2), slice(self.half // 2, self.half)
        if phase == 2:
            for side in range(2):
                add_into(held, (side, x, every, one), far_a[side])
                add_into(held, (y, side, every, two), far_b[side])
        elif phase == 3:
            add_into(held, (y, x, every, one), next_a[...])
            add_into(held, (y, x, every, two), next_b[...])


def call(
    kernel,
    grid,
    args,
    in_specs,
    out_specs,
    out_shape,
    scratch_shapes=(),
    riders=(),
    table=None,
    collective_id=None,
    vmem=48,
    flops=0,
    traffic=0,
    name=None,
):
    anywhere = pl.BlockSpec(memory_space=pl.ANY)
    sizes = [len(args), len(out_shape), len(scratch_shapes)]
    rider_in = [array for rider in riders for array in rider.inputs]
    rider_out = [shape for rider in riders for shape in rider.outputs]
    rider_scratch = [entry for rider in riders for entry in rider.semaphores() + list(rider.scratch)]
    aliases = {}
    at_in, at_out = sizes[0], sizes[1]
    for rider in riders:
        for source, target in rider.aliases:
            aliases[at_in + source] = at_out + target
        at_in += len(rider.inputs)
        at_out += len(rider.outputs)

    def body(*refs):
        refs = list(refs)

        def take(count):
            found = refs[:count]
            del refs[:count]
            return found

        own_in, their_in = take(sizes[0]), take(len(rider_in))
        own_out, their_out = take(sizes[1]), take(len(rider_out))
        own_scratch, their_scratch = take(sizes[2]), refs
        if not riders:
            return kernel(*own_in, *own_out, *own_scratch)
        here = Here()
        step = pl.program_id(0)
        reach = max(rider.reach for rider in riders)

        @pl.when(step == 0)
        def start():
            here.meet(reach)

        for rider in riders:
            counts = (len(rider.inputs), len(rider.outputs), 3 + len(rider.scratch))
            parts = []
            for pool, count in zip((their_in, their_out, their_scratch), counts):
                parts.append(pool[:count])
                del pool[:count]
            if rider.inside:
                parts[0] = own_scratch[-rider.inside :]
            rider.bind(here, *parts)

        def run(events):
            for which, phase in events:
                riders[which].run(phase)

        for at in sorted(table):
            if at < grid:

                @pl.when(step == at)
                def early():
                    run(table[at])

        kernel(*own_in, *own_out, *own_scratch)

        @pl.when(step == grid - 1)
        def late():
            for at in sorted(table):
                if at >= grid:
                    run(table[at])
            for rider in riders:
                rider.finish()

    found = pl.pallas_call(
        body,
        grid=(grid,),
        in_specs=list(in_specs) + [anywhere] * len(rider_in),
        out_specs=list(out_specs) + [anywhere] * len(rider_out),
        out_shape=list(out_shape) + rider_out,
        scratch_shapes=list(scratch_shapes) + rider_scratch,
        input_output_aliases=aliases,
        compiler_params=pltpu.CompilerParams(
            dimension_semantics=("arbitrary",),
            vmem_limit_bytes=vmem << 20,
            **({"collective_id": collective_id, "has_side_effects": True} if riders else {}),
        ),
        cost_estimate=pl.CostEstimate(flops=flops, bytes_accessed=traffic, transcendentals=0),
        name=name,
    )(*args, *rider_in)
    own, found = found[: sizes[1]], found[sizes[1] :]
    carried = []
    for rider in riders:
        carried.append(found[: len(rider.outputs)])
        found = found[len(rider.outputs) :]
    return own, carried


def whole_rows(gathered):
    return gathered.reshape(-1, gathered.shape[-1])


def finish_sum(part):
    count = lax.axis_size("seq")
    bit = 8
    while bit < count:
        pairs = [(source, source ^ bit) for source in range(count)]
        part = (part.astype(f32) + lax.ppermute(part, "seq", pairs).astype(f32)).astype(bf16)
        bit *= 2
    return part


def mid_kernel(
    x_ref,
    o_ref,
    hid_ref,
    cot_ref,
    live_ref,
    hgain_ref,
    fgain_ref,
    mats_in,
    ffn_in,
    down_in,
    out_ref,
    y_ref,
    h2_ref,
    u_ref,
    dab_ref,
    dd_ref,
    dyw_ref,
    dgate_ref,
    do_ref,
    dres_ref,
    dhg_ref,
    dfg_ref,
    mats_ref,
    ffn_ref,
    down_ref,
    sems,
):
    step = pl.program_id(0)
    inner = down_ref.shape[0]
    copies = [
        pltpu.make_async_copy(source, target, sems.at[index])
        for index, (source, target) in enumerate(
            ((mats_in, mats_ref), (ffn_in, ffn_ref), (down_in, down_ref))
        )
    ]

    @pl.when(step == 0)
    def begin():
        for copy in copies:
            copy.start()
        dhg_ref[...] = jnp.zeros_like(dhg_ref)
        dfg_ref[...] = jnp.zeros_like(dfg_ref)
        copies[0].wait()

    hgain, fgain = hgain_ref[...], fgain_ref[...]
    gate_pre = mm(hid_ref[...], mats_ref[:, :D])
    gate = jax.nn.sigmoid(gate_pre)
    gate_silu = gate_pre * gate

    def head_scale(part):
        return lax.rsqrt(jnp.mean(part * part, axis=-1, keepdims=True) + 1e-05)

    mixed = o_ref[...]
    normal = in_heads(lambda part: part * head_scale(part), mixed)
    scaled = normal * hgain
    y = (scaled * gate_silu).astype(bf16)
    y_ref[...] = y
    x1 = x_ref[...].astype(f32) + mm(y, mats_ref[:, D:])
    x1_scale = lax.rsqrt(jnp.mean(x1 * x1, axis=-1, keepdims=True) + 1e-06)
    h2 = (x1 * x1_scale * fgain).astype(bf16)
    h2_ref[...] = h2
    live = live_ref[...]
    grad_out = live * cot_ref[...].astype(f32)
    dd = grad_out.astype(bf16)
    dd_ref[...] = dd

    @pl.when(step == 0)
    def rest():
        copies[1].wait()
        copies[2].wait()

    forward = jnp.zeros_like(x1)
    dh2 = jnp.zeros_like(x1)
    for at in range(0, inner, CH):
        one, two = slice(at, at + CH), slice(inner + at, inner + at + CH)
        a = mm(h2, ffn_ref[:, one])
        b = mm(h2, ffn_ref[:, two])
        sig = jax.nn.sigmoid(a)
        silu = a * sig
        u = (silu * b).astype(bf16)
        u_ref[:, one] = u
        forward = forward + mm(u, down_ref[one, :])
        du = mm_t(dd, down_ref[one, :])
        da = (du * b * (sig + silu * (1.0 - sig))).astype(bf16)
        db = (du * silu).astype(bf16)
        dab_ref[:, one] = da
        dab_ref[:, two] = db
        dh2 = dh2 + mm_t(da, ffn_ref[:, one]) + mm_t(db, ffn_ref[:, two])
    out_ref[...] = (live * (x1 + forward)).astype(bf16)
    x1_normal = x1 * x1_scale
    dfg_ref[...] += jnp.sum(dh2 * x1_normal, axis=0, keepdims=True)
    dh2 = dh2 * fgain
    dx1 = grad_out + x1_scale * (
        dh2 - x1_normal * jnp.mean(dh2 * x1_normal, axis=-1, keepdims=True)
    )
    dres_ref[...] = dx1
    dyw = dx1.astype(bf16)
    dyw_ref[...] = dyw
    dy = mm_t(dyw, mats_ref[:, D:])
    dgate_ref[...] = (dy * scaled * (gate + gate_silu * (1.0 - gate))).astype(bf16)
    dscaled = dy * gate_silu
    dhg_ref[...] += jnp.sum(dscaled * normal, axis=0, keepdims=True)

    def head_back(part, part_normal, grad):
        return head_scale(part) * (
            grad - part_normal * jnp.mean(grad * part_normal, axis=-1, keepdims=True)
        )

    do_ref[...] = in_heads(head_back, mixed, normal, dscaled * hgain).astype(bf16)


def mid(x, mixed, hidden, first_own, cotangent, live, hgain, fgain, mats, ffn, down):
    rows = x.shape[0]
    inner = down.shape[0]
    shape = jax.ShapeDtypeStruct

    def block(columns):
        return pl.BlockSpec((ROWS, columns), lambda step: (step, 0))

    row = pl.BlockSpec((1, D), lambda step: (0, 0))
    anywhere = pl.BlockSpec(memory_space=pl.ANY)
    outs = [
        shape((rows, D), bf16),
        shape((rows, D), bf16),
        shape((rows, D), bf16),
        shape((rows, inner), bf16),
        shape((rows, 2 * inner), bf16),
        shape((rows, D), bf16),
        shape((rows, D), bf16),
        shape((rows, D), bf16),
        shape((rows, D), bf16),
        shape((rows, D), f32),
    ]
    found, _ = call(
        mid_kernel,
        rows // ROWS,
        (x, mixed, hidden, cotangent, live, hgain, fgain, mats, ffn, down),
        [
            block(D),
            block(D),
            pl.BlockSpec((ROWS, D), lambda step: (step + first_own, 0)),
            block(D),
            block(1),
            row,
            row,
            anywhere,
            anywhere,
            anywhere,
        ],
        [block(out.shape[1]) for out in outs] + [row, row],
        outs + [shape((1, D), f32)] * 2,
        [
            pltpu.VMEM(mats.shape, bf16),
            pltpu.VMEM(ffn.shape, bf16),
            pltpu.VMEM(down.shape, bf16),
            pltpu.SemaphoreType.DMA((3,)),
        ],
        vmem=62,
        flops=8 * rows * D * (D + 3 * inner // 2),
        traffic=50 << 20,
        name="mid",
    )
    return found


def mid_grads_kernel(
    hid_ref, y_ref, h2_ref, u_ref, dab_ref, dd_ref, dyw_ref, dgate_ref,
    down_ref, ffn_ref, mats_ref, hid_t, y_t, h2_t,
):
    step = pl.program_id(0)
    width = ffn_ref.shape[1]

    @pl.when(step == 0)
    def begin():
        hid_t[...] = hid_ref[...].T
        y_t[...] = y_ref[...].T
        h2_t[...] = h2_ref[...].T

    ffn_ref[...] = mm(h2_t[...], dab_ref[...]).astype(bf16)
    down_ref[...] = mm(u_ref[...].T, dd_ref[...]).astype(bf16)
    for index in range(2 * D // width):
        at = width * index

        @pl.when(step == index)
        def mats():
            if at < D:
                mats_ref[...] = mm(hid_t[...], dgate_ref[:, at : at + width]).astype(bf16)
            else:
                mats_ref[...] = mm(y_t[...], dyw_ref[:, at - D : at - D + width]).astype(bf16)


def mid_grads(hidden, first_own, y, h2, u, dab, dd, dyw, dgate):
    rows, inner = u.shape
    width = 2 * CH
    steps = 2 * inner // width
    shape = jax.ShapeDtypeStruct

    def fixed(array):
        return pl.BlockSpec(array.shape, lambda step: (0, 0))

    found, _ = call(
        mid_grads_kernel,
        steps,
        (hidden, y, h2, u, dab, dd, dyw, dgate),
        [
            pl.BlockSpec((rows, D), lambda step: (first_own, 0)),
            fixed(y),
            fixed(h2),
            pl.BlockSpec((rows, inner // steps), lambda step: (0, step)),
            pl.BlockSpec((rows, width), lambda step: (0, step)),
            fixed(dd),
            fixed(dyw),
            fixed(dgate),
        ],
        [
            pl.BlockSpec((inner // steps, D), lambda step: (step, 0)),
            pl.BlockSpec((D, width), lambda step: (0, step)),
            pl.BlockSpec((D, width), lambda step: (0, jnp.minimum(step, 2 * D // width - 1))),
        ],
        [shape((inner, D), bf16), shape((D, 2 * inner), bf16), shape((D, 2 * D), bf16)],
        [pltpu.VMEM((D, rows), bf16)] * 3,
        vmem=62,
        flops=2 * rows * D * (2 * D + 3 * inner),
        traffic=40 << 20,
        name="mid_grads",
    )
    return found


def front_grads_kernel(
    hid_ref, pre_ref, qpre_ref, dkv_ref, dkvpre_ref, dq_ref, dqpre_ref, dbp_ref, small_ref,
    hid_t, pre_t, qpre_t, out_ref,
):
    step = pl.program_id(0)
    width = EXTRA
    split = out_ref.shape[:-1]
    first_query = 2 * D // width
    column = jnp.where(
        step < first_query,
        D + step * width,
        jnp.where(step < 3 * D // width, (step - first_query) * width, 3 * D),
    )
    at_step = pl.ds(pl.multiple_of(column, width), width)

    def put(value):
        out_ref[:, :, :, :, at_step] = value.astype(bf16).reshape(split + (width,))
    own = dq_ref.shape[0]
    main = hid_t.shape[1]

    @pl.when(step == 0)
    def begin():
        hid_t[...] = hid_ref[...].T
        pre_t[...] = pre_ref[...].T
        qpre_t[...] = qpre_ref[...].T

    @pl.when((step >= first_query) & (step < 3 * D // width))
    def queries():
        at = pl.ds(pl.multiple_of((step - first_query) * width, width), width)
        put(mm(hid_t[:, main - own :], dq_ref[:, at]) + mm(qpre_t[...], dqpre_ref[:, at]))

    @pl.when(step < first_query)
    def others():
        put(mm(hid_t[...], dkv_ref[...]) + mm(pre_t[...], dkvpre_ref[...]))

    @pl.when(step == 3 * D // width)
    def rest():
        lane = lax.broadcasted_iota(jnp.int32, (D, SMALL), 1)
        gates = mm(hid_t[...], dbp_ref[...]).astype(bf16)
        first = jnp.where(lane < HEADS, gates, small_ref[...])
        put(jnp.concatenate([first, jnp.zeros((D, width - SMALL), bf16)], axis=1))


def front_grads(hidden, dkv, dq, dqpre, dbp, small, **riding):
    own = dq.shape[0]
    main = dbp.shape[0]
    width = EXTRA
    blocks = 3 * D // width

    def fixed(array):
        return pl.BlockSpec(array.shape, lambda step: (0, 0))

    def kv_block(step):
        return jnp.minimum(step, 2 * D // width - 1)

    places = lax.axis_size("wshard")
    _, carried = call(
        front_grads_kernel,
        blocks + 1,
        (hidden, hidden, hidden, dkv, dkv, dq, dqpre, dbp, small),
        [
            pl.BlockSpec((main, D), lambda step: (0, 0)),
            pl.BlockSpec((PRE, D), lambda step: (main // PRE, 0)),
            pl.BlockSpec((PRE, D), lambda step: ((main - own) // PRE - 1, 0)),
            pl.BlockSpec((main, width), lambda step: (0, kv_block(step))),
            pl.BlockSpec((PRE, width), lambda step: (main // PRE, kv_block(step))),
            fixed(dq),
            fixed(dqpre),
            fixed(dbp),
            fixed(small),
        ],
        [],
        [],
        [
            pltpu.VMEM((D, main), bf16),
            pltpu.VMEM((D, PRE), bf16),
            pltpu.VMEM((D, PRE), bf16),
            pltpu.VMEM((places, 2, 2, D // places // 4, 3 * D + EXTRA), bf16),
        ],
        vmem=62,
        flops=2 * D * D * (2 * main + own),
        traffic=25 << 20,
        name="end",
        **riding,
    )
    return carried


def on_device(
    tokens,
    slot_lengths,
    live_lengths,
    norm_gain,
    w_qkv,
    w_beta,
    w_outgate,
    conv_weight,
    ridge,
    head_gain,
    w_out,
    ffn_gain,
    w_gate,
    w_up,
    w_down,
    cotangent,
):
    row_count = tokens.shape[1]
    depth = (WINDOW + row_count - 1) // row_count
    halo_rows = depth * row_count
    main_rows = halo_rows + row_count
    shards = lax.axis_size("wshard")
    shard_rows = norm_gain.shape[0]
    tap_columns = TAPS * conv_weight.shape[1] // shard_rows
    ffn = w_gate.shape[1]

    own_tokens = tokens[0]
    small = jnp.concatenate(
        [
            w_beta,
            jnp.stack([norm_gain, ridge, head_gain, ffn_gain]).T,
            conv_weight.reshape(shard_rows, tap_columns),
        ],
        axis=1,
    )
    small = jnp.pad(small, ((0, 0), (0, EXTRA - small.shape[1])))
    out_mats = jnp.concatenate([w_outgate, w_out], axis=1)
    ffn_mats = jnp.concatenate([w_gate, w_up], axis=1)

    riders = [
        Gather(jnp.concatenate([w_qkv, small], axis=1)),
        WindowTokens(own_tokens, depth),
        Gather(ffn_mats, 0, 0),
    ]
    events = [(1, 0), (0, 0), (0, 1), (2, 0), (1, 1), (0, 2), (0, 3), (0, 4), (1, 2), (2, 1)]
    _, ((w_front,), (ext_tokens,), (ffn_in,)) = call(
        lambda: None, 1, (), [], [], [], riders=riders, table={0: events}, collective_id=0, name="begin"
    )
    w_front = whole_rows(w_front)
    small = w_front[:, 3 * D :].astype(f32)
    gain_in, all_ridge, gain_head, gain_ffn = (small[:, HEADS + index] for index in range(4))
    taps = small[:, HEADS + 4 : HEADS + 4 + tap_columns]
    taps = taps.reshape(shards, TAPS, -1).transpose(1, 0, 2).reshape(TAPS, 3 * D)

    rank = lax.axis_index("seq")
    first = rank * row_count - halo_rows
    lengths, live = slot_lengths[0], live_lengths[0]

    def positions(start, shape, dim):
        return start + lax.broadcasted_iota(jnp.int32, shape, dim)

    conv_at = positions(first, (main_rows, TAPS), 0)
    tap_at = lax.broadcasted_iota(jnp.int32, (main_rows, TAPS), 1)
    same = (slot_of(conv_at, lengths) == slot_of(conv_at - tap_at, lengths)).astype(f32)
    key_at = positions(first, (main_rows, 1), 0)
    query_at = positions(first + halo_rows, (1, row_count), 1)
    spacing = query_at - key_at
    mask = (
        (spacing >= 0)
        & (spacing < WINDOW)
        & (slot_of(key_at, lengths) == slot_of(query_at, lengths))
        & is_live(key_at, lengths, live)
    ).astype(bf16)
    own_at = positions(first + halo_rows, (row_count, 1), 0)
    valid_own = is_live(own_at, lengths, live).astype(f32)
    gain_row = gain_in[None, :]
    ridge_column = all_ridge[:, None]

    (hidden, kv_in, q_in, q_pre, queries, keys, values, beta), ((ffn_in,), (mats,), (all_down,)) = front(
        ext_tokens,
        same,
        gain_row,
        w_front,
        taps,
        row_count,
        riders=[Gather(None, 1, 2, ffn_in), Gather(out_mats, 0, 0), Gather(w_down, 0, 0)],
        table={0: [(0, 1), (1, 0), (2, 0)], 4: [(0, 2)], 99: [(1, 1), (2, 1), (0, 3)]},
        collective_id=1,
    )
    (mixed, image0, image1), ((ffn_in,), (mats,), (all_down,)) = attn_fwd(
        queries,
        keys,
        values,
        beta,
        mask,
        ridge_column,
        riders=[Gather(None, 3, 3, ffn_in), Gather(None, 1, 3, mats), Gather(None, 1, 3, all_down)],
        table={
            0: [(1, 1), (2, 1), (0, 3)],
            2: [(1, 2)],
            3: [(2, 2)],
            5: [(1, 3)],
            99: [(2, 3), (0, 4), (1, 4), (2, 4)],
        },
        collective_id=2,
    )
    mats, ffn_in, all_down = (whole_rows(part) for part in (mats, ffn_in, all_down))
    first_own = halo_rows // ROWS
    output, y, h2, u, d_ab, d_down_in, d_out_in, d_gate, d_mixed, d_xout, d_ghead, d_gffn = mid(
        own_tokens,
        mixed,
        hidden,
        first_own,
        cotangent[0],
        valid_own,
        gain_head[None, :],
        gain_ffn[None, :],
        mats,
        ffn_in,
        all_down,
    )
    grad_down, grad_ffn, grad_mats = mid_grads(
        hidden, halo_rows // row_count, y, h2, u, d_ab, d_down_in, d_out_in, d_gate
    )

    part_rows = shard_rows // 8
    (d_query, d_key, d_value, d_beta, d_ridge), ((sum_down,), (sum_ffn0,), (sum_mats,)) = attn_bwd(
        queries,
        keys,
        values,
        beta,
        mask,
        ridge_column,
        image0,
        image1,
        d_mixed,
        riders=[SumFar(grad_down), SumFar(grad_ffn, 0, part_rows), SumPlace(grad_mats)],
        table={
            0: [(2, 0), (0, 0), (1, 0)],
            1: [(2, 1), (0, 1)],
            2: [(1, 1)],
            4: [(0, 2)],
            7: [(1, 2)],
            99: [(0, 3), (1, 3), (2, 2), (2, 3), (0, 4), (1, 4)],
        },
        collective_id=3,
    )
    (
        (d_kv_in, d_q_in, d_q_pre, d_beta_pre, d_gain, d_taps),
        ((sum_down,), (sum_ffn0,), (sum_ffn1,), (total_mats,), (d_tokens,)),
    ) = back(
        ext_tokens,
        kv_in,
        same,
        q_in,
        q_pre,
        d_key,
        d_value,
        d_query,
        beta,
        d_beta,
        d_gate,
        d_xout,
        gain_row,
        w_front,
        mats,
        taps,
        riders=[
            SumNear(sum_down, stop=True),
            SumNear(sum_ffn0, stop=True),
            SumFar(grad_ffn, part_rows, part_rows),
            SumSpread(sum_mats),
            WindowGrads(row_count, D, depth),
        ],
        table={
            0: [(2, 0), (3, 0), (3, 1), (0, 0), (1, 0)],
            1: [(3, 2), (2, 1)],
            3: [(2, 2), (3, 3)],
            4: [(4, 0)],
            5: [(4, 1), (0, 1), (1, 1), (3, 4)],
            6: [(4, 2), (2, 3), (3, 5)],
            99: [(4, 3), (2, 4), (0, 2), (1, 2), (3, 6), (4, 4), (4, 5)],
        },
        collective_id=4,
    )
    d_small = jnp.concatenate(
        [
            jnp.zeros((D, HEADS), f32),
            d_gain.reshape(D, 1),
            d_ridge,
            d_ghead.reshape(D, 1),
            d_gffn.reshape(D, 1),
            d_taps.reshape(TAPS, shards, -1).transpose(1, 0, 2).reshape(D, tap_columns),
        ],
        axis=1,
    ).astype(bf16)
    d_small = jnp.pad(d_small, ((0, 0), (0, SMALL - d_small.shape[1])))
    rows = shard_rows // 4
    fars = [
        SumFar(None, 0, rows, D, D),
        SumFar(None, 0, rows, D, 2 * D),
        SumFar(None, 0, rows, D, 0),
        SumFar(None, 0, rows, EXTRA, 3 * D),
    ]
    riders = [SumNear(sum_ffn1)] + fars + [SumNear(after=far) for far in fars]
    riders += [SumNear(total=sum_down), SumNear(total=sum_ffn0)]
    late = [
        (3, 0), (4, 0), (9, 3), (10, 3), (2, 1), (1, 2), (3, 1), (4, 1), (2, 2), (1, 3), (1, 4), (5, 0),
        (3, 2), (4, 2), (0, 1), (2, 3), (2, 4), (6, 0), (5, 1), (3, 3), (4, 3), (3, 4), (4, 4),
        (7, 0), (8, 0), (0, 2), (6, 1), (5, 2), (6, 2), (5, 3), (7, 1), (8, 1), (6, 3), (0, 3),
        (7, 2), (8, 2), (7, 3), (8, 3), (5, 4), (6, 4), (0, 4), (7, 4), (8, 4),
        (9, 4), (10, 4),
    ]
    carried = front_grads(
        hidden,
        d_kv_in,
        d_q_in,
        d_q_pre,
        d_beta_pre,
        d_small,
        riders=riders,
        table={
            0: [(0, 0), (9, 0), (10, 0), (9, 1), (10, 1)],
            2: [(9, 2), (10, 2), (1, 0)],
            4: [(1, 1), (2, 0)],
            99: late,
        },
        collective_id=5,
    )
    (total_ffn1,), _, _, _, _, (total_k,), (total_v,), (total_q,), (total_small,) = carried[:9]
    (total_down,), (total_ffn0,) = carried[9:]
    def final(*sums):
        whole = jnp.concatenate([finish_sum(part) for part in sums], axis=2)
        return whole.reshape(-1, whole.shape[-1])

    total_down = final(total_down)
    total_ffn = final(total_ffn0, total_ffn1)
    total_middle = final(total_mats)
    total_front = jnp.concatenate([final(total_q), final(total_k), final(total_v)], axis=1)
    t_small = final(total_small).astype(f32)
    return (
        output[None],
        d_tokens[None],
        t_small[:, HEADS],
        total_front.astype(f32),
        t_small[:, :HEADS],
        total_middle[:, :D].astype(f32),
        t_small[:, HEADS + 4 : HEADS + 4 + tap_columns].reshape(TAPS, -1),
        t_small[:, HEADS + 1],
        t_small[:, HEADS + 2],
        total_middle[:, D:].astype(f32),
        t_small[:, HEADS + 3],
        total_ffn[:, :ffn].astype(f32),
        total_ffn[:, ffn:].astype(f32),
        total_down.astype(f32),
    )


def solution(mesh):
    return jax.shard_map(
        on_device,
        mesh=mesh,
        in_specs=(
            P("wshard", "seq", None),
            P("wshard", None),
            P("wshard", None),
            P("wshard"),
            P("wshard", None),
            P("wshard", None),
            P("wshard", None),
            P(None, "wshard"),
            P("wshard"),
            P("wshard"),
            P("wshard", None),
            P("wshard"),
            P("wshard", None),
            P("wshard", None),
            P("wshard", None),
            P("wshard", "seq", None),
        ),
        out_specs=(
            P("wshard", "seq", None),
            P("wshard", "seq", None),
            P("wshard"),
            P("wshard", None),
            P("wshard", None),
            P("wshard", None),
            P(None, "wshard"),
            P("wshard"),
            P("wshard"),
            P("wshard", None),
            P("wshard"),
            P("wshard", None),
            P("wshard", None),
            P("wshard", None),
        ),
        check_vma=False,
    )
```

```python
import functools
import jax
import jax.numpy as jnp
from jax import lax
from jax.experimental import pallas as pl
from jax.experimental.pallas import tpu as pltpu
from jax.sharding import PartitionSpec as P

D = 1024
HEADS = 8
HEAD_DIM = 128
TAPS = 4
WINDOW = 1024
PRE = 16
SMALL = 128
EXTRA = 512
MESH = pl.DeviceIdType.MESH
f32 = jnp.float32
bf16 = jnp.bfloat16
QB = 256
CH = 256
KEYS = 640
ROWS = 256


def slot_info(lengths, live, first):
    table = jnp.array(
        [
            [1, 0, 0, 0, 0, 0],
            [1, 1, 0, 0, 0, 0],
            [0, 0, 0, 1, 0, 0],
            [1, 0, 0, 0, 1, 0],
            [1, 1, 0, 0, 0, 1],
            [0, 0, 0, 0, 0, 0],
            [0, 0, 0, 0, 0, 0],
            [0, 0, 0, 0, 0, 0],
        ],
        jnp.int32,
    )
    found = jnp.sum(table * jnp.concatenate([lengths, live])[None, :], axis=1, keepdims=True)
    row = lax.broadcasted_iota(jnp.int32, (8, 128), 0)
    return found + jnp.where(row == 5, first, 0)


def slot_of(info, positions):
    found = (positions >= 0).astype(jnp.int32)
    for index in range(2):
        found = found + (positions >= info[index : index + 1, 0:1]).astype(jnp.int32)
    return found


def is_live(info, positions):
    found = (positions >= 0) & (positions < info[2:3, 0:1])
    for index in range(2):
        found = found | (
            (positions >= info[index : index + 1, 0:1])
            & (positions < info[index + 3 : index + 4, 0:1])
        )
    return found


def rows_from(info, start, count):
    return info[5:6, 0:1] + start + lax.broadcasted_iota(jnp.int32, (count, 1), 0)


def same_slots(info, start):
    at = rows_from(info, start, ROWS)
    own = slot_of(info, at)
    return [(own == slot_of(info, at - tap)).astype(f32) for tap in range(TAPS)]


def window_mask(info, mask_ref):
    keys, queries = mask_ref.shape
    at_query = (
        info[5:6, 0:1] + (keys - queries) + lax.broadcasted_iota(jnp.int32, (1, queries), 1)
    )
    query_slot = slot_of(info, at_query)
    for start in range(0, keys, ROWS):
        at = rows_from(info, start, ROWS)
        key_slot = jnp.where(is_live(info, at), slot_of(info, at), -1)
        spacing = at_query - at
        inside = (spacing >= 0) & (spacing < WINDOW) & (key_slot == query_slot)
        mask_ref[start : start + ROWS, :] = inside.astype(f32).astype(bf16)


def mm(left, right):
    return jnp.dot(left, right, preferred_element_type=f32)


def mm_t(left, right):
    return lax.dot_general(left, right, (((1,), (1,)), ((), ())), preferred_element_type=f32)


def conv_total(ext_ref, slot, same, taps):
    total = taps[0:1] * ext_ref[slot, 8 : 8 + ROWS, :]
    for tap in range(1, TAPS):
        total = total + taps[tap : tap + 1] * ext_ref[slot, 8 - tap : 8 - tap + ROWS, :] * same[tap]
    return total


def unit_scale(active):
    return lax.rsqrt(jnp.sum(active * active, axis=-1, keepdims=True) + 1e-06)


def in_heads(work, *arrays):
    width = arrays[0].shape[1]
    return jnp.concatenate(
        [
            work(*(array[:, at : at + HEAD_DIM] for array in arrays))
            for at in range(0, width, HEAD_DIM)
        ],
        axis=1,
    )


def row_norm(x, gain):
    return (x * lax.rsqrt(jnp.mean(x * x, axis=-1, keepdims=True) + 1e-06) * gain).astype(bf16)


def front_kernel(
    first_own,
    x_ref,
    info_ref,
    w_ref,
    hid_ref,
    kvin_ref,
    qin_ref,
    qpre_ref,
    q_ref,
    k_ref,
    v_ref,
    beta_ref,
    params_ref,
    taps_ref,
    ext_ref,
    tail_ref,
):
    step = pl.program_id(0)
    shards = lax.axis_size("wshard")

    @pl.when(step == 0)
    def unpack():
        small = w_ref[:, 3 * D : 3 * D + SMALL].astype(f32).T
        params_ref[...] = small[HEADS : HEADS + 8]
        wide = D // shards
        for place in range(shards):
            for third in range(3):
                row = HEADS + 4 + TAPS * third
                at = 3 * wide * place + wide * third
                taps_ref[:, at : at + wide] = small[
                    row : row + TAPS, wide * place : wide * (place + 1)
                ]

    gain = params_ref[0:1, :]
    main_rows = k_ref.shape[0]
    before_at = pl.ds(main_rows, PRE)
    rows_at = pl.ds(pl.multiple_of(jnp.maximum(step - 1, 0) * ROWS, ROWS), ROWS)
    own_at = pl.ds(pl.multiple_of(jnp.maximum(step - 1 - first_own, 0) * ROWS, ROWS), ROWS)
    kv_slots = 2 * D // CH

    @pl.when(step == 0)
    def before():
        hidden = row_norm(x_ref[before_at].astype(f32), gain)
        hid_ref[before_at] = hidden
        for slot in range(kv_slots):
            rows = mm(hidden, w_ref[:, D + CH * slot : D + CH * (slot + 1)]).astype(bf16)
            kvin_ref[before_at, CH * slot : CH * (slot + 1)] = rows
            ext_ref[slot, ROWS : ROWS + 8, :] = rows.astype(f32)[PRE - 8 :]

    def through(slot, hidden, same, column, in_ref, in_rows, at):
        ext_ref[slot, 0:8, :] = ext_ref[slot, ROWS : ROWS + 8, :]
        rows = mm(hidden, w_ref[:, column : column + CH]).astype(bf16)
        in_ref[in_rows, at : at + CH] = rows
        ext_ref[slot, 8 : 8 + ROWS, :] = rows.astype(f32)
        total = conv_total(ext_ref, slot, same, taps_ref[:, column : column + CH])
        return total * jax.nn.sigmoid(total)

    def unit(active):
        return in_heads(lambda part: part * unit_scale(part), active).astype(bf16)

    @pl.when(step > 0)
    def main():
        same = same_slots(info_ref[...], (step - 1) * ROWS)
        hidden = row_norm(x_ref[rows_at].astype(f32), gain)
        hid_ref[rows_at] = hidden
        for slot in range(kv_slots):
            at = CH * slot
            active = through(slot, hidden, same, D + at, kvin_ref, rows_at, at)
            if at < D:
                k_ref[rows_at, at : at + CH] = unit(active)
            else:
                v_ref[rows_at, at - D : at - D + CH] = active.astype(bf16)
        gates = jax.nn.sigmoid(mm(hidden, w_ref[:, 3 * D : 3 * D + SMALL])).astype(bf16)
        lane = lax.broadcasted_iota(jnp.int32, (ROWS, SMALL), 1)
        beta_ref[rows_at] = jnp.where(lane < HEADS, gates.astype(f32), 0.0)

        @pl.when(step == first_own + 1)
        def own_history():
            rows = mm(tail_ref[...], w_ref[:, :D]).astype(bf16)
            qpre_ref[...] = rows
            for slot in range(D // CH):
                ext_ref[kv_slots + slot, ROWS : ROWS + 8, :] = rows.astype(f32)[
                    PRE - 8 :, CH * slot : CH * (slot + 1)
                ]

        @pl.when(step > first_own)
        def own():
            for slot in range(D // CH):
                at = CH * slot
                active = through(kv_slots + slot, hidden, same, at, qin_ref, own_at, at)
                q_ref[own_at, at : at + CH] = unit(active)

        tail_ref[...] = hidden[ROWS - PRE :]


def front(ext_tokens, info, w_front, own_rows, **riding):
    ext_rows = ext_tokens.shape[0]
    main_rows = ext_rows - PRE
    blocks = main_rows // ROWS
    first_own = (main_rows - own_rows) // ROWS

    def fixed(array):
        return pl.BlockSpec(array.shape, lambda step: (0, 0), pipeline_mode=pl.Buffered(1))

    shape = jax.ShapeDtypeStruct
    outs = [
        shape((ext_rows, D), bf16),
        shape((ext_rows, 2 * D), bf16),
        shape((own_rows, D), bf16),
        shape((PRE, D), bf16),
        shape((own_rows, D), bf16),
        shape((main_rows, D), bf16),
        shape((main_rows, D), bf16),
        shape((main_rows, SMALL), f32),
        shape((8, D), f32),
        shape((TAPS, 3 * D), f32),
    ]
    return call(
        functools.partial(front_kernel, first_own),
        blocks + 1,
        (ext_tokens, info, w_front),
        [fixed(array) for array in (ext_tokens, info, w_front)],
        [fixed(array) for array in outs],
        outs,
        [
            pltpu.VMEM((3 * D // CH, 8 + ROWS, CH), f32),
            pltpu.VMEM((PRE, D), bf16),
        ],
        vmem=62,
        flops=4 * (main_rows * 2 + own_rows) * D * D,
        traffic=30 << 20,
        name="front",
        **riding,
    )


def back_kernel(
    blocks,
    first_own,
    x_ref,
    kvin_ref,
    kvprev_ref,
    info_ref,
    qin_ref,
    qprev_ref,
    qpre_ref,
    dk_ref,
    dv_ref,
    dq_ref,
    beta_ref,
    dbeta_ref,
    dgate_ref,
    dres_ref,
    params_ref,
    w_ref,
    wog_ref,
    taps_ref,
    dkvin_ref,
    dqin_ref,
    dqpre_ref,
    dbp_ref,
    dgain_ref,
    dtaps_ref,
    ext_ref,
    buf_ref,
    dh_ref,
    dxhalo_ref,
    dxown_ref,
):
    step = pl.program_id(0)
    block = blocks - 1 - step
    kv_slots = 2 * D // CH
    gain = params_ref[0:1, :]

    @pl.when(step == 0)
    def clear():
        dgain_ref[...] = jnp.zeros_like(dgain_ref)
        dtaps_ref[...] = jnp.zeros_like(dtaps_ref)
        buf_ref[:, :, ROWS : ROWS + 8, :] = jnp.zeros_like(buf_ref[:, :, ROWS : ROWS + 8, :])

    def norm_back(x, dh):
        scale = lax.rsqrt(jnp.mean(x * x, axis=-1, keepdims=True) + 1e-06)
        normal = x * scale
        dgain_ref[...] += jnp.sum(dh * normal, axis=0, keepdims=True)
        scaled = dh * gain
        return scale * (scaled - normal * jnp.mean(scaled * normal, axis=-1, keepdims=True))

    def shifted(slot, start, count):
        total = buf_ref[slot, 0, start + 1 : start + 1 + count, :]
        for tap in range(2, TAPS):
            total = total + buf_ref[slot, tap - 1, start + tap : start + tap + count, :]
        return total

    def through(slot, column, history, rows, grad, unit, same):
        ext_ref[slot, 0:8, :] = history
        ext_ref[slot, 8 : 8 + ROWS, :] = rows.astype(f32)
        taps = taps_ref[:, column : column + CH]
        total = conv_total(ext_ref, slot, same, taps)
        gate = jax.nn.sigmoid(total)
        active = total * gate
        if unit:

            def unit_back(part, part_grad):
                scale = unit_scale(part)
                normal = part * scale
                return scale * (
                    part_grad - normal * jnp.sum(part_grad * normal, axis=-1, keepdims=True)
                )

            grad = in_heads(unit_back, active, grad)
        grad = grad * (gate + active * (1.0 - gate))
        result = grad * taps[0:1]
        dtaps_ref[0:1, column : column + CH] += jnp.sum(
            grad * ext_ref[slot, 8 : 8 + ROWS, :], axis=0, keepdims=True
        )
        for tap in range(1, TAPS):
            held = grad * same[tap]
            dtaps_ref[tap : tap + 1, column : column + CH] += jnp.sum(
                held * ext_ref[slot, 8 - tap : 8 - tap + ROWS, :], axis=0, keepdims=True
            )
            buf_ref[slot, tap - 1, 0:ROWS, :] = held * taps[tap : tap + 1]
        result = (result + shifted(slot, 0, ROWS)).astype(bf16)
        for tap in range(1, TAPS):
            buf_ref[slot, tap - 1, ROWS : ROWS + 8, :] = buf_ref[slot, tap - 1, 0:8, :]
        return result

    def before_rows(slot):
        for tap in range(1, TAPS):
            buf_ref[slot, tap - 1, ROWS - PRE : ROWS, :] = jnp.zeros((PRE, CH), f32)
        return shifted(slot, ROWS - PRE, PRE).astype(bf16)

    @pl.when(step < blocks)
    def main():
        same = same_slots(info_ref[...], block * ROWS)
        beta = beta_ref[...]
        gates = (dbeta_ref[...] * beta * (1.0 - beta)).astype(bf16)
        dbp_ref[...] = gates
        dh = mm_t(gates, w_ref[:, 3 * D : 3 * D + SMALL])
        for slot in range(kv_slots):
            at = CH * slot
            grad = dk_ref[:, at : at + CH] if at < D else dv_ref[:, at - D : at - D + CH]
            history = kvprev_ref[PRE - 8 : PRE, at : at + CH].astype(f32)
            rows = kvin_ref[:, at : at + CH]
            rows = through(slot, D + at, history, rows, grad, at < D, same)
            dkvin_ref[:, at : at + CH] = rows
            dh = dh + mm_t(rows, w_ref[:, D + at : D + at + CH])
        dh_ref[...] = dh

        @pl.when(block >= first_own)
        def own():
            dh = mm_t(dgate_ref[...], wog_ref[...])
            for slot in range(D // CH):
                at = CH * slot
                history = jnp.where(
                    block == first_own,
                    qpre_ref[PRE - 8 :, at : at + CH].astype(f32),
                    qprev_ref[PRE - 8 :, at : at + CH].astype(f32),
                )
                rows = qin_ref[:, at : at + CH]
                rows = through(
                    kv_slots + slot, at, history, rows, dq_ref[:, at : at + CH], True, same
                )
                dqin_ref[:, at : at + CH] = rows
                dh = dh + mm_t(rows, w_ref[:, at : at + CH])
            at = pl.ds(pl.multiple_of((block - first_own) * ROWS, ROWS), ROWS)
            dxown_ref[at] = dres_ref[...] + norm_back(x_ref[...].astype(f32), dh_ref[...] + dh)

        @pl.when(block == first_own - 1)
        def own_history():
            dh = jnp.zeros((PRE, D), f32)
            for slot in range(D // CH):
                at = CH * slot
                rows = before_rows(kv_slots + slot)
                dqpre_ref[:, at : at + CH] = rows
                dh = dh + mm_t(rows, w_ref[:, at : at + CH])
            dh_ref[ROWS - PRE : ROWS, :] += dh

        @pl.when(block < first_own)
        def halo():
            at = pl.ds(pl.multiple_of(block * ROWS, ROWS), ROWS)
            dxhalo_ref[at] = norm_back(x_ref[...].astype(f32), dh_ref[...]).astype(bf16)

    @pl.when(step == blocks)
    def before():
        dh = jnp.zeros((PRE, D), f32)
        for slot in range(kv_slots):
            at = CH * slot
            rows = before_rows(slot)
            dkvin_ref[0:PRE, at : at + CH] = rows
            dh = dh + mm_t(rows, w_ref[:, D + at : D + at + CH])
        dxhalo_ref[first_own * ROWS : first_own * ROWS + PRE, :] = norm_back(x_ref[0:PRE].astype(f32), dh).astype(bf16)


def back(
    ext_tokens, kvin, info, qin, qpre, dk, dv, dq, beta, dbeta, dgate, dres, params, w_front, mats, taps, **riding
):
    ext_rows = ext_tokens.shape[0]
    main_rows = ext_rows - PRE
    own_rows = dq.shape[0]
    blocks = main_rows // ROWS
    first_own = (main_rows - own_rows) // ROWS
    small_blocks = ROWS // PRE

    def ext_block(step):
        return (jnp.where(step == blocks, blocks, blocks - 1 - step), 0)

    def main_block(step):
        return (jnp.maximum(blocks - 1 - step, 0), 0)

    def prev_block(step):
        block = blocks - 1 - step
        return (jnp.where(block <= 0, blocks * small_blocks, small_blocks * block - 1), 0)

    def own_block(step):
        return (jnp.maximum(blocks - 1 - step - first_own, 0), 0)

    def own_prev_block(step):
        return (jnp.maximum(small_blocks * (blocks - 1 - step - first_own) - 1, 0), 0)

    def fixed(array):
        return pl.BlockSpec(array.shape, lambda step: (0, 0), pipeline_mode=pl.Buffered(1))

    shape = jax.ShapeDtypeStruct
    return call(
        functools.partial(back_kernel, blocks, first_own),
        blocks + 1,
        (
            ext_tokens,
            kvin,
            kvin,
            info,
            qin,
            qin,
            qpre,
            dk,
            dv,
            dq,
            beta,
            dbeta,
            dgate,
            dres,
            params,
            w_front,
            mats,
            taps,
        ),
        [
            pl.BlockSpec((ROWS, D), ext_block),
            pl.BlockSpec((ROWS, 2 * D), ext_block),
            pl.BlockSpec((PRE, 2 * D), prev_block),
            fixed(info),
            pl.BlockSpec((ROWS, D), own_block),
            pl.BlockSpec((PRE, D), own_prev_block),
            fixed(qpre),
            pl.BlockSpec((ROWS, D), main_block),
            pl.BlockSpec((ROWS, D), main_block),
            pl.BlockSpec((ROWS, D), own_block),
            pl.BlockSpec((ROWS, SMALL), main_block),
            pl.BlockSpec((ROWS, SMALL), main_block),
            pl.BlockSpec((ROWS, D), own_block),
            pl.BlockSpec((ROWS, D), own_block),
            fixed(params),
            fixed(w_front),
            pl.BlockSpec((D, D), lambda step: (0, 0), pipeline_mode=pl.Buffered(1)),
            fixed(taps),
        ],
        [
            pl.BlockSpec((ROWS, 2 * D), ext_block),
            pl.BlockSpec((ROWS, D), own_block),
            pl.BlockSpec((PRE, D), lambda step: (0, 0)),
            pl.BlockSpec((ROWS, SMALL), main_block),
            pl.BlockSpec((1, D), lambda step: (0, 0)),
            pl.BlockSpec((TAPS, 3 * D), lambda step: (0, 0)),
        ],
        [
            shape((ext_rows, 2 * D), bf16),
            shape((own_rows, D), bf16),
            shape((PRE, D), bf16),
            shape((main_rows, SMALL), bf16),
            shape((1, D), f32),
            shape((TAPS, 3 * D), f32),
        ],
        [
            pltpu.VMEM((3 * D // CH, 8 + ROWS, CH), f32),
            pltpu.VMEM((3 * D // CH, TAPS - 1, ROWS + 8, CH), f32),
            pltpu.VMEM((ROWS, D), f32),
            pltpu.VMEM((main_rows - own_rows + PRE, D), bf16),
            pltpu.VMEM((own_rows, D), f32),
        ],
        vmem=62,
        flops=6 * (main_rows * 2 + own_rows) * D * D,
        traffic=40 << 20,
        name="back",
        **riding,
    )


def total(v):
    return jnp.sum(v,axis=0,keepdims=True)

def head_column(beta_ref, h):
    beta=beta_ref[...]
    lane=lax.broadcasted_iota(jnp.int32,beta.shape,1)
    return jnp.sum(jnp.where(lane==h,beta,0.0),axis=1,keepdims=True)

def attn_fwd_kernel(q_ref,k_ref,v_ref,beta_ref,info_ref,small_ref,o_ref,a0_ref,a1_ref,kt_ref,vt_ref,w_ref,mask_ref):
    h=pl.program_id(0)
    rows=q_ref.shape[0]
    span=WINDOW+QB
    kt_ref[...]=k_ref[...].T
    vt_ref[...]=v_ref[...].T
    column=head_column(beta_ref,h)
    ridge=small_ref[:,HEADS+1:HEADS+2].astype(f32)

    @pl.when(h==0)
    def fill():
        window_mask(info_ref[...],mask_ref)

    blocks=range(rows//QB)
    chunks=range(span//KEYS)
    for b in blocks:
        for c in chunks:
            at=slice(QB*b+KEYS*c,QB*b+KEYS*(c+1))
            w_ref[b,KEYS*c:KEYS*(c+1),:]=mask_ref[at,QB*b:QB*(b+1)].astype(f32)*column[at]
    def apply(b,vector,right):
        low=vector.astype(bf16)
        out=jnp.zeros((HEAD_DIM,QB),f32)
        for c in chunks:
            at=slice(QB*b+KEYS*c,QB*b+KEYS*(c+1))
            s=mm(k_ref[at,:],low)
            s=(w_ref[b,KEYS*c:KEYS*(c+1),:]*s).astype(bf16)
            out=out+mm(right[:,at],s)
        return out
    q=[q_ref[QB*b:QB*(b+1),:].astype(f32).T for b in blocks]
    a0=[apply(b,q[b],kt_ref)+ridge*q[b] for b in blocks]
    for b in blocks: a0_ref[:,QB*b:QB*(b+1)]=a0[b]
    x1=[];p1=[];r1=[];e1=[]
    for b in blocks:
        e0=total(q[b]*q[b])
        s0=e0/total(q[b]*a0[b])
        x1.append(s0*q[b])
        r=q[b]-s0*a0[b]
        e=total(r*r)
        r1.append(r);e1.append(e)
        p1.append(r+e/e0*q[b])
    a1=[apply(b,p1[b],kt_ref)+ridge*p1[b] for b in blocks]
    for b in blocks: a1_ref[:,QB*b:QB*(b+1)]=a1[b]
    x2=[x1[b]+e1[b]/total(p1[b]*a1[b])*p1[b] for b in blocks]
    for b in blocks:
        o_ref[QB*b:QB*(b+1),:]=apply(b,x2[b],vt_ref).T

def attn_fwd(q,k,v,beta,info,w_front,**riding):
    rows=q.shape[0]; keys=k.shape[0]
    head=lambda n: pl.BlockSpec((n,HEAD_DIM),lambda h:(0,h))
    heads_t=pl.BlockSpec((HEAD_DIM,rows),lambda h:(h,0))
    fixed=lambda a: pl.BlockSpec(a.shape,lambda h:(0,0))
    small=pl.BlockSpec((HEAD_DIM,SMALL),lambda h:(h,3*D//SMALL))
    flops=6*2*rows*(WINDOW+QB)*D
    return call(
        attn_fwd_kernel,
        HEADS,
        (q, k, v, beta, info, w_front),
        [head(rows), head(keys), head(keys), fixed(beta), fixed(info), small],
        [head(rows), heads_t, heads_t],
        [jax.ShapeDtypeStruct((rows, D), f32)] + [jax.ShapeDtypeStruct((D, rows), f32)] * 2,
        [pltpu.VMEM((HEAD_DIM, keys), bf16)] * 2 + [pltpu.VMEM((rows // QB, WINDOW + QB, QB), f32), pltpu.VMEM((keys, rows), bf16)],
        vmem=62,
        flops=2 * flops,
        traffic=20 << 20,
        name="attn_fwd",
        **riding,
    )


def attn_bwd_kernel(q_ref,k_ref,v_ref,beta_ref,info_ref,small_ref,a0_ref,a1_ref,do_ref,dq_ref,dk_ref,dv_ref,dbeta_ref,dridge_ref,kt_ref,w_ref,acc_ref,mask_ref):
    h=pl.program_id(0)
    rows=q_ref.shape[0]
    span=WINDOW+QB
    kt_ref[...]=k_ref[...].T
    column=head_column(beta_ref,h)
    ridge=small_ref[:,HEADS+1:HEADS+2].astype(f32)

    @pl.when(h==0)
    def fill():
        window_mask(info_ref[...],mask_ref)

    blocks=range(rows//QB)
    chunks=range(span//KEYS)
    dk_ref[...]=jnp.zeros_like(dk_ref)
    dv_ref[...]=jnp.zeros_like(dv_ref)
    acc_ref[...]=jnp.zeros_like(acc_ref)
    for b in blocks:
        for c in chunks:
            at=slice(QB*b+KEYS*c,QB*b+KEYS*(c+1))
            w_ref[b,KEYS*c:KEYS*(c+1),:]=mask_ref[at,QB*b:QB*(b+1)].astype(f32)*column[at]
    def apply_back(b,vector,grad,grad_rows,right_ref,dright_ref):
        low=vector.astype(bf16)
        low_rows=vector.T.astype(bf16)
        out=jnp.zeros((HEAD_DIM,QB),f32)
        for c in chunks:
            at=slice(QB*b+KEYS*c,QB*b+KEYS*(c+1))
            w=w_ref[b,KEYS*c:KEYS*(c+1),:]
            s=mm(k_ref[at,:],low)
            dw=mm(right_ref[at,:],grad)
            masked=dw*mask_ref[at,QB*b:QB*(b+1)].astype(f32)
            for_beta=masked*s
            part=for_beta[:,:128]
            for lane in range(128,QB,128):
                part=part+for_beta[:,lane:lane+128]
            acc_ref[at,:]+=part
            ws=(w*s).astype(bf16)
            ds=(w*dw).astype(bf16)
            out=out+mm(kt_ref[:,at],ds)
            dright_ref[at,:]+=mm(ws,grad_rows)
            dk_ref[at,:]+=mm(ds,low_rows)
        return out
    st=[]
    for b in blocks:
        cols=slice(QB*b,QB*(b+1))
        q=q_ref[cols,:].astype(f32).T
        a0=a0_ref[:,cols]; a1=a1_ref[:,cols]
        e0=total(q*q); d0=total(q*a0); s0=e0/d0
        x1=s0*q; r1=q-s0*a0; e1=total(r1*r1); b0=e1/e0
        p1=r1+b0*q; d1=total(p1*a1); s1=e1/d1
        x2=x1+s1*p1
        st.append((q,a0,a1,e0,d0,s0,r1,e1,b0,p1,d1,s1,x2))
    dx2=[]
    for b in blocks:
        do=do_ref[QB*b:QB*(b+1),:]
        dx2.append(apply_back(b,st[b][12],do.astype(f32).T.astype(bf16),do,v_ref,dv_ref))
    da1=[];dp1=[];de1=[];dr=0
    for b in blocks:
        q,a0,a1,e0,d0,s0,r1,e1,b0,p1,d1,s1,x2=st[b]
        ds1=total(dx2[b]*p1)
        de1.append(ds1/d1)
        dd1=-ds1*s1/d1
        g=dd1*p1
        da1.append(g)
        dp1.append(s1*dx2[b]+dd1*a1+ridge*g)
        dr=dr+jnp.sum(g*p1,axis=1,keepdims=True)
    for b in blocks:
        g=da1[b]
        dp1[b]=dp1[b]+apply_back(b,st[b][9],g.astype(bf16),g.T.astype(bf16),k_ref,dk_ref)
    da0=[];dq=[]
    for b in blocks:
        q,a0,a1,e0,d0,s0,r1,e1,b0,p1,d1,s1,x2=st[b]
        db0=total(dp1[b]*q)
        dpq=b0*dp1[b]
        de=de1[b]+db0/e0
        de0=-db0*b0/e0
        dr1=dp1[b]+2.0*de*r1
        ds0=total(dx2[b]*q)-total(dr1*a0)
        dpq=dpq+s0*dx2[b]
        g=-s0*dr1
        de0=de0+ds0/d0
        dd0=-ds0*s0/d0
        dpq=dpq+dd0*a0
        g=g+dd0*q
        dpq=dpq+dr1+2.0*de0*q+ridge*g
        da0.append(g);dq.append(dpq)
        dr=dr+jnp.sum(g*q,axis=1,keepdims=True)
    for b in blocks:
        g=da0[b]
        t=dq[b]+apply_back(b,st[b][0],g.astype(bf16),g.T.astype(bf16),k_ref,dk_ref)
        dq_ref[QB*b:QB*(b+1),:]=t.T
    dridge_ref[...]=dr
    found=jnp.sum(acc_ref[...],axis=1,keepdims=True)
    lane=lax.broadcasted_iota(jnp.int32,dbeta_ref.shape,1)
    @pl.when(h==0)
    def _():
        dbeta_ref[...]=jnp.zeros_like(dbeta_ref)
    dbeta_ref[...]=jnp.where(lane==h,found,dbeta_ref[...])

def attn_bwd(q,k,v,beta,info,w_front,a0,a1,do,**riding):
    rows=q.shape[0]; keys=k.shape[0]
    head=lambda n: pl.BlockSpec((n,HEAD_DIM),lambda h:(0,h))
    heads_t=pl.BlockSpec((HEAD_DIM,rows),lambda h:(h,0))
    fixed=lambda a: pl.BlockSpec(a.shape,lambda h:(0,0))
    rd=pl.BlockSpec((HEAD_DIM,1),lambda h:(h,0))
    small=pl.BlockSpec((HEAD_DIM,SMALL),lambda h:(h,3*D//SMALL))
    flops=15*2*rows*(WINDOW+QB)*D
    return call(
        attn_bwd_kernel,
        HEADS,
        (q, k, v, beta, info, w_front, a0, a1, do),
        [head(rows), head(keys), head(keys), fixed(beta), fixed(info), small, heads_t, heads_t, head(rows)],
        [head(rows), head(keys), head(keys), fixed(beta), rd],
        [
            jax.ShapeDtypeStruct((rows, D), f32),
            jax.ShapeDtypeStruct((keys, D), f32),
            jax.ShapeDtypeStruct((keys, D), f32),
            jax.ShapeDtypeStruct(beta.shape, f32),
            jax.ShapeDtypeStruct((D, 1), f32),
        ],
        [
            pltpu.VMEM((HEAD_DIM, keys), bf16),
            pltpu.VMEM((rows // QB, WINDOW + QB, QB), f32),
            pltpu.VMEM((keys, 128), f32),
            pltpu.VMEM((keys, rows), bf16),
        ],
        vmem=62,
        flops=2 * flops,
        traffic=30 << 20,
        name="attn_bwd",
        **riding,
    )


class Here:
    def __init__(self):
        self.rank = lax.axis_index("seq")
        self.ranks = lax.axis_size("seq")
        self.place = lax.axis_index("wshard")
        self.shards = lax.axis_size("wshard")
        self.core = self.rank % 2
        self.x = (self.rank // 2) % 2
        self.y = (self.rank // 4) % 2
        self.core_next = self.rank + 1 - 2 * self.core
        self.x_next = self.rank + 2 - 4 * self.x
        self.y_next = self.rank + 4 - 8 * self.y

    def other(self, step):
        return (self.place + step) % self.shards

    def along(self, step):
        return (self.rank + step + self.ranks) % self.ranks

    def meet(self, reach):
        barrier = pltpu.get_barrier_semaphore()
        near = [self.core_next, self.x_next, self.y_next]
        for step in range(1, reach + 1):
            near += [self.along(step), self.along(-step)]
        for device in near:
            pl.semaphore_signal(barrier, inc=1, device_id={"seq": device}, device_id_type=MESH)
        for step in range(1, self.shards):
            pl.semaphore_signal(
                barrier, inc=1, device_id={"wshard": self.other(step)}, device_id_type=MESH
            )
        pl.semaphore_wait(barrier, len(near) + self.shards - 1)


def span(start, size):
    return pl.ds(pl.multiple_of(start, 128), size)


class Rider:
    reach = 0
    first, last = 0, 0
    inside = 0
    inputs, outputs, scratch, aliases = (), (), (), ()

    def bind(self, here, inputs, outputs, scratch):
        self.here = here
        self.inputs_, self.outputs_ = inputs, outputs
        self.send_sems, self.recv_sems, self.local_sems = scratch[:3]
        self.held = scratch[3:]

    def semaphores(self):
        return [
            pltpu.SemaphoreType.DMA((self.remote_count,)),
            pltpu.SemaphoreType.DMA((self.remote_count,)),
            pltpu.SemaphoreType.DMA((self.local_count,)),
        ]

    def send(self, index, source, target, **device):
        return pltpu.make_async_remote_copy(
            src_ref=source,
            dst_ref=target,
            send_sem=self.send_sems.at[index],
            recv_sem=self.recv_sems.at[index],
            device_id=device,
            device_id_type=MESH,
        )

    def keep(self, index, source, target):
        return pltpu.make_async_copy(source, target, self.local_sems.at[index])

    def remote(self, phase):
        return []

    def local(self, phase):
        return []

    def work(self, phase):
        pass

    def run(self, phase):
        if phase > self.first:
            for copy in self.remote(phase - 1):
                copy.wait_recv()
            for copy in self.local(phase - 1):
                copy.wait()
        if phase <= self.last:
            self.work(phase)
            for copy in self.remote(phase) + self.local(phase):
                copy.start()

    def finish(self):
        for phase in range(self.first, self.last + 1):
            for copy in self.remote(phase):
                copy.wait_send()


class Gather(Rider):
    remote_count, local_count = 18, 2

    def __init__(self, shard, first=0, last=3, begun=None):
        self.first, self.last = first, last
        if begun is None:
            split = shard.reshape(2, 2, shard.shape[0] // 4, shard.shape[1])
            places = lax.axis_size("wshard")
            self.inputs = (split,)
            self.outputs = (jax.ShapeDtypeStruct((places,) + split.shape, shard.dtype),)
            self.scratch = (pltpu.VMEM(split.shape, shard.dtype),)
        else:
            self.inputs = (begun,)
            self.outputs = (jax.ShapeDtypeStruct(begun.shape, begun.dtype),)
            self.aliases = ((0, 0),)

    def work(self, phase):
        if phase == 0:
            copy = self.keep(1, self.inputs_[0], self.held[0])
            copy.start()
            copy.wait()

    def local(self, phase):
        if phase:
            return []
        return [self.keep(0, self.held[0], self.outputs_[0].at[self.here.place])]

    def remote(self, phase):
        here, (target,) = self.here, self.outputs_
        half = target.shape[-1] // 2
        quarter = half // 2
        mine = span(here.core * half, half)
        one = span(here.core * half, quarter)
        two = span(here.core * half + quarter, quarter)
        y, x = here.y, here.x
        if phase == 0:
            return [
                self.send(
                    step - 1,
                    self.inputs_[0].at[y, x, :, mine],
                    target.at[here.place, y, x, :, mine],
                    wshard=here.other(step),
                )
                for step in range(1, here.shards)
            ]
        found = []
        for step in range(1, here.shards):
            at = target.at[here.other(step)]
            if phase == 1:
                found.append((at.at[y, x, :, one], here.x_next))
                found.append((at.at[y, x, :, two], here.y_next))
            elif phase == 2:
                found.append((at.at[y, :, :, one], here.y_next))
                found.append((at.at[:, x, :, two], here.x_next))
            else:
                found.append((at.at[:, :, :, mine], here.core_next))
        start = {1: 3, 2: 9, 3: 15}[phase]
        return [
            self.send(start + index, ref, ref, seq=near) for index, (ref, near) in enumerate(found)
        ]


class WindowTokens(Rider):
    last = 1
    remote_count, local_count = 0, 2

    def __init__(self, tokens, depth):
        self.depth = depth
        self.reach = depth + 1
        self.remote_count = depth + 1
        self.rows = tokens.shape[0]
        self.inputs = (tokens,)
        rows = self.rows * (depth + 1) + PRE
        self.outputs = (jax.ShapeDtypeStruct((rows, tokens.shape[1]), tokens.dtype),)
        self.scratch = (pltpu.VMEM(tokens.shape, tokens.dtype),)

    def work(self, phase):
        if phase == 0:
            copy = self.keep(1, self.inputs_[0], self.held[0])
            copy.start()
            copy.wait()

    def local(self, phase):
        rows = pl.ds(self.depth * self.rows, self.rows)
        return [self.keep(0, self.held[0], self.outputs_[0].at[rows])] if phase == 0 else []

    def remote(self, phase):
        here, rows, depth = self.here, self.rows, self.depth
        (own,), (ext,) = self.inputs_, self.outputs_
        if phase == 1:
            start = pl.multiple_of((1 - here.core) * depth * rows + here.core * (depth - 2) * rows, 16)
            ref = ext.at[pl.ds((depth - 1) * rows, rows)]
            return [self.send(0, ext.at[pl.ds(start, rows)], ref, seq=here.core_next)]
        found = [
            self.send(
                hop - 1, own, ext.at[pl.ds((depth - hop) * rows, rows)], seq=here.along(hop)
            )
            for hop in range(2, depth + 1)
        ]
        found.append(
            self.send(
                depth,
                own.at[pl.ds(rows - PRE, PRE)],
                ext.at[pl.ds((depth + 1) * rows, PRE)],
                seq=here.along(depth + 1),
            )
        )
        return found


class WindowGrads(Rider):
    inside = 2
    last = 4
    remote_count, local_count = 4, 1

    def __init__(self, rows, columns, depth):
        assert depth == 2
        self.rows = rows
        self.reach = depth + 1
        self.outputs = (jax.ShapeDtypeStruct((rows, columns), bf16),)
        self.scratch = (
            pltpu.VMEM((rows, columns), bf16),
            pltpu.VMEM((rows, columns), bf16),
            pltpu.VMEM((PRE, columns), bf16),
        )

    def remote(self, phase):
        here, rows = self.here, self.rows
        grads, _ = self.inputs_
        given, near, far = self.held
        if phase == 0:
            return [self.send(0, grads.at[pl.ds(rows, rows)], given, seq=here.core_next)]
        if phase == 1 or phase == 2:
            half = pl.ds((2 - phase) * (rows // 2), rows // 2)
            return [self.send(phase, grads.at[half], near.at[half], seq=here.along(-2))]
        if phase == 3:
            return [self.send(3, grads.at[pl.ds(2 * rows, PRE)], far, seq=here.along(-3))]
        return []

    def run(self, phase):
        grads, own = self.inputs_
        given, near, far = self.held
        half = self.rows // 2
        chunk = 2 * PRE
        if phase == 1:
            self.remote(0)[0].wait_recv()
        if phase == 1 or phase == 2:

            @pl.when(self.here.core == 1)
            def join():
                def add(index, carry):
                    start = (2 - phase) * half + index * chunk
                    at = pl.ds(pl.multiple_of(start, chunk), chunk)
                    add_into(grads, at, given[at])
                    return carry

                lax.fori_loop(0, half // chunk, add, 0)

        if phase == 4:
            for earlier in (1, 2, 3):
                self.remote(earlier)[0].wait_recv()
            own[self.rows - PRE :, :] += far[...].astype(f32)
            first_core = (self.here.core == 0).astype(f32)

            def add_up(index, carry):
                at = pl.ds(pl.multiple_of(index * chunk, chunk), chunk)
                value = own[at] + near[at].astype(f32) + first_core * given[at].astype(f32)
                given[at] = value.astype(bf16)
                return carry

            lax.fori_loop(0, self.rows // chunk, add_up, 0)
            self.keep(0, given, self.outputs_[0]).start()
        elif phase == 5:
            self.keep(0, given, self.outputs_[0]).wait()
        else:
            self.remote(phase)[0].start()


def add_into(target, at, value):
    target[at] = (target[at].astype(f32) + value.astype(f32)).astype(bf16)


class SumFar(Rider):
    last = 3
    remote_count, local_count = 5, 2

    def __init__(self, grad=None, start=0, size=None, columns=None, offset=0):
        places = lax.axis_size("wshard")
        self.inside = int(grad is None)
        self.offset = offset
        if not self.inside:
            columns = grad.shape[-1]
            grad = grad.reshape(places, 2, 2, grad.shape[0] // places // 4, columns)
            size = grad.shape[3] if size is None else size
            self.inputs = (grad,)
        self.rows = pl.ds(start, size)
        half = columns // 2
        quarter = half // 2
        self.outputs = (jax.ShapeDtypeStruct((places, size, half), bf16),)
        self.scratch = (
            pltpu.VMEM((places, 2, 2, size, half), bf16),
            pltpu.VMEM((places, 2, 2, size, half), bf16),
            pltpu.VMEM((places, 2, size, quarter), bf16),
            pltpu.VMEM((places, 2, size, quarter), bf16),
            pltpu.VMEM((places, size, quarter), bf16),
            pltpu.VMEM((places, size, quarter), bf16),
        )
        self.half = half

    def local(self, phase):
        here, held = self.here, self.held[0]
        if phase == 0:
            mine = span(self.offset + here.core * self.half, self.half)
            return [self.keep(0, self.inputs_[0].at[:, :, :, self.rows, mine], held)]
        if phase == 3:
            return [self.keep(1, held.at[:, here.y, here.x], self.outputs_[0])]
        return []

    def remote(self, phase):
        here = self.here
        y, x = here.y, here.x
        held, core_in, far_a, far_b, next_a, next_b = self.held
        one, two = pl.ds(0, self.half // 2), pl.ds(self.half // 2, self.half // 2)
        if phase == 0:
            yours = span(self.offset + (1 - here.core) * self.half, self.half)
            ref = self.inputs_[0].at[:, :, :, self.rows, yours]
            return [self.send(0, ref, core_in, seq=here.core_next)]
        if phase == 1:
            return [
                self.send(1, held.at[:, :, 1 - x, :, one], far_a, seq=here.x_next),
                self.send(2, held.at[:, 1 - y, :, :, two], far_b, seq=here.y_next),
            ]
        if phase == 2:
            return [
                self.send(3, held.at[:, 1 - y, x, :, one], next_a, seq=here.y_next),
                self.send(4, held.at[:, y, 1 - x, :, two], next_b, seq=here.x_next),
            ]
        return []

    def work(self, phase):
        y, x = self.here.y, self.here.x
        held, core_in, far_a, far_b, next_a, next_b = self.held
        places = held.shape[0]
        one, two = slice(0, self.half // 2), slice(self.half // 2, self.half)
        every = slice(None)
        if phase == 1:

            def add(index, carry):
                at = (index // 4, (index // 2) % 2, index % 2)
                add_into(held, at, core_in[at])
                return carry

            lax.fori_loop(0, 4 * places, add, 0)
        elif phase == 2:

            def add(index, carry):
                place, side = index // 2, index % 2
                add_into(held, (place, side, x, every, one), far_a[place, side])
                add_into(held, (place, y, side, every, two), far_b[place, side])
                return carry

            lax.fori_loop(0, 2 * places, add, 0)
        elif phase == 3:

            def add(place, carry):
                add_into(held, (place, y, x, every, one), next_a[place])
                add_into(held, (place, y, x, every, two), next_b[place])
                return carry

            lax.fori_loop(0, places, add, 0)


class SumNear(Rider):
    last = 3
    local_count = 2

    def __init__(self, sums=None, after=None, stop=False, total=None):
        self.after, self.stop, self.resume = after, stop, total is not None
        if self.resume:
            (size, half), places = total.shape, lax.axis_size("wshard")
            self.inputs = (total,)
        else:
            places, size, half = (sums if after is None else after.outputs[0]).shape
            self.inputs = (sums,) if after is None else ()
        self.remote_count = places - 1 + 5
        self.half = half
        self.outputs = (jax.ShapeDtypeStruct((2, 2, size, 2 * half), bf16),)
        if stop:
            self.last = 1
            self.outputs = (jax.ShapeDtypeStruct((size, half), bf16),)
        arrived = (1, 16, 128) if self.resume else (places, size, half)
        self.scratch = (pltpu.VMEM(arrived, bf16), pltpu.VMEM((size, half), bf16))

    def bind(self, here, inputs, outputs, scratch):
        super().bind(here, inputs, outputs, scratch)
        if self.after is not None:
            self.inputs_ = self.after.outputs_

    def local(self, phase):
        here = self.here
        arrived, total = self.held
        if phase == 0 and self.resume:
            return [self.keep(0, self.inputs_[0], total)]
        if phase == 0:
            return [self.keep(0, self.inputs_[0].at[here.place], arrived.at[0])]
        if phase == 1 and self.stop:
            return [self.keep(1, total, self.outputs_[0])]
        if phase == 1:
            mine = span(here.core * self.half, self.half)
            return [self.keep(1, total, self.outputs_[0].at[here.y, here.x, :, mine])]
        return []

    def remote(self, phase):
        here = self.here
        y, x = here.y, here.x
        arrived, total = self.held
        (out,) = self.outputs_
        quarter = self.half // 2
        others = here.shards - 1
        if (phase == 0 and self.resume) or (phase == 1 and self.stop):
            return []
        if phase == 0:
            return [
                self.send(
                    step - 1,
                    self.inputs_[0].at[here.other(step)],
                    arrived.at[step],
                    wshard=here.other(step),
                )
                for step in range(1, here.shards)
            ]
        one = span(here.core * self.half, quarter)
        two = span(here.core * self.half + quarter, quarter)
        if phase == 1:
            held_one, held_two = total.at[:, pl.ds(0, quarter)], total.at[:, pl.ds(quarter, quarter)]
            return [
                self.send(others, held_one, out.at[y, x, :, one], seq=here.y_next),
                self.send(others + 1, held_two, out.at[y, x, :, two], seq=here.x_next),
            ]
        if phase == 2:
            both_one, both_two = out.at[:, x, :, one], out.at[y, :, :, two]
            return [
                self.send(others + 2, both_one, both_one, seq=here.x_next),
                self.send(others + 3, both_two, both_two, seq=here.y_next),
            ]
        ref = out.at[:, :, :, span(here.core * self.half, self.half)]
        return [self.send(others + 4, ref, ref, seq=here.core_next)]

    def work(self, phase):
        if phase == 1 and not self.resume:
            arrived, total = self.held
            value = arrived[0].astype(f32)
            for step in range(1, arrived.shape[0]):
                value = value + arrived[step].astype(f32)
            total[...] = value.astype(bf16)


class SumPlace(Rider):
    last = 2
    local_count = 2

    def __init__(self, grad):
        places = lax.axis_size("wshard")
        size, columns = grad.shape[0] // places // 4, grad.shape[1]
        self.half = columns // 2
        self.remote_count = places
        self.inputs = (grad.reshape(places, 2, 2, size, columns),)
        part = (2, 2, size, self.half)
        self.outputs = (jax.ShapeDtypeStruct(part, bf16),)
        self.scratch = (
            pltpu.VMEM((places,) + part, bf16),
            pltpu.VMEM((places,) + part, bf16),
            pltpu.VMEM((places - 1,) + part, bf16),
        )

    def local(self, phase):
        held, core_in, _ = self.held
        if phase == 0:
            mine = span(self.here.core * self.half, self.half)
            return [self.keep(0, self.inputs_[0].at[:, :, :, :, mine], held)]
        if phase == 2:
            return [self.keep(1, core_in.at[0], self.outputs_[0])]
        return []

    def remote(self, phase):
        here = self.here
        held, core_in, arrived = self.held
        if phase == 0:
            yours = span((1 - here.core) * self.half, self.half)
            return [self.send(0, self.inputs_[0].at[:, :, :, :, yours], core_in, seq=here.core_next)]
        if phase == 1:
            return [
                self.send(
                    step,
                    held.at[here.other(step)],
                    arrived.at[step - 1],
                    wshard=here.other(step),
                )
                for step in range(1, here.shards)
            ]
        return []

    def work(self, phase):
        held, core_in, arrived = self.held
        if phase == 1:

            def add(index, carry):
                at = (index // 4, (index // 2) % 2, index % 2)
                add_into(held, at, core_in[at])
                return carry

            lax.fori_loop(0, 4 * held.shape[0], add, 0)
        elif phase == 2:

            def gather_up(index, carry):
                at = (index // 2, index % 2)
                value = held[(self.here.place,) + at].astype(f32)
                for step in range(arrived.shape[0]):
                    value = value + arrived[(step,) + at].astype(f32)
                core_in[(0,) + at] = value.astype(bf16)
                return carry

            lax.fori_loop(0, 4, gather_up, 0)


class SumSpread(Rider):
    last = 5
    remote_count, local_count = 9, 2

    def __init__(self, sums):
        _, _, size, half = sums.shape
        self.half = half
        quarter = half // 2
        self.inputs = (sums,)
        self.outputs = (jax.ShapeDtypeStruct((2, 2, size, 2 * half), bf16),)
        self.scratch = (
            pltpu.VMEM((2, 2, size, half), bf16),
            pltpu.VMEM((2, size, quarter), bf16),
            pltpu.VMEM((2, size, quarter), bf16),
            pltpu.VMEM((size, quarter), bf16),
            pltpu.VMEM((size, quarter), bf16),
        )

    def local(self, phase):
        here, held = self.here, self.held[0]
        if phase == 0:
            return [self.keep(0, self.inputs_[0], held)]
        if phase == 3:
            mine = span(here.core * self.half, self.half)
            return [self.keep(1, held.at[here.y, here.x], self.outputs_[0].at[here.y, here.x, :, mine])]
        return []

    def remote(self, phase):
        here, (out,) = self.here, self.outputs_
        y, x, quarter = here.y, here.x, self.half // 2
        held, far_a, far_b, next_a, next_b = self.held
        one, two = pl.ds(0, quarter), pl.ds(quarter, quarter)
        out_one = span(here.core * self.half, quarter)
        out_two = span(here.core * self.half + quarter, quarter)
        if phase == 1:
            return [
                self.send(0, held.at[:, 1 - x, :, one], far_a, seq=here.x_next),
                self.send(1, held.at[1 - y, :, :, two], far_b, seq=here.y_next),
            ]
        if phase == 2:
            return [
                self.send(2, held.at[1 - y, x, :, one], next_a, seq=here.y_next),
                self.send(3, held.at[y, 1 - x, :, two], next_b, seq=here.x_next),
            ]
        if phase == 3:
            return [
                self.send(4, held.at[y, x, :, one], out.at[y, x, :, out_one], seq=here.y_next),
                self.send(5, held.at[y, x, :, two], out.at[y, x, :, out_two], seq=here.x_next),
            ]
        if phase == 4:
            both_one, both_two = out.at[:, x, :, out_one], out.at[y, :, :, out_two]
            return [
                self.send(6, both_one, both_one, seq=here.x_next),
                self.send(7, both_two, both_two, seq=here.y_next),
            ]
        if phase == 5:
            ref = out.at[:, :, :, span(here.core * self.half, self.half)]
            return [self.send(8, ref, ref, seq=here.core_next)]
        return []

    def work(self, phase):
        y, x = self.here.y, self.here.x
        held, far_a, far_b, next_a, next_b = self.held
        every = slice(None)
        one, two = slice(0, self.half // 2), slice(self.half // 2, self.half)
        if phase == 2:
            for side in range(2):
                add_into(held, (side, x, every, one), far_a[side])
                add_into(held, (y, side, every, two), far_b[side])
        elif phase == 3:
            add_into(held, (y, x, every, one), next_a[...])
            add_into(held, (y, x, every, two), next_b[...])


def call(
    kernel,
    grid,
    args,
    in_specs,
    out_specs,
    out_shape,
    scratch_shapes=(),
    riders=(),
    table=None,
    collective_id=None,
    vmem=48,
    flops=0,
    traffic=0,
    name=None,
):
    anywhere = pl.BlockSpec(memory_space=pl.ANY)
    sizes = [len(args), len(out_shape), len(scratch_shapes)]
    rider_in = [array for rider in riders for array in rider.inputs]
    rider_out = [shape for rider in riders for shape in rider.outputs]
    rider_scratch = [entry for rider in riders for entry in rider.semaphores() + list(rider.scratch)]
    aliases = {}
    at_in, at_out = sizes[0], sizes[1]
    for rider in riders:
        for source, target in rider.aliases:
            aliases[at_in + source] = at_out + target
        at_in += len(rider.inputs)
        at_out += len(rider.outputs)

    def body(*refs):
        refs = list(refs)

        def take(count):
            found = refs[:count]
            del refs[:count]
            return found

        own_in, their_in = take(sizes[0]), take(len(rider_in))
        own_out, their_out = take(sizes[1]), take(len(rider_out))
        own_scratch, their_scratch = take(sizes[2]), refs
        if not riders:
            return kernel(*own_in, *own_out, *own_scratch)
        here = Here()
        step = pl.program_id(0)
        reach = max(rider.reach for rider in riders)

        @pl.when(step == 0)
        def start():
            here.meet(reach)

        for rider in riders:
            counts = (len(rider.inputs), len(rider.outputs), 3 + len(rider.scratch))
            parts = []
            for pool, count in zip((their_in, their_out, their_scratch), counts):
                parts.append(pool[:count])
                del pool[:count]
            if rider.inside:
                parts[0] = own_scratch[-rider.inside :]
            rider.bind(here, *parts)

        def run(events):
            for which, phase in events:
                riders[which].run(phase)

        for at in sorted(table):
            if at < grid:

                @pl.when(step == at)
                def early():
                    run(table[at])

        kernel(*own_in, *own_out, *own_scratch)

        @pl.when(step == grid - 1)
        def late():
            for at in sorted(table):
                if at >= grid:
                    run(table[at])
            for rider in riders:
                rider.finish()

    found = pl.pallas_call(
        body,
        grid=(grid,),
        in_specs=list(in_specs) + [anywhere] * len(rider_in),
        out_specs=list(out_specs) + [anywhere] * len(rider_out),
        out_shape=list(out_shape) + rider_out,
        scratch_shapes=list(scratch_shapes) + rider_scratch,
        input_output_aliases=aliases,
        compiler_params=pltpu.CompilerParams(
            dimension_semantics=("arbitrary",),
            vmem_limit_bytes=vmem << 20,
            **({"collective_id": collective_id, "has_side_effects": True} if riders else {}),
        ),
        cost_estimate=pl.CostEstimate(flops=flops, bytes_accessed=traffic, transcendentals=0),
        name=name,
    )(*args, *rider_in)
    own, found = found[: sizes[1]], found[sizes[1] :]
    carried = []
    for rider in riders:
        carried.append(found[: len(rider.outputs)])
        found = found[len(rider.outputs) :]
    return own, carried


def whole_rows(gathered):
    return gathered.reshape(-1, gathered.shape[-1])


def finish_sum(part):
    count = lax.axis_size("seq")
    bit = 8
    while bit < count:
        pairs = [(source, source ^ bit) for source in range(count)]
        part = (part.astype(f32) + lax.ppermute(part, "seq", pairs).astype(f32)).astype(bf16)
        bit *= 2
    return part


def mid_kernel(
    before,
    x_ref,
    o_ref,
    hid_ref,
    cot_ref,
    info_ref,
    params_ref,
    mats_in,
    ffn_in,
    down_in,
    out_ref,
    y_ref,
    h2_ref,
    u_ref,
    dab_ref,
    dd_ref,
    dyw_ref,
    dgate_ref,
    do_ref,
    dres_ref,
    dhg_ref,
    dfg_ref,
    mats_ref,
    ffn_ref,
    down_ref,
    sems,
):
    step = pl.program_id(0)
    inner = down_ref.shape[0]
    copies = [
        pltpu.make_async_copy(source, target, sems.at[index])
        for index, (source, target) in enumerate(
            ((mats_in, mats_ref), (ffn_in, ffn_ref), (down_in, down_ref))
        )
    ]

    @pl.when(step == 0)
    def begin():
        for copy in copies:
            copy.start()
        dhg_ref[...] = jnp.zeros_like(dhg_ref)
        dfg_ref[...] = jnp.zeros_like(dfg_ref)
        copies[0].wait()

    hgain, fgain = params_ref[2:3, :], params_ref[3:4, :]
    gate_pre = mm(hid_ref[...], mats_ref[:, :D])
    gate = jax.nn.sigmoid(gate_pre)
    gate_silu = gate_pre * gate

    def head_scale(part):
        return lax.rsqrt(jnp.mean(part * part, axis=-1, keepdims=True) + 1e-05)

    mixed = o_ref[...]
    normal = in_heads(lambda part: part * head_scale(part), mixed)
    scaled = normal * hgain
    y = (scaled * gate_silu).astype(bf16)
    y_ref[...] = y
    x1 = x_ref[...].astype(f32) + mm(y, mats_ref[:, D:])
    x1_scale = lax.rsqrt(jnp.mean(x1 * x1, axis=-1, keepdims=True) + 1e-06)
    h2 = (x1 * x1_scale * fgain).astype(bf16)
    h2_ref[...] = h2
    info = info_ref[...]
    live = is_live(info, rows_from(info, before + step * ROWS, ROWS)).astype(f32)
    grad_out = live * cot_ref[...].astype(f32)
    dd = grad_out.astype(bf16)
    dd_ref[...] = dd

    @pl.when(step == 0)
    def rest():
        copies[1].wait()
        copies[2].wait()

    forward = jnp.zeros_like(x1)
    dh2 = jnp.zeros_like(x1)
    for at in range(0, inner, CH):
        one, two = slice(at, at + CH), slice(inner + at, inner + at + CH)
        a = mm(h2, ffn_ref[:, one])
        b = mm(h2, ffn_ref[:, two])
        sig = jax.nn.sigmoid(a)
        silu = a * sig
        u = (silu * b).astype(bf16)
        u_ref[:, one] = u
        forward = forward + mm(u, down_ref[one, :])
        du = mm_t(dd, down_ref[one, :])
        da = (du * b * (sig + silu * (1.0 - sig))).astype(bf16)
        db = (du * silu).astype(bf16)
        dab_ref[:, one] = da
        dab_ref[:, two] = db
        dh2 = dh2 + mm_t(da, ffn_ref[:, one]) + mm_t(db, ffn_ref[:, two])
    out_ref[...] = (live * (x1 + forward)).astype(bf16)
    x1_normal = x1 * x1_scale
    dfg_ref[...] += jnp.sum(dh2 * x1_normal, axis=0, keepdims=True)
    dh2 = dh2 * fgain
    dx1 = grad_out + x1_scale * (
        dh2 - x1_normal * jnp.mean(dh2 * x1_normal, axis=-1, keepdims=True)
    )
    dres_ref[...] = dx1
    dyw = dx1.astype(bf16)
    dyw_ref[...] = dyw
    dy = mm_t(dyw, mats_ref[:, D:])
    dgate_ref[...] = (dy * scaled * (gate + gate_silu * (1.0 - gate))).astype(bf16)
    dscaled = dy * gate_silu
    dhg_ref[...] += jnp.sum(dscaled * normal, axis=0, keepdims=True)

    def head_back(part, part_normal, grad):
        return head_scale(part) * (
            grad - part_normal * jnp.mean(grad * part_normal, axis=-1, keepdims=True)
        )

    do_ref[...] = in_heads(head_back, mixed, normal, dscaled * hgain).astype(bf16)


def mid(x, mixed, hidden, first_own, cotangent, info, params, mats, ffn, down):
    rows = x.shape[0]
    inner = down.shape[0]
    shape = jax.ShapeDtypeStruct

    def block(columns):
        return pl.BlockSpec((ROWS, columns), lambda step: (step, 0))

    row = pl.BlockSpec((1, D), lambda step: (0, 0))
    anywhere = pl.BlockSpec(memory_space=pl.ANY)
    outs = [
        shape((rows, D), bf16),
        shape((rows, D), bf16),
        shape((rows, D), bf16),
        shape((rows, inner), bf16),
        shape((rows, 2 * inner), bf16),
        shape((rows, D), bf16),
        shape((rows, D), bf16),
        shape((rows, D), bf16),
        shape((rows, D), bf16),
        shape((rows, D), f32),
    ]
    found, _ = call(
        functools.partial(mid_kernel, first_own * ROWS),
        rows // ROWS,
        (x, mixed, hidden, cotangent, info, params, mats, ffn, down),
        [
            block(D),
            block(D),
            pl.BlockSpec((ROWS, D), lambda step: (step + first_own, 0)),
            block(D),
            pl.BlockSpec(info.shape, lambda step: (0, 0)),
            pl.BlockSpec(params.shape, lambda step: (0, 0)),
            anywhere,
            anywhere,
            anywhere,
        ],
        [block(out.shape[1]) for out in outs] + [row, row],
        outs + [shape((1, D), f32)] * 2,
        [
            pltpu.VMEM(mats.shape, bf16),
            pltpu.VMEM(ffn.shape, bf16),
            pltpu.VMEM(down.shape, bf16),
            pltpu.SemaphoreType.DMA((3,)),
        ],
        vmem=62,
        flops=8 * rows * D * (D + 3 * inner // 2),
        traffic=50 << 20,
        name="mid",
    )
    return found


def mid_grads_kernel(
    hid_ref, y_ref, h2_ref, u_ref, dab_ref, dd_ref, dyw_ref, dgate_ref,
    down_ref, ffn_ref, mats_ref, hid_t, y_t, h2_t,
):
    step = pl.program_id(0)
    width = ffn_ref.shape[1]

    @pl.when(step == 0)
    def begin():
        hid_t[...] = hid_ref[...].T
        y_t[...] = y_ref[...].T
        h2_t[...] = h2_ref[...].T

    ffn_ref[...] = mm(h2_t[...], dab_ref[...]).astype(bf16)
    down_ref[...] = mm(u_ref[...].T, dd_ref[...]).astype(bf16)
    for index in range(2 * D // width):
        at = width * index

        @pl.when(step == index)
        def mats():
            if at < D:
                mats_ref[...] = mm(hid_t[...], dgate_ref[:, at : at + width]).astype(bf16)
            else:
                mats_ref[...] = mm(y_t[...], dyw_ref[:, at - D : at - D + width]).astype(bf16)


def mid_grads(hidden, first_own, y, h2, u, dab, dd, dyw, dgate):
    rows, inner = u.shape
    width = 2 * CH
    steps = 2 * inner // width
    shape = jax.ShapeDtypeStruct

    def fixed(array):
        return pl.BlockSpec(array.shape, lambda step: (0, 0))

    found, _ = call(
        mid_grads_kernel,
        steps,
        (hidden, y, h2, u, dab, dd, dyw, dgate),
        [
            pl.BlockSpec((rows, D), lambda step: (first_own, 0)),
            fixed(y),
            fixed(h2),
            pl.BlockSpec((rows, inner // steps), lambda step: (0, step)),
            pl.BlockSpec((rows, width), lambda step: (0, step)),
            fixed(dd),
            fixed(dyw),
            fixed(dgate),
        ],
        [
            pl.BlockSpec((inner // steps, D), lambda step: (step, 0)),
            pl.BlockSpec((D, width), lambda step: (0, step)),
            pl.BlockSpec((D, width), lambda step: (0, jnp.minimum(step, 2 * D // width - 1))),
        ],
        [shape((inner, D), bf16), shape((D, 2 * inner), bf16), shape((D, 2 * D), bf16)],
        [pltpu.VMEM((D, rows), bf16)] * 3,
        vmem=62,
        flops=2 * rows * D * (2 * D + 3 * inner),
        traffic=40 << 20,
        name="mid_grads",
    )
    return found


def front_grads_kernel(
    hid_ref, pre_ref, qpre_ref, dkv_ref, dkvpre_ref, dq_ref, dqpre_ref, dbp_ref, small_ref,
    hid_t, pre_t, qpre_t, out_ref,
):
    step = pl.program_id(0)
    width = EXTRA
    split = out_ref.shape[:-1]
    first_query = 2 * D // width
    column = jnp.where(
        step < first_query,
        D + step * width,
        jnp.where(step < 3 * D // width, (step - first_query) * width, 3 * D),
    )
    at_step = pl.ds(pl.multiple_of(column, width), width)

    def put(value):
        out_ref[:, :, :, :, at_step] = value.astype(bf16).reshape(split + (width,))
    own = dq_ref.shape[0]
    main = hid_t.shape[1]

    @pl.when(step == 0)
    def begin():
        hid_t[...] = hid_ref[...].T
        pre_t[...] = pre_ref[...].T
        qpre_t[...] = qpre_ref[...].T

    @pl.when((step >= first_query) & (step < 3 * D // width))
    def queries():
        at = pl.ds(pl.multiple_of((step - first_query) * width, width), width)
        put(mm(hid_t[:, main - own :], dq_ref[:, at]) + mm(qpre_t[...], dqpre_ref[:, at]))

    @pl.when(step < first_query)
    def others():
        put(mm(hid_t[...], dkv_ref[...]) + mm(pre_t[...], dkvpre_ref[...]))

    @pl.when(step == 3 * D // width)
    def rest():
        lane = lax.broadcasted_iota(jnp.int32, (D, SMALL), 1)
        gates = mm(hid_t[...], dbp_ref[...]).astype(bf16)
        first = jnp.where(lane < HEADS, gates, small_ref[...])
        put(jnp.concatenate([first, jnp.zeros((D, width - SMALL), bf16)], axis=1))


def front_grads(hidden, dkv, dq, dqpre, dbp, small, **riding):
    own = dq.shape[0]
    main = dbp.shape[0]
    width = EXTRA
    blocks = 3 * D // width

    def fixed(array):
        return pl.BlockSpec(array.shape, lambda step: (0, 0))

    def kv_block(step):
        return jnp.minimum(step, 2 * D // width - 1)

    places = lax.axis_size("wshard")
    _, carried = call(
        front_grads_kernel,
        blocks + 1,
        (hidden, hidden, hidden, dkv, dkv, dq, dqpre, dbp, small),
        [
            pl.BlockSpec((main, D), lambda step: (0, 0)),
            pl.BlockSpec((PRE, D), lambda step: (main // PRE, 0)),
            pl.BlockSpec((PRE, D), lambda step: ((main - own) // PRE - 1, 0)),
            pl.BlockSpec((main, width), lambda step: (0, kv_block(step))),
            pl.BlockSpec((PRE, width), lambda step: (main // PRE, kv_block(step))),
            fixed(dq),
            fixed(dqpre),
            fixed(dbp),
            fixed(small),
        ],
        [],
        [],
        [
            pltpu.VMEM((D, main), bf16),
            pltpu.VMEM((D, PRE), bf16),
            pltpu.VMEM((D, PRE), bf16),
            pltpu.VMEM((places, 2, 2, D // places // 4, 3 * D + EXTRA), bf16),
        ],
        vmem=62,
        flops=2 * D * D * (2 * main + own),
        traffic=25 << 20,
        name="end",
        **riding,
    )
    return carried


def widen_kernel(down_in, ffn0_in, ffn1_in, mats_in, k_in, v_in, q_in, down, gate, up, og, out, qkv):
    down[...] = down_in[0, 0].astype(f32)
    for source, start in ((ffn0_in, 0), (ffn1_in, ffn0_in.shape[2])):
        rows = slice(start, start + source.shape[2])
        inner = gate.shape[1]
        gate[rows, :] = source[0, 0, :, :inner].astype(f32)
        up[rows, :] = source[0, 0, :, inner:].astype(f32)
    og[...] = mats_in[0, 0, :, :D].astype(f32)
    out[...] = mats_in[0, 0, :, D:].astype(f32)
    for index, source in enumerate((q_in, k_in, v_in)):
        qkv[:, D * index : D * (index + 1)] = source[0, 0].astype(f32)


def widen(down, ffn0, ffn1, mats, keys, values, queries):
    ins = (down, ffn0, ffn1, mats, keys, values, queries)
    rows, inner = mats.shape[2], ffn0.shape[3] // 2
    widths = [(down.shape[2], D), (rows, inner), (rows, inner), (rows, D), (rows, D), (rows, 3 * D)]
    found, _ = call(
        widen_kernel,
        4,
        ins,
        [
            pl.BlockSpec((1, 1) + part.shape[2:], lambda step: (step // 2, step % 2, 0, 0))
            for part in ins
        ],
        [pl.BlockSpec(width, lambda step: (step, 0)) for width in widths],
        [jax.ShapeDtypeStruct((4 * height, width), f32) for height, width in widths],
        vmem=62,
        traffic=25 << 20,
        name="widen",
    )
    return found


def on_device(
    tokens,
    slot_lengths,
    live_lengths,
    norm_gain,
    w_qkv,
    w_beta,
    w_outgate,
    conv_weight,
    ridge,
    head_gain,
    w_out,
    ffn_gain,
    w_gate,
    w_up,
    w_down,
    cotangent,
):
    row_count = tokens.shape[1]
    depth = (WINDOW + row_count - 1) // row_count
    halo_rows = depth * row_count
    main_rows = halo_rows + row_count
    shards = lax.axis_size("wshard")
    shard_rows = norm_gain.shape[0]
    tap_columns = TAPS * conv_weight.shape[1] // shard_rows

    own_tokens = tokens[0]
    small = jnp.concatenate(
        [
            w_beta,
            jnp.stack([norm_gain, ridge, head_gain, ffn_gain]).T,
            conv_weight.reshape(TAPS, 3, shard_rows).transpose(2, 1, 0).reshape(shard_rows, -1),
        ],
        axis=1,
    )
    small = jnp.pad(small, ((0, 0), (0, EXTRA - small.shape[1])))
    out_mats = jnp.concatenate([w_outgate, w_out], axis=1)
    ffn_mats = jnp.concatenate([w_gate, w_up], axis=1)

    riders = [
        Gather(jnp.concatenate([w_qkv, small], axis=1)),
        WindowTokens(own_tokens, depth),
        Gather(ffn_mats, 0, 0),
    ]
    events = [(1, 0), (0, 0), (0, 1), (2, 0), (1, 1), (0, 2), (0, 3), (0, 4), (1, 2), (2, 1)]
    _, ((w_front,), (ext_tokens,), (ffn_in,)) = call(
        lambda: None, 1, (), [], [], [], riders=riders, table={0: events}, collective_id=0, name="begin"
    )
    w_front = whole_rows(w_front)
    rank = lax.axis_index("seq")
    info = slot_info(slot_lengths[0], live_lengths[0], rank * row_count - halo_rows)

    (hidden, kv_in, q_in, q_pre, queries, keys, values, beta, params, taps), ((ffn_in,), (mats,), (all_down,)) = front(
        ext_tokens,
        info,
        w_front,
        row_count,
        riders=[Gather(None, 1, 2, ffn_in), Gather(out_mats, 0, 0), Gather(w_down, 0, 0)],
        table={0: [(0, 1), (1, 0), (2, 0)], 4: [(0, 2)], 99: [(1, 1), (2, 1), (0, 3)]},
        collective_id=1,
    )
    (mixed, image0, image1), ((ffn_in,), (mats,), (all_down,)) = attn_fwd(
        queries,
        keys,
        values,
        beta,
        info,
        w_front,
        riders=[Gather(None, 3, 3, ffn_in), Gather(None, 1, 3, mats), Gather(None, 1, 3, all_down)],
        table={
            0: [(1, 1), (2, 1), (0, 3)],
            2: [(1, 2)],
            3: [(2, 2)],
            5: [(1, 3)],
            99: [(2, 3), (0, 4), (1, 4), (2, 4)],
        },
        collective_id=2,
    )
    mats, ffn_in, all_down = (whole_rows(part) for part in (mats, ffn_in, all_down))
    first_own = halo_rows // ROWS
    output, y, h2, u, d_ab, d_down_in, d_out_in, d_gate, d_mixed, d_xout, d_ghead, d_gffn = mid(
        own_tokens,
        mixed,
        hidden,
        first_own,
        cotangent[0],
        info,
        params,
        mats,
        ffn_in,
        all_down,
    )
    grad_down, grad_ffn, grad_mats = mid_grads(
        hidden, halo_rows // row_count, y, h2, u, d_ab, d_down_in, d_out_in, d_gate
    )

    part_rows = shard_rows // 8
    (d_query, d_key, d_value, d_beta, d_ridge), ((sum_down,), (sum_ffn0,), (sum_mats,)) = attn_bwd(
        queries,
        keys,
        values,
        beta,
        info,
        w_front,
        image0,
        image1,
        d_mixed,
        riders=[SumFar(grad_down), SumFar(grad_ffn, 0, part_rows), SumPlace(grad_mats)],
        table={
            0: [(2, 0), (0, 0), (1, 0)],
            1: [(2, 1), (0, 1)],
            2: [(1, 1)],
            4: [(0, 2)],
            7: [(1, 2)],
            99: [(0, 3), (1, 3), (2, 2), (2, 3), (0, 4), (1, 4)],
        },
        collective_id=3,
    )
    (
        (d_kv_in, d_q_in, d_q_pre, d_beta_pre, d_gain, d_taps),
        ((sum_down,), (sum_ffn0,), (sum_ffn1,), (total_mats,), (d_tokens,)),
    ) = back(
        ext_tokens,
        kv_in,
        info,
        q_in,
        q_pre,
        d_key,
        d_value,
        d_query,
        beta,
        d_beta,
        d_gate,
        d_xout,
        params,
        w_front,
        mats,
        taps,
        riders=[
            SumNear(sum_down, stop=True),
            SumNear(sum_ffn0, stop=True),
            SumFar(grad_ffn, part_rows, part_rows),
            SumSpread(sum_mats),
            WindowGrads(row_count, D, depth),
        ],
        table={
            0: [(2, 0), (3, 0), (3, 1), (0, 0), (1, 0)],
            1: [(3, 2), (2, 1)],
            3: [(2, 2), (3, 3)],
            4: [(4, 0)],
            5: [(4, 1), (0, 1), (1, 1), (3, 4)],
            6: [(4, 2), (2, 3), (3, 5)],
            99: [(4, 3), (2, 4), (0, 2), (1, 2), (3, 6), (4, 4), (4, 5)],
        },
        collective_id=4,
    )
    d_small = jnp.concatenate(
        [
            jnp.zeros((D, HEADS), f32),
            d_gain.reshape(D, 1),
            d_ridge,
            d_ghead.reshape(D, 1),
            d_gffn.reshape(D, 1),
            d_taps.reshape(TAPS, shards, 3, -1).transpose(1, 3, 2, 0).reshape(D, tap_columns),
        ],
        axis=1,
    ).astype(bf16)
    d_small = jnp.pad(d_small, ((0, 0), (0, SMALL - d_small.shape[1])))
    rows = shard_rows // 4
    fars = [
        SumFar(None, 0, rows, D, D),
        SumFar(None, 0, rows, D, 2 * D),
        SumFar(None, 0, rows, D, 0),
        SumFar(None, 0, rows, EXTRA, 3 * D),
    ]
    riders = [SumNear(sum_ffn1)] + fars + [SumNear(after=far) for far in fars]
    riders += [SumNear(total=sum_down), SumNear(total=sum_ffn0)]
    late = [
        (3, 0), (4, 0), (9, 3), (10, 3), (2, 1), (1, 2), (3, 1), (4, 1), (2, 2), (1, 3), (1, 4), (5, 0),
        (3, 2), (4, 2), (0, 1), (2, 3), (2, 4), (6, 0), (5, 1), (3, 3), (4, 3), (3, 4), (4, 4),
        (7, 0), (8, 0), (0, 2), (6, 1), (5, 2), (6, 2), (5, 3), (7, 1), (8, 1), (6, 3), (0, 3),
        (7, 2), (8, 2), (7, 3), (8, 3), (5, 4), (6, 4), (0, 4), (7, 4), (8, 4),
        (9, 4), (10, 4),
    ]
    carried = front_grads(
        hidden,
        d_kv_in,
        d_q_in,
        d_q_pre,
        d_beta_pre,
        d_small,
        riders=riders,
        table={
            0: [(0, 0), (9, 0), (10, 0), (9, 1), (10, 1)],
            2: [(9, 2), (10, 2), (1, 0)],
            4: [(1, 1), (2, 0)],
            99: late,
        },
        collective_id=5,
    )
    (total_ffn1,), _, _, _, _, (total_k,), (total_v,), (total_q,), (total_small,) = carried[:9]
    (total_down,), (total_ffn0,) = carried[9:]
    sums = (total_down, total_ffn0, total_ffn1, total_mats, total_k, total_v, total_q)
    t_down, t_gate, t_up, t_og, t_out, t_qkv = widen(*(finish_sum(part) for part in sums))
    t_small = finish_sum(total_small)[..., :SMALL].reshape(shard_rows, SMALL).astype(f32)
    t_taps = t_small[:, HEADS + 4 : HEADS + 4 + tap_columns]
    return (
        output[None],
        d_tokens[None],
        t_small[:, HEADS],
        t_qkv,
        t_small[:, :HEADS],
        t_og,
        t_taps.reshape(shard_rows, 3, TAPS).transpose(2, 1, 0).reshape(TAPS, -1),
        t_small[:, HEADS + 1],
        t_small[:, HEADS + 2],
        t_out,
        t_small[:, HEADS + 3],
        t_gate,
        t_up,
        t_down,
    )


def solution(mesh):
    return jax.shard_map(
        on_device,
        mesh=mesh,
        in_specs=(
            P("wshard", "seq", None),
            P("wshard", None),
            P("wshard", None),
            P("wshard"),
            P("wshard", None),
            P("wshard", None),
            P("wshard", None),
            P(None, "wshard"),
            P("wshard"),
            P("wshard"),
            P("wshard", None),
            P("wshard"),
            P("wshard", None),
            P("wshard", None),
            P("wshard", None),
            P("wshard", "seq", None),
        ),
        out_specs=(
            P("wshard", "seq", None),
            P("wshard", "seq", None),
            P("wshard"),
            P("wshard", None),
            P("wshard", None),
            P("wshard", None),
            P(None, "wshard"),
            P("wshard"),
            P("wshard"),
            P("wshard", None),
            P("wshard"),
            P("wshard", None),
            P("wshard", None),
            P("wshard", None),
        ),
        check_vma=False,
    )
```

```python
import functools
import jax
import jax.numpy as jnp
from jax import lax
from jax.experimental import pallas as pl
from jax.experimental.pallas import tpu as pltpu
from jax.sharding import PartitionSpec as P

D = 1024
HEADS = 8
HEAD_DIM = 128
TAPS = 4
WINDOW = 1024
PRE = 16
SMALL = 128
EXTRA = 512
MESH = pl.DeviceIdType.MESH
f32 = jnp.float32
bf16 = jnp.bfloat16
QB = 256
CH = 256
KEYS = 640
CW = 128
ROWS = 256


def slot_info(lengths, live, first):
    table = jnp.array(
        [
            [1, 0, 0, 0, 0, 0],
            [1, 1, 0, 0, 0, 0],
            [0, 0, 0, 1, 0, 0],
            [1, 0, 0, 0, 1, 0],
            [1, 1, 0, 0, 0, 1],
            [0, 0, 0, 0, 0, 0],
            [0, 0, 0, 0, 0, 0],
            [0, 0, 0, 0, 0, 0],
        ],
        jnp.int32,
    )
    found = jnp.sum(table * jnp.concatenate([lengths, live])[None, :], axis=1, keepdims=True)
    row = lax.broadcasted_iota(jnp.int32, (8, 128), 0)
    return found + jnp.where(row == 5, first, 0)


def slot_of(info, positions):
    found = (positions >= 0).astype(jnp.int32)
    for index in range(2):
        found = found + (positions >= info[index : index + 1, 0:1]).astype(jnp.int32)
    return found


def is_live(info, positions):
    found = (positions >= 0) & (positions < info[2:3, 0:1])
    for index in range(2):
        found = found | (
            (positions >= info[index : index + 1, 0:1])
            & (positions < info[index + 3 : index + 4, 0:1])
        )
    return found


def rows_from(info, start, count):
    return info[5:6, 0:1] + start + lax.broadcasted_iota(jnp.int32, (count, 1), 0)


def same_slots(info, start):
    at = rows_from(info, start, ROWS)
    own = slot_of(info, at)
    return [(own == slot_of(info, at - tap)).astype(f32) for tap in range(TAPS)]


def window_mask(info, mask_ref):
    keys, queries = mask_ref.shape
    at_query = (
        info[5:6, 0:1] + (keys - queries) + lax.broadcasted_iota(jnp.int32, (1, queries), 1)
    )
    query_slot = slot_of(info, at_query)
    for start in range(0, keys, ROWS):
        at = rows_from(info, start, ROWS)
        key_slot = jnp.where(is_live(info, at), slot_of(info, at), -1)
        spacing = at_query - at
        inside = (spacing >= 0) & (spacing < WINDOW) & (key_slot == query_slot)
        mask_ref[start : start + ROWS, :] = inside.astype(f32).astype(bf16)


def mm(left, right):
    return jnp.dot(left, right, preferred_element_type=f32)


def mm_t(left, right):
    return lax.dot_general(left, right, (((1,), (1,)), ((), ())), preferred_element_type=f32)


def conv_total(ext_ref, slot, same, taps):
    total = taps[0:1] * ext_ref[slot, 8 : 8 + ROWS, :]
    for tap in range(1, TAPS):
        total = total + taps[tap : tap + 1] * ext_ref[slot, 8 - tap : 8 - tap + ROWS, :] * same[tap]
    return total


def unit_scale(active):
    return lax.rsqrt(jnp.sum(active * active, axis=-1, keepdims=True) + 1e-06)


def in_heads(work, *arrays):
    width = arrays[0].shape[1]
    return jnp.concatenate(
        [
            work(*(array[:, at : at + HEAD_DIM] for array in arrays))
            for at in range(0, width, HEAD_DIM)
        ],
        axis=1,
    )


def row_norm(x, gain):
    return (x * lax.rsqrt(jnp.mean(x * x, axis=-1, keepdims=True) + 1e-06) * gain).astype(bf16)


def front_kernel(
    first_own,
    x_ref,
    info_ref,
    w_ref,
    hid_ref,
    kvin_ref,
    qin_ref,
    qpre_ref,
    q_ref,
    k_ref,
    v_ref,
    beta_ref,
    params_ref,
    taps_ref,
    ext_ref,
    tail_ref,
):
    step = pl.program_id(0)
    shards = lax.axis_size("wshard")

    @pl.when(step == 0)
    def unpack():
        small = w_ref[:, 3 * D : 3 * D + SMALL].astype(f32).T
        params_ref[...] = small[HEADS : HEADS + 8]
        wide = D // shards
        for place in range(shards):
            for third in range(3):
                row = HEADS + 4 + TAPS * third
                at = 3 * wide * place + wide * third
                taps_ref[:, at : at + wide] = small[
                    row : row + TAPS, wide * place : wide * (place + 1)
                ]

    gain = params_ref[0:1, :]
    main_rows = x_ref.shape[0] - PRE
    before_at = pl.ds(main_rows, PRE)
    rows_at = pl.ds(pl.multiple_of(jnp.maximum(step - 1, 0) * ROWS, ROWS), ROWS)
    kv_slots = 2 * D // CW

    @pl.when(step == 0)
    def before():
        hidden = row_norm(x_ref[before_at].astype(f32), gain)
        hid_ref[0:PRE] = hidden
        for slot in range(kv_slots):
            rows = mm(hidden, w_ref[:, D + CW * slot : D + CW * (slot + 1)]).astype(bf16)
            kvin_ref[0:PRE, CW * slot : CW * (slot + 1)] = rows
            ext_ref[slot, ROWS : ROWS + 8, :] = rows.astype(f32)[PRE - 8 :]

    def through(slot, hidden, same, column, in_ref, at):
        ext_ref[slot, 0:8, :] = ext_ref[slot, ROWS : ROWS + 8, :]
        rows = mm(hidden, w_ref[:, column : column + CW]).astype(bf16)
        in_ref[:, at : at + CW] = rows
        ext_ref[slot, 8 : 8 + ROWS, :] = rows.astype(f32)
        total = conv_total(ext_ref, slot, same, taps_ref[:, column : column + CW])
        return total * jax.nn.sigmoid(total)

    def unit(active):
        return in_heads(lambda part: part * unit_scale(part), active).astype(bf16)

    @pl.when(step > 0)
    def main():
        same = same_slots(info_ref[...], (step - 1) * ROWS)
        hidden = row_norm(x_ref[rows_at].astype(f32), gain)
        hid_ref[...] = hidden
        for slot in range(kv_slots):
            at = CW * slot
            active = through(slot, hidden, same, D + at, kvin_ref, at)
            if at < D:
                k_ref[:, at : at + CW] = unit(active)
            else:
                v_ref[:, at - D : at - D + CW] = active.astype(bf16)
        gates = jax.nn.sigmoid(mm(hidden, w_ref[:, 3 * D : 3 * D + SMALL])).astype(bf16)
        lane = lax.broadcasted_iota(jnp.int32, (ROWS, SMALL), 1)
        beta_ref[...] = jnp.where(lane < HEADS, gates.astype(f32), 0.0)

        @pl.when(step == first_own + 1)
        def own_history():
            rows = mm(tail_ref[...], w_ref[:, :D]).astype(bf16)
            qpre_ref[...] = rows
            for slot in range(D // CW):
                ext_ref[kv_slots + slot, ROWS : ROWS + 8, :] = rows.astype(f32)[
                    PRE - 8 :, CW * slot : CW * (slot + 1)
                ]

        @pl.when(step > first_own)
        def own():
            for slot in range(D // CW):
                at = CW * slot
                active = through(kv_slots + slot, hidden, same, at, qin_ref, at)
                q_ref[:, at : at + CW] = unit(active)

        tail_ref[...] = hidden[ROWS - PRE :]


def front(ext_tokens, info, w_front, own_rows, **riding):
    ext_rows = ext_tokens.shape[0]
    main_rows = ext_rows - PRE
    blocks = main_rows // ROWS
    first_own = (main_rows - own_rows) // ROWS

    def ext_block(step):
        return (jnp.where(step == 0, blocks, step - 1), 0)

    def main_block(step):
        return (jnp.maximum(step - 1, 0), 0)

    def own_block(step):
        return (jnp.maximum(step - 1 - first_own, 0), 0)

    def fixed(array):
        return pl.BlockSpec(array.shape, lambda step: (0, 0), pipeline_mode=pl.Buffered(1))

    shape = jax.ShapeDtypeStruct
    outs = [
        shape((ext_rows, D), bf16),
        shape((ext_rows, 2 * D), bf16),
        shape((own_rows, D), bf16),
        shape((PRE, D), bf16),
        shape((own_rows, D), bf16),
        shape((main_rows, D), bf16),
        shape((main_rows, D), bf16),
        shape((main_rows, SMALL), f32),
        shape((8, D), f32),
        shape((TAPS, 3 * D), f32),
    ]
    return call(
        functools.partial(front_kernel, first_own),
        blocks + 1,
        (ext_tokens, info, w_front),
        [fixed(array) for array in (ext_tokens, info, w_front)],
        [
            pl.BlockSpec((ROWS, D), ext_block),
            pl.BlockSpec((ROWS, 2 * D), ext_block),
            pl.BlockSpec((ROWS, D), own_block),
            pl.BlockSpec((PRE, D), lambda step: (0, 0)),
            pl.BlockSpec((ROWS, D), own_block),
            pl.BlockSpec((ROWS, D), main_block),
            pl.BlockSpec((ROWS, D), main_block),
            pl.BlockSpec((ROWS, SMALL), main_block),
            pl.BlockSpec((8, D), lambda step: (0, 0)),
            pl.BlockSpec((TAPS, 3 * D), lambda step: (0, 0)),
        ],
        outs,
        [
            pltpu.VMEM((3 * D // CW, 8 + ROWS, CW), f32),
            pltpu.VMEM((PRE, D), bf16),
        ],
        vmem=62,
        flops=4 * (main_rows * 2 + own_rows) * D * D,
        traffic=30 << 20,
        name="front",
        **riding,
    )


def back_kernel(
    blocks,
    first_own,
    x_ref,
    kvin_ref,
    kvprev_ref,
    info_ref,
    qin_ref,
    qprev_ref,
    qpre_ref,
    dk_ref,
    dv_ref,
    dq_ref,
    beta_ref,
    dbeta_ref,
    dgate_ref,
    dres_ref,
    params_ref,
    w_ref,
    wog_ref,
    taps_ref,
    dkvin_ref,
    dqin_ref,
    dqpre_ref,
    dbp_ref,
    dgain_ref,
    dtaps_ref,
    ext_ref,
    buf_ref,
    dh_ref,
    dxhalo_ref,
    dxown_ref,
):
    step = pl.program_id(0)
    block = blocks - 1 - step
    kv_slots = 2 * D // CW
    gain = params_ref[0:1, :]

    @pl.when(step == 0)
    def clear():
        dgain_ref[...] = jnp.zeros_like(dgain_ref)
        dtaps_ref[...] = jnp.zeros_like(dtaps_ref)
        buf_ref[:, :, ROWS : ROWS + 8, :] = jnp.zeros_like(buf_ref[:, :, ROWS : ROWS + 8, :])

    def norm_back(x, dh):
        scale = lax.rsqrt(jnp.mean(x * x, axis=-1, keepdims=True) + 1e-06)
        normal = x * scale
        dgain_ref[...] += jnp.sum(dh * normal, axis=0, keepdims=True)
        scaled = dh * gain
        return scale * (scaled - normal * jnp.mean(scaled * normal, axis=-1, keepdims=True))

    def shifted(slot, start, count):
        total = buf_ref[slot, 0, start + 1 : start + 1 + count, :]
        for tap in range(2, TAPS):
            total = total + buf_ref[slot, tap - 1, start + tap : start + tap + count, :]
        return total

    def through(slot, column, history, rows, grad, unit, same):
        ext_ref[slot, 0:8, :] = history
        ext_ref[slot, 8 : 8 + ROWS, :] = rows.astype(f32)
        taps = taps_ref[:, column : column + CW]
        total = conv_total(ext_ref, slot, same, taps)
        gate = jax.nn.sigmoid(total)
        active = total * gate
        if unit:

            def unit_back(part, part_grad):
                scale = unit_scale(part)
                normal = part * scale
                return scale * (
                    part_grad - normal * jnp.sum(part_grad * normal, axis=-1, keepdims=True)
                )

            grad = in_heads(unit_back, active, grad)
        grad = grad * (gate + active * (1.0 - gate))
        result = grad * taps[0:1]
        dtaps_ref[0:1, column : column + CW] += jnp.sum(
            grad * ext_ref[slot, 8 : 8 + ROWS, :], axis=0, keepdims=True
        )
        for tap in range(1, TAPS):
            held = grad * same[tap]
            dtaps_ref[tap : tap + 1, column : column + CW] += jnp.sum(
                held * ext_ref[slot, 8 - tap : 8 - tap + ROWS, :], axis=0, keepdims=True
            )
            buf_ref[slot, tap - 1, 0:ROWS, :] = held * taps[tap : tap + 1]
        result = (result + shifted(slot, 0, ROWS)).astype(bf16)
        for tap in range(1, TAPS):
            buf_ref[slot, tap - 1, ROWS : ROWS + 8, :] = buf_ref[slot, tap - 1, 0:8, :]
        return result

    def before_rows(slot):
        for tap in range(1, TAPS):
            buf_ref[slot, tap - 1, ROWS - PRE : ROWS, :] = jnp.zeros((PRE, CW), f32)
        return shifted(slot, ROWS - PRE, PRE).astype(bf16)

    @pl.when(step < blocks)
    def main():
        same = same_slots(info_ref[...], block * ROWS)
        beta = beta_ref[...]
        gates = (dbeta_ref[...] * beta * (1.0 - beta)).astype(bf16)
        dbp_ref[...] = gates
        dh = mm_t(gates, w_ref[:, 3 * D : 3 * D + SMALL])
        for slot in range(kv_slots):
            at = CW * slot
            grad = dk_ref[:, at : at + CW] if at < D else dv_ref[:, at - D : at - D + CW]
            history = kvprev_ref[PRE - 8 : PRE, at : at + CW].astype(f32)
            rows = kvin_ref[:, at : at + CW]
            rows = through(slot, D + at, history, rows, grad, at < D, same)
            dkvin_ref[:, at : at + CW] = rows
            dh = dh + mm_t(rows, w_ref[:, D + at : D + at + CW])
        dh_ref[...] = dh

        @pl.when(block >= first_own)
        def own():
            dh = mm_t(dgate_ref[...], wog_ref[...])
            for slot in range(D // CW):
                at = CW * slot
                history = jnp.where(
                    block == first_own,
                    qpre_ref[PRE - 8 :, at : at + CW].astype(f32),
                    qprev_ref[PRE - 8 :, at : at + CW].astype(f32),
                )
                rows = qin_ref[:, at : at + CW]
                rows = through(
                    kv_slots + slot, at, history, rows, dq_ref[:, at : at + CW], True, same
                )
                dqin_ref[:, at : at + CW] = rows
                dh = dh + mm_t(rows, w_ref[:, at : at + CW])
            at = pl.ds(pl.multiple_of((block - first_own) * ROWS, ROWS), ROWS)
            dxown_ref[at] = dres_ref[...] + norm_back(x_ref[...].astype(f32), dh_ref[...] + dh)

        @pl.when(block == first_own - 1)
        def own_history():
            dh = jnp.zeros((PRE, D), f32)
            for slot in range(D // CW):
                at = CW * slot
                rows = before_rows(kv_slots + slot)
                dqpre_ref[:, at : at + CW] = rows
                dh = dh + mm_t(rows, w_ref[:, at : at + CW])
            dh_ref[ROWS - PRE : ROWS, :] += dh

        @pl.when(block < first_own)
        def halo():
            at = pl.ds(pl.multiple_of(block * ROWS, ROWS), ROWS)
            dxhalo_ref[at] = norm_back(x_ref[...].astype(f32), dh_ref[...]).astype(bf16)

    @pl.when(step == blocks)
    def before():
        dh = jnp.zeros((PRE, D), f32)
        for slot in range(kv_slots):
            at = CW * slot
            rows = before_rows(slot)
            dkvin_ref[0:PRE, at : at + CW] = rows
            dh = dh + mm_t(rows, w_ref[:, D + at : D + at + CW])
        dxhalo_ref[first_own * ROWS : first_own * ROWS + PRE, :] = norm_back(x_ref[0:PRE].astype(f32), dh).astype(bf16)


def back(
    ext_tokens, kvin, info, qin, qpre, dk, dv, dq, beta, dbeta, dgate, dres, params, w_front, mats, taps, **riding
):
    ext_rows = ext_tokens.shape[0]
    main_rows = ext_rows - PRE
    own_rows = dq.shape[0]
    blocks = main_rows // ROWS
    first_own = (main_rows - own_rows) // ROWS
    small_blocks = ROWS // PRE

    def ext_block(step):
        return (jnp.where(step == blocks, blocks, blocks - 1 - step), 0)

    def main_block(step):
        return (jnp.maximum(blocks - 1 - step, 0), 0)

    def prev_block(step):
        block = blocks - 1 - step
        return (jnp.where(block <= 0, blocks * small_blocks, small_blocks * block - 1), 0)

    def own_block(step):
        return (jnp.maximum(blocks - 1 - step - first_own, 0), 0)

    def own_prev_block(step):
        return (jnp.maximum(small_blocks * (blocks - 1 - step - first_own) - 1, 0), 0)

    def fixed(array):
        return pl.BlockSpec(array.shape, lambda step: (0, 0), pipeline_mode=pl.Buffered(1))

    shape = jax.ShapeDtypeStruct
    return call(
        functools.partial(back_kernel, blocks, first_own),
        blocks + 1,
        (
            ext_tokens,
            kvin,
            kvin,
            info,
            qin,
            qin,
            qpre,
            dk,
            dv,
            dq,
            beta,
            dbeta,
            dgate,
            dres,
            params,
            w_front,
            mats,
            taps,
        ),
        [
            pl.BlockSpec((ROWS, D), ext_block),
            pl.BlockSpec((ROWS, 2 * D), ext_block),
            pl.BlockSpec((PRE, 2 * D), prev_block),
            fixed(info),
            pl.BlockSpec((ROWS, D), own_block),
            pl.BlockSpec((PRE, D), own_prev_block),
            fixed(qpre),
            pl.BlockSpec((ROWS, D), main_block),
            pl.BlockSpec((ROWS, D), main_block),
            pl.BlockSpec((ROWS, D), own_block),
            pl.BlockSpec((ROWS, SMALL), main_block),
            pl.BlockSpec((ROWS, SMALL), main_block),
            pl.BlockSpec((ROWS, D), own_block),
            pl.BlockSpec((ROWS, D), own_block),
            fixed(params),
            fixed(w_front),
            pl.BlockSpec((D, D), lambda step: (0, 0), pipeline_mode=pl.Buffered(1)),
            fixed(taps),
        ],
        [
            pl.BlockSpec((ROWS, 2 * D), ext_block),
            pl.BlockSpec((ROWS, D), own_block),
            pl.BlockSpec((PRE, D), lambda step: (0, 0)),
            pl.BlockSpec((ROWS, SMALL), main_block),
            pl.BlockSpec((1, D), lambda step: (0, 0)),
            pl.BlockSpec((TAPS, 3 * D), lambda step: (0, 0)),
        ],
        [
            shape((ext_rows, 2 * D), bf16),
            shape((own_rows, D), bf16),
            shape((PRE, D), bf16),
            shape((main_rows, SMALL), bf16),
            shape((1, D), f32),
            shape((TAPS, 3 * D), f32),
        ],
        [
            pltpu.VMEM((3 * D // CW, 8 + ROWS, CW), f32),
            pltpu.VMEM((3 * D // CW, TAPS - 1, ROWS + 8, CW), f32),
            pltpu.VMEM((ROWS, D), f32),
            pltpu.VMEM((main_rows - own_rows + PRE, D), bf16),
            pltpu.VMEM((own_rows, D), f32),
        ],
        vmem=62,
        flops=6 * (main_rows * 2 + own_rows) * D * D,
        traffic=40 << 20,
        name="back",
        **riding,
    )


def total(v):
    return jnp.sum(v,axis=0,keepdims=True)

def head_column(beta_ref, h):
    beta=beta_ref[...]
    lane=lax.broadcasted_iota(jnp.int32,beta.shape,1)
    return jnp.sum(jnp.where(lane==h,beta,0.0),axis=1,keepdims=True)

def attn_fwd_kernel(q_ref,k_ref,v_ref,beta_ref,info_ref,small_ref,o_ref,a0_ref,a1_ref,kt_ref,vt_ref,w_ref,mask_ref):
    h=pl.program_id(0)
    rows=q_ref.shape[0]
    span=WINDOW+QB
    kt_ref[...]=k_ref[...].T
    vt_ref[...]=v_ref[...].T
    column=head_column(beta_ref,h)
    ridge=small_ref[:,HEADS+1:HEADS+2].astype(f32)

    @pl.when(h==0)
    def fill():
        window_mask(info_ref[...],mask_ref)

    blocks=range(rows//QB)
    chunks=range(span//KEYS)
    for b in blocks:
        for c in chunks:
            at=slice(QB*b+KEYS*c,QB*b+KEYS*(c+1))
            w_ref[b,KEYS*c:KEYS*(c+1),:]=mask_ref[at,QB*b:QB*(b+1)].astype(f32)*column[at]
    def apply(b,vector,right):
        low=vector.astype(bf16)
        out=jnp.zeros((HEAD_DIM,QB),f32)
        for c in chunks:
            at=slice(QB*b+KEYS*c,QB*b+KEYS*(c+1))
            s=mm(k_ref[at,:],low)
            s=(w_ref[b,KEYS*c:KEYS*(c+1),:]*s).astype(bf16)
            out=out+mm(right[:,at],s)
        return out
    q=[q_ref[QB*b:QB*(b+1),:].astype(f32).T for b in blocks]
    a0=[apply(b,q[b],kt_ref)+ridge*q[b] for b in blocks]
    for b in blocks: a0_ref[:,QB*b:QB*(b+1)]=a0[b]
    x1=[];p1=[];r1=[];e1=[]
    for b in blocks:
        e0=total(q[b]*q[b])
        s0=e0/total(q[b]*a0[b])
        x1.append(s0*q[b])
        r=q[b]-s0*a0[b]
        e=total(r*r)
        r1.append(r);e1.append(e)
        p1.append(r+e/e0*q[b])
    a1=[apply(b,p1[b],kt_ref)+ridge*p1[b] for b in blocks]
    for b in blocks: a1_ref[:,QB*b:QB*(b+1)]=a1[b]
    x2=[x1[b]+e1[b]/total(p1[b]*a1[b])*p1[b] for b in blocks]
    for b in blocks:
        o_ref[QB*b:QB*(b+1),:]=apply(b,x2[b],vt_ref).T

def attn_fwd(q,k,v,beta,info,w_front,**riding):
    rows=q.shape[0]; keys=k.shape[0]
    head=lambda n: pl.BlockSpec((n,HEAD_DIM),lambda h:(0,h))
    heads_t=pl.BlockSpec((HEAD_DIM,rows),lambda h:(h,0))
    fixed=lambda a: pl.BlockSpec(a.shape,lambda h:(0,0))
    small=pl.BlockSpec((HEAD_DIM,SMALL),lambda h:(h,3*D//SMALL))
    flops=6*2*rows*(WINDOW+QB)*D
    return call(
        attn_fwd_kernel,
        HEADS,
        (q, k, v, beta, info, w_front),
        [head(rows), head(keys), head(keys), fixed(beta), fixed(info), small],
        [head(rows), heads_t, heads_t],
        [jax.ShapeDtypeStruct((rows, D), f32)] + [jax.ShapeDtypeStruct((D, rows), f32)] * 2,
        [pltpu.VMEM((HEAD_DIM, keys), bf16)] * 2 + [pltpu.VMEM((rows // QB, WINDOW + QB, QB), f32), pltpu.VMEM((keys, rows), bf16)],
        vmem=62,
        flops=2 * flops,
        traffic=20 << 20,
        name="attn_fwd",
        **riding,
    )


def attn_bwd_kernel(q_ref,k_ref,v_ref,beta_ref,info_ref,small_ref,a0_ref,a1_ref,do_ref,dq_ref,dk_ref,dv_ref,dbeta_ref,dridge_ref,kt_ref,w_ref,acc_ref,mask_ref):
    h=pl.program_id(0)
    rows=q_ref.shape[0]
    span=WINDOW+QB
    kt_ref[...]=k_ref[...].T
    column=head_column(beta_ref,h)
    ridge=small_ref[:,HEADS+1:HEADS+2].astype(f32)

    @pl.when(h==0)
    def fill():
        window_mask(info_ref[...],mask_ref)

    blocks=range(rows//QB)
    chunks=range(span//KEYS)
    dk_ref[...]=jnp.zeros_like(dk_ref)
    dv_ref[...]=jnp.zeros_like(dv_ref)
    acc_ref[...]=jnp.zeros_like(acc_ref)
    for b in blocks:
        for c in chunks:
            at=slice(QB*b+KEYS*c,QB*b+KEYS*(c+1))
            w_ref[b,KEYS*c:KEYS*(c+1),:]=mask_ref[at,QB*b:QB*(b+1)].astype(f32)*column[at]
    def apply_back(b,vector,grad,grad_rows,right_ref,dright_ref):
        low=vector.astype(bf16)
        low_rows=vector.T.astype(bf16)
        out=jnp.zeros((HEAD_DIM,QB),f32)
        for c in chunks:
            at=slice(QB*b+KEYS*c,QB*b+KEYS*(c+1))
            w=w_ref[b,KEYS*c:KEYS*(c+1),:]
            s=mm(k_ref[at,:],low)
            dw=mm(right_ref[at,:],grad)
            masked=dw*mask_ref[at,QB*b:QB*(b+1)].astype(f32)
            for_beta=masked*s
            part=for_beta[:,:128]
            for lane in range(128,QB,128):
                part=part+for_beta[:,lane:lane+128]
            acc_ref[at,:]+=part
            ws=(w*s).astype(bf16)
            ds=(w*dw).astype(bf16)
            out=out+mm(kt_ref[:,at],ds)
            dright_ref[at,:]+=mm(ws,grad_rows)
            dk_ref[at,:]+=mm(ds,low_rows)
        return out
    st=[]
    for b in blocks:
        cols=slice(QB*b,QB*(b+1))
        q=q_ref[cols,:].astype(f32).T
        a0=a0_ref[:,cols]; a1=a1_ref[:,cols]
        e0=total(q*q); d0=total(q*a0); s0=e0/d0
        x1=s0*q; r1=q-s0*a0; e1=total(r1*r1); b0=e1/e0
        p1=r1+b0*q; d1=total(p1*a1); s1=e1/d1
        x2=x1+s1*p1
        st.append((q,a0,a1,e0,d0,s0,r1,e1,b0,p1,d1,s1,x2))
    dx2=[]
    for b in blocks:
        do=do_ref[QB*b:QB*(b+1),:]
        dx2.append(apply_back(b,st[b][12],do.astype(f32).T.astype(bf16),do,v_ref,dv_ref))
    da1=[];dp1=[];de1=[];dr=0
    for b in blocks:
        q,a0,a1,e0,d0,s0,r1,e1,b0,p1,d1,s1,x2=st[b]
        ds1=total(dx2[b]*p1)
        de1.append(ds1/d1)
        dd1=-ds1*s1/d1
        g=dd1*p1
        da1.append(g)
        dp1.append(s1*dx2[b]+dd1*a1+ridge*g)
        dr=dr+jnp.sum(g*p1,axis=1,keepdims=True)
    for b in blocks:
        g=da1[b]
        dp1[b]=dp1[b]+apply_back(b,st[b][9],g.astype(bf16),g.T.astype(bf16),k_ref,dk_ref)
    da0=[];dq=[]
    for b in blocks:
        q,a0,a1,e0,d0,s0,r1,e1,b0,p1,d1,s1,x2=st[b]
        db0=total(dp1[b]*q)
        dpq=b0*dp1[b]
        de=de1[b]+db0/e0
        de0=-db0*b0/e0
        dr1=dp1[b]+2.0*de*r1
        ds0=total(dx2[b]*q)-total(dr1*a0)
        dpq=dpq+s0*dx2[b]
        g=-s0*dr1
        de0=de0+ds0/d0
        dd0=-ds0*s0/d0
        dpq=dpq+dd0*a0
        g=g+dd0*q
        dpq=dpq+dr1+2.0*de0*q+ridge*g
        da0.append(g);dq.append(dpq)
        dr=dr+jnp.sum(g*q,axis=1,keepdims=True)
    for b in blocks:
        g=da0[b]
        t=dq[b]+apply_back(b,st[b][0],g.astype(bf16),g.T.astype(bf16),k_ref,dk_ref)
        dq_ref[QB*b:QB*(b+1),:]=t.T
    dridge_ref[...]=dr
    found=jnp.sum(acc_ref[...],axis=1,keepdims=True)
    lane=lax.broadcasted_iota(jnp.int32,dbeta_ref.shape,1)
    @pl.when(h==0)
    def _():
        dbeta_ref[...]=jnp.zeros_like(dbeta_ref)
    dbeta_ref[...]=jnp.where(lane==h,found,dbeta_ref[...])

def attn_bwd(q,k,v,beta,info,w_front,a0,a1,do,**riding):
    rows=q.shape[0]; keys=k.shape[0]
    head=lambda n: pl.BlockSpec((n,HEAD_DIM),lambda h:(0,h))
    heads_t=pl.BlockSpec((HEAD_DIM,rows),lambda h:(h,0))
    fixed=lambda a: pl.BlockSpec(a.shape,lambda h:(0,0))
    rd=pl.BlockSpec((HEAD_DIM,1),lambda h:(h,0))
    small=pl.BlockSpec((HEAD_DIM,SMALL),lambda h:(h,3*D//SMALL))
    flops=15*2*rows*(WINDOW+QB)*D
    return call(
        attn_bwd_kernel,
        HEADS,
        (q, k, v, beta, info, w_front, a0, a1, do),
        [head(rows), head(keys), head(keys), fixed(beta), fixed(info), small, heads_t, heads_t, head(rows)],
        [head(rows), head(keys), head(keys), fixed(beta), rd],
        [
            jax.ShapeDtypeStruct((rows, D), f32),
            jax.ShapeDtypeStruct((keys, D), f32),
            jax.ShapeDtypeStruct((keys, D), f32),
            jax.ShapeDtypeStruct(beta.shape, f32),
            jax.ShapeDtypeStruct((D, 1), f32),
        ],
        [
            pltpu.VMEM((HEAD_DIM, keys), bf16),
            pltpu.VMEM((rows // QB, WINDOW + QB, QB), f32),
            pltpu.VMEM((keys, 128), f32),
            pltpu.VMEM((keys, rows), bf16),
        ],
        vmem=62,
        flops=2 * flops,
        traffic=30 << 20,
        name="attn_bwd",
        **riding,
    )


class Here:
    def __init__(self):
        self.rank = lax.axis_index("seq")
        self.ranks = lax.axis_size("seq")
        self.place = lax.axis_index("wshard")
        self.shards = lax.axis_size("wshard")
        self.core = self.rank % 2
        self.x = (self.rank // 2) % 2
        self.y = (self.rank // 4) % 2
        self.core_next = self.rank + 1 - 2 * self.core
        self.x_next = self.rank + 2 - 4 * self.x
        self.y_next = self.rank + 4 - 8 * self.y

    def other(self, step):
        return (self.place + step) % self.shards

    def along(self, step):
        return (self.rank + step + self.ranks) % self.ranks

    def meet(self, reach):
        barrier = pltpu.get_barrier_semaphore()
        near = [self.core_next, self.x_next, self.y_next]
        for step in range(1, reach + 1):
            near += [self.along(step), self.along(-step)]
        for device in near:
            pl.semaphore_signal(barrier, inc=1, device_id={"seq": device}, device_id_type=MESH)
        for step in range(1, self.shards):
            pl.semaphore_signal(
                barrier, inc=1, device_id={"wshard": self.other(step)}, device_id_type=MESH
            )
        pl.semaphore_wait(barrier, len(near) + self.shards - 1)


def span(start, size):
    return pl.ds(pl.multiple_of(start, 128), size)


class Rider:
    reach = 0
    first, last = 0, 0
    inside = 0
    inputs, outputs, scratch, aliases = (), (), (), ()

    def bind(self, here, inputs, outputs, scratch):
        self.here = here
        self.inputs_, self.outputs_ = inputs, outputs
        self.send_sems, self.recv_sems, self.local_sems = scratch[:3]
        self.held = scratch[3:]

    def semaphores(self):
        return [
            pltpu.SemaphoreType.DMA((self.remote_count,)),
            pltpu.SemaphoreType.DMA((self.remote_count,)),
            pltpu.SemaphoreType.DMA((self.local_count,)),
        ]

    def send(self, index, source, target, **device):
        return pltpu.make_async_remote_copy(
            src_ref=source,
            dst_ref=target,
            send_sem=self.send_sems.at[index],
            recv_sem=self.recv_sems.at[index],
            device_id=device,
            device_id_type=MESH,
        )

    def keep(self, index, source, target):
        return pltpu.make_async_copy(source, target, self.local_sems.at[index])

    def remote(self, phase):
        return []

    def local(self, phase):
        return []

    def work(self, phase):
        pass

    def run(self, phase):
        if phase > self.first:
            for copy in self.remote(phase - 1):
                copy.wait_recv()
            for copy in self.local(phase - 1):
                copy.wait()
        if phase <= self.last:
            self.work(phase)
            for copy in self.remote(phase) + self.local(phase):
                copy.start()

    def finish(self):
        for phase in range(self.first, self.last + 1):
            for copy in self.remote(phase):
                copy.wait_send()


class Gather(Rider):
    remote_count, local_count = 18, 2

    def bind(self, here, inputs, outputs, scratch):
        super().bind(here, inputs, outputs, scratch)
        if self.share is not None:
            self.inputs_, self.outputs_ = self.share.inputs_, self.share.outputs_

    def __init__(self, shard, first=0, last=3, begun=None, columns=None, share=None):
        self.first, self.last, self.share = first, last, share
        self.columns = columns
        if share is not None:
            return
        if begun is None:
            split = shard.reshape(2, 2, shard.shape[0] // 4, shard.shape[1])
            places = lax.axis_size("wshard")
            self.inputs = (split,)
            self.outputs = (jax.ShapeDtypeStruct((places,) + split.shape, shard.dtype),)
            self.scratch = (pltpu.VMEM(split.shape, shard.dtype),)
        else:
            self.inputs = (begun,)
            self.outputs = (jax.ShapeDtypeStruct(begun.shape, begun.dtype),)
            self.aliases = ((0, 0),)

    def work(self, phase):
        if phase == 0 and self.share is None:
            copy = self.keep(1, self.inputs_[0], self.held[0])
            copy.start()
            copy.wait()

    def local(self, phase):
        if phase or self.share is not None:
            return []
        return [self.keep(0, self.held[0], self.outputs_[0].at[self.here.place])]

    def remote(self, phase):
        here, (target,) = self.here, self.outputs_
        offset, width = self.columns or (0, target.shape[-1])
        half = width // 2
        quarter = half // 2
        mine = span(offset + here.core * half, half)
        one = span(offset + here.core * half, quarter)
        two = span(offset + here.core * half + quarter, quarter)
        y, x = here.y, here.x
        if phase == 0:
            return [
                self.send(
                    step - 1,
                    self.inputs_[0].at[y, x, :, mine],
                    target.at[here.place, y, x, :, mine],
                    wshard=here.other(step),
                )
                for step in range(1, here.shards)
            ]
        found = []
        for step in range(1, here.shards):
            at = target.at[here.other(step)]
            if phase == 1:
                found.append((at.at[y, x, :, one], here.x_next))
                found.append((at.at[y, x, :, two], here.y_next))
            elif phase == 2:
                found.append((at.at[y, :, :, one], here.y_next))
                found.append((at.at[:, x, :, two], here.x_next))
            else:
                found.append((at.at[:, :, :, mine], here.core_next))
        start = {1: 3, 2: 9, 3: 15}[phase]
        return [
            self.send(start + index, ref, ref, seq=near) for index, (ref, near) in enumerate(found)
        ]


class WindowTokens(Rider):
    last = 1
    remote_count, local_count = 0, 2

    def __init__(self, tokens, depth):
        self.depth = depth
        self.reach = depth + 1
        self.remote_count = depth + 1
        self.rows = tokens.shape[0]
        self.inputs = (tokens,)
        rows = self.rows * (depth + 1) + PRE
        self.outputs = (jax.ShapeDtypeStruct((rows, tokens.shape[1]), tokens.dtype),)
        self.scratch = (pltpu.VMEM(tokens.shape, tokens.dtype),)

    def work(self, phase):
        if phase == 0:
            copy = self.keep(1, self.inputs_[0], self.held[0])
            copy.start()
            copy.wait()

    def local(self, phase):
        rows = pl.ds(self.depth * self.rows, self.rows)
        return [self.keep(0, self.held[0], self.outputs_[0].at[rows])] if phase == 0 else []

    def remote(self, phase):
        here, rows, depth = self.here, self.rows, self.depth
        (own,), (ext,) = self.inputs_, self.outputs_
        if phase == 1:
            start = pl.multiple_of((1 - here.core) * depth * rows + here.core * (depth - 2) * rows, 16)
            ref = ext.at[pl.ds((depth - 1) * rows, rows)]
            return [self.send(0, ext.at[pl.ds(start, rows)], ref, seq=here.core_next)]
        found = [
            self.send(
                hop - 1, own, ext.at[pl.ds((depth - hop) * rows, rows)], seq=here.along(hop)
            )
            for hop in range(2, depth + 1)
        ]
        found.append(
            self.send(
                depth,
                own.at[pl.ds(rows - PRE, PRE)],
                ext.at[pl.ds((depth + 1) * rows, PRE)],
                seq=here.along(depth + 1),
            )
        )
        return found


class WindowGrads(Rider):
    inside = 2
    last = 4
    remote_count, local_count = 4, 1

    def __init__(self, rows, columns, depth):
        assert depth == 2
        self.rows = rows
        self.reach = depth + 1
        self.outputs = (jax.ShapeDtypeStruct((rows, columns), bf16),)
        self.scratch = (
            pltpu.VMEM((rows, columns), bf16),
            pltpu.VMEM((rows, columns), bf16),
            pltpu.VMEM((PRE, columns), bf16),
        )

    def remote(self, phase):
        here, rows = self.here, self.rows
        grads, _ = self.inputs_
        given, near, far = self.held
        if phase == 0:
            return [self.send(0, grads.at[pl.ds(rows, rows)], given, seq=here.core_next)]
        if phase == 1 or phase == 2:
            half = pl.ds((2 - phase) * (rows // 2), rows // 2)
            return [self.send(phase, grads.at[half], near.at[half], seq=here.along(-2))]
        if phase == 3:
            return [self.send(3, grads.at[pl.ds(2 * rows, PRE)], far, seq=here.along(-3))]
        return []

    def run(self, phase):
        grads, own = self.inputs_
        given, near, far = self.held
        half = self.rows // 2
        chunk = 2 * PRE
        if phase == 1:
            self.remote(0)[0].wait_recv()
        if phase == 1 or phase == 2:

            @pl.when(self.here.core == 1)
            def join():
                def add(index, carry):
                    start = (2 - phase) * half + index * chunk
                    at = pl.ds(pl.multiple_of(start, chunk), chunk)
                    add_into(grads, at, given[at])
                    return carry

                lax.fori_loop(0, half // chunk, add, 0)

        if phase == 4:
            for earlier in (1, 2, 3):
                self.remote(earlier)[0].wait_recv()
            own[self.rows - PRE :, :] += far[...].astype(f32)
            first_core = (self.here.core == 0).astype(f32)

            def add_up(index, carry):
                at = pl.ds(pl.multiple_of(index * chunk, chunk), chunk)
                value = own[at] + near[at].astype(f32) + first_core * given[at].astype(f32)
                given[at] = value.astype(bf16)
                return carry

            lax.fori_loop(0, self.rows // chunk, add_up, 0)
            self.keep(0, given, self.outputs_[0]).start()
        elif phase == 5:
            self.keep(0, given, self.outputs_[0]).wait()
        else:
            self.remote(phase)[0].start()


def add_into(target, at, value):
    target[at] = (target[at].astype(f32) + value.astype(f32)).astype(bf16)


class SumFar(Rider):
    last = 3
    remote_count, local_count = 5, 2

    def __init__(self, grad=None, start=0, size=None, columns=None, offset=0):
        places = lax.axis_size("wshard")
        self.inside = int(grad is None)
        self.offset = offset
        if not self.inside:
            columns = grad.shape[-1]
            grad = grad.reshape(places, 2, 2, grad.shape[0] // places // 4, columns)
            size = grad.shape[3] if size is None else size
            self.inputs = (grad,)
        self.rows = pl.ds(start, size)
        half = columns // 2
        quarter = half // 2
        self.outputs = (jax.ShapeDtypeStruct((places, size, half), bf16),)
        self.scratch = (
            pltpu.VMEM((places, 2, 2, size, half), bf16),
            pltpu.VMEM((places, 2, 2, size, half), bf16),
            pltpu.VMEM((places, 2, size, quarter), bf16),
            pltpu.VMEM((places, 2, size, quarter), bf16),
            pltpu.VMEM((places, size, quarter), bf16),
            pltpu.VMEM((places, size, quarter), bf16),
        )
        self.half = half

    def local(self, phase):
        here, held = self.here, self.held[0]
        if phase == 0:
            mine = span(self.offset + here.core * self.half, self.half)
            return [self.keep(0, self.inputs_[0].at[:, :, :, self.rows, mine], held)]
        if phase == 3:
            return [self.keep(1, held.at[:, here.y, here.x], self.outputs_[0])]
        return []

    def remote(self, phase):
        here = self.here
        y, x = here.y, here.x
        held, core_in, far_a, far_b, next_a, next_b = self.held
        one, two = pl.ds(0, self.half // 2), pl.ds(self.half // 2, self.half // 2)
        if phase == 0:
            yours = span(self.offset + (1 - here.core) * self.half, self.half)
            ref = self.inputs_[0].at[:, :, :, self.rows, yours]
            return [self.send(0, ref, core_in, seq=here.core_next)]
        if phase == 1:
            return [
                self.send(1, held.at[:, :, 1 - x, :, one], far_a, seq=here.x_next),
                self.send(2, held.at[:, 1 - y, :, :, two], far_b, seq=here.y_next),
            ]
        if phase == 2:
            return [
                self.send(3, held.at[:, 1 - y, x, :, one], next_a, seq=here.y_next),
                self.send(4, held.at[:, y, 1 - x, :, two], next_b, seq=here.x_next),
            ]
        return []

    def work(self, phase):
        y, x = self.here.y, self.here.x
        held, core_in, far_a, far_b, next_a, next_b = self.held
        places = held.shape[0]
        one, two = slice(0, self.half // 2), slice(self.half // 2, self.half)
        every = slice(None)
        if phase == 1:

            def add(index, carry):
                at = (index // 4, (index // 2) % 2, index % 2)
                add_into(held, at, core_in[at])
                return carry

            lax.fori_loop(0, 4 * places, add, 0)
        elif phase == 2:

            def add(index, carry):
                place, side = index // 2, index % 2
                add_into(held, (place, side, x, every, one), far_a[place, side])
                add_into(held, (place, y, side, every, two), far_b[place, side])
                return carry

            lax.fori_loop(0, 2 * places, add, 0)
        elif phase == 3:

            def add(place, carry):
                add_into(held, (place, y, x, every, one), next_a[place])
                add_into(held, (place, y, x, every, two), next_b[place])
                return carry

            lax.fori_loop(0, places, add, 0)


class SumNear(Rider):
    last = 3
    local_count = 2

    def __init__(self, sums=None, after=None, stop=False, total=None):
        self.after, self.stop, self.resume = after, stop, total is not None
        if self.resume:
            (size, half), places = total.shape, lax.axis_size("wshard")
            self.inputs = (total,)
        else:
            places, size, half = (sums if after is None else after.outputs[0]).shape
            self.inputs = (sums,) if after is None else ()
        self.remote_count = places - 1 + 5
        self.half = half
        self.outputs = (jax.ShapeDtypeStruct((2, 2, size, 2 * half), bf16),)
        if stop:
            self.last = 1
            self.outputs = (jax.ShapeDtypeStruct((size, half), bf16),)
        arrived = (1, 16, 128) if self.resume else (places, size, half)
        self.scratch = (pltpu.VMEM(arrived, bf16), pltpu.VMEM((size, half), bf16))

    def bind(self, here, inputs, outputs, scratch):
        super().bind(here, inputs, outputs, scratch)
        if self.after is not None:
            self.inputs_ = self.after.outputs_

    def local(self, phase):
        here = self.here
        arrived, total = self.held
        if phase == 0 and self.resume:
            return [self.keep(0, self.inputs_[0], total)]
        if phase == 0:
            return [self.keep(0, self.inputs_[0].at[here.place], arrived.at[0])]
        if phase == 1 and self.stop:
            return [self.keep(1, total, self.outputs_[0])]
        if phase == 1:
            mine = span(here.core * self.half, self.half)
            return [self.keep(1, total, self.outputs_[0].at[here.y, here.x, :, mine])]
        return []

    def remote(self, phase):
        here = self.here
        y, x = here.y, here.x
        arrived, total = self.held
        (out,) = self.outputs_
        quarter = self.half // 2
        others = here.shards - 1
        if (phase == 0 and self.resume) or (phase == 1 and self.stop):
            return []
        if phase == 0:
            return [
                self.send(
                    step - 1,
                    self.inputs_[0].at[here.other(step)],
                    arrived.at[step],
                    wshard=here.other(step),
                )
                for step in range(1, here.shards)
            ]
        one = span(here.core * self.half, quarter)
        two = span(here.core * self.half + quarter, quarter)
        if phase == 1:
            held_one, held_two = total.at[:, pl.ds(0, quarter)], total.at[:, pl.ds(quarter, quarter)]
            return [
                self.send(others, held_one, out.at[y, x, :, one], seq=here.y_next),
                self.send(others + 1, held_two, out.at[y, x, :, two], seq=here.x_next),
            ]
        if phase == 2:
            both_one, both_two = out.at[:, x, :, one], out.at[y, :, :, two]
            return [
                self.send(others + 2, both_one, both_one, seq=here.x_next),
                self.send(others + 3, both_two, both_two, seq=here.y_next),
            ]
        ref = out.at[:, :, :, span(here.core * self.half, self.half)]
        return [self.send(others + 4, ref, ref, seq=here.core_next)]

    def work(self, phase):
        if phase == 1 and not self.resume:
            arrived, total = self.held
            value = arrived[0].astype(f32)
            for step in range(1, arrived.shape[0]):
                value = value + arrived[step].astype(f32)
            total[...] = value.astype(bf16)


class SumPlace(Rider):
    last = 2
    local_count = 2

    def __init__(self, grad):
        places = lax.axis_size("wshard")
        size, columns = grad.shape[0] // places // 4, grad.shape[1]
        self.half = columns // 2
        self.remote_count = places
        self.inputs = (grad.reshape(places, 2, 2, size, columns),)
        part = (2, 2, size, self.half)
        self.outputs = (jax.ShapeDtypeStruct(part, bf16),)
        self.scratch = (
            pltpu.VMEM((places,) + part, bf16),
            pltpu.VMEM((places,) + part, bf16),
            pltpu.VMEM((places - 1,) + part, bf16),
        )

    def local(self, phase):
        held, core_in, _ = self.held
        if phase == 0:
            mine = span(self.here.core * self.half, self.half)
            return [self.keep(0, self.inputs_[0].at[:, :, :, :, mine], held)]
        if phase == 2:
            return [self.keep(1, core_in.at[0], self.outputs_[0])]
        return []

    def remote(self, phase):
        here = self.here
        held, core_in, arrived = self.held
        if phase == 0:
            yours = span((1 - here.core) * self.half, self.half)
            return [self.send(0, self.inputs_[0].at[:, :, :, :, yours], core_in, seq=here.core_next)]
        if phase == 1:
            return [
                self.send(
                    step,
                    held.at[here.other(step)],
                    arrived.at[step - 1],
                    wshard=here.other(step),
                )
                for step in range(1, here.shards)
            ]
        return []

    def work(self, phase):
        held, core_in, arrived = self.held
        if phase == 1:

            def add(index, carry):
                at = (index // 4, (index // 2) % 2, index % 2)
                add_into(held, at, core_in[at])
                return carry

            lax.fori_loop(0, 4 * held.shape[0], add, 0)
        elif phase == 2:

            def gather_up(index, carry):
                at = (index // 2, index % 2)
                value = held[(self.here.place,) + at].astype(f32)
                for step in range(arrived.shape[0]):
                    value = value + arrived[(step,) + at].astype(f32)
                core_in[(0,) + at] = value.astype(bf16)
                return carry

            lax.fori_loop(0, 4, gather_up, 0)


class SumSpread(Rider):
    last = 5
    remote_count, local_count = 9, 2

    def __init__(self, sums):
        _, _, size, half = sums.shape
        self.half = half
        quarter = half // 2
        self.inputs = (sums,)
        self.outputs = (jax.ShapeDtypeStruct((2, 2, size, 2 * half), bf16),)
        self.scratch = (
            pltpu.VMEM((2, 2, size, half), bf16),
            pltpu.VMEM((2, size, quarter), bf16),
            pltpu.VMEM((2, size, quarter), bf16),
            pltpu.VMEM((size, quarter), bf16),
            pltpu.VMEM((size, quarter), bf16),
        )

    def local(self, phase):
        here, held = self.here, self.held[0]
        if phase == 0:
            return [self.keep(0, self.inputs_[0], held)]
        if phase == 3:
            mine = span(here.core * self.half, self.half)
            return [self.keep(1, held.at[here.y, here.x], self.outputs_[0].at[here.y, here.x, :, mine])]
        return []

    def remote(self, phase):
        here, (out,) = self.here, self.outputs_
        y, x, quarter = here.y, here.x, self.half // 2
        held, far_a, far_b, next_a, next_b = self.held
        one, two = pl.ds(0, quarter), pl.ds(quarter, quarter)
        out_one = span(here.core * self.half, quarter)
        out_two = span(here.core * self.half + quarter, quarter)
        if phase == 1:
            return [
                self.send(0, held.at[:, 1 - x, :, one], far_a, seq=here.x_next),
                self.send(1, held.at[1 - y, :, :, two], far_b, seq=here.y_next),
            ]
        if phase == 2:
            return [
                self.send(2, held.at[1 - y, x, :, one], next_a, seq=here.y_next),
                self.send(3, held.at[y, 1 - x, :, two], next_b, seq=here.x_next),
            ]
        if phase == 3:
            return [
                self.send(4, held.at[y, x, :, one], out.at[y, x, :, out_one], seq=here.y_next),
                self.send(5, held.at[y, x, :, two], out.at[y, x, :, out_two], seq=here.x_next),
            ]
        if phase == 4:
            both_one, both_two = out.at[:, x, :, out_one], out.at[y, :, :, out_two]
            return [
                self.send(6, both_one, both_one, seq=here.x_next),
                self.send(7, both_two, both_two, seq=here.y_next),
            ]
        if phase == 5:
            ref = out.at[:, :, :, span(here.core * self.half, self.half)]
            return [self.send(8, ref, ref, seq=here.core_next)]
        return []

    def work(self, phase):
        y, x = self.here.y, self.here.x
        held, far_a, far_b, next_a, next_b = self.held
        every = slice(None)
        one, two = slice(0, self.half // 2), slice(self.half // 2, self.half)
        if phase == 2:
            for side in range(2):
                add_into(held, (side, x, every, one), far_a[side])
                add_into(held, (y, side, every, two), far_b[side])
        elif phase == 3:
            add_into(held, (y, x, every, one), next_a[...])
            add_into(held, (y, x, every, two), next_b[...])


def call(
    kernel,
    grid,
    args,
    in_specs,
    out_specs,
    out_shape,
    scratch_shapes=(),
    riders=(),
    table=None,
    collective_id=None,
    vmem=48,
    flops=0,
    traffic=0,
    name=None,
):
    anywhere = pl.BlockSpec(memory_space=pl.ANY)
    sizes = [len(args), len(out_shape), len(scratch_shapes)]
    rider_in = [array for rider in riders for array in rider.inputs]
    rider_out = [shape for rider in riders for shape in rider.outputs]
    rider_scratch = [entry for rider in riders for entry in rider.semaphores() + list(rider.scratch)]
    aliases = {}
    at_in, at_out = sizes[0], sizes[1]
    for rider in riders:
        for source, target in rider.aliases:
            aliases[at_in + source] = at_out + target
        at_in += len(rider.inputs)
        at_out += len(rider.outputs)

    def body(*refs):
        refs = list(refs)

        def take(count):
            found = refs[:count]
            del refs[:count]
            return found

        own_in, their_in = take(sizes[0]), take(len(rider_in))
        own_out, their_out = take(sizes[1]), take(len(rider_out))
        own_scratch, their_scratch = take(sizes[2]), refs
        if not riders:
            return kernel(*own_in, *own_out, *own_scratch)
        here = Here()
        step = pl.program_id(0)
        reach = max(rider.reach for rider in riders)

        @pl.when(step == 0)
        def start():
            here.meet(reach)

        for rider in riders:
            counts = (len(rider.inputs), len(rider.outputs), 3 + len(rider.scratch))
            parts = []
            for pool, count in zip((their_in, their_out, their_scratch), counts):
                parts.append(pool[:count])
                del pool[:count]
            if rider.inside:
                parts[0] = own_scratch[-rider.inside :]
            rider.bind(here, *parts)

        def run(events):
            for which, phase in events:
                riders[which].run(phase)

        for at in sorted(table):
            if at < grid:

                @pl.when(step == at)
                def early():
                    run(table[at])

        kernel(*own_in, *own_out, *own_scratch)

        @pl.when(step == grid - 1)
        def late():
            for at in sorted(table):
                if at >= grid:
                    run(table[at])
            for rider in riders:
                rider.finish()

    found = pl.pallas_call(
        body,
        grid=(grid,),
        in_specs=list(in_specs) + [anywhere] * len(rider_in),
        out_specs=list(out_specs) + [anywhere] * len(rider_out),
        out_shape=list(out_shape) + rider_out,
        scratch_shapes=list(scratch_shapes) + rider_scratch,
        input_output_aliases=aliases,
        compiler_params=pltpu.CompilerParams(
            dimension_semantics=("arbitrary",),
            vmem_limit_bytes=vmem << 20,
            **({"collective_id": collective_id, "has_side_effects": True} if riders else {}),
        ),
        cost_estimate=pl.CostEstimate(flops=flops, bytes_accessed=traffic, transcendentals=0),
        name=name,
    )(*args, *rider_in)
    own, found = found[: sizes[1]], found[sizes[1] :]
    carried = []
    for rider in riders:
        carried.append(found[: len(rider.outputs)])
        found = found[len(rider.outputs) :]
    return own, carried


def whole_rows(gathered):
    return gathered.reshape(-1, gathered.shape[-1])


def finish_sum(part):
    count = lax.axis_size("seq")
    bit = 8
    while bit < count:
        pairs = [(source, source ^ bit) for source in range(count)]
        part = (part.astype(f32) + lax.ppermute(part, "seq", pairs).astype(f32)).astype(bf16)
        bit *= 2
    return part


def mid_kernel(
    before,
    x_ref,
    o_ref,
    hid_ref,
    cot_ref,
    info_ref,
    params_ref,
    mats_in,
    ffn_in,
    down_in,
    out_ref,
    y_ref,
    h2_ref,
    u_ref,
    dab_ref,
    dd_ref,
    dyw_ref,
    dgate_ref,
    do_ref,
    dres_ref,
    dhg_ref,
    dfg_ref,
    mats_ref,
    ffn_ref,
    down_ref,
    sems,
):
    step = pl.program_id(0)
    inner = down_ref.shape[0]
    copies = [
        pltpu.make_async_copy(source, target, sems.at[index])
        for index, (source, target) in enumerate(
            ((mats_in, mats_ref), (ffn_in, ffn_ref), (down_in, down_ref))
        )
    ]

    @pl.when(step == 0)
    def begin():
        for copy in copies:
            copy.start()
        dhg_ref[...] = jnp.zeros_like(dhg_ref)
        dfg_ref[...] = jnp.zeros_like(dfg_ref)
        copies[0].wait()

    hgain, fgain = params_ref[2:3, :], params_ref[3:4, :]
    gate_pre = mm(hid_ref[...], mats_ref[:, :D])
    gate = jax.nn.sigmoid(gate_pre)
    gate_silu = gate_pre * gate

    def head_scale(part):
        return lax.rsqrt(jnp.mean(part * part, axis=-1, keepdims=True) + 1e-05)

    mixed = o_ref[...]
    normal = in_heads(lambda part: part * head_scale(part), mixed)
    scaled = normal * hgain
    y = (scaled * gate_silu).astype(bf16)
    y_ref[...] = y
    x1 = x_ref[...].astype(f32) + mm(y, mats_ref[:, D:])
    x1_scale = lax.rsqrt(jnp.mean(x1 * x1, axis=-1, keepdims=True) + 1e-06)
    h2 = (x1 * x1_scale * fgain).astype(bf16)
    h2_ref[...] = h2
    info = info_ref[...]
    live = is_live(info, rows_from(info, before + step * ROWS, ROWS)).astype(f32)
    grad_out = live * cot_ref[...].astype(f32)
    dd = grad_out.astype(bf16)
    dd_ref[...] = dd

    @pl.when(step == 0)
    def rest():
        copies[1].wait()
        copies[2].wait()

    forward = jnp.zeros_like(x1)
    dh2 = jnp.zeros_like(x1)
    for at in range(0, inner, CH):
        one, two = slice(at, at + CH), slice(inner + at, inner + at + CH)
        a = mm(h2, ffn_ref[:, one])
        b = mm(h2, ffn_ref[:, two])
        sig = jax.nn.sigmoid(a)
        silu = a * sig
        u = (silu * b).astype(bf16)
        u_ref[:, one] = u
        forward = forward + mm(u, down_ref[one, :])
        du = mm_t(dd, down_ref[one, :])
        da = (du * b * (sig + silu * (1.0 - sig))).astype(bf16)
        db = (du * silu).astype(bf16)
        dab_ref[:, one] = da
        dab_ref[:, two] = db
        dh2 = dh2 + mm_t(da, ffn_ref[:, one]) + mm_t(db, ffn_ref[:, two])
    out_ref[...] = (live * (x1 + forward)).astype(bf16)
    x1_normal = x1 * x1_scale
    dfg_ref[...] += jnp.sum(dh2 * x1_normal, axis=0, keepdims=True)
    dh2 = dh2 * fgain
    dx1 = grad_out + x1_scale * (
        dh2 - x1_normal * jnp.mean(dh2 * x1_normal, axis=-1, keepdims=True)
    )
    dres_ref[...] = dx1
    dyw = dx1.astype(bf16)
    dyw_ref[...] = dyw
    dy = mm_t(dyw, mats_ref[:, D:])
    dgate_ref[...] = (dy * scaled * (gate + gate_silu * (1.0 - gate))).astype(bf16)
    dscaled = dy * gate_silu
    dhg_ref[...] += jnp.sum(dscaled * normal, axis=0, keepdims=True)

    def head_back(part, part_normal, grad):
        return head_scale(part) * (
            grad - part_normal * jnp.mean(grad * part_normal, axis=-1, keepdims=True)
        )

    do_ref[...] = in_heads(head_back, mixed, normal, dscaled * hgain).astype(bf16)


def mid(x, mixed, hidden, first_own, cotangent, info, params, mats, ffn, down):
    rows = x.shape[0]
    inner = down.shape[0]
    shape = jax.ShapeDtypeStruct

    def block(columns):
        return pl.BlockSpec((ROWS, columns), lambda step: (step, 0))

    row = pl.BlockSpec((1, D), lambda step: (0, 0))
    anywhere = pl.BlockSpec(memory_space=pl.ANY)
    outs = [
        shape((rows, D), bf16),
        shape((rows, D), bf16),
        shape((rows, D), bf16),
        shape((rows, inner), bf16),
        shape((rows, 2 * inner), bf16),
        shape((rows, D), bf16),
        shape((rows, D), bf16),
        shape((rows, D), bf16),
        shape((rows, D), bf16),
        shape((rows, D), f32),
    ]
    found, _ = call(
        functools.partial(mid_kernel, first_own * ROWS),
        rows // ROWS,
        (x, mixed, hidden, cotangent, info, params, mats, ffn, down),
        [
            block(D),
            block(D),
            pl.BlockSpec((ROWS, D), lambda step: (step + first_own, 0)),
            block(D),
            pl.BlockSpec(info.shape, lambda step: (0, 0)),
            pl.BlockSpec(params.shape, lambda step: (0, 0)),
            anywhere,
            anywhere,
            anywhere,
        ],
        [block(out.shape[1]) for out in outs] + [row, row],
        outs + [shape((1, D), f32)] * 2,
        [
            pltpu.VMEM(mats.shape, bf16),
            pltpu.VMEM(ffn.shape, bf16),
            pltpu.VMEM(down.shape, bf16),
            pltpu.SemaphoreType.DMA((3,)),
        ],
        vmem=62,
        flops=8 * rows * D * (D + 3 * inner // 2),
        traffic=50 << 20,
        name="mid",
    )
    return found


def mid_grads_kernel(
    hid_ref, y_ref, h2_ref, u_ref, dab_ref, dd_ref, dyw_ref, dgate_ref,
    down_ref, ffn_ref, mats_ref, hid_t, y_t, h2_t,
):
    step = pl.program_id(0)
    width = ffn_ref.shape[1]

    @pl.when(step == 0)
    def begin():
        hid_t[...] = hid_ref[...].T
        y_t[...] = y_ref[...].T
        h2_t[...] = h2_ref[...].T

    ffn_ref[...] = mm(h2_t[...], dab_ref[...]).astype(bf16)
    down_ref[...] = mm(u_ref[...].T, dd_ref[...]).astype(bf16)
    for index in range(2 * D // width):
        at = width * index

        @pl.when(step == index)
        def mats():
            if at < D:
                mats_ref[...] = mm(hid_t[...], dgate_ref[:, at : at + width]).astype(bf16)
            else:
                mats_ref[...] = mm(y_t[...], dyw_ref[:, at - D : at - D + width]).astype(bf16)


def mid_grads(hidden, first_own, y, h2, u, dab, dd, dyw, dgate):
    rows, inner = u.shape
    width = 2 * CH
    steps = 2 * inner // width
    shape = jax.ShapeDtypeStruct

    def fixed(array):
        return pl.BlockSpec(array.shape, lambda step: (0, 0))

    found, _ = call(
        mid_grads_kernel,
        steps,
        (hidden, y, h2, u, dab, dd, dyw, dgate),
        [
            pl.BlockSpec((rows, D), lambda step: (first_own, 0)),
            fixed(y),
            fixed(h2),
            pl.BlockSpec((rows, inner // steps), lambda step: (0, step)),
            pl.BlockSpec((rows, width), lambda step: (0, step)),
            fixed(dd),
            fixed(dyw),
            fixed(dgate),
        ],
        [
            pl.BlockSpec((inner // steps, D), lambda step: (step, 0)),
            pl.BlockSpec((D, width), lambda step: (0, step)),
            pl.BlockSpec((D, width), lambda step: (0, jnp.minimum(step, 2 * D // width - 1))),
        ],
        [shape((inner, D), bf16), shape((D, 2 * inner), bf16), shape((D, 2 * D), bf16)],
        [pltpu.VMEM((D, rows), bf16)] * 3,
        vmem=62,
        flops=2 * rows * D * (2 * D + 3 * inner),
        traffic=40 << 20,
        name="mid_grads",
    )
    return found


def front_grads_kernel(
    hid_ref, pre_ref, qpre_ref, dkv_ref, dkvpre_ref, dq_ref, dqpre_ref, dbp_ref, small_ref,
    hid_t, pre_t, qpre_t, out_ref,
):
    step = pl.program_id(0)
    width = EXTRA
    split = out_ref.shape[:-1]
    first_query = 2 * D // width
    column = jnp.where(
        step < first_query,
        D + step * width,
        jnp.where(step < 3 * D // width, (step - first_query) * width, 3 * D),
    )
    at_step = pl.ds(pl.multiple_of(column, width), width)

    def put(value):
        out_ref[:, :, :, :, at_step] = value.astype(bf16).reshape(split + (width,))
    own = dq_ref.shape[0]
    main = hid_t.shape[1]

    @pl.when(step == 0)
    def begin():
        hid_t[...] = hid_ref[...].T
        pre_t[...] = pre_ref[...].T
        qpre_t[...] = qpre_ref[...].T

    @pl.when((step >= first_query) & (step < 3 * D // width))
    def queries():
        at = pl.ds(pl.multiple_of((step - first_query) * width, width), width)
        put(mm(hid_t[:, main - own :], dq_ref[:, at]) + mm(qpre_t[...], dqpre_ref[:, at]))

    @pl.when(step < first_query)
    def others():
        put(mm(hid_t[...], dkv_ref[...]) + mm(pre_t[...], dkvpre_ref[...]))

    @pl.when(step == 3 * D // width)
    def rest():
        lane = lax.broadcasted_iota(jnp.int32, (D, SMALL), 1)
        gates = mm(hid_t[...], dbp_ref[...]).astype(bf16)
        first = jnp.where(lane < HEADS, gates, small_ref[...])
        put(jnp.concatenate([first, jnp.zeros((D, width - SMALL), bf16)], axis=1))


def front_grads(hidden, dkv, dq, dqpre, dbp, small, **riding):
    own = dq.shape[0]
    main = dbp.shape[0]
    width = EXTRA
    blocks = 3 * D // width

    def fixed(array):
        return pl.BlockSpec(array.shape, lambda step: (0, 0))

    def kv_block(step):
        return jnp.minimum(step, 2 * D // width - 1)

    places = lax.axis_size("wshard")
    _, carried = call(
        front_grads_kernel,
        blocks + 1,
        (hidden, hidden, hidden, dkv, dkv, dq, dqpre, dbp, small),
        [
            pl.BlockSpec((main, D), lambda step: (0, 0)),
            pl.BlockSpec((PRE, D), lambda step: (main // PRE, 0)),
            pl.BlockSpec((PRE, D), lambda step: ((main - own) // PRE - 1, 0)),
            pl.BlockSpec((main, width), lambda step: (0, kv_block(step))),
            pl.BlockSpec((PRE, width), lambda step: (main // PRE, kv_block(step))),
            fixed(dq),
            fixed(dqpre),
            fixed(dbp),
            fixed(small),
        ],
        [],
        [],
        [
            pltpu.VMEM((D, main), bf16),
            pltpu.VMEM((D, PRE), bf16),
            pltpu.VMEM((D, PRE), bf16),
            pltpu.VMEM((places, 2, 2, D // places // 4, 3 * D + EXTRA), bf16),
        ],
        vmem=62,
        flops=2 * D * D * (2 * main + own),
        traffic=25 << 20,
        name="end",
        **riding,
    )
    return carried


def widen_kernel(down_in, ffn0_in, ffn1_in, mats_in, k_in, v_in, q_in, down, gate, up, og, out, qkv):
    down[...] = down_in[0, 0].astype(f32)
    for source, start in ((ffn0_in, 0), (ffn1_in, ffn0_in.shape[2])):
        rows = slice(start, start + source.shape[2])
        inner = gate.shape[1]
        gate[rows, :] = source[0, 0, :, :inner].astype(f32)
        up[rows, :] = source[0, 0, :, inner:].astype(f32)
    og[...] = mats_in[0, 0, :, :D].astype(f32)
    out[...] = mats_in[0, 0, :, D:].astype(f32)
    for index, source in enumerate((q_in, k_in, v_in)):
        qkv[:, D * index : D * (index + 1)] = source[0, 0].astype(f32)


def widen(down, ffn0, ffn1, mats, keys, values, queries):
    ins = (down, ffn0, ffn1, mats, keys, values, queries)
    rows, inner = mats.shape[2], ffn0.shape[3] // 2
    widths = [(down.shape[2], D), (rows, inner), (rows, inner), (rows, D), (rows, D), (rows, 3 * D)]
    found, _ = call(
        widen_kernel,
        4,
        ins,
        [
            pl.BlockSpec((1, 1) + part.shape[2:], lambda step: (step // 2, step % 2, 0, 0))
            for part in ins
        ],
        [pl.BlockSpec(width, lambda step: (step, 0)) for width in widths],
        [jax.ShapeDtypeStruct((4 * height, width), f32) for height, width in widths],
        vmem=62,
        traffic=25 << 20,
        name="widen",
    )
    return found


def on_device(
    tokens,
    slot_lengths,
    live_lengths,
    norm_gain,
    w_qkv,
    w_beta,
    w_outgate,
    conv_weight,
    ridge,
    head_gain,
    w_out,
    ffn_gain,
    w_gate,
    w_up,
    w_down,
    cotangent,
):
    row_count = tokens.shape[1]
    depth = (WINDOW + row_count - 1) // row_count
    halo_rows = depth * row_count
    main_rows = halo_rows + row_count
    shards = lax.axis_size("wshard")
    shard_rows = norm_gain.shape[0]
    tap_columns = TAPS * conv_weight.shape[1] // shard_rows

    own_tokens = tokens[0]
    small = jnp.concatenate(
        [
            w_beta,
            jnp.stack([norm_gain, ridge, head_gain, ffn_gain]).T,
            conv_weight.reshape(TAPS, 3, shard_rows).transpose(2, 1, 0).reshape(shard_rows, -1),
        ],
        axis=1,
    )
    small = jnp.pad(small, ((0, 0), (0, EXTRA - small.shape[1])))
    out_mats = jnp.concatenate([w_outgate, w_out], axis=1)
    ffn_mats = jnp.concatenate([w_gate, w_up], axis=1)

    one = Gather(jnp.concatenate([w_qkv, small], axis=1), columns=(0, 2 * D))
    two = Gather(None, columns=(2 * D, D + EXTRA), share=one)
    riders = [one, two, WindowTokens(own_tokens, depth), Gather(ffn_mats, 0, 0)]
    events = [(2, 0), (0, 0), (1, 0), (0, 1), (1, 1), (3, 0), (2, 1), (0, 2), (1, 2), (0, 3), (1, 3), (0, 4), (1, 4), (2, 2), (3, 1)]
    _, ((w_front,), _, (ext_tokens,), (ffn_in,)) = call(
        lambda: None, 1, (), [], [], [], riders=riders, table={0: events}, collective_id=0, name="begin"
    )
    w_front = whole_rows(w_front)
    rank = lax.axis_index("seq")
    info = slot_info(slot_lengths[0], live_lengths[0], rank * row_count - halo_rows)

    (hidden, kv_in, q_in, q_pre, queries, keys, values, beta, params, taps), ((ffn_in,), (mats,), (all_down,)) = front(
        ext_tokens,
        info,
        w_front,
        row_count,
        riders=[Gather(None, 1, 2, ffn_in), Gather(out_mats, 0, 0), Gather(w_down, 0, 0)],
        table={0: [(0, 1), (1, 0), (2, 0)], 4: [(0, 2)], 99: [(1, 1), (2, 1), (0, 3)]},
        collective_id=1,
    )
    (mixed, image0, image1), ((ffn_in,), (mats,), (all_down,)) = attn_fwd(
        queries,
        keys,
        values,
        beta,
        info,
        w_front,
        riders=[Gather(None, 3, 3, ffn_in), Gather(None, 1, 3, mats), Gather(None, 1, 3, all_down)],
        table={
            0: [(1, 1), (2, 1), (0, 3)],
            2: [(1, 2)],
            3: [(2, 2)],
            5: [(1, 3)],
            99: [(2, 3), (0, 4), (1, 4), (2, 4)],
        },
        collective_id=2,
    )
    mats, ffn_in, all_down = (whole_rows(part) for part in (mats, ffn_in, all_down))
    first_own = halo_rows // ROWS
    output, y, h2, u, d_ab, d_down_in, d_out_in, d_gate, d_mixed, d_xout, d_ghead, d_gffn = mid(
        own_tokens,
        mixed,
        hidden,
        first_own,
        cotangent[0],
        info,
        params,
        mats,
        ffn_in,
        all_down,
    )
    grad_down, grad_ffn, grad_mats = mid_grads(
        hidden, halo_rows // row_count, y, h2, u, d_ab, d_down_in, d_out_in, d_gate
    )

    part_rows = shard_rows // 8
    (d_query, d_key, d_value, d_beta, d_ridge), ((sum_down,), (sum_ffn0,), (sum_mats,)) = attn_bwd(
        queries,
        keys,
        values,
        beta,
        info,
        w_front,
        image0,
        image1,
        d_mixed,
        riders=[SumFar(grad_down), SumFar(grad_ffn, 0, part_rows), SumPlace(grad_mats)],
        table={
            0: [(2, 0), (0, 0), (1, 0)],
            1: [(2, 1), (0, 1)],
            2: [(1, 1)],
            4: [(0, 2)],
            7: [(1, 2)],
            99: [(0, 3), (1, 3), (2, 2), (2, 3), (0, 4), (1, 4)],
        },
        collective_id=3,
    )
    (
        (d_kv_in, d_q_in, d_q_pre, d_beta_pre, d_gain, d_taps),
        ((sum_down,), (sum_ffn0,), (sum_ffn1,), (total_mats,), (d_tokens,)),
    ) = back(
        ext_tokens,
        kv_in,
        info,
        q_in,
        q_pre,
        d_key,
        d_value,
        d_query,
        beta,
        d_beta,
        d_gate,
        d_xout,
        params,
        w_front,
        mats,
        taps,
        riders=[
            SumNear(sum_down, stop=True),
            SumNear(sum_ffn0, stop=True),
            SumFar(grad_ffn, part_rows, part_rows),
            SumSpread(sum_mats),
            WindowGrads(row_count, D, depth),
        ],
        table={
            0: [(2, 0), (3, 0), (3, 1), (0, 0), (1, 0)],
            1: [(3, 2), (2, 1)],
            3: [(3, 3), (2, 2)],
            4: [(4, 0), (3, 4)],
            5: [(4, 1), (0, 1), (1, 1), (3, 5)],
            6: [(4, 2), (2, 3)],
            99: [(4, 3), (2, 4), (0, 2), (1, 2), (3, 6), (4, 4), (4, 5)],
        },
        collective_id=4,
    )
    d_small = jnp.concatenate(
        [
            jnp.zeros((D, HEADS), f32),
            d_gain.reshape(D, 1),
            d_ridge,
            d_ghead.reshape(D, 1),
            d_gffn.reshape(D, 1),
            d_taps.reshape(TAPS, shards, 3, -1).transpose(1, 3, 2, 0).reshape(D, tap_columns),
        ],
        axis=1,
    ).astype(bf16)
    d_small = jnp.pad(d_small, ((0, 0), (0, SMALL - d_small.shape[1])))
    rows = shard_rows // 4
    fars = [
        SumFar(None, 0, rows, D, D),
        SumFar(None, 0, rows, D, 2 * D),
        SumFar(None, 0, rows, D, 0),
        SumFar(None, 0, rows, EXTRA, 3 * D),
    ]
    riders = [SumNear(sum_ffn1)] + fars + [SumNear(after=far) for far in fars]
    riders += [SumNear(total=sum_down), SumNear(total=sum_ffn0)]
    late = [
        (3, 0), (4, 0), (9, 3), (10, 3), (2, 1), (1, 2), (3, 1), (4, 1), (2, 2), (1, 3), (1, 4), (5, 0),
        (3, 2), (4, 2), (0, 1), (2, 3), (2, 4), (6, 0), (5, 1), (3, 3), (4, 3), (3, 4), (4, 4),
        (7, 0), (8, 0), (0, 2), (6, 1), (5, 2), (6, 2), (5, 3), (7, 1), (8, 1), (6, 3), (0, 3),
        (7, 2), (8, 2), (7, 3), (8, 3), (5, 4), (6, 4), (0, 4), (7, 4), (8, 4),
        (9, 4), (10, 4),
    ]
    carried = front_grads(
        hidden,
        d_kv_in,
        d_q_in,
        d_q_pre,
        d_beta_pre,
        d_small,
        riders=riders,
        table={
            0: [(0, 0), (9, 0), (10, 0), (9, 1), (10, 1)],
            2: [(9, 2), (10, 2), (1, 0)],
            4: [(1, 1), (2, 0)],
            99: late,
        },
        collective_id=5,
    )
    (total_ffn1,), _, _, _, _, (total_k,), (total_v,), (total_q,), (total_small,) = carried[:9]
    (total_down,), (total_ffn0,) = carried[9:]
    sums = (total_down, total_ffn0, total_ffn1, total_mats, total_k, total_v, total_q)
    t_down, t_gate, t_up, t_og, t_out, t_qkv = widen(*(finish_sum(part) for part in sums))
    t_small = finish_sum(total_small)[..., :SMALL].reshape(shard_rows, SMALL).astype(f32)
    t_taps = t_small[:, HEADS + 4 : HEADS + 4 + tap_columns]
    return (
        output[None],
        d_tokens[None],
        t_small[:, HEADS],
        t_qkv,
        t_small[:, :HEADS],
        t_og,
        t_taps.reshape(shard_rows, 3, TAPS).transpose(2, 1, 0).reshape(TAPS, -1),
        t_small[:, HEADS + 1],
        t_small[:, HEADS + 2],
        t_out,
        t_small[:, HEADS + 3],
        t_gate,
        t_up,
        t_down,
    )


def solution(mesh):
    return jax.shard_map(
        on_device,
        mesh=mesh,
        in_specs=(
            P("wshard", "seq", None),
            P("wshard", None),
            P("wshard", None),
            P("wshard"),
            P("wshard", None),
            P("wshard", None),
            P("wshard", None),
            P(None, "wshard"),
            P("wshard"),
            P("wshard"),
            P("wshard", None),
            P("wshard"),
            P("wshard", None),
            P("wshard", None),
            P("wshard", None),
            P("wshard", "seq", None),
        ),
        out_specs=(
            P("wshard", "seq", None),
            P("wshard", "seq", None),
            P("wshard"),
            P("wshard", None),
            P("wshard", None),
            P("wshard", None),
            P(None, "wshard"),
            P("wshard"),
            P("wshard"),
            P("wshard", None),
            P("wshard"),
            P("wshard", None),
            P("wshard", None),
            P("wshard", None),
        ),
        check_vma=False,
    )
```
